32 devices in a mesh: dom: 16 (over z, x, core), sub: 2 (over y).
Axes of the slice: x: 2, y: 2, z: 4, core: 2. Of those that a mesh axis runs over, the one named last changes fastest.
Arguments:
- element_load: float32 [16, 8, 16, 8, 128], P('dom', None, 'sub'), may hold values from -48 to 48
- mobility: float32 [16, 8, 16, 8, 128], P('dom', None, 'sub'), may hold values from 0.5 to 4
- metric: float32 [3, 16, 16, 16], P(None, 'dom', 'sub'), may hold values from 0.5 to 2
Outputs:
- pressure: float32 [16, 8, 16, 8, 128], P('dom', None, 'sub')
- coarse_residual: float32 [16, 16, 17], P('dom', 'sub')
The draws below stay inside these ranges and needn't reach their ends.
All inputs are finite; a program needn't handle non-finite values.
Results may differ from the reference program's by a relative error of at most 0.00008.
Values sent between devices are 32-bit elements; how exact they have to be, the bound alone decides.
No kernel may reach another device: no remote copies, remote signals or barrier semaphores. Data moves between devices by JAX's collectives and lax.ppermute only.
A program may use at most 64 MiB of HBM per device.

```python
import math
import jax
import jax.numpy as jnp
import numpy as np
from jax import lax

GLL_PTS = 8
EZ = 16
NX = 16
NY = 16
N_DOM = 16


def level_of(key, shape, split, least, largest):
    factor_of, own = 1.0, jax.random.fold_in(key, 6)
    for dim, blocks in split:
        steps = jnp.exp(jax.random.uniform(jax.random.fold_in(own, dim), (blocks,), jnp.float32, least / len(split), largest / len(split)))
        factor_of = factor_of * jnp.repeat(steps, shape[dim] // blocks).reshape([-1 if axis == dim else 1 for axis in range(len(shape))])
    return factor_of


def scatter_about(key, dims, scale, bound, cuts=(), dtype=jnp.bfloat16):
    gain = level_of(key, dims, cuts, -0.22, 0.18) if cuts else 1.0
    entries = jax.random.normal(key, dims, jnp.float32) * scale * gain
    return jnp.minimum(jnp.maximum(entries, -bound), bound).astype(dtype)


def setup_inputs(seed: int = 0) -> dict:
    seeds = jax.random.split(jax.random.key(seed), 4)
    element_load = scatter_about(seeds[0], (NX, GLL_PTS, NY, GLL_PTS, GLL_PTS * EZ), 8.0, 48.0, ((0, 16), (2, 2)), jnp.float32)
    mobility = jnp.clip(jnp.exp(math.log(4.0) - 2.0794415 * jax.random.uniform(seeds[1], (NX, GLL_PTS, NY, GLL_PTS, GLL_PTS * EZ), jnp.float32) ** level_of(seeds[1], (NX, GLL_PTS, NY, GLL_PTS, GLL_PTS * EZ), ((0, 16), (2, 2)), -0.2, 0.2)), 0.5, 4.0)
    metric = jnp.clip(jnp.exp(math.log(2.0) - 1.3862944 * jax.random.uniform(seeds[2], (3, NX, NY, EZ), jnp.float32) ** level_of(seeds[2], (3, NX, NY, EZ), ((1, 16), (2, 2)), -0.2, 0.2)), 0.5, 2.0)
    return {"element_load": element_load, "mobility": mobility, "metric": metric}


GLL_NODES = np.array([-1.0, -0.8717401485096066, -0.5917001814331423, -0.2092992179024789, 0.2092992179024789, 0.5917001814331423, 0.8717401485096066, 1.0])
GLL_WEIGHTS = np.array([0.03571428571428571, 0.2107042271435061, 0.3411226924835044, 0.4124587946587038, 0.4124587946587038, 0.3411226924835044, 0.2107042271435061, 0.03571428571428571])
THETA = 1.65
DELTA = 1.35
RHO_FIRST = DELTA / THETA
RHO_SECOND = 1.0 / (2.0 * THETA / DELTA - RHO_FIRST)
EXACT = lax.Precision.HIGHEST


def derivative_table():
    identity = np.eye(8)
    differences = GLL_NODES[:, None] - GLL_NODES[None, :] + identity
    barycentric = 1.0 / np.prod(differences, axis=1)
    matrix = (barycentric[None, :] / barycentric[:, None]) / differences
    matrix = matrix * (1.0 - identity)
    row_sums = np.sum(matrix, axis=1)
    return matrix - identity * row_sums[:, None]


def make_tables():
    derivative = jnp.asarray(derivative_table(), jnp.float32)
    weights = jnp.asarray(GLL_WEIGHTS, jnp.float32)
    coarse_basis = jnp.asarray(np.stack([(1.0 - GLL_NODES) / 8.0, (1.0 + GLL_NODES) / 8.0], axis=1), jnp.float32)
    return derivative, weights, coarse_basis


def point_factors(mobility, metric, weights):
    spread = jnp.repeat(metric, 8, axis=3)[:, :, None, :, None, :]
    layers_z = mobility.shape[-1] // 8
    z_weights = jnp.tile(weights, layers_z)
    quadrature = weights[:, None, None, None] * weights[None, None, :, None] * z_weights
    return spread * (mobility * quadrature)


def apply_local(values, factors, derivative):
    full_shape = values.shape
    per_cell = values.reshape(full_shape[:4] + (full_shape[4] // 8, 8))
    grad_x = jnp.einsum('ai,xiyjc->xayjc', derivative, values, precision=EXACT)
    grad_y = jnp.einsum('bj,xiyjc->xiybc', derivative, values, precision=EXACT)
    grad_z = jnp.einsum('ck,xiyjek->xiyjec', derivative, per_cell, precision=EXACT).reshape(full_shape)
    flux_x = factors[0] * grad_x
    flux_y = factors[1] * grad_y
    flux_z = (factors[2] * grad_z).reshape(per_cell.shape)
    back_x = jnp.einsum('ai,xayjc->xiyjc', derivative, flux_x, precision=EXACT)
    back_y = jnp.einsum('bj,xiybc->xiyjc', derivative, flux_y, precision=EXACT)
    back_z = jnp.einsum('ck,xiyjec->xiyjek', derivative, flux_z, precision=EXACT).reshape(full_shape)
    return back_x + back_y + back_z


def diagonal_of(factors, derivative):
    squared = derivative * derivative
    full_shape = factors.shape[1:]
    per_cell = factors[2].reshape(full_shape[:4] + (full_shape[4] // 8, 8))
    part_x = jnp.einsum('ai,xayjc->xiyjc', squared, factors[0], precision=EXACT)
    part_y = jnp.einsum('bj,xiybc->xiyjc', squared, factors[1], precision=EXACT)
    part_z = jnp.einsum('ck,xiyjec->xiyjek', squared, per_cell, precision=EXACT).reshape(full_shape)
    return part_x + part_y + part_z


def split_blocks(array):
    return array.reshape((N_DOM, array.shape[0] // N_DOM) + array.shape[1:])


def metric_blocks(metric):
    return jnp.moveaxis(metric.reshape((3, N_DOM, metric.shape[1] // N_DOM) + metric.shape[2:]), 1, 0)


def operator_pass(values, mobility, metric):
    derivative, weights, coarse_basis = make_tables()

    def one_block(pieces):
        factors = point_factors(pieces[1], pieces[2], weights)
        return apply_local(pieces[0], factors, derivative)

    result = lax.map(one_block, (split_blocks(values), split_blocks(mobility), metric_blocks(metric)))
    return result.reshape(values.shape)


def assemble(values):
    upper = values[:, 7]
    bottom = values[:, 0]
    new_upper = upper + jnp.roll(bottom, -1, axis=0)
    new_bottom = bottom + jnp.roll(upper, 1, axis=0)
    values = jnp.concatenate([new_bottom[:, None], values[:, 1:7], new_upper[:, None]], axis=1)
    upper = values[:, :, :, 7]
    bottom = values[:, :, :, 0]
    new_upper = upper + jnp.roll(bottom, -1, axis=2)
    new_bottom = bottom + jnp.roll(upper, 1, axis=2)
    values = jnp.concatenate([new_bottom[:, :, :, None], values[:, :, :, 1:7], new_upper[:, :, :, None]], axis=3)
    full_shape = values.shape
    per_cell = values.reshape(full_shape[:4] + (full_shape[4] // 8, 8))
    upper = per_cell[..., 7]
    bottom = per_cell[..., 0]
    wall_pad = jnp.zeros_like(upper[..., :1])
    new_upper = upper + jnp.concatenate([bottom[..., 1:], wall_pad], axis=-1)
    new_bottom = bottom + jnp.concatenate([wall_pad, upper[..., :-1]], axis=-1)
    per_cell = jnp.concatenate([new_bottom[..., None], per_cell[..., 1:7], new_upper[..., None]], axis=-1)
    return per_cell.reshape(full_shape)


def coarse_pass(final_local, coarse_basis):
    full_shape = final_local.shape
    per_cell = final_local.reshape(full_shape[:4] + (full_shape[4] // 8, 8))
    along_z = jnp.einsum('ks,xiyjek->xiyjes', coarse_basis, per_cell, precision=EXACT)
    corners = jnp.einsum('ip,jq,xiyjes->xpyqes', coarse_basis, coarse_basis, along_z, precision=EXACT)
    edge_pad = jnp.zeros_like(corners[..., :1, 0])
    vertex_z = jnp.concatenate([corners[..., 0], edge_pad], axis=-1) + jnp.concatenate([edge_pad, corners[..., 1]], axis=-1)
    vertex_y = vertex_z[:, :, :, 0] + jnp.roll(vertex_z[:, :, :, 1], 1, axis=2)
    return vertex_y[:, 0] + jnp.roll(vertex_y[:, 1], 1, axis=0)


def reference(element_load, mobility, metric):
    derivative, weights, coarse_basis = make_tables()

    def diag_block(pieces):
        return diagonal_of(point_factors(pieces[0], pieces[1], weights), derivative)

    diag_local = lax.map(diag_block, (split_blocks(mobility), metric_blocks(metric))).reshape(mobility.shape)
    right_side = assemble(element_load)
    inverse = 1.0 / assemble(diag_local)
    first_step = inverse * right_side / THETA
    resid_first = right_side - assemble(operator_pass(first_step, mobility, metric))
    pressure = first_step + (RHO_SECOND * RHO_FIRST * first_step + (2.0 * RHO_SECOND / DELTA) * (inverse * resid_first))
    final_local = element_load - operator_pass(pressure, mobility, metric)
    return pressure, coarse_pass(final_local, coarse_basis)
```

```python
import functools

import jax
import jax.numpy as jnp
import numpy as np
from jax import lax
from jax.experimental import pallas as pl
from jax.experimental.pallas import tpu as pltpu
from jax.sharding import PartitionSpec as P

GLL_NODES = np.array(
    [
        -1.0,
        -0.8717401485096066,
        -0.5917001814331423,
        -0.2092992179024789,
        0.2092992179024789,
        0.5917001814331423,
        0.8717401485096066,
        1.0,
    ]
)
GLL_WEIGHTS = np.array(
    [
        0.03571428571428571,
        0.2107042271435061,
        0.3411226924835044,
        0.4124587946587038,
        0.4124587946587038,
        0.3411226924835044,
        0.2107042271435061,
        0.03571428571428571,
    ]
)
THETA = 1.65
DELTA = 1.35
RHO_FIRST = DELTA / THETA
RHO_SECOND = 1.0 / (2.0 * THETA / DELTA - RHO_FIRST)
KEEP = 1.0 + RHO_SECOND * RHO_FIRST
GAIN = 2.0 * RHO_SECOND / DELTA
EXACT = lax.Precision.HIGHEST
PTS = 8
F32 = jnp.float32


def derivative_table():
    identity = np.eye(8)
    differences = GLL_NODES[:, None] - GLL_NODES[None, :] + identity
    barycentric = 1.0 / np.prod(differences, axis=1)
    matrix = barycentric[None, :] / barycentric[:, None] / differences
    matrix = matrix * (1.0 - identity)
    row_sums = np.sum(matrix, axis=1)
    return matrix - identity * row_sums[:, None]


D = derivative_table()
W = GLL_WEIGHTS
HAT = np.stack([(1.0 - GLL_NODES) / 8.0, (1.0 + GLL_NODES) / 8.0], axis=1)
SLOPE = (-0.125, 0.125)


def small_tables(width):
    cells = width // PTS
    grad = np.tile(D.T, (1, cells))
    back = np.tile(D, (1, cells))
    square = np.tile(D * D, (1, cells))
    weight = np.tile(W[None], (PTS, cells))
    return jnp.asarray(np.stack([grad, back, square, weight]), F32)


def restrict_tables(width):
    cells = width // PTS
    hat = np.zeros((width, 128))
    slope = np.zeros((width, 128))
    for c in range(cells):
        rows = slice(c * PTS, (c + 1) * PTS)
        hat[rows, c], hat[rows, c + 1] = HAT[:, 0], HAT[:, 1]
        slope[rows, c], slope[rows, c + 1] = SLOPE
    return jnp.asarray(np.stack([hat, slope]), F32)


def dot(a, b):
    return jnp.dot(a, b, precision=EXACT, preferred_element_type=F32)


def cell_blocks(rows):
    width = rows.shape[1]
    cell = lax.broadcasted_iota(jnp.int32, rows.shape, 1) // PTS
    return jnp.concatenate(
        [jnp.where(cell == g, rows, 0.0) for g in range(width // PTS)], axis=0
    )


def contract(matrix, lines, parity):
    n = len(lines)
    half = n // 2
    plus = [lines[c] + lines[n - 1 - c] for c in range(half)]
    minus = [lines[c] - lines[n - 1 - c] for c in range(half)]
    top, low = [], []
    for r in range(half):
        even = sum(float(0.5 * (matrix[r, c] + matrix[r, n - 1 - c])) * plus[c] for c in range(half))
        odd = sum(float(0.5 * (matrix[r, c] - matrix[r, n - 1 - c])) * minus[c] for c in range(half))
        top.append(even + odd)
        low.append(even - odd if parity > 0 else odd - even)
    return top + low[::-1]


def spread_metric(metric, weight_row):
    cells = metric.shape[2]
    width = weight_row.shape[1]
    cell = lax.broadcasted_iota(jnp.int32, (cells, width), 1) // PTS
    row = lax.broadcasted_iota(jnp.int32, (cells, width), 0)
    pick = jnp.where(cell == row, 1.0, 0.0).astype(F32)
    return [dot(metric[d], pick) * weight_row for d in range(3)]


def column_masks(shape):
    lane = lax.broadcasted_iota(jnp.int32, shape, len(shape) - 1)
    up = (lane % PTS == PTS - 1) & (lane != shape[-1] - 1)
    down = (lane % PTS == 0) & (lane != 0)
    return up, down


def sum_z(v, masks):
    width = v.shape[-1]
    axis = v.ndim - 1
    up = pltpu.roll(v, width - 1, axis)
    down = pltpu.roll(v, 1, axis)
    return v + jnp.where(masks[0], up, jnp.where(masks[1], down, 0.0))


def sum_y_local(ref, ny):
    for i in range(PTS):
        low, high = ref[i, 0], ref[i, PTS - 1]
        row = lax.broadcasted_iota(jnp.int32, low.shape, 0)
        ref[i, PTS - 1] = high + jnp.where(row == ny - 1, 0.0, pltpu.roll(low, ny - 1, 0))
        ref[i, 0] = low + jnp.where(row == 0, 0.0, pltpu.roll(high, 1, 0))


def edge_planes(ref, ny):
    low = jnp.concatenate([ref[i, 0, 0:1] for i in range(PTS)], axis=0)
    high = jnp.concatenate([ref[i, PTS - 1, ny - 1 : ny] for i in range(PTS)], axis=0)
    return low, high


def stiffness(v_ref, mob, spread, out_ref, work_ref, tables):
    grad = cell_blocks(tables[0])
    back = cell_blocks(tables[1])
    _, _, ny, width = v_ref.shape
    for j in range(PTS):
        flux = contract(D, [v_ref[i, j] for i in range(PTS)], -1)
        flux = [flux[i] * (mob(i, j) * (float(W[i] * W[j]) * spread[0])) for i in range(PTS)]
        for i, value in enumerate(contract(D.T, flux, -1)):
            out_ref[i, j] = value
    for i in range(PTS):
        flux = contract(D, [v_ref[i, j] for j in range(PTS)], -1)
        flux = [flux[j] * (mob(i, j) * (float(W[i] * W[j]) * spread[1])) for j in range(PTS)]
        for j, value in enumerate(contract(D.T, flux, -1)):
            out_ref[i, j] += value
    for i in range(PTS):
        work_ref[i] = dot(v_ref[i].reshape(PTS * ny, width), grad).reshape(PTS, ny, width)
        for j in range(PTS):
            work_ref[i, j] *= mob(i, j) * (float(W[i] * W[j]) * spread[2])
        out_ref[i] += dot(work_ref[i].reshape(PTS * ny, width), back).reshape(PTS, ny, width)


def plane(ref, ny):
    return lambda i, j: ref[i, pl.ds(j, ny, stride=PTS)]


def diag_kernel(load_ref, mob_ref, metric_ref, tab_ref, fields_ref, xface_ref, yface_ref):
    tables = tab_ref[...]
    ny, width = fields_ref.shape[3:]
    spread = spread_metric(metric_ref[...], tables[3])
    squared = cell_blocks(tables[2])
    square = D * D
    mob, load = plane(mob_ref, ny), plane(load_ref, ny)
    diag_ref = fields_ref.at[1]
    for j in range(PTS):
        factor = [mob(i, j) * (float(W[i] * W[j]) * spread[0]) for i in range(PTS)]
        for i, value in enumerate(contract(square.T, factor, 1)):
            diag_ref[i, j] = value
    for i in range(PTS):
        factor = [mob(i, j) * (float(W[i] * W[j]) * spread[1]) for j in range(PTS)]
        for j, value in enumerate(contract(square.T, factor, 1)):
            diag_ref[i, j] += value
    for i in range(PTS):
        factor = jnp.concatenate(
            [mob(i, j) * (float(W[i] * W[j]) * spread[2]) for j in range(PTS)], axis=0
        )
        diag_ref[i] += dot(factor, squared).reshape(PTS, ny, width)
        fields_ref[0, i] = jnp.stack([load(i, j) for j in range(PTS)], axis=0)
    masks = column_masks((PTS, ny, width))
    for f in range(2):
        for i in range(PTS):
            fields_ref[f, i] = sum_z(fields_ref[f, i], masks)
        sum_y_local(fields_ref.at[f], ny)
        xface_ref[f, 0] = fields_ref[f, 0]
        xface_ref[f, 1] = fields_ref[f, PTS - 1]
        yface_ref[0, f], yface_ref[1, f] = edge_planes(fields_ref.at[f], ny)


def merge_kernel(side_ref, xface_ref, below_ref, above_ref, first_ref, second_ref):
    even = side_ref[0] == 0
    fields, _, _, ny, width = xface_ref.shape
    row = lax.broadcasted_iota(jnp.int32, (ny, width), 0)
    for f in range(fields):
        for j in range(PTS):
            low, high = xface_ref[f, 0, j], xface_ref[f, 1, j]
            if j == 0:
                low = low + jnp.where(row == 0, below_ref[f, 0:1], 0.0)
                high = high + jnp.where(row == 0, below_ref[f, PTS - 1 : PTS], 0.0)
            if j == PTS - 1:
                low = low + jnp.where(row == ny - 1, above_ref[f, 0:1], 0.0)
                high = high + jnp.where(row == ny - 1, above_ref[f, PTS - 1 : PTS], 0.0)
            first_ref[f, j] = jnp.where(even, high, low)
            second_ref[f, j] = jnp.where(even, low, high)


def add_arrivals(get, put, f, even, below_ref, above_ref, first_ref, second_ref, ny, width):
    row = lax.broadcasted_iota(jnp.int32, (ny, width), 0)
    for i in range(PTS):
        put(i, 0, get(i, 0) + jnp.where(row == 0, below_ref[f, i : i + 1], 0.0))
        put(
            i,
            PTS - 1,
            get(i, PTS - 1) + jnp.where(row == ny - 1, above_ref[f, i : i + 1], 0.0),
        )
    for j in range(PTS):
        first, second = first_ref[f, j], second_ref[f, j]
        put(0, j, get(0, j) + jnp.where(even, second, first))
        put(PTS - 1, j, get(PTS - 1, j) + jnp.where(even, first, second))


def smooth_kernel(
    side_ref, fields_ref, mob_ref, metric_ref, tab_ref, below_ref, above_ref, first_ref, second_ref,
    partial_ref, gain_ref, xface_ref, yface_ref, value_ref, out_ref, work_ref,
):
    tables = tab_ref[...]
    ny, width = out_ref.shape[2:]
    spread = spread_metric(metric_ref[...], tables[3])
    even = side_ref[0] == 0
    mob = plane(mob_ref, ny)
    for f, ref in ((0, partial_ref), (1, gain_ref)):
        for i in range(PTS):
            ref[i] = fields_ref[f, i]

        def put(i, j, value, ref=ref):
            ref[i, j] = value

        add_arrivals(
            lambda i, j, ref=ref: ref[i, j], put, f, even,
            below_ref, above_ref, first_ref, second_ref, ny, width,
        )
    for i in range(PTS):
        inverse = 1.0 / gain_ref[i]
        right = partial_ref[i]
        value = inverse * right * (1.0 / THETA)
        value_ref[i] = value
        partial_ref[i] = KEEP * value + GAIN * (inverse * right)
        gain_ref[i] = GAIN * inverse
    stiffness(value_ref, mob, spread, out_ref, work_ref, tables)
    masks = column_masks((PTS, ny, width))
    for i in range(PTS):
        out_ref[i] = sum_z(out_ref[i], masks)
    sum_y_local(out_ref, ny)
    xface_ref[0, 0] = out_ref[0]
    xface_ref[0, 1] = out_ref[PTS - 1]
    yface_ref[0, 0], yface_ref[1, 0] = edge_planes(out_ref, ny)
    for i in range(PTS):
        partial_ref[i] -= gain_ref[i] * out_ref[i]


def coarse_kernel(
    side_ref, load_ref, partial_ref, gain_ref, mob_ref, metric_ref, tab_ref, restrict_ref,
    below_ref, above_ref, first_ref, second_ref,
    pressure_ref, planes_ref, tops_ref, value_ref, work_ref,
):
    tables = tab_ref[...]
    ny, width = value_ref.shape[2:]
    spread = spread_metric(metric_ref[...], tables[3])
    even = side_ref[0] == 0
    mob, load = plane(mob_ref, ny), plane(load_ref, ny)
    row = lax.broadcasted_iota(jnp.int32, (ny, width), 0)
    for i in range(PTS):
        value_ref[i] = partial_ref[i]
    for i in range(PTS):
        value_ref[i, 0] -= gain_ref[i, 0] * jnp.where(row == 0, below_ref[0, i : i + 1], 0.0)
        value_ref[i, PTS - 1] -= gain_ref[i, PTS - 1] * jnp.where(
            row == ny - 1, above_ref[0, i : i + 1], 0.0
        )
    for j in range(PTS):
        first, second = first_ref[0, j], second_ref[0, j]
        value_ref[0, j] -= gain_ref[0, j] * jnp.where(even, second, first)
        value_ref[PTS - 1, j] -= gain_ref[PTS - 1, j] * jnp.where(even, first, second)
    for i in range(PTS):
        for j in range(PTS):
            pressure_ref[i, pl.ds(j, ny, stride=PTS)] = value_ref[i, j]
    grad = cell_blocks(tables[0])
    zero = jnp.zeros((ny, width), F32)
    smooth = {(p, q): zero for p in range(2) for q in range(2)}
    slope = {(p, q): zero for p in range(2) for q in range(2)}
    for j in range(PTS):
        flux = contract(D, [value_ref[i, j] for i in range(PTS)], -1)
        total = sum(flux[i] * mob(i, j) * float(W[i] * W[j]) for i in range(PTS)) * spread[0]
        for p in range(2):
            for q in range(2):
                smooth[p, q] -= float(SLOPE[p] * HAT[j, q]) * total
    for i in range(PTS):
        flux = contract(D, [value_ref[i, j] for j in range(PTS)], -1)
        total = sum(flux[j] * mob(i, j) * float(W[i] * W[j]) for j in range(PTS)) * spread[1]
        for p in range(2):
            for q in range(2):
                smooth[p, q] -= float(HAT[i, p] * SLOPE[q]) * total
    for i in range(PTS):
        work_ref[i] = dot(value_ref[i].reshape(PTS * ny, width), grad).reshape(PTS, ny, width)
        flux = [work_ref[i, j] * mob(i, j) for j in range(PTS)]
        for q in range(2):
            total = sum(float(W[i] * W[j] * HAT[j, q]) * flux[j] for j in range(PTS))
            from_load = sum(float(HAT[j, q]) * load(i, j) for j in range(PTS))
            for p in range(2):
                slope[p, q] += float(HAT[i, p]) * total
                smooth[p, q] += float(HAT[i, p]) * from_load
    keys = [(p, q) for p in range(2) for q in range(2)]
    corners = dot(jnp.concatenate([smooth[k] for k in keys], axis=0), restrict_ref[0]) - dot(
        jnp.concatenate([slope[k] * spread[2] for k in keys], axis=0), restrict_ref[1]
    )
    row = lax.broadcasted_iota(jnp.int32, (ny, corners.shape[1]), 0)
    for p in range(2):
        lower = corners[(2 * p) * ny : (2 * p + 1) * ny]
        upper = corners[(2 * p + 1) * ny : (2 * p + 2) * ny]
        planes_ref[p] = lower + jnp.where(row == 0, 0.0, pltpu.roll(upper, 1, 0))
        tops_ref[p : p + 1] = upper[ny - 1 : ny]


def call(body, outs, scratch, *args):
    specs = [
        pl.BlockSpec(memory_space=pltpu.SMEM if a.dtype == jnp.int32 else pltpu.VMEM) for a in args
    ]
    return pl.pallas_call(
        body,
        out_shape=[jax.ShapeDtypeStruct(s, F32) for s in outs],
        in_specs=specs,
        out_specs=[pl.BlockSpec(memory_space=pltpu.VMEM) for _ in outs],
        scratch_shapes=[pltpu.VMEM(s, F32) for s in scratch],
        compiler_params=pltpu.CompilerParams(vmem_limit_bytes=16 * 1024 * 1024),
    )(*args)


def from_y(faces):
    size = lax.axis_size("sub")
    if size == 2:
        got = lax.ppermute(faces, "sub", [(0, 1), (1, 0)])
        return got[1], got[0]
    below = lax.ppermute(faces[1], "sub", [(i, (i + 1) % size) for i in range(size)])
    above = lax.ppermute(faces[0], "sub", [(i, (i - 1) % size) for i in range(size)])
    return below, above


def inner_pairs(size):
    return [(i, i ^ 1) for i in range(size)]


def outer_pairs(size):
    return [(i, (i + 1) % size if i % 2 else (i - 1) % size) for i in range(size)]


def exchange(side, xface, yface):
    size = lax.axis_size("dom")
    below, above = from_y(yface)
    face = (xface.shape[0],) + xface.shape[2:]
    first, second = call(merge_kernel, [face, face], [], side, xface, below, above)
    second = lax.ppermute(second, "dom", outer_pairs(size))
    first = lax.ppermute(first, "dom", inner_pairs(size))
    return below, above, first, second


def shards(element_load, mobility, metric):
    _, _, ny, _, width = element_load.shape
    load = element_load.reshape(PTS, ny * PTS, width)
    mob = mobility.reshape(PTS, ny * PTS, width)
    metric = metric[:, 0]
    side = (lax.axis_index("dom") % 2).astype(jnp.int32).reshape(1)
    tables = small_tables(width)
    restrict = restrict_tables(width)
    field = (PTS, PTS, ny, width)
    face = (PTS, ny, width)
    fields, xface, yface = call(
        diag_kernel,
        [(2,) + field, (2, 2) + face, (2, 2, PTS, width)],
        [],
        load, mob, metric, tables,
    )
    arrivals = exchange(side, xface, yface)
    partial, gain, xface, yface = call(
        smooth_kernel,
        [field, field, (1, 2) + face, (2, 1, PTS, width)],
        [field, field, field],
        side, fields, mob, metric, tables, *arrivals,
    )
    arrivals = exchange(side, xface, yface)
    pressure, planes, tops = call(
        coarse_kernel,
        [(PTS, ny * PTS, width), (2, ny, 128), (2, 128)],
        [field, field],
        side, load, partial, gain, mob, metric, tables, restrict, *arrivals,
    )
    size = lax.axis_size("sub")
    below = lax.ppermute(tops, "sub", [(i, (i + 1) % size) for i in range(size)])
    planes = planes.at[:, 0].add(below)
    size = lax.axis_size("dom")
    upper = planes[1]
    outer = lax.ppermute(upper, "dom", [p for p in outer_pairs(size) if p[0] % 2 == 1])
    inner = lax.ppermute(upper, "dom", [p for p in inner_pairs(size) if p[0] % 2 == 0])
    coarse = planes[0] + (inner + outer)
    coarse = coarse[None, :, : width // PTS + 1]
    return pressure.reshape(element_load.shape), coarse


def solution(mesh):
    in_specs = (
        P("dom", None, "sub", None, None),
        P("dom", None, "sub", None, None),
        P(None, "dom", "sub", None),
    )
    out_specs = (P("dom", None, "sub", None, None), P("dom", "sub", None))
    return jax.shard_map(shards, mesh=mesh, in_specs=in_specs, out_specs=out_specs, check_vma=False)
```

```python
import jax
import jax.numpy as jnp
import numpy as np
from jax import lax
from jax.experimental import pallas as pl
from jax.experimental.pallas import tpu as pltpu
from jax.sharding import PartitionSpec as P

GLL_NODES = np.array(
    [
        -1.0,
        -0.8717401485096066,
        -0.5917001814331423,
        -0.2092992179024789,
        0.2092992179024789,
        0.5917001814331423,
        0.8717401485096066,
        1.0,
    ]
)
GLL_WEIGHTS = np.array(
    [
        0.03571428571428571,
        0.2107042271435061,
        0.3411226924835044,
        0.4124587946587038,
        0.4124587946587038,
        0.3411226924835044,
        0.2107042271435061,
        0.03571428571428571,
    ]
)
THETA = 1.65
DELTA = 1.35
RHO_FIRST = DELTA / THETA
RHO_SECOND = 1.0 / (2.0 * THETA / DELTA - RHO_FIRST)
KEEP = 1.0 + RHO_SECOND * RHO_FIRST
GAIN = 2.0 * RHO_SECOND / DELTA
EXACT = lax.Precision.HIGHEST
PTS = 8
F32 = jnp.float32


def derivative_table():
    identity = np.eye(8)
    differences = GLL_NODES[:, None] - GLL_NODES[None, :] + identity
    barycentric = 1.0 / np.prod(differences, axis=1)
    matrix = barycentric[None, :] / barycentric[:, None] / differences
    matrix = matrix * (1.0 - identity)
    row_sums = np.sum(matrix, axis=1)
    return matrix - identity * row_sums[:, None]


D = derivative_table()
W = GLL_WEIGHTS
HAT = np.stack([(1.0 - GLL_NODES) / 8.0, (1.0 + GLL_NODES) / 8.0], axis=1)
SLOPE = (-0.125, 0.125)


def small_tables(width):
    cells = width // PTS
    grad = np.tile(D.T, (1, cells))
    back = np.tile(D, (1, cells))
    square = np.tile(D * D, (1, cells))
    weight = np.tile(W[None], (PTS, cells))
    return jnp.asarray(np.stack([grad, back, square, weight]), F32)


def restrict_tables(width):
    cells = width // PTS
    hat = np.zeros((width, 128))
    slope = np.zeros((width, 128))
    for c in range(cells):
        rows = slice(c * PTS, (c + 1) * PTS)
        hat[rows, c], hat[rows, c + 1] = HAT[:, 0], HAT[:, 1]
        slope[rows, c], slope[rows, c + 1] = SLOPE
    return jnp.asarray(np.stack([hat, slope]), F32)


def dot(a, b):
    return jnp.dot(a, b, precision=EXACT, preferred_element_type=F32)


def halves(a):
    high = a.astype(jnp.bfloat16)
    return high, (a - high.astype(F32)).astype(jnp.bfloat16)


def paired(b):
    high, low = halves(b)
    return jnp.concatenate(
        [
            jnp.concatenate([high, low], axis=1),
            jnp.concatenate([high, jnp.zeros_like(low)], axis=1),
        ],
        axis=0,
    )


def dot_split(a, b_pair):
    both = jnp.dot(
        jnp.concatenate(halves(a), axis=1), b_pair, preferred_element_type=F32
    )
    n = both.shape[1] // 2
    return both[:, :n] + both[:, n:]


def cell_blocks(rows):
    width = rows.shape[1]
    cell = lax.broadcasted_iota(jnp.int32, rows.shape, 1) // PTS
    return jnp.concatenate(
        [jnp.where(cell == g, rows, 0.0) for g in range(width // PTS)], axis=0
    )


def contract(matrix, lines, parity):
    n = len(lines)
    half = n // 2
    plus = [lines[c] + lines[n - 1 - c] for c in range(half)]
    minus = [lines[c] - lines[n - 1 - c] for c in range(half)]
    top, low = [], []
    for r in range(half):
        even = sum(float(0.5 * (matrix[r, c] + matrix[r, n - 1 - c])) * plus[c] for c in range(half))
        odd = sum(float(0.5 * (matrix[r, c] - matrix[r, n - 1 - c])) * minus[c] for c in range(half))
        top.append(even + odd)
        low.append(even - odd if parity > 0 else odd - even)
    return top + low[::-1]


def spread_metric(metric, weight_row):
    cells = metric.shape[2]
    width = weight_row.shape[1]
    cell = lax.broadcasted_iota(jnp.int32, (cells, width), 1) // PTS
    row = lax.broadcasted_iota(jnp.int32, (cells, width), 0)
    pick = jnp.where(cell == row, 1.0, 0.0).astype(F32)
    return [dot(metric[d], pick) * weight_row for d in range(3)]


def column_masks(shape):
    lane = lax.broadcasted_iota(jnp.int32, shape, len(shape) - 1)
    up = (lane % PTS == PTS - 1) & (lane != shape[-1] - 1)
    down = (lane % PTS == 0) & (lane != 0)
    return up, down


def sum_z(v, masks):
    width = v.shape[-1]
    axis = v.ndim - 1
    up = pltpu.roll(v, width - 1, axis)
    down = pltpu.roll(v, 1, axis)
    return v + jnp.where(masks[0], up, jnp.where(masks[1], down, 0.0))


def sum_y_local(ref, ny):
    for i in range(PTS):
        low, high = ref[i, 0], ref[i, PTS - 1]
        row = lax.broadcasted_iota(jnp.int32, low.shape, 0)
        ref[i, PTS - 1] = high + jnp.where(row == ny - 1, 0.0, pltpu.roll(low, ny - 1, 0))
        ref[i, 0] = low + jnp.where(row == 0, 0.0, pltpu.roll(high, 1, 0))


def edge_planes(ref, ny):
    low = jnp.concatenate([ref[i, 0, 0:1] for i in range(PTS)], axis=0)
    high = jnp.concatenate([ref[i, PTS - 1, ny - 1 : ny] for i in range(PTS)], axis=0)
    return low, high


def stiffness(v_ref, mob, spread, out_ref, work_ref, tables):
    grad = paired(cell_blocks(tables[0]))
    back = paired(cell_blocks(tables[1]))
    _, _, ny, width = v_ref.shape
    for j in range(PTS):
        flux = contract(D, [v_ref[i, j] for i in range(PTS)], -1)
        flux = [flux[i] * (mob(i, j) * (float(W[i] * W[j]) * spread[0])) for i in range(PTS)]
        for i, value in enumerate(contract(D.T, flux, -1)):
            out_ref[i, j] = value
    for i in range(PTS):
        flux = contract(D, [v_ref[i, j] for j in range(PTS)], -1)
        flux = [flux[j] * (mob(i, j) * (float(W[i] * W[j]) * spread[1])) for j in range(PTS)]
        for j, value in enumerate(contract(D.T, flux, -1)):
            out_ref[i, j] += value
    for i in range(PTS):
        work_ref[i] = dot_split(v_ref[i].reshape(PTS * ny, width), grad).reshape(PTS, ny, width)
        for j in range(PTS):
            work_ref[i, j] *= mob(i, j) * (float(W[i] * W[j]) * spread[2])
        out_ref[i] += dot_split(work_ref[i].reshape(PTS * ny, width), back).reshape(PTS, ny, width)


def plane(ref, ny):
    return lambda i, j: ref[i, pl.ds(j, ny, stride=PTS)]


def edge_kernel(
    load_in, mob_in, metric_in, tab_in, restrict_in,
    load_ref, mob_ref, spread_ref, tab_ref, restrict_ref, yface_ref, metric_ref, sems,
):
    copies = [
        pltpu.make_async_copy(source, target, sems.at[n])
        for n, (source, target) in enumerate(
            [
                (tab_in, tab_ref),
                (metric_in, metric_ref),
                (mob_in, mob_ref),
                (load_in, load_ref),
                (restrict_in, restrict_ref),
            ]
        )
    ]
    for copy in copies:
        copy.start()
    copies[0].wait()
    copies[1].wait()
    ny, width = spread_ref.shape[1:]
    tables = tab_ref[...]
    spread = spread_metric(metric_ref[...], tables[3])
    for d in range(3):
        spread_ref[d] = spread[d]
    squared = paired(cell_blocks(tables[2]))
    square = D * D
    mob, load = plane(mob_ref, ny), plane(load_ref, ny)
    masks = column_masks((PTS * ny, width))
    copies[2].wait()
    ends = (0, PTS - 1)
    sums = [[], []]
    for i in range(PTS):
        factor = [mob(i, j) * (float(W[i]) * spread[1]) for j in range(PTS)]
        for s in range(2):
            sums[s].append(sum(float(square[j, ends[s]] * W[j]) * factor[j] for j in range(PTS)))
    for s in range(2):
        j = ends[s]
        points = [mob(i, j) * float(W[i] * W[j]) for i in range(PTS)]
        along = contract(square.T, [p * spread[0] for p in points], 1)
        column = dot_split(jnp.concatenate([p * spread[2] for p in points], axis=0), squared)
        total = column + jnp.concatenate([along[i] + sums[s][i] for i in range(PTS)], axis=0)
        total = sum_z(total, masks)
        e = 0 if s == 0 else ny - 1
        yface_ref[s, 1] = jnp.concatenate(
            [total[i * ny + e : i * ny + e + 1] for i in range(PTS)], axis=0
        )
    copies[3].wait()
    for s in range(2):
        e = 0 if s == 0 else ny - 1
        row = e * PTS + ends[s]
        value = jnp.concatenate([load_ref[i, row : row + 1] for i in range(PTS)], axis=0)
        yface_ref[s, 0] = sum_z(value, column_masks((PTS, width)))
    copies[4].wait()


def diag_kernel(load_ref, mob_ref, spread_ref, tab_ref, fields_ref, xface_ref):
    tables = tab_ref[...]
    ny, width = fields_ref.shape[3:]
    spread = [spread_ref[d] for d in range(3)]
    squared = paired(cell_blocks(tables[2]))
    square = D * D
    mob, load = plane(mob_ref, ny), plane(load_ref, ny)
    diag_ref = fields_ref.at[1]
    for j in range(PTS):
        factor = [mob(i, j) * (float(W[i] * W[j]) * spread[0]) for i in range(PTS)]
        for i, value in enumerate(contract(square.T, factor, 1)):
            diag_ref[i, j] = value
    for i in range(PTS):
        factor = [mob(i, j) * (float(W[i] * W[j]) * spread[1]) for j in range(PTS)]
        for j, value in enumerate(contract(square.T, factor, 1)):
            diag_ref[i, j] += value
    for i in range(PTS):
        factor = jnp.concatenate(
            [mob(i, j) * (float(W[i] * W[j]) * spread[2]) for j in range(PTS)], axis=0
        )
        diag_ref[i] += dot_split(factor, squared).reshape(PTS, ny, width)
        fields_ref[0, i] = jnp.stack([load(i, j) for j in range(PTS)], axis=0)
    masks = column_masks((PTS, ny, width))
    for f in range(2):
        for i in range(PTS):
            fields_ref[f, i] = sum_z(fields_ref[f, i], masks)
        sum_y_local(fields_ref.at[f], ny)
        xface_ref[f, 0] = fields_ref[f, 0]
        xface_ref[f, 1] = fields_ref[f, PTS - 1]


def merge_kernel(side_ref, xface_ref, below_ref, above_ref, outer_ref, inner_ref):
    even = side_ref[0] == 0
    fields, _, _, ny, width = xface_ref.shape
    row = lax.broadcasted_iota(jnp.int32, (ny, width), 0)
    for f in range(fields):
        for j in range(PTS):
            low, high = xface_ref[f, 0, j], xface_ref[f, 1, j]
            if j == 0:
                low = low + jnp.where(row == 0, below_ref[f, 0:1], 0.0)
                high = high + jnp.where(row == 0, below_ref[f, PTS - 1 : PTS], 0.0)
            if j == PTS - 1:
                low = low + jnp.where(row == ny - 1, above_ref[f, 0:1], 0.0)
                high = high + jnp.where(row == ny - 1, above_ref[f, PTS - 1 : PTS], 0.0)
            inner_ref[f, j] = jnp.where(even, high, low)
            outer_ref[f, j] = jnp.where(even, low, high)


def add_arrivals(get, put, f, even, below_ref, above_ref, outer_ref, inner_ref, ny, width):
    row = lax.broadcasted_iota(jnp.int32, (ny, width), 0)
    for i in range(PTS):
        put(i, 0, get(i, 0) + jnp.where(row == 0, below_ref[f, i : i + 1], 0.0))
        put(
            i,
            PTS - 1,
            get(i, PTS - 1) + jnp.where(row == ny - 1, above_ref[f, i : i + 1], 0.0),
        )
    for j in range(PTS):
        inner, outer = inner_ref[f, j], outer_ref[f, j]
        put(0, j, get(0, j) + jnp.where(even, outer, inner))
        put(PTS - 1, j, get(PTS - 1, j) + jnp.where(even, inner, outer))


def smooth_kernel(
    side_ref, fields_ref, mob_ref, spread_ref, tab_ref, below_ref, above_ref, outer_ref, inner_ref,
    partial_ref, gain_ref, xface_ref, yface_ref, value_ref, out_ref, work_ref,
):
    tables = tab_ref[...]
    ny, width = out_ref.shape[2:]
    spread = [spread_ref[d] for d in range(3)]
    even = side_ref[0] == 0
    mob = plane(mob_ref, ny)
    for f, ref in ((0, partial_ref), (1, gain_ref)):
        for i in range(PTS):
            ref[i] = fields_ref[f, i]

        def put(i, j, value, ref=ref):
            ref[i, j] = value

        add_arrivals(
            lambda i, j, ref=ref: ref[i, j], put, f, even,
            below_ref, above_ref, outer_ref, inner_ref, ny, width,
        )
    for i in range(PTS):
        inverse = 1.0 / gain_ref[i]
        right = partial_ref[i]
        value = inverse * right * (1.0 / THETA)
        value_ref[i] = value
        partial_ref[i] = KEEP * value + GAIN * (inverse * right)
        gain_ref[i] = GAIN * inverse
    stiffness(value_ref, mob, spread, out_ref, work_ref, tables)
    masks = column_masks((PTS, ny, width))
    for i in range(PTS):
        out_ref[i] = sum_z(out_ref[i], masks)
    sum_y_local(out_ref, ny)
    xface_ref[0, 0] = out_ref[0]
    xface_ref[0, 1] = out_ref[PTS - 1]
    yface_ref[0, 0], yface_ref[1, 0] = edge_planes(out_ref, ny)
    for i in range(PTS):
        partial_ref[i] -= gain_ref[i] * out_ref[i]


def coarse_kernel(
    side_ref, load_ref, partial_ref, gain_ref, mob_ref, spread_ref, tab_ref, restrict_ref,
    below_ref, above_ref, outer_ref, inner_ref,
    pressure_out, planes_ref, tops_ref, value_ref, work_ref, pressure_ref, sem,
):
    tables = tab_ref[...]
    ny, width = value_ref.shape[2:]
    spread = [spread_ref[d] for d in range(3)]
    even = side_ref[0] == 0
    mob, load = plane(mob_ref, ny), plane(load_ref, ny)
    row = lax.broadcasted_iota(jnp.int32, (ny, width), 0)
    for i in range(PTS):
        value_ref[i] = partial_ref[i]
    for i in range(PTS):
        value_ref[i, 0] -= gain_ref[i, 0] * jnp.where(row == 0, below_ref[0, i : i + 1], 0.0)
        value_ref[i, PTS - 1] -= gain_ref[i, PTS - 1] * jnp.where(
            row == ny - 1, above_ref[0, i : i + 1], 0.0
        )
    for j in range(PTS):
        inner, outer = inner_ref[0, j], outer_ref[0, j]
        value_ref[0, j] -= gain_ref[0, j] * jnp.where(even, outer, inner)
        value_ref[PTS - 1, j] -= gain_ref[PTS - 1, j] * jnp.where(even, inner, outer)
    for i in range(PTS):
        for j in range(PTS):
            pressure_ref[i, pl.ds(j, ny, stride=PTS)] = value_ref[i, j]
    copy = pltpu.make_async_copy(pressure_ref, pressure_out, sem)
    copy.start()
    grad = paired(cell_blocks(tables[0]))
    zero = jnp.zeros((ny, width), F32)
    smooth = {(p, q): zero for p in range(2) for q in range(2)}
    slope = {(p, q): zero for p in range(2) for q in range(2)}
    for j in range(PTS):
        flux = contract(D, [value_ref[i, j] for i in range(PTS)], -1)
        total = sum(flux[i] * mob(i, j) * float(W[i] * W[j]) for i in range(PTS)) * spread[0]
        for p in range(2):
            for q in range(2):
                smooth[p, q] -= float(SLOPE[p] * HAT[j, q]) * total
    for i in range(PTS):
        flux = contract(D, [value_ref[i, j] for j in range(PTS)], -1)
        total = sum(flux[j] * mob(i, j) * float(W[i] * W[j]) for j in range(PTS)) * spread[1]
        for p in range(2):
            for q in range(2):
                smooth[p, q] -= float(HAT[i, p] * SLOPE[q]) * total
    for i in range(PTS):
        work_ref[i] = dot_split(value_ref[i].reshape(PTS * ny, width), grad).reshape(PTS, ny, width)
        flux = [work_ref[i, j] * mob(i, j) for j in range(PTS)]
        for q in range(2):
            total = sum(float(W[i] * W[j] * HAT[j, q]) * flux[j] for j in range(PTS))
            from_load = sum(float(HAT[j, q]) * load(i, j) for j in range(PTS))
            for p in range(2):
                slope[p, q] += float(HAT[i, p]) * total
                smooth[p, q] += float(HAT[i, p]) * from_load
    keys = [(p, q) for p in range(2) for q in range(2)]
    corners = dot(jnp.concatenate([smooth[k] for k in keys], axis=0), restrict_ref[0]) - dot(
        jnp.concatenate([slope[k] * spread[2] for k in keys], axis=0), restrict_ref[1]
    )
    row = lax.broadcasted_iota(jnp.int32, (ny, corners.shape[1]), 0)
    for p in range(2):
        lower = corners[(2 * p) * ny : (2 * p + 1) * ny]
        upper = corners[(2 * p + 1) * ny : (2 * p + 2) * ny]
        planes_ref[p] = lower + jnp.where(row == 0, 0.0, pltpu.roll(upper, 1, 0))
        tops_ref[p : p + 1] = upper[ny - 1 : ny]
    copy.wait()


def call(body, outs, scratch, *args, spaces=None, out_spaces=None):
    spaces = spaces or [pltpu.SMEM if a.dtype == jnp.int32 else pltpu.VMEM for a in args]
    return pl.pallas_call(
        body,
        out_shape=[jax.ShapeDtypeStruct(s, F32) for s in outs],
        in_specs=[pl.BlockSpec(memory_space=m) for m in spaces],
        out_specs=[pl.BlockSpec(memory_space=m) for m in out_spaces or [pltpu.VMEM] * len(outs)],
        scratch_shapes=[pltpu.VMEM(s, F32) if isinstance(s, tuple) else s for s in scratch],
        compiler_params=pltpu.CompilerParams(vmem_limit_bytes=16 * 1024 * 1024),
    )(*args)


def from_y(faces):
    size = lax.axis_size("sub")
    if size == 2:
        got = lax.ppermute(faces, "sub", [(0, 1), (1, 0)])
        return got[1], got[0]
    below = lax.ppermute(faces[1], "sub", [(i, (i + 1) % size) for i in range(size)])
    above = lax.ppermute(faces[0], "sub", [(i, (i - 1) % size) for i in range(size)])
    return below, above


def inner_pairs(size):
    return [(i, i ^ 1) for i in range(size)]


def outer_pairs(size):
    return [(i, (i + 1) % size if i % 2 else (i - 1) % size) for i in range(size)]


def exchange_x(side, xface, below, above):
    size = lax.axis_size("dom")
    face = (xface.shape[0],) + xface.shape[2:]
    outer, inner = call(merge_kernel, [face, face], [], side, xface, below, above)
    outer = lax.ppermute(outer, "dom", outer_pairs(size))
    inner = lax.ppermute(inner, "dom", inner_pairs(size))
    return below, above, outer, inner


def shards(element_load, mobility, metric):
    _, _, ny, _, width = element_load.shape
    load = element_load.reshape(PTS, ny * PTS, width)
    mob = mobility.reshape(PTS, ny * PTS, width)
    metric = metric[:, 0]
    side = (lax.axis_index("dom") % 2).astype(jnp.int32).reshape(1)
    tables = small_tables(width)
    restrict = restrict_tables(width)
    field = (PTS, PTS, ny, width)
    face = (PTS, ny, width)
    load, mob, spread, tables, restrict, yface = call(
        edge_kernel,
        [load.shape, mob.shape, (3, ny, width), tables.shape, restrict.shape, (2, 2, PTS, width)],
        [metric.shape, pltpu.SemaphoreType.DMA((5,))],
        *(pltpu.with_memory_space_constraint(a, pltpu.HBM) for a in (load, mob, metric, tables, restrict)),
        spaces=[pltpu.HBM] * 5,
    )
    arrivals = from_y(yface)
    fields, xface = call(
        diag_kernel, [(2,) + field, (2, 2) + face], [], load, mob, spread, tables
    )
    arrivals = exchange_x(side, xface, *arrivals)
    partial, gain, xface, yface = call(
        smooth_kernel,
        [field, field, (1, 2) + face, (2, 1, PTS, width)],
        [field, field, field],
        side, fields, mob, spread, tables, *arrivals,
    )
    arrivals = exchange_x(side, xface, *from_y(yface))
    pressure, planes, tops = call(
        coarse_kernel,
        [(PTS, ny * PTS, width), (2, ny, 128), (2, 128)],
        [field, field, (PTS, ny * PTS, width), pltpu.SemaphoreType.DMA(())],
        side, load, partial, gain, mob, spread, tables, restrict, *arrivals,
        out_spaces=[pltpu.HBM, pltpu.VMEM, pltpu.VMEM],
    )
    size = lax.axis_size("sub")
    below = lax.ppermute(tops, "sub", [(i, (i + 1) % size) for i in range(size)])
    planes = planes.at[:, 0].add(below)
    size = lax.axis_size("dom")
    inner = lax.ppermute(planes[1], "dom", inner_pairs(size))
    outer = lax.ppermute(planes[1], "dom", outer_pairs(size))
    coarse = planes[0] + jnp.where(side == 0, outer, inner)
    coarse = coarse[None, :, : width // PTS + 1]
    return pressure.reshape(element_load.shape), coarse


def solution(mesh):
    in_specs = (
        P("dom", None, "sub", None, None),
        P("dom", None, "sub", None, None),
        P(None, "dom", "sub", None),
    )
    out_specs = (P("dom", None, "sub", None, None), P("dom", "sub", None))
    return jax.shard_map(shards, mesh=mesh, in_specs=in_specs, out_specs=out_specs, check_vma=False)
```

```python
import jax
import jax.numpy as jnp
import numpy as np
from jax import lax
from jax.experimental import pallas as pl
from jax.experimental.pallas import tpu as pltpu
from jax.sharding import PartitionSpec as P

GLL_NODES = np.array(
    [
        -1.0,
        -0.8717401485096066,
        -0.5917001814331423,
        -0.2092992179024789,
        0.2092992179024789,
        0.5917001814331423,
        0.8717401485096066,
        1.0,
    ]
)
GLL_WEIGHTS = np.array(
    [
        0.03571428571428571,
        0.2107042271435061,
        0.3411226924835044,
        0.4124587946587038,
        0.4124587946587038,
        0.3411226924835044,
        0.2107042271435061,
        0.03571428571428571,
    ]
)
THETA = 1.65
DELTA = 1.35
RHO_FIRST = DELTA / THETA
RHO_SECOND = 1.0 / (2.0 * THETA / DELTA - RHO_FIRST)
KEEP = 1.0 + RHO_SECOND * RHO_FIRST
GAIN = 2.0 * RHO_SECOND / DELTA
EXACT = lax.Precision.HIGHEST
PTS = 8
F32 = jnp.float32


def derivative_table():
    identity = np.eye(8)
    differences = GLL_NODES[:, None] - GLL_NODES[None, :] + identity
    barycentric = 1.0 / np.prod(differences, axis=1)
    matrix = barycentric[None, :] / barycentric[:, None] / differences
    matrix = matrix * (1.0 - identity)
    row_sums = np.sum(matrix, axis=1)
    return matrix - identity * row_sums[:, None]


D = derivative_table()
W = GLL_WEIGHTS
HAT = np.stack([(1.0 - GLL_NODES) / 8.0, (1.0 + GLL_NODES) / 8.0], axis=1)
SLOPE = (-0.125, 0.125)


def small_tables(width):
    cells = width // PTS
    grad = np.tile(D.T, (1, cells))
    back = np.tile(D, (1, cells))
    square = np.tile(D * D, (1, cells))
    weight = np.tile(W[None], (PTS, cells))
    row_weight = np.tile(W[:, None], (1, width))
    return jnp.asarray(np.stack([grad, back, square, weight, row_weight]), F32)


def restrict_tables(width):
    cells = width // PTS
    hat = np.zeros((width, 128))
    slope = np.zeros((width, 128))
    for c in range(cells):
        rows = slice(c * PTS, (c + 1) * PTS)
        hat[rows, c], hat[rows, c + 1] = HAT[:, 0], HAT[:, 1]
        slope[rows, c], slope[rows, c + 1] = SLOPE
    return jnp.asarray(np.stack([hat, slope]), F32)


def dot(a, b):
    return jnp.dot(a, b, precision=EXACT, preferred_element_type=F32)


def halves(a):
    high = a.astype(jnp.bfloat16)
    return high, (a - high.astype(F32)).astype(jnp.bfloat16)


def paired(b):
    high, low = halves(b)
    return jnp.concatenate(
        [
            jnp.concatenate([high, low], axis=1),
            jnp.concatenate([high, jnp.zeros_like(low)], axis=1),
        ],
        axis=0,
    )


def dot_split(a, b_pair):
    both = jnp.dot(
        jnp.concatenate(halves(a), axis=1), b_pair, preferred_element_type=F32
    )
    n = both.shape[1] // 2
    return both[:, :n] + both[:, n:]


def cell_blocks(rows):
    width = rows.shape[1]
    cell = lax.broadcasted_iota(jnp.int32, rows.shape, 1) // PTS
    return jnp.concatenate(
        [jnp.where(cell == g, rows, 0.0) for g in range(width // PTS)], axis=0
    )


def contract(matrix, lines, parity):
    n = len(lines)
    half = n // 2
    plus = [lines[c] + lines[n - 1 - c] for c in range(half)]
    minus = [lines[c] - lines[n - 1 - c] for c in range(half)]
    top, low = [], []
    for r in range(half):
        even = sum(float(0.5 * (matrix[r, c] + matrix[r, n - 1 - c])) * plus[c] for c in range(half))
        odd = sum(float(0.5 * (matrix[r, c] - matrix[r, n - 1 - c])) * minus[c] for c in range(half))
        top.append(even + odd)
        low.append(even - odd if parity > 0 else odd - even)
    return top + low[::-1]


def spread_metric(metric, weight_row):
    cells = metric.shape[2]
    width = weight_row.shape[1]
    cell = lax.broadcasted_iota(jnp.int32, (cells, width), 1) // PTS
    row = lax.broadcasted_iota(jnp.int32, (cells, width), 0)
    pick = jnp.where(cell == row, 1.0, 0.0).astype(F32)
    return [dot(metric[d], pick) * weight_row for d in range(3)]


def column_masks(shape):
    lane = lax.broadcasted_iota(jnp.int32, shape, len(shape) - 1)
    up = (lane % PTS == PTS - 1) & (lane != shape[-1] - 1)
    down = (lane % PTS == 0) & (lane != 0)
    return up, down


def sum_z(v, masks):
    width = v.shape[-1]
    axis = v.ndim - 1
    up = pltpu.roll(v, width - 1, axis)
    down = pltpu.roll(v, 1, axis)
    return v + jnp.where(masks[0], up, jnp.where(masks[1], down, 0.0))


def sum_y_local(ref, ny):
    for i in range(PTS):
        low, high = ref[i, 0], ref[i, PTS - 1]
        row = lax.broadcasted_iota(jnp.int32, low.shape, 0)
        ref[i, PTS - 1] = high + jnp.where(row == ny - 1, 0.0, pltpu.roll(low, ny - 1, 0))
        ref[i, 0] = low + jnp.where(row == 0, 0.0, pltpu.roll(high, 1, 0))


def edge_planes(ref, ny):
    low = jnp.concatenate([ref[i, 0, 0:1] for i in range(PTS)], axis=0)
    high = jnp.concatenate([ref[i, PTS - 1, ny - 1 : ny] for i in range(PTS)], axis=0)
    return low, high


def stiffness(v_ref, mob, spread, out_ref, work_ref, tables):
    grad = paired(cell_blocks(tables[0]))
    back = paired(cell_blocks(tables[1]))
    _, _, ny, width = v_ref.shape
    for j in range(PTS):
        flux = contract(D, [v_ref[i, j] for i in range(PTS)], -1)
        flux = [flux[i] * (mob(i, j) * (float(W[i] * W[j]) * spread[0])) for i in range(PTS)]
        for i, value in enumerate(contract(D.T, flux, -1)):
            out_ref[i, j] = value
    for i in range(PTS):
        flux = contract(D, [v_ref[i, j] for j in range(PTS)], -1)
        flux = [flux[j] * (mob(i, j) * (float(W[i] * W[j]) * spread[1])) for j in range(PTS)]
        for j, value in enumerate(contract(D.T, flux, -1)):
            out_ref[i, j] += value
    for i in range(PTS):
        work_ref[i] = dot_split(v_ref[i].reshape(PTS * ny, width), grad).reshape(PTS, ny, width)
        for j in range(PTS):
            work_ref[i, j] *= mob(i, j) * (float(W[i] * W[j]) * spread[2])
        out_ref[i] += dot_split(work_ref[i].reshape(PTS * ny, width), back).reshape(PTS, ny, width)


def plane(ref, ny):
    return lambda i, j: ref[i, pl.ds(j, ny, stride=PTS)]


def edge_kernel(
    load_in, mob_in, metric_in, tab_in, restrict_in,
    load_ref, mob_ref, spread_ref, tab_ref, restrict_ref, yface_ref, metric_ref, sems,
):
    copies = [
        pltpu.make_async_copy(source, target, sems.at[n])
        for n, (source, target) in enumerate(
            [
                (tab_in, tab_ref),
                (metric_in, metric_ref),
                (mob_in, mob_ref),
                (load_in, load_ref),
                (restrict_in, restrict_ref),
            ]
        )
    ]
    for copy in copies:
        copy.start()
    copies[0].wait()
    copies[1].wait()
    ny, width = spread_ref.shape[1:]
    tables = tab_ref[...]
    spread = spread_metric(metric_ref[...], tables[3])
    for d in range(3):
        spread_ref[d] = spread[d]
    squared = paired(cell_blocks(tables[2]))
    square = D * D
    mob, load = plane(mob_ref, ny), plane(load_ref, ny)
    masks = column_masks((PTS * ny, width))
    copies[2].wait()
    ends = (0, PTS - 1)
    sums = [[], []]
    for i in range(PTS):
        factor = [mob(i, j) * (float(W[i]) * spread[1]) for j in range(PTS)]
        for s in range(2):
            sums[s].append(sum(float(square[j, ends[s]] * W[j]) * factor[j] for j in range(PTS)))
    for s in range(2):
        j = ends[s]
        points = [mob(i, j) * float(W[i] * W[j]) for i in range(PTS)]
        along = contract(square.T, [p * spread[0] for p in points], 1)
        column = dot_split(jnp.concatenate([p * spread[2] for p in points], axis=0), squared)
        total = column + jnp.concatenate([along[i] + sums[s][i] for i in range(PTS)], axis=0)
        total = sum_z(total, masks)
        e = 0 if s == 0 else ny - 1
        yface_ref[s, 1] = jnp.concatenate(
            [total[i * ny + e : i * ny + e + 1] for i in range(PTS)], axis=0
        )
    copies[3].wait()
    for s in range(2):
        e = 0 if s == 0 else ny - 1
        row = e * PTS + ends[s]
        value = jnp.concatenate([load_ref[i, row : row + 1] for i in range(PTS)], axis=0)
        yface_ref[s, 0] = sum_z(value, column_masks((PTS, width)))
        points = jnp.concatenate([mob_ref[i, row : row + 1] for i in range(PTS)], axis=0)
        points = points * (float(W[ends[s]]) * tables[4])
        yface_ref[s, 2] = points * spread[0][e : e + 1]
        yface_ref[s, 3] = points * spread[2][e : e + 1]
    copies[4].wait()


def diag_kernel(load_ref, mob_ref, spread_ref, tab_ref, fields_ref, xface_ref, factor_ref):
    tables = tab_ref[...]
    ny, width = fields_ref.shape[3:]
    spread = [spread_ref[d] for d in range(3)]
    squared = paired(cell_blocks(tables[2]))
    square = D * D
    mob, load = plane(mob_ref, ny), plane(load_ref, ny)
    diag_ref = fields_ref.at[1]
    for j in range(PTS):
        factor = [mob(i, j) * (float(W[i] * W[j]) * spread[0]) for i in range(PTS)]
        for i, value in enumerate(contract(square.T, factor, 1)):
            diag_ref[i, j] = value
    for i in range(PTS):
        factor = [mob(i, j) * (float(W[i] * W[j]) * spread[1]) for j in range(PTS)]
        for j, value in enumerate(contract(square.T, factor, 1)):
            diag_ref[i, j] += value
    for i in range(PTS):
        factor = jnp.concatenate(
            [mob(i, j) * (float(W[i] * W[j]) * spread[2]) for j in range(PTS)], axis=0
        )
        diag_ref[i] += dot_split(factor, squared).reshape(PTS, ny, width)
        fields_ref[0, i] = jnp.stack([load(i, j) for j in range(PTS)], axis=0)
    masks = column_masks((PTS, ny, width))
    for f in range(2):
        for i in range(PTS):
            fields_ref[f, i] = sum_z(fields_ref[f, i], masks)
        sum_y_local(fields_ref.at[f], ny)
        xface_ref[f, 0] = fields_ref[f, 0]
        xface_ref[f, 1] = fields_ref[f, PTS - 1]
    for s, i in enumerate((0, PTS - 1)):
        for n, e in enumerate((0, ny - 1)):
            points = mob_ref[i, e * PTS : (e + 1) * PTS] * (float(W[i]) * tables[4])
            factor_ref[s, n] = points * spread[1][e : e + 1]


def merge_kernel(side_ref, xface_ref, factor_ref, below_ref, above_ref, outer_ref, inner_ref):
    below_ref, above_ref = below_ref.at[1], above_ref.at[0]
    even = side_ref[0] == 0
    fields, _, _, ny, width = xface_ref.shape
    row = lax.broadcasted_iota(jnp.int32, (ny, width), 0)
    for f in range(fields):
        for j in range(PTS):
            low, high = xface_ref[f, 0, j], xface_ref[f, 1, j]
            if j == 0:
                low = low + jnp.where(row == 0, below_ref[f, 0:1], 0.0)
                high = high + jnp.where(row == 0, below_ref[f, PTS - 1 : PTS], 0.0)
            if j == PTS - 1:
                low = low + jnp.where(row == ny - 1, above_ref[f, 0:1], 0.0)
                high = high + jnp.where(row == ny - 1, above_ref[f, PTS - 1 : PTS], 0.0)
            at = (f * PTS + j) * ny
            inner_ref[at : at + ny] = jnp.where(even, high, low)
            outer_ref[at : at + ny] = jnp.where(even, low, high)
    for n in range(2):
        at = fields * PTS * ny + n * PTS
        low, high = factor_ref[0, n], factor_ref[1, n]
        inner_ref[at : at + PTS] = jnp.where(even, high, low)
        outer_ref[at : at + PTS] = jnp.where(even, low, high)


def add_arrivals(get, put, f, even, below_ref, above_ref, outer_ref, inner_ref, ny, width):
    row = lax.broadcasted_iota(jnp.int32, (ny, width), 0)
    for i in range(PTS):
        put(i, 0, get(i, 0) + jnp.where(row == 0, below_ref[f, i : i + 1], 0.0))
        put(
            i,
            PTS - 1,
            get(i, PTS - 1) + jnp.where(row == ny - 1, above_ref[f, i : i + 1], 0.0),
        )
    for j in range(PTS):
        at = (f * PTS + j) * ny
        inner, outer = inner_ref[at : at + ny], outer_ref[at : at + ny]
        put(0, j, get(0, j) + jnp.where(even, outer, inner))
        put(PTS - 1, j, get(PTS - 1, j) + jnp.where(even, inner, outer))


def corner_sums(even, value_ref, tables, below_ref, above_ref, outer_ref, inner_ref, masks):
    ny, width = value_ref.shape[2:]
    ends = (0, PTS - 1)
    grad = paired(cell_blocks(tables[0]))
    back = paired(cell_blocks(tables[1]))
    along_xz = [[None, None], [None, None]]
    lines, line_factors = [], []
    for t, ref in enumerate((below_ref, above_ref)):
        flux = contract(D, [value_ref[i, ends[t]] for i in range(PTS)], -1)
        flux = contract(D.T, [flux[i] * ref[2, i : i + 1] for i in range(PTS)], -1)
        for s in range(2):
            along_xz[s][t] = flux[ends[s]]
            lines.append(value_ref[ends[s], ends[t]])
            line_factors.append(jnp.broadcast_to(ref[3, ends[s] : ends[s] + 1], (ny, width)))
    flux = dot_split(jnp.concatenate(lines, axis=0), grad) * jnp.concatenate(line_factors, axis=0)
    flux = dot_split(flux, back)
    along_y = [[None, None], [None, None]]
    base = 2 * PTS * ny
    for s in range(2):
        gradient = contract(D, [value_ref[ends[s], j] for j in range(PTS)], -1)
        for t in range(2):
            at = base + t * PTS
            inner, outer = inner_ref[at : at + PTS], outer_ref[at : at + PTS]
            own = even if s == 0 else jnp.logical_not(even)
            factor = jnp.where(own, outer, inner)
            total = [gradient[j] * factor[j : j + 1] for j in range(PTS)]
            along_y[s][t] = sum(float(D[j, ends[t]]) * total[j] for j in range(PTS))
            n = (t * 2 + s) * ny
            along_xz[s][t] = sum_z(along_xz[s][t] + flux[n : n + ny], masks)
            along_y[s][t] = sum_z(along_y[s][t], masks)
    return along_xz, along_y


def smooth_kernel(
    side_ref, fields_ref, mob_ref, spread_ref, tab_ref, below_ref, above_ref, outer_ref, inner_ref,
    partial_ref, gain_ref, to_outer_ref, to_inner_ref, yface_ref, value_ref, out_ref, work_ref,
):
    tables = tab_ref[...]
    ny, width = out_ref.shape[2:]
    spread = [spread_ref[d] for d in range(3)]
    below_ref, above_ref = below_ref.at[1], above_ref.at[0]
    even = side_ref[0] == 0
    mob = plane(mob_ref, ny)
    for f, ref in ((0, partial_ref), (1, gain_ref)):
        for i in range(PTS):
            ref[i] = fields_ref[f, i]

        def put(i, j, value, ref=ref):
            ref[i, j] = value

        add_arrivals(
            lambda i, j, ref=ref: ref[i, j], put, f, even,
            below_ref, above_ref, outer_ref, inner_ref, ny, width,
        )
    for i in range(PTS):
        inverse = 1.0 / gain_ref[i]
        right = partial_ref[i]
        value = inverse * right * (1.0 / THETA)
        value_ref[i] = value
        partial_ref[i] = KEEP * value + GAIN * (inverse * right)
        gain_ref[i] = GAIN * inverse
    stiffness(value_ref, mob, spread, out_ref, work_ref, tables)
    masks = column_masks((PTS, ny, width))
    for i in range(PTS):
        out_ref[i] = sum_z(out_ref[i], masks)
    sum_y_local(out_ref, ny)
    along_xz, along_y = corner_sums(
        even, value_ref, tables, below_ref, above_ref, outer_ref, inner_ref, column_masks((ny, width))
    )
    row = lax.broadcasted_iota(jnp.int32, (ny, width), 0)
    end_rows = (row == 0, row == ny - 1)
    for j in range(PTS):
        low, high = out_ref[0, j], out_ref[PTS - 1, j]
        if j in (0, PTS - 1):
            t = 0 if j == 0 else 1
            low = low + jnp.where(end_rows[t], along_xz[0][t], 0.0)
            high = high + jnp.where(end_rows[t], along_xz[1][t], 0.0)
        to_inner_ref[j * ny : (j + 1) * ny] = jnp.where(even, high, low)
        to_outer_ref[j * ny : (j + 1) * ny] = jnp.where(even, low, high)
    for t, (e, edge) in enumerate(zip((0, ny - 1), edge_planes(out_ref, ny))):
        at = lax.broadcasted_iota(jnp.int32, edge.shape, 0)
        edge = edge + jnp.where(at == 0, along_y[0][t][e : e + 1], 0.0)
        yface_ref[t, 0] = edge + jnp.where(at == PTS - 1, along_y[1][t][e : e + 1], 0.0)
    for i in range(PTS):
        partial_ref[i] -= gain_ref[i] * out_ref[i]


def coarse_kernel(
    side_ref, load_ref, partial_ref, gain_ref, mob_ref, spread_ref, tab_ref, restrict_ref,
    outer_ref, below_ref, above_ref, inner_ref,
    pressure_out, planes_ref, tops_ref, value_ref, work_ref, pressure_ref, sem,
):
    tables = tab_ref[...]
    ny, width = value_ref.shape[2:]
    spread = [spread_ref[d] for d in range(3)]
    below_ref, above_ref = below_ref.at[1], above_ref.at[0]
    even = side_ref[0] == 0
    mob, load = plane(mob_ref, ny), plane(load_ref, ny)
    row = lax.broadcasted_iota(jnp.int32, (ny, width), 0)
    for i in range(PTS):
        value_ref[i] = partial_ref[i]
    for i in range(PTS):
        value_ref[i, 0] -= gain_ref[i, 0] * jnp.where(row == 0, below_ref[0, i : i + 1], 0.0)
        value_ref[i, PTS - 1] -= gain_ref[i, PTS - 1] * jnp.where(
            row == ny - 1, above_ref[0, i : i + 1], 0.0
        )
    for j in range(PTS):
        inner, outer = inner_ref[j * ny : (j + 1) * ny], outer_ref[j * ny : (j + 1) * ny]
        value_ref[0, j] -= gain_ref[0, j] * jnp.where(even, outer, inner)
        value_ref[PTS - 1, j] -= gain_ref[PTS - 1, j] * jnp.where(even, inner, outer)
    for i in range(PTS):
        for j in range(PTS):
            pressure_ref[i, pl.ds(j, ny, stride=PTS)] = value_ref[i, j]
    copy = pltpu.make_async_copy(pressure_ref, pressure_out, sem)
    copy.start()
    grad = paired(cell_blocks(tables[0]))
    zero = jnp.zeros((ny, width), F32)
    smooth = {(p, q): zero for p in range(2) for q in range(2)}
    slope = {(p, q): zero for p in range(2) for q in range(2)}
    for j in range(PTS):
        flux = contract(D, [value_ref[i, j] for i in range(PTS)], -1)
        total = sum(flux[i] * mob(i, j) * float(W[i] * W[j]) for i in range(PTS)) * spread[0]
        for p in range(2):
            for q in range(2):
                smooth[p, q] -= float(SLOPE[p] * HAT[j, q]) * total
    for i in range(PTS):
        flux = contract(D, [value_ref[i, j] for j in range(PTS)], -1)
        total = sum(flux[j] * mob(i, j) * float(W[i] * W[j]) for j in range(PTS)) * spread[1]
        for p in range(2):
            for q in range(2):
                smooth[p, q] -= float(HAT[i, p] * SLOPE[q]) * total
    for i in range(PTS):
        work_ref[i] = dot_split(value_ref[i].reshape(PTS * ny, width), grad).reshape(PTS, ny, width)
        flux = [work_ref[i, j] * mob(i, j) for j in range(PTS)]
        for q in range(2):
            total = sum(float(W[i] * W[j] * HAT[j, q]) * flux[j] for j in range(PTS))
            from_load = sum(float(HAT[j, q]) * load(i, j) for j in range(PTS))
            for p in range(2):
                slope[p, q] += float(HAT[i, p]) * total
                smooth[p, q] += float(HAT[i, p]) * from_load
    keys = [(p, q) for p in range(2) for q in range(2)]
    corners = dot(jnp.concatenate([smooth[k] for k in keys], axis=0), restrict_ref[0]) - dot(
        jnp.concatenate([slope[k] * spread[2] for k in keys], axis=0), restrict_ref[1]
    )
    row = lax.broadcasted_iota(jnp.int32, (ny, corners.shape[1]), 0)
    for p in range(2):
        lower = corners[(2 * p) * ny : (2 * p + 1) * ny]
        upper = corners[(2 * p + 1) * ny : (2 * p + 2) * ny]
        planes_ref[p] = lower + jnp.where(row == 0, 0.0, pltpu.roll(upper, 1, 0))
        tops_ref[p : p + 1] = upper[ny - 1 : ny]
    copy.wait()


def call(body, outs, scratch, *args, spaces=None, out_spaces=None):
    spaces = spaces or [pltpu.SMEM if a.dtype == jnp.int32 else pltpu.VMEM for a in args]
    return pl.pallas_call(
        body,
        out_shape=[jax.ShapeDtypeStruct(s, F32) for s in outs],
        in_specs=[pl.BlockSpec(memory_space=m) for m in spaces],
        out_specs=[pl.BlockSpec(memory_space=m) for m in out_spaces or [pltpu.VMEM] * len(outs)],
        scratch_shapes=[pltpu.VMEM(s, F32) if isinstance(s, tuple) else s for s in scratch],
        compiler_params=pltpu.CompilerParams(vmem_limit_bytes=16 * 1024 * 1024),
    )(*args)


def from_y(faces):
    size = lax.axis_size("sub")
    up = lax.ppermute(faces, "sub", [(i, (i + 1) % size) for i in range(size)])
    if size == 2:
        return up, up
    return up, lax.ppermute(faces, "sub", [(i, (i - 1) % size) for i in range(size)])


def inner_pairs(size):
    return [(i, i ^ 1) for i in range(size)]


def outer_pairs(size):
    return [(i, (i + 1) % size if i % 2 else (i - 1) % size) for i in range(size)]


def to_x(outer, inner):
    size = lax.axis_size("dom")
    outer = lax.ppermute(outer, "dom", outer_pairs(size))
    inner = lax.ppermute(inner, "dom", inner_pairs(size))
    return outer, inner


def shards(element_load, mobility, metric):
    _, _, ny, _, width = element_load.shape
    load = element_load.reshape(PTS, ny * PTS, width)
    mob = mobility.reshape(PTS, ny * PTS, width)
    metric = metric[:, 0]
    side = (lax.axis_index("dom") % 2).astype(jnp.int32).reshape(1)
    tables = small_tables(width)
    restrict = restrict_tables(width)
    field = (PTS, PTS, ny, width)
    face = (PTS, ny, width)
    load, mob, spread, tables, restrict, yface = call(
        edge_kernel,
        [load.shape, mob.shape, (3, ny, width), tables.shape, restrict.shape, (2, 4, PTS, width)],
        [metric.shape, pltpu.SemaphoreType.DMA((5,))],
        *(pltpu.with_memory_space_constraint(a, pltpu.HBM) for a in (load, mob, metric, tables, restrict)),
        spaces=[pltpu.HBM] * 5,
    )
    below, above = from_y(yface)
    fields, xface, factor = call(
        diag_kernel, [(2,) + field, (2, 2) + face, (2, 2, PTS, width)], [], load, mob, spread, tables
    )
    rows = (2 * PTS * ny + 2 * PTS, width)
    outer, inner = to_x(*call(merge_kernel, [rows, rows], [], side, xface, factor, below, above))
    partial, gain, outer, inner, yface = call(
        smooth_kernel,
        [field, field, (PTS * ny, width), (PTS * ny, width), (2, 1, PTS, width)],
        [field, field, field],
        side, fields, mob, spread, tables, below, above, outer, inner,
    )
    outer, inner = to_x(outer, inner)
    below, above = from_y(yface)
    pressure, planes, tops = call(
        coarse_kernel,
        [(PTS, ny * PTS, width), (2, ny, 128), (2, 128)],
        [field, field, (PTS, ny * PTS, width), pltpu.SemaphoreType.DMA(())],
        side, load, partial, gain, mob, spread, tables, restrict, outer, below, above, inner,
        out_spaces=[pltpu.HBM, pltpu.VMEM, pltpu.VMEM],
    )
    size = lax.axis_size("sub")
    below = lax.ppermute(tops, "sub", [(i, (i + 1) % size) for i in range(size)])
    planes = planes.at[:, 0].add(below)
    size = lax.axis_size("dom")
    inner = lax.ppermute(planes[1], "dom", inner_pairs(size))
    outer = lax.ppermute(planes[1], "dom", outer_pairs(size))
    coarse = planes[0] + jnp.where(side == 0, outer, inner)
    coarse = coarse[None, :, : width // PTS + 1]
    return pressure.reshape(element_load.shape), coarse


def solution(mesh):
    in_specs = (
        P("dom", None, "sub", None, None),
        P("dom", None, "sub", None, None),
        P(None, "dom", "sub", None),
    )
    out_specs = (P("dom", None, "sub", None, None), P("dom", "sub", None))
    return jax.shard_map(shards, mesh=mesh, in_specs=in_specs, out_specs=out_specs, check_vma=False)
```

```python
import jax
import jax.numpy as jnp
import numpy as np
from jax import lax
from jax.experimental import pallas as pl
from jax.experimental.pallas import tpu as pltpu
from jax.sharding import PartitionSpec as P

GLL_NODES = np.array(
    [
        -1.0,
        -0.8717401485096066,
        -0.5917001814331423,
        -0.2092992179024789,
        0.2092992179024789,
        0.5917001814331423,
        0.8717401485096066,
        1.0,
    ]
)
GLL_WEIGHTS = np.array(
    [
        0.03571428571428571,
        0.2107042271435061,
        0.3411226924835044,
        0.4124587946587038,
        0.4124587946587038,
        0.3411226924835044,
        0.2107042271435061,
        0.03571428571428571,
    ]
)
THETA = 1.65
DELTA = 1.35
RHO_FIRST = DELTA / THETA
RHO_SECOND = 1.0 / (2.0 * THETA / DELTA - RHO_FIRST)
KEEP = 1.0 + RHO_SECOND * RHO_FIRST
GAIN = 2.0 * RHO_SECOND / DELTA
EXACT = lax.Precision.HIGHEST
PTS = 8
F32 = jnp.float32


def derivative_table():
    identity = np.eye(8)
    differences = GLL_NODES[:, None] - GLL_NODES[None, :] + identity
    barycentric = 1.0 / np.prod(differences, axis=1)
    matrix = barycentric[None, :] / barycentric[:, None] / differences
    matrix = matrix * (1.0 - identity)
    row_sums = np.sum(matrix, axis=1)
    return matrix - identity * row_sums[:, None]


D = derivative_table()
W = GLL_WEIGHTS
HAT = np.stack([(1.0 - GLL_NODES) / 8.0, (1.0 + GLL_NODES) / 8.0], axis=1)
SLOPE = (-0.125, 0.125)


def small_tables(width):
    cells = width // PTS
    grad = np.tile(D.T, (1, cells))
    back = np.tile(D, (1, cells))
    square = np.tile(D * D, (1, cells))
    weight = np.tile(W[None], (PTS, cells))
    row_weight = np.tile(W[:, None], (1, width))
    return jnp.asarray(np.stack([grad, back, square, weight, row_weight]), F32)


def restrict_tables(width):
    cells = width // PTS
    hat = np.zeros((width, 128))
    slope = np.zeros((width, 128))
    for c in range(cells):
        rows = slice(c * PTS, (c + 1) * PTS)
        hat[rows, c], hat[rows, c + 1] = HAT[:, 0], HAT[:, 1]
        slope[rows, c], slope[rows, c + 1] = SLOPE
    return jnp.asarray(np.concatenate([hat, slope]), F32)


def dot(a, b):
    return jnp.dot(a, b, precision=EXACT, preferred_element_type=F32)


def halves(a):
    high = a.astype(jnp.bfloat16)
    return high, (a - high.astype(F32)).astype(jnp.bfloat16)


def paired(b):
    high, low = halves(b)
    return jnp.concatenate(
        [
            jnp.concatenate([high, low], axis=1),
            jnp.concatenate([high, jnp.zeros_like(low)], axis=1),
        ],
        axis=0,
    )


def dot_split(a, b_pair):
    both = jnp.dot(
        jnp.concatenate(halves(a), axis=1), b_pair, preferred_element_type=F32
    )
    n = both.shape[1] // 2
    return both[:, :n] + both[:, n:]


def cell_blocks(rows):
    width = rows.shape[1]
    cell = lax.broadcasted_iota(jnp.int32, rows.shape, 1) // PTS
    return jnp.concatenate(
        [jnp.where(cell == g, rows, 0.0) for g in range(width // PTS)], axis=0
    )


def contract(matrix, lines, parity):
    n = len(lines)
    half = n // 2
    plus = [lines[c] + lines[n - 1 - c] for c in range(half)]
    minus = [lines[c] - lines[n - 1 - c] for c in range(half)]
    top, low = [], []
    for r in range(half):
        even = sum(float(0.5 * (matrix[r, c] + matrix[r, n - 1 - c])) * plus[c] for c in range(half))
        odd = sum(float(0.5 * (matrix[r, c] - matrix[r, n - 1 - c])) * minus[c] for c in range(half))
        top.append(even + odd)
        low.append(even - odd if parity > 0 else odd - even)
    return top + low[::-1]


def spread_metric(metric, weight_row):
    cells = metric.shape[2]
    width = weight_row.shape[1]
    cell = lax.broadcasted_iota(jnp.int32, (cells, width), 1) // PTS
    row = lax.broadcasted_iota(jnp.int32, (cells, width), 0)
    pick = jnp.where(cell == row, 1.0, 0.0).astype(F32)
    return [dot(metric[d], pick) * weight_row for d in range(3)]


def column_masks(shape):
    lane = lax.broadcasted_iota(jnp.int32, shape, len(shape) - 1)
    up = (lane % PTS == PTS - 1) & (lane != shape[-1] - 1)
    down = (lane % PTS == 0) & (lane != 0)
    return up, down


def sum_z(v, masks):
    width = v.shape[-1]
    axis = v.ndim - 1
    up = pltpu.roll(v, width - 1, axis)
    down = pltpu.roll(v, 1, axis)
    return v + jnp.where(masks[0], up, jnp.where(masks[1], down, 0.0))


def sum_y_local(ref, ny):
    for i in range(PTS):
        low, high = ref[i, 0], ref[i, PTS - 1]
        row = lax.broadcasted_iota(jnp.int32, low.shape, 0)
        ref[i, PTS - 1] = high + jnp.where(row == ny - 1, 0.0, pltpu.roll(low, ny - 1, 0))
        ref[i, 0] = low + jnp.where(row == 0, 0.0, pltpu.roll(high, 1, 0))


def edge_planes(ref, ny):
    low = jnp.concatenate([ref[i, 0, 0:1] for i in range(PTS)], axis=0)
    high = jnp.concatenate([ref[i, PTS - 1, ny - 1 : ny] for i in range(PTS)], axis=0)
    return low, high


def plane(ref, ny):
    return lambda i, j: ref[i, pl.ds(j, ny, stride=PTS)]


def edge_kernel(
    load_in, mob_in, metric_in, tab_in, restrict_in,
    load_ref, mob_ref, spread_ref, tab_ref, restrict_ref, yface_ref, metric_ref, sems,
):
    copies = [
        pltpu.make_async_copy(source, target, sems.at[n])
        for n, (source, target) in enumerate(
            [
                (tab_in, tab_ref),
                (metric_in, metric_ref),
                (mob_in, mob_ref),
                (load_in, load_ref),
                (restrict_in, restrict_ref),
            ]
        )
    ]
    for copy in copies:
        copy.start()
    copies[0].wait()
    copies[1].wait()
    ny, width = spread_ref.shape[1:]
    tables = tab_ref[...]
    spread = spread_metric(metric_ref[...], tables[3])
    for d in range(3):
        spread_ref[d] = spread[d]
    squared = paired(cell_blocks(tables[2]))
    square = D * D
    mob, load = plane(mob_ref, ny), plane(load_ref, ny)
    masks = column_masks((PTS * ny, width))
    copies[2].wait()
    ends = (0, PTS - 1)
    sums = [[], []]
    for i in range(PTS):
        factor = [mob(i, j) * (float(W[i]) * spread[1]) for j in range(PTS)]
        for s in range(2):
            sums[s].append(sum(float(square[j, ends[s]] * W[j]) * factor[j] for j in range(PTS)))
    for s in range(2):
        j = ends[s]
        points = [mob(i, j) * float(W[i] * W[j]) for i in range(PTS)]
        along = contract(square.T, [p * spread[0] for p in points], 1)
        column = dot_split(jnp.concatenate([p * spread[2] for p in points], axis=0), squared)
        total = column + jnp.concatenate([along[i] + sums[s][i] for i in range(PTS)], axis=0)
        total = sum_z(total, masks)
        e = 0 if s == 0 else ny - 1
        yface_ref[s, 1] = jnp.concatenate(
            [total[i * ny + e : i * ny + e + 1] for i in range(PTS)], axis=0
        )
    copies[3].wait()
    for s in range(2):
        e = 0 if s == 0 else ny - 1
        row = e * PTS + ends[s]
        value = jnp.concatenate([load_ref[i, row : row + 1] for i in range(PTS)], axis=0)
        yface_ref[s, 0] = sum_z(value, column_masks((PTS, width)))
        points = jnp.concatenate([mob_ref[i, row : row + 1] for i in range(PTS)], axis=0)
        points = points * (float(W[ends[s]]) * tables[4])
        yface_ref[s, 2] = points * spread[0][e : e + 1]
        yface_ref[s, 3] = points * spread[2][e : e + 1]
    copies[4].wait()


def diag_kernel(load_ref, mob_ref, spread_ref, tab_ref, fields_ref, xface_ref, factor_ref):
    tables = tab_ref[...]
    ny, width = fields_ref.shape[3:]
    spread = [spread_ref[d] for d in range(3)]
    squared = paired(cell_blocks(tables[2]))
    square = D * D
    mob, load = plane(mob_ref, ny), plane(load_ref, ny)
    diag_ref = fields_ref.at[1]
    for j in range(PTS):
        factor = [mob(i, j) * (float(W[i] * W[j]) * spread[0]) for i in range(PTS)]
        for i, value in enumerate(contract(square.T, factor, 1)):
            diag_ref[i, j] = value
    for i in range(PTS):
        factor = [mob(i, j) * (float(W[i] * W[j]) * spread[1]) for j in range(PTS)]
        for j, value in enumerate(contract(square.T, factor, 1)):
            diag_ref[i, j] += value
    for i in range(PTS):
        factor = jnp.concatenate(
            [mob(i, j) * (float(W[i] * W[j]) * spread[2]) for j in range(PTS)], axis=0
        )
        diag_ref[i] += dot_split(factor, squared).reshape(PTS, ny, width)
        fields_ref[0, i] = jnp.stack([load(i, j) for j in range(PTS)], axis=0)
    masks = column_masks((PTS, ny, width))
    for f in range(2):
        for i in range(PTS):
            fields_ref[f, i] = sum_z(fields_ref[f, i], masks)
        sum_y_local(fields_ref.at[f], ny)
        xface_ref[f, 0] = fields_ref[f, 0]
        xface_ref[f, 1] = fields_ref[f, PTS - 1]
    for s, i in enumerate((0, PTS - 1)):
        for n, e in enumerate((0, ny - 1)):
            points = mob_ref[i, e * PTS : (e + 1) * PTS] * (float(W[i]) * tables[4])
            factor_ref[s, n] = points * spread[1][e : e + 1]


def merge_kernel(side_ref, xface_ref, factor_ref, below_ref, above_ref, outer_ref, inner_ref):
    below_ref, above_ref = below_ref.at[1], above_ref.at[0]
    even = side_ref[0] == 0
    fields, _, _, ny, width = xface_ref.shape
    row = lax.broadcasted_iota(jnp.int32, (ny, width), 0)
    for f in range(fields):
        for j in range(PTS):
            low, high = xface_ref[f, 0, j], xface_ref[f, 1, j]
            if j == 0:
                low = low + jnp.where(row == 0, below_ref[f, 0:1], 0.0)
                high = high + jnp.where(row == 0, below_ref[f, PTS - 1 : PTS], 0.0)
            if j == PTS - 1:
                low = low + jnp.where(row == ny - 1, above_ref[f, 0:1], 0.0)
                high = high + jnp.where(row == ny - 1, above_ref[f, PTS - 1 : PTS], 0.0)
            at = (f * PTS + j) * ny
            inner_ref[at : at + ny] = jnp.where(even, high, low)
            outer_ref[at : at + ny] = jnp.where(even, low, high)
    for n in range(2):
        at = fields * PTS * ny + n * PTS
        low, high = factor_ref[0, n], factor_ref[1, n]
        inner_ref[at : at + PTS] = jnp.where(even, high, low)
        outer_ref[at : at + PTS] = jnp.where(even, low, high)


def inside_kernel(
    fields_ref, mob_ref, spread_ref, tab_ref, below_ref, above_ref,
    rough_ref, value_ref, partial_ref, gain_ref, out_ref, pair_ref, work_ref,
):
    below_ref, above_ref = below_ref.at[1], above_ref.at[0]
    tables = tab_ref[...]
    ny, width = out_ref.shape[2:]
    spread = [spread_ref[d] for d in range(3)]
    mob = plane(mob_ref, ny)
    row = lax.broadcasted_iota(jnp.int32, (ny, width), 0)
    zero = jnp.zeros((ny, width), F32)
    for i in range(PTS):
        for j in range(PTS):
            sums = [fields_ref[f, i, j] for f in range(2)]
            for f in range(2):
                if j == 0:
                    sums[f] += jnp.where(row == 0, below_ref[f, i : i + 1], 0.0)
                if j == PTS - 1:
                    sums[f] += jnp.where(row == ny - 1, above_ref[f, i : i + 1], 0.0)
            if i in (0, PTS - 1):
                for f in range(2):
                    rough_ref[f, 0 if i == 0 else 1, j] = sums[f]
                value_ref[i, j] = partial_ref[i, j] = gain_ref[i, j] = zero
            else:
                value_ref[i, j], partial_ref[i, j], gain_ref[i, j] = first_step(*sums)
    grad = paired(cell_blocks(tables[0]))
    back = paired(cell_blocks(tables[1]))
    for j in range(PTS):
        factor = [mob(i, j) * (float(W[i] * W[j]) * spread[0]) for i in range(PTS)]
        for n, (p, q) in enumerate(((0, 0), (0, PTS - 1), (PTS - 1, PTS - 1))):
            pair_ref[n, j] = sum(float(D[a, p] * D[a, q]) * factor[a] for a in range(PTS))
        flux = contract(D, [value_ref[i, j] for i in range(PTS)], -1)
        flux = [flux[i] * factor[i] for i in range(PTS)]
        for i, value in enumerate(contract(D.T, flux, -1)):
            out_ref[i, j] = value
    for i in range(1, PTS - 1):
        flux = contract(D, [value_ref[i, j] for j in range(PTS)], -1)
        flux = [flux[j] * (mob(i, j) * (float(W[i] * W[j]) * spread[1])) for j in range(PTS)]
        for j, value in enumerate(contract(D.T, flux, -1)):
            out_ref[i, j] += value
        work_ref[...] = dot_split(value_ref[i].reshape(PTS * ny, width), grad).reshape(PTS, ny, width)
        for j in range(PTS):
            work_ref[j] *= mob(i, j) * (float(W[i] * W[j]) * spread[2])
        out_ref[i] += dot_split(work_ref[...].reshape(PTS * ny, width), back).reshape(PTS, ny, width)


def first_step(right, diagonal):
    inverse = 1.0 / diagonal
    scaled = inverse * right
    value = scaled * (1.0 / THETA)
    return value, KEEP * value + GAIN * scaled, GAIN * inverse


def faces_kernel(
    side_ref, rough_ref, value_ref, out_ref, pair_ref, mob_ref, spread_ref, tab_ref,
    below_ref, above_ref, outer_ref, inner_ref,
    to_outer_ref, to_inner_ref, yface_ref, vface_ref, fface_ref, pface_ref, gface_ref, line_ref,
):
    below_ref, above_ref = below_ref.at[1], above_ref.at[0]
    even = side_ref[0] == 0
    tables = tab_ref[...]
    ny, width = out_ref.shape[2:]
    spread = [spread_ref[d] for d in range(3)]
    mob = plane(mob_ref, ny)
    ends = (0, PTS - 1)
    rows = (0, ny - 1)
    row = lax.broadcasted_iota(jnp.int32, (ny, width), 0)
    masks = column_masks((ny, width))

    def arrived(at, count):
        inner, outer = inner_ref[at : at + count], outer_ref[at : at + count]
        return jnp.where(even, outer, inner), jnp.where(even, inner, outer)

    value = [[None] * PTS, [None] * PTS]
    for j in range(PTS):
        load = arrived(j * ny, ny)
        diagonal = arrived((PTS + j) * ny, ny)
        for s in range(2):
            value[s][j], pface_ref[s, j], gface_ref[s, j] = first_step(
                rough_ref[0, s, j] + load[s], rough_ref[1, s, j] + diagonal[s]
            )
            vface_ref[s, j] = value[s][j]
    lines = [value[s][j] for s in range(2) for j in range(PTS)]
    factors = [
        mob(ends[s], j) * (float(W[ends[s]] * W[j]) * spread[2]) for s in range(2) for j in range(PTS)
    ]
    for s in range(2):
        for t, ref in enumerate((below_ref, above_ref)):
            lines.append(value[s][ends[t]])
            factors.append(jnp.broadcast_to(ref[3, ends[s] : ends[s] + 1], (ny, width)))
    grad = paired(cell_blocks(tables[0]))
    back = paired(cell_blocks(tables[1]))
    flux = dot_split(jnp.concatenate(lines, axis=0), grad) * jnp.concatenate(factors, axis=0)
    line_ref[...] = dot_split(flux, back)
    edge_y = [[None, None], [None, None]]
    total = [[None] * PTS, [None] * PTS]
    for s in range(2):
        gradient = contract(D, value[s], -1)
        flux = [
            gradient[j] * (mob(ends[s], j) * (float(W[ends[s]] * W[j]) * spread[1])) for j in range(PTS)
        ]
        total[s] = contract(D.T, flux, -1)
        for t in range(2):
            factor = arrived(2 * PTS * ny + t * PTS, PTS)[s]
            edge_y[s][t] = sum(
                float(D[j, ends[t]]) * (gradient[j] * factor[j : j + 1]) for j in range(PTS)
            )[rows[t] : rows[t] + 1]
    for j in range(PTS):
        total[0][j] += out_ref[0, j] + pair_ref[0, j] * value[0][j] + pair_ref[1, j] * value[1][j]
        total[1][j] += out_ref[PTS - 1, j] + pair_ref[1, j] * value[0][j] + pair_ref[2, j] * value[1][j]
    for s in range(2):
        for j in range(PTS):
            at = (s * PTS + j) * ny
            total[s][j] += line_ref[at : at + ny]
    for t in range(2):
        j = ends[t]
        flux = [
            mob(a, j)
            * (float(W[a] * W[j]) * spread[0])
            * (float(D[a, 0]) * value[0][j] + float(D[a, PTS - 1]) * value[1][j])
            for a in range(PTS)
        ]
        flux = contract(D.T, flux, -1)
        edge = [total[0][j]] + [out_ref[i, j] + flux[i] for i in range(1, PTS - 1)] + [total[1][j]]
        edge = [v[rows[t] : rows[t] + 1] for v in edge]
        edge[0] += edge_y[0][t]
        edge[PTS - 1] += edge_y[1][t]
        yface_ref[t, 0] = sum_z(jnp.concatenate(edge, axis=0), column_masks((PTS, width)))
    extra = [[None, None], [None, None]]
    for t, ref in enumerate((below_ref, above_ref)):
        j = ends[t]
        points = [value[0][j]] + [value_ref[i, j] for i in range(1, PTS - 1)] + [value[1][j]]
        flux = contract(D, points, -1)
        flux = contract(D.T, [flux[i] * ref[2, i : i + 1] for i in range(PTS)], -1)
        for s in range(2):
            at = (2 * PTS + 2 * s + t) * ny
            extra[s][t] = sum_z(flux[ends[s]] + line_ref[at : at + ny], masks)
            extra[s][t] = jnp.where(row == rows[t], extra[s][t], 0.0)
    for s in range(2):
        for j in range(PTS):
            total[s][j] = sum_z(total[s][j], masks)
        low, high = total[s][0], total[s][PTS - 1]
        total[s][PTS - 1] = high + jnp.where(row == ny - 1, 0.0, pltpu.roll(low, ny - 1, 0))
        total[s][0] = low + jnp.where(row == 0, 0.0, pltpu.roll(high, 1, 0))
    for j in range(PTS):
        fface_ref[0, j], fface_ref[1, j] = total[0][j], total[1][j]
        low, high = total[0][j], total[1][j]
        if j in ends:
            t = ends.index(j)
            low, high = low + extra[0][t], high + extra[1][t]
        to_inner_ref[j * ny : (j + 1) * ny] = jnp.where(even, high, low)
        to_outer_ref[j * ny : (j + 1) * ny] = jnp.where(even, low, high)


def partial_kernel(
    load_ref, mob_ref, spread_ref, tab_ref, out_ref, partial_ref, gain_ref,
    vface_ref, fface_ref, pface_ref, gface_ref,
    sofar_ref, sums_ref, face_weights_ref, plane_weights_ref, weights_ref, work_ref,
):
    tables = tab_ref[...]
    ny, width = sofar_ref.shape[2:]
    spread = [spread_ref[d] for d in range(3)]
    mob, load = plane(mob_ref, ny), plane(load_ref, ny)
    masks = column_masks((PTS, ny, width))
    back = paired(cell_blocks(tables[1]))
    ends = (0, PTS - 1)
    for j in range(PTS):
        factor = [mob(a, j) * (float(W[a] * W[j]) * spread[0]) for a in range(PTS)]
        for i, value in enumerate(contract(D.T, factor, -1)):
            weights_ref[0, i, j] = value
        low, high = vface_ref[0, j], vface_ref[1, j]
        flux = [
            factor[a] * (float(D[a, 0]) * low + float(D[a, PTS - 1]) * high) for a in range(PTS)
        ]
        flux = contract(D.T, flux, -1)
        for i in range(1, PTS - 1):
            work_ref[i, j] = out_ref[i, j] + flux[i]
    for i in range(1, PTS - 1):
        work_ref[i] = sum_z(work_ref[i], masks)
        low, high = work_ref[i, 0], work_ref[i, PTS - 1]
        row = lax.broadcasted_iota(jnp.int32, low.shape, 0)
        work_ref[i, PTS - 1] = high + jnp.where(row == ny - 1, 0.0, pltpu.roll(low, ny - 1, 0))
        work_ref[i, 0] = low + jnp.where(row == 0, 0.0, pltpu.roll(high, 1, 0))
        sofar_ref[i] = partial_ref[i] - gain_ref[i] * work_ref[i]
    for s in range(2):
        sofar_ref[ends[s]] = pface_ref[s] - gface_ref[s] * fface_ref[s]
    for i in range(PTS):
        factor = [mob(i, j) * (float(W[i] * W[j]) * spread[1]) for j in range(PTS)]
        for j, value in enumerate(contract(D.T, factor, -1)):
            weights_ref[1, i, j] = value
        factor = jnp.concatenate(
            [mob(i, j) * (float(W[i] * W[j]) * spread[2]) for j in range(PTS)], axis=0
        )
        weights_ref[2, i] = dot_split(factor, back).reshape(PTS, ny, width)
    for s in range(2):
        for d in range(3):
            face_weights_ref[d, s] = weights_ref[d, ends[s]]
            for i in range(PTS):
                plane_weights_ref[d, s, i] = weights_ref[d, i, ends[s]]
    points = [(i, j) for i in range(PTS) for j in range(PTS)]
    sums = restricted(
        points,
        lambda i, j: sofar_ref[i, j],
        lambda d, i, j: weights_ref[d, i, j],
        jnp.zeros((ny, width), F32),
    )
    for i in range(PTS):
        for q in range(2):
            from_load = sum(float(HAT[j, q]) * load(i, j) for j in range(PTS))
            for p in range(2):
                if HAT[i, p]:
                    sums[2 * p + q] = sums[2 * p + q] + float(HAT[i, p]) * from_load
    for n in range(8):
        sums_ref[n] = sums[n]


def restricted(points, value, weight, zero):
    sums = [zero] * 8
    along_x = {}
    along_y = {}
    along_z = {}
    for i, j in points:
        v = value(i, j)
        along_x[j] = along_x.get(j, 0.0) + weight(0, i, j) * v
        along_y[i] = along_y.get(i, 0.0) + weight(1, i, j) * v
        product = weight(2, i, j) * v
        for q in range(2):
            if HAT[j, q]:
                along_z[i, q] = along_z.get((i, q), 0.0) + float(HAT[j, q]) * product
    x_sums = [
        sum(float(HAT[j, q]) * total for j, total in along_x.items() if HAT[j, q]) for q in range(2)
    ]
    y_sums = [
        sum(float(HAT[i, p]) * total for i, total in along_y.items() if HAT[i, p]) for p in range(2)
    ]
    for p in range(2):
        for q in range(2):
            sums[2 * p + q] = -(SLOPE[p] * x_sums[q] + SLOPE[q] * y_sums[p])
            sums[4 + 2 * p + q] = -sum(
                float(HAT[i, p]) * total for (i, r), total in along_z.items() if r == q and HAT[i, p]
            )
    return sums


def corrections(even, gain_ref, gface_ref, outer_ref, below_ref, above_ref, inner_ref):
    ny, width = gain_ref.shape[2:]
    row = lax.broadcasted_iota(jnp.int32, (ny, width), 0)
    change = {}
    for j in range(PTS):
        inner, outer = inner_ref[j * ny : (j + 1) * ny], outer_ref[j * ny : (j + 1) * ny]
        change[0, j] = jnp.where(even, outer, inner)
        change[PTS - 1, j] = jnp.where(even, inner, outer)
    for i in range(PTS):
        low = jnp.where(row == 0, below_ref[0, i : i + 1], 0.0)
        high = jnp.where(row == ny - 1, above_ref[0, i : i + 1], 0.0)
        change[i, 0] = change[i, 0] + low if (i, 0) in change else low
        change[i, PTS - 1] = change[i, PTS - 1] + high if (i, PTS - 1) in change else high
    faces = {0: 0, PTS - 1: 1}
    for i, j in change:
        gain = gface_ref[faces[i], j] if i in faces else gain_ref[i, j]
        change[i, j] = -(gain * change[i, j])
    return change


def coarse_kernel(
    side_ref, gain_ref, gface_ref, sums_ref, face_weights_ref, plane_weights_ref, restrict_ref,
    outer_ref, below_ref, above_ref, inner_ref,
    planes_ref, tops_ref,
):
    below_ref, above_ref = below_ref.at[1], above_ref.at[0]
    ny, width = gain_ref.shape[2:]
    even = side_ref[0] == 0
    change = corrections(even, gain_ref, gface_ref, outer_ref, below_ref, above_ref, inner_ref)
    faces = {0: 0, PTS - 1: 1}

    def weight(d, i, j):
        return face_weights_ref[d, faces[i], j] if i in faces else plane_weights_ref[d, faces[j], i]

    sums = restricted(list(change), lambda i, j: change[i, j], weight, jnp.zeros((ny, width), F32))
    sums = [sums_ref[n] + sums[n] for n in range(8)]
    both = jnp.concatenate(
        [jnp.concatenate(sums[:4], axis=0), jnp.concatenate(sums[4:], axis=0)], axis=1
    )
    corners = dot_split(both, paired(restrict_ref[...]))
    row = lax.broadcasted_iota(jnp.int32, (ny, corners.shape[1]), 0)
    for p in range(2):
        lower = corners[(2 * p) * ny : (2 * p + 1) * ny]
        upper = corners[(2 * p + 1) * ny : (2 * p + 2) * ny]
        planes_ref[p] = lower + jnp.where(row == 0, 0.0, pltpu.roll(upper, 1, 0))
        tops_ref[p : p + 1] = upper[ny - 1 : ny]


def pressure_kernel(
    side_ref, sofar_ref, gain_ref, gface_ref, outer_ref, below_ref, above_ref, inner_ref,
    pressure_out, pressure_ref, sem,
):
    below_ref, above_ref = below_ref.at[1], above_ref.at[0]
    ny = sofar_ref.shape[2]
    even = side_ref[0] == 0
    change = corrections(even, gain_ref, gface_ref, outer_ref, below_ref, above_ref, inner_ref)
    for i in range(PTS):
        for j in range(PTS):
            value = sofar_ref[i, j]
            if (i, j) in change:
                value = value + change[i, j]
            pressure_ref[i, pl.ds(j, ny, stride=PTS)] = value
    copy = pltpu.make_async_copy(pressure_ref, pressure_out, sem)
    copy.start()
    copy.wait()


def call(body, outs, scratch, *args, spaces=None, out_spaces=None):
    spaces = spaces or [pltpu.SMEM if a.dtype == jnp.int32 else pltpu.VMEM for a in args]
    return pl.pallas_call(
        body,
        out_shape=[jax.ShapeDtypeStruct(s, F32) for s in outs],
        in_specs=[pl.BlockSpec(memory_space=m) for m in spaces],
        out_specs=[pl.BlockSpec(memory_space=m) for m in out_spaces or [pltpu.VMEM] * len(outs)],
        scratch_shapes=[pltpu.VMEM(s, F32) if isinstance(s, tuple) else s for s in scratch],
        compiler_params=pltpu.CompilerParams(vmem_limit_bytes=16 * 1024 * 1024),
    )(*args)


def from_y(faces):
    size = lax.axis_size("sub")
    up = lax.ppermute(faces, "sub", [(i, (i + 1) % size) for i in range(size)])
    if size == 2:
        return up, up
    return up, lax.ppermute(faces, "sub", [(i, (i - 1) % size) for i in range(size)])


def inner_pairs(size):
    return [(i, i ^ 1) for i in range(size)]


def outer_pairs(size):
    return [(i, (i + 1) % size if i % 2 else (i - 1) % size) for i in range(size)]


def to_x(outer, inner):
    size = lax.axis_size("dom")
    outer = lax.ppermute(outer, "dom", outer_pairs(size))
    inner = lax.ppermute(inner, "dom", inner_pairs(size))
    return outer, inner


def shards(element_load, mobility, metric):
    _, _, ny, _, width = element_load.shape
    load = element_load.reshape(PTS, ny * PTS, width)
    mob = mobility.reshape(PTS, ny * PTS, width)
    metric = metric[:, 0]
    side = (lax.axis_index("dom") % 2).astype(jnp.int32).reshape(1)
    tables = small_tables(width)
    restrict = restrict_tables(width)
    field = (PTS, PTS, ny, width)
    face = (PTS, ny, width)
    load, mob, spread, tables, restrict, yface = call(
        edge_kernel,
        [load.shape, mob.shape, (3, ny, width), tables.shape, restrict.shape, (2, 4, PTS, width)],
        [metric.shape, pltpu.SemaphoreType.DMA((5,))],
        *(pltpu.with_memory_space_constraint(a, pltpu.HBM) for a in (load, mob, metric, tables, restrict)),
        spaces=[pltpu.HBM] * 5,
    )
    below, above = from_y(yface)
    fields, xface, factor = call(
        diag_kernel, [(2,) + field, (2, 2) + face, (2, 2, PTS, width)], [], load, mob, spread, tables
    )
    rows = (2 * PTS * ny + 2 * PTS, width)
    outer, inner = to_x(*call(merge_kernel, [rows, rows], [], side, xface, factor, below, above))
    faces = (2,) + face
    rough, value, partial, gain, out, pair = call(
        inside_kernel,
        [(2,) + faces, field, field, field, field, (3,) + face],
        [face],
        fields, mob, spread, tables, below, above,
    )
    outer, inner, yface, vface, fface, pface, gface = call(
        faces_kernel,
        [(PTS * ny, width), (PTS * ny, width), (2, 1, PTS, width), faces, faces, faces, faces],
        [((2 * PTS + 4) * ny, width)],
        side, rough, value, out, pair, mob, spread, tables, below, above, outer, inner,
    )
    outer, inner = to_x(outer, inner)
    below, above = from_y(yface)
    sofar, sums, face_weights, plane_weights = call(
        partial_kernel,
        [field, (8, ny, width), (3,) + faces, (3,) + faces],
        [(3,) + field, field],
        load, mob, spread, tables, out, partial, gain, vface, fface, pface, gface,
    )
    planes, tops = call(
        coarse_kernel,
        [(2, ny, 128), (2, 128)],
        [],
        side, gain, gface, sums, face_weights, plane_weights, restrict, outer, below, above, inner,
    )
    (pressure,) = call(
        pressure_kernel,
        [(PTS, ny * PTS, width)],
        [(PTS, ny * PTS, width), pltpu.SemaphoreType.DMA(())],
        side, sofar, gain, gface, outer, below, above, inner,
        out_spaces=[pltpu.HBM],
    )
    size = lax.axis_size("sub")
    below = lax.ppermute(tops, "sub", [(i, (i + 1) % size) for i in range(size)])
    planes = planes.at[:, 0].add(below)
    size = lax.axis_size("dom")
    inner = lax.ppermute(planes[1], "dom", inner_pairs(size))
    outer = lax.ppermute(planes[1], "dom", outer_pairs(size))
    coarse = planes[0] + jnp.where(side == 0, outer, inner)
    coarse = coarse[None, :, : width // PTS + 1]
    return pressure.reshape(element_load.shape), coarse


def solution(mesh):
    in_specs = (
        P("dom", None, "sub", None, None),
        P("dom", None, "sub", None, None),
        P(None, "dom", "sub", None),
    )
    out_specs = (P("dom", None, "sub", None, None), P("dom", "sub", None))
    return jax.shard_map(shards, mesh=mesh, in_specs=in_specs, out_specs=out_specs, check_vma=False)
```

```python
import jax
import jax.numpy as jnp
import numpy as np
from jax import lax
from jax.experimental import pallas as pl
from jax.experimental.pallas import tpu as pltpu
from jax.sharding import PartitionSpec as P

GLL_NODES = np.array(
    [
        -1.0,
        -0.8717401485096066,
        -0.5917001814331423,
        -0.2092992179024789,
        0.2092992179024789,
        0.5917001814331423,
        0.8717401485096066,
        1.0,
    ]
)
GLL_WEIGHTS = np.array(
    [
        0.03571428571428571,
        0.2107042271435061,
        0.3411226924835044,
        0.4124587946587038,
        0.4124587946587038,
        0.3411226924835044,
        0.2107042271435061,
        0.03571428571428571,
    ]
)
THETA = 1.65
DELTA = 1.35
RHO_FIRST = DELTA / THETA
RHO_SECOND = 1.0 / (2.0 * THETA / DELTA - RHO_FIRST)
KEEP = 1.0 + RHO_SECOND * RHO_FIRST
GAIN = 2.0 * RHO_SECOND / DELTA
EXACT = lax.Precision.HIGHEST
PTS = 8
F32 = jnp.float32
FLOPS_JOIN = 5_000_000_000


def derivative_table():
    identity = np.eye(8)
    differences = GLL_NODES[:, None] - GLL_NODES[None, :] + identity
    barycentric = 1.0 / np.prod(differences, axis=1)
    matrix = barycentric[None, :] / barycentric[:, None] / differences
    matrix = matrix * (1.0 - identity)
    row_sums = np.sum(matrix, axis=1)
    return matrix - identity * row_sums[:, None]


D = derivative_table()
W = GLL_WEIGHTS
HAT = np.stack([(1.0 - GLL_NODES) / 8.0, (1.0 + GLL_NODES) / 8.0], axis=1)
SLOPE = (-0.125, 0.125)


def small_tables(width):
    cells = width // PTS
    grad = np.tile(D.T, (1, cells))
    back = np.tile(D, (1, cells))
    square = np.tile(D * D, (1, cells))
    weight = np.tile(W[None], (PTS, cells))
    row_weight = np.tile(W[:, None], (1, width))
    return jnp.asarray(np.stack([grad, back, square, weight, row_weight]), F32)


def restrict_tables(width):
    cells = width // PTS
    hat = np.zeros((width, 128))
    slope = np.zeros((width, 128))
    for c in range(cells):
        rows = slice(c * PTS, (c + 1) * PTS)
        hat[rows, c], hat[rows, c + 1] = HAT[:, 0], HAT[:, 1]
        slope[rows, c], slope[rows, c + 1] = SLOPE
    return jnp.asarray(np.concatenate([hat, slope]), F32)


def dot(a, b):
    return jnp.dot(a, b, precision=EXACT, preferred_element_type=F32)


def halves(a):
    high = a.astype(jnp.bfloat16)
    return high, (a - high.astype(F32)).astype(jnp.bfloat16)


def paired(b):
    high, low = halves(b)
    return jnp.concatenate(
        [
            jnp.concatenate([high, low], axis=1),
            jnp.concatenate([high, jnp.zeros_like(low)], axis=1),
        ],
        axis=0,
    )


def dot_split(a, b_pair):
    both = jnp.dot(
        jnp.concatenate(halves(a), axis=1), b_pair, preferred_element_type=F32
    )
    n = both.shape[1] // 2
    return both[:, :n] + both[:, n:]


def cell_blocks(rows):
    width = rows.shape[1]
    cell = lax.broadcasted_iota(jnp.int32, rows.shape, 1) // PTS
    return jnp.concatenate(
        [jnp.where(cell == g, rows, 0.0) for g in range(width // PTS)], axis=0
    )


def contract(matrix, lines, parity):
    n = len(lines)
    half = n // 2
    plus = [lines[c] + lines[n - 1 - c] for c in range(half)]
    minus = [lines[c] - lines[n - 1 - c] for c in range(half)]
    top, low = [], []
    for r in range(half):
        even = sum(float(0.5 * (matrix[r, c] + matrix[r, n - 1 - c])) * plus[c] for c in range(half))
        odd = sum(float(0.5 * (matrix[r, c] - matrix[r, n - 1 - c])) * minus[c] for c in range(half))
        top.append(even + odd)
        low.append(even - odd if parity > 0 else odd - even)
    return top + low[::-1]


def spread_metric(metric, weight_row):
    cells = metric.shape[2]
    width = weight_row.shape[1]
    cell = lax.broadcasted_iota(jnp.int32, (cells, width), 1) // PTS
    row = lax.broadcasted_iota(jnp.int32, (cells, width), 0)
    pick = jnp.where(cell == row, 1.0, 0.0).astype(F32)
    return [dot(metric[d], pick) * weight_row for d in range(3)]


def column_masks(shape):
    lane = lax.broadcasted_iota(jnp.int32, shape, len(shape) - 1)
    up = (lane % PTS == PTS - 1) & (lane != shape[-1] - 1)
    down = (lane % PTS == 0) & (lane != 0)
    return up, down


def sum_z(v, masks):
    width = v.shape[-1]
    axis = v.ndim - 1
    up = pltpu.roll(v, width - 1, axis)
    down = pltpu.roll(v, 1, axis)
    return v + jnp.where(masks[0], up, jnp.where(masks[1], down, 0.0))


def sum_y_local(ref, ny):
    for i in range(PTS):
        low, high = ref[i, 0], ref[i, PTS - 1]
        row = lax.broadcasted_iota(jnp.int32, low.shape, 0)
        ref[i, PTS - 1] = high + jnp.where(row == ny - 1, 0.0, pltpu.roll(low, ny - 1, 0))
        ref[i, 0] = low + jnp.where(row == 0, 0.0, pltpu.roll(high, 1, 0))


def edge_planes(ref, ny):
    low = jnp.concatenate([ref[i, 0, 0:1] for i in range(PTS)], axis=0)
    high = jnp.concatenate([ref[i, PTS - 1, ny - 1 : ny] for i in range(PTS)], axis=0)
    return low, high


def plane(ref, ny):
    return lambda i, j: ref[i, pl.ds(j, ny, stride=PTS)]


def edge_kernel(
    load_in, mob_in, metric_in, tab_in, restrict_in,
    load_ref, mob_ref, spread_ref, tab_ref, restrict_ref, yface_ref, metric_ref, sems,
):
    copies = [
        pltpu.make_async_copy(source, target, sems.at[n])
        for n, (source, target) in enumerate(
            [
                (tab_in, tab_ref),
                (metric_in, metric_ref),
                (mob_in, mob_ref),
                (load_in, load_ref),
                (restrict_in, restrict_ref),
            ]
        )
    ]
    for copy in copies:
        copy.start()
    copies[0].wait()
    copies[1].wait()
    ny, width = spread_ref.shape[1:]
    tables = tab_ref[...]
    spread = spread_metric(metric_ref[...], tables[3])
    for d in range(3):
        spread_ref[d] = spread[d]
    squared = paired(cell_blocks(tables[2]))
    square = D * D
    mob, load = plane(mob_ref, ny), plane(load_ref, ny)
    masks = column_masks((PTS * ny, width))
    copies[2].wait()
    ends = (0, PTS - 1)
    sums, weights = [[], []], [[], []]
    for i in range(PTS):
        factor = [mob(i, j) * (float(W[i]) * spread[1]) for j in range(PTS)]
        for s in range(2):
            e = 0 if s == 0 else ny - 1
            sums[s].append(sum(float(square[j, ends[s]] * W[j]) * factor[j] for j in range(PTS)))
            weights[s].append(
                sum(float(D[j, ends[s]] * W[j]) * factor[j] for j in range(PTS))[e : e + 1]
            )
    for s in range(2):
        j = ends[s]
        points = [mob(i, j) * float(W[i] * W[j]) for i in range(PTS)]
        along = contract(square.T, [p * spread[0] for p in points], 1)
        column = dot_split(jnp.concatenate([p * spread[2] for p in points], axis=0), squared)
        total = column + jnp.concatenate([along[i] + sums[s][i] for i in range(PTS)], axis=0)
        total = sum_z(total, masks)
        e = 0 if s == 0 else ny - 1
        yface_ref[s, 1] = jnp.concatenate(
            [total[i * ny + e : i * ny + e + 1] for i in range(PTS)], axis=0
        )
    copies[3].wait()
    for s in range(2):
        e = 0 if s == 0 else ny - 1
        row = e * PTS + ends[s]
        value = jnp.concatenate([load_ref[i, row : row + 1] for i in range(PTS)], axis=0)
        yface_ref[s, 0] = sum_z(value, column_masks((PTS, width)))
        points = jnp.concatenate([mob_ref[i, row : row + 1] for i in range(PTS)], axis=0)
        points = points * (float(W[ends[s]]) * tables[4])
        yface_ref[s, 2] = points * spread[0][e : e + 1]
        yface_ref[s, 3] = points * spread[2][e : e + 1]
        yface_ref[s, 4] = jnp.concatenate(weights[s], axis=0)
    copies[4].wait()


def diag_kernel(
    side_ref, load_ref, mob_ref, spread_ref, tab_ref,
    fields_ref, xface_ref, factor_ref, to_outer_ref, to_inner_ref,
):
    tables = tab_ref[...]
    ny, width = fields_ref.shape[3:]
    spread = [spread_ref[d] for d in range(3)]
    squared = paired(cell_blocks(tables[2]))
    square = D * D
    mob, load = plane(mob_ref, ny), plane(load_ref, ny)
    diag_ref = fields_ref.at[1]
    even = side_ref[0] == 0

    def post(at, low, high):
        to_inner_ref[at : at + ny] = jnp.where(even, high, low)
        to_outer_ref[at : at + ny] = jnp.where(even, low, high)

    for d in (1, 2):
        post((2 * PTS + d - 1) * ny, spread[d], spread[d])
    for j in range(PTS):
        factor = [mob(i, j) * (float(W[i] * W[j]) * spread[0]) for i in range(PTS)]
        post(j * ny, *(sum(float(D[a, i]) * factor[a] for a in range(PTS)) for i in (0, PTS - 1)))
        post((PTS + j) * ny, *(float(W[i] * W[j]) * mob(i, j) for i in (0, PTS - 1)))
        for i, value in enumerate(contract(square.T, factor, 1)):
            diag_ref[i, j] = value
    for i in range(PTS):
        factor = [mob(i, j) * (float(W[i] * W[j]) * spread[1]) for j in range(PTS)]
        for j, value in enumerate(contract(square.T, factor, 1)):
            diag_ref[i, j] += value
    for i in range(PTS):
        factor = jnp.concatenate(
            [mob(i, j) * (float(W[i] * W[j]) * spread[2]) for j in range(PTS)], axis=0
        )
        diag_ref[i] += dot_split(factor, squared).reshape(PTS, ny, width)
        fields_ref[0, i] = jnp.stack([load(i, j) for j in range(PTS)], axis=0)
    masks = column_masks((PTS, ny, width))
    for f in range(2):
        for i in range(PTS):
            fields_ref[f, i] = sum_z(fields_ref[f, i], masks)
        sum_y_local(fields_ref.at[f], ny)
        xface_ref[f, 0] = fields_ref[f, 0]
        xface_ref[f, 1] = fields_ref[f, PTS - 1]
    for s, i in enumerate((0, PTS - 1)):
        for n, e in enumerate((0, ny - 1)):
            points = mob_ref[i, e * PTS : (e + 1) * PTS] * (float(W[i]) * tables[4])
            factor_ref[s, n] = points * spread[1][e : e + 1]


def merge_kernel(side_ref, xface_ref, factor_ref, below_ref, above_ref, outer_ref, inner_ref):
    below_ref, above_ref = below_ref.at[1], above_ref.at[0]
    even = side_ref[0] == 0
    fields, _, _, ny, width = xface_ref.shape
    row = lax.broadcasted_iota(jnp.int32, (ny, width), 0)
    for f in range(fields):
        for j in range(PTS):
            low, high = xface_ref[f, 0, j], xface_ref[f, 1, j]
            if j == 0:
                low = low + jnp.where(row == 0, below_ref[f, 0:1], 0.0)
                high = high + jnp.where(row == 0, below_ref[f, PTS - 1 : PTS], 0.0)
            if j == PTS - 1:
                low = low + jnp.where(row == ny - 1, above_ref[f, 0:1], 0.0)
                high = high + jnp.where(row == ny - 1, above_ref[f, PTS - 1 : PTS], 0.0)
            at = (f * PTS + j) * ny
            inner_ref[at : at + ny] = jnp.where(even, high, low)
            outer_ref[at : at + ny] = jnp.where(even, low, high)
    for n in range(2):
        at = fields * PTS * ny + n * PTS
        low, high = factor_ref[0, n], factor_ref[1, n]
        inner_ref[at : at + PTS] = jnp.where(even, high, low)
        outer_ref[at : at + PTS] = jnp.where(even, low, high)


def inside_kernel(
    fields_ref, load_ref, mob_ref, spread_ref, tab_ref, below_ref, above_ref,
    rough_ref, value_ref, partial_ref, gain_ref, out_ref, pair_ref, weights_ref, sums_ref, edge_weights_ref,
    work_ref,
):
    below_ref, above_ref = below_ref.at[1], above_ref.at[0]
    tables = tab_ref[...]
    ny, width = out_ref.shape[2:]
    spread = [spread_ref[d] for d in range(3)]
    mob, load = plane(mob_ref, ny), plane(load_ref, ny)
    row = lax.broadcasted_iota(jnp.int32, (ny, width), 0)
    zero = jnp.zeros((ny, width), F32)
    for i in range(PTS):
        for j in range(PTS):
            sums = [fields_ref[f, i, j] for f in range(2)]
            for f in range(2):
                if j == 0:
                    sums[f] += jnp.where(row == 0, below_ref[f, i : i + 1], 0.0)
                if j == PTS - 1:
                    sums[f] += jnp.where(row == ny - 1, above_ref[f, i : i + 1], 0.0)
            if i in (0, PTS - 1):
                for f in range(2):
                    rough_ref[f, 0 if i == 0 else 1, j] = sums[f]
                value_ref[i, j] = partial_ref[i, j] = gain_ref[i, j] = zero
            else:
                value_ref[i, j], partial_ref[i, j], gain_ref[i, j] = first_step(*sums)
    grad = paired(cell_blocks(tables[0]))
    back = paired(cell_blocks(tables[1]))
    for j in range(PTS):
        factor = [mob(i, j) * (float(W[i] * W[j]) * spread[0]) for i in range(PTS)]
        for n, (p, q) in enumerate(((0, 0), (0, PTS - 1), (PTS - 1, PTS - 1))):
            pair_ref[n, j] = sum(float(D[a, p] * D[a, q]) * factor[a] for a in range(PTS))
        flux = contract(D, [value_ref[i, j] for i in range(PTS)], -1)
        flux = [flux[i] * factor[i] for i in range(PTS)]
        for i, value in enumerate(contract(D.T, flux, -1)):
            out_ref[i, j] = value
        for i, value in enumerate(contract(D.T, factor, -1)):
            weights_ref[0, i, j] = value
    for i in range(1, PTS - 1):
        flux = contract(D, [value_ref[i, j] for j in range(PTS)], -1)
        flux = [flux[j] * (mob(i, j) * (float(W[i] * W[j]) * spread[1])) for j in range(PTS)]
        for j, value in enumerate(contract(D.T, flux, -1)):
            out_ref[i, j] += value
        work_ref[...] = dot_split(value_ref[i].reshape(PTS * ny, width), grad).reshape(PTS, ny, width)
        for j in range(PTS):
            work_ref[j] *= mob(i, j) * (float(W[i] * W[j]) * spread[2])
        out_ref[i] += dot_split(work_ref[...].reshape(PTS * ny, width), back).reshape(PTS, ny, width)
    for i in range(PTS):
        factor = [mob(i, j) * (float(W[i] * W[j]) * spread[1]) for j in range(PTS)]
        for j, value in enumerate(contract(D.T, factor, -1)):
            weights_ref[1, i, j] = value
        factor = jnp.concatenate(
            [mob(i, j) * (float(W[i] * W[j]) * spread[2]) for j in range(PTS)], axis=0
        )
        weights_ref[2, i] = dot_split(factor, back).reshape(PTS, ny, width)
    sums = [zero] * 4
    for i in range(PTS):
        for q in range(2):
            from_load = sum(float(HAT[j, q]) * load(i, j) for j in range(PTS))
            for p in range(2):
                if HAT[i, p]:
                    sums[2 * p + q] = sums[2 * p + q] + float(HAT[i, p]) * from_load
    for n in range(4):
        sums_ref[n] = sums[n]
    for t, ref in enumerate((below_ref, above_ref)):
        edge_weights_ref[t, 0] = dot(tables[0][:, :PTS], ref[2])
        edge_weights_ref[t, 1] = ref[4]
        edge_weights_ref[t, 2] = dot_split(ref[3], back)


def first_step(right, diagonal):
    inverse = 1.0 / diagonal
    scaled = inverse * right
    value = scaled * (1.0 / THETA)
    return value, KEEP * value + GAIN * scaled, GAIN * inverse


def faces_kernel(
    side_ref, rough_ref, value_ref, out_ref, pair_ref, mob_ref, spread_ref, tab_ref,
    below_ref, above_ref, partial_ref, gain_ref, weights_ref, load_sums_ref, edge_weights_ref,
    outer_ref, inner_ref,
    to_outer_ref, to_inner_ref, yface_ref, gface_ref, sofar_ref, sums_ref, line_ref, work_ref,
):
    below_ref, above_ref = below_ref.at[1], above_ref.at[0]
    even = side_ref[0] == 0
    tables = tab_ref[...]
    ny, width = out_ref.shape[2:]
    spread = [spread_ref[d] for d in range(3)]
    mob = plane(mob_ref, ny)
    ends = (0, PTS - 1)
    rows = (0, ny - 1)
    row = lax.broadcasted_iota(jnp.int32, (ny, width), 0)
    masks = column_masks((ny, width))

    def arrived(at, count):
        inner, outer = inner_ref[at : at + count], outer_ref[at : at + count]
        return jnp.where(even, outer, inner), jnp.where(even, inner, outer)

    value = [[None] * PTS, [None] * PTS]
    pface = [[None] * PTS, [None] * PTS]
    gface = [[None] * PTS, [None] * PTS]
    for j in range(PTS):
        load = arrived(j * ny, ny)
        diagonal = arrived((PTS + j) * ny, ny)
        for s in range(2):
            value[s][j], pface[s][j], gface[s][j] = first_step(
                rough_ref[0, s, j] + load[s], rough_ref[1, s, j] + diagonal[s]
            )
            gface_ref[s, j] = gface[s][j]
    lines = [value[s][j] for s in range(2) for j in range(PTS)]
    factors = [
        mob(ends[s], j) * (float(W[ends[s]] * W[j]) * spread[2]) for s in range(2) for j in range(PTS)
    ]
    for s in range(2):
        for t, ref in enumerate((below_ref, above_ref)):
            lines.append(value[s][ends[t]])
            factors.append(jnp.broadcast_to(ref[3, ends[s] : ends[s] + 1], (ny, width)))
    grad = paired(cell_blocks(tables[0]))
    back = paired(cell_blocks(tables[1]))
    flux = dot_split(jnp.concatenate(lines, axis=0), grad) * jnp.concatenate(factors, axis=0)
    line_ref[...] = dot_split(flux, back)
    edge_y = [[None, None], [None, None]]
    total = [[None] * PTS, [None] * PTS]
    for s in range(2):
        gradient = contract(D, value[s], -1)
        flux = [
            gradient[j] * (mob(ends[s], j) * (float(W[ends[s]] * W[j]) * spread[1])) for j in range(PTS)
        ]
        total[s] = contract(D.T, flux, -1)
        for t in range(2):
            factor = arrived(2 * PTS * ny + t * PTS, PTS)[s]
            edge_y[s][t] = sum(
                float(D[j, ends[t]]) * (gradient[j] * factor[j : j + 1]) for j in range(PTS)
            )[rows[t] : rows[t] + 1]
    for j in range(PTS):
        total[0][j] += out_ref[0, j] + pair_ref[0, j] * value[0][j] + pair_ref[1, j] * value[1][j]
        total[1][j] += out_ref[PTS - 1, j] + pair_ref[1, j] * value[0][j] + pair_ref[2, j] * value[1][j]
    for s in range(2):
        for j in range(PTS):
            at = (s * PTS + j) * ny
            total[s][j] += line_ref[at : at + ny]
    for j in range(PTS):
        flux = [
            mob(a, j)
            * (float(W[a] * W[j]) * spread[0])
            * (float(D[a, 0]) * value[0][j] + float(D[a, PTS - 1]) * value[1][j])
            for a in range(PTS)
        ]
        flux = contract(D.T, flux, -1)
        for i in range(1, PTS - 1):
            work_ref[i, j] = out_ref[i, j] + flux[i]
    ymessage = []
    for t in range(2):
        j = ends[t]
        edge = [total[0][j]] + [work_ref[i, j] for i in range(1, PTS - 1)] + [total[1][j]]
        edge = [v[rows[t] : rows[t] + 1] for v in edge]
        edge[0] += edge_y[0][t]
        edge[PTS - 1] += edge_y[1][t]
        ymessage.append(sum_z(jnp.concatenate(edge, axis=0), column_masks((PTS, width))))
        yface_ref[t, 0] = ymessage[t]
    extra = [[None, None], [None, None]]
    for t, ref in enumerate((below_ref, above_ref)):
        j = ends[t]
        points = [value[0][j]] + [value_ref[i, j] for i in range(1, PTS - 1)] + [value[1][j]]
        flux = contract(D, points, -1)
        flux = contract(D.T, [flux[i] * ref[2, i : i + 1] for i in range(PTS)], -1)
        for s in range(2):
            at = (2 * PTS + 2 * s + t) * ny
            extra[s][t] = sum_z(flux[ends[s]] + line_ref[at : at + ny], masks)
            extra[s][t] = jnp.where(row == rows[t], extra[s][t], 0.0)
    for s in range(2):
        for j in range(PTS):
            total[s][j] = sum_z(total[s][j], masks)
        low, high = total[s][0], total[s][PTS - 1]
        total[s][PTS - 1] = high + jnp.where(row == ny - 1, 0.0, pltpu.roll(low, ny - 1, 0))
        total[s][0] = low + jnp.where(row == 0, 0.0, pltpu.roll(high, 1, 0))
    for j in range(PTS):
        low, high = total[0][j], total[1][j]
        if j in ends:
            t = ends.index(j)
            low, high = low + extra[0][t], high + extra[1][t]
        to_inner_ref[j * ny : (j + 1) * ny] = jnp.where(even, high, low)
        to_outer_ref[j * ny : (j + 1) * ny] = jnp.where(even, low, high)
        for s in range(2):
            sofar_ref[ends[s], j] = pface[s][j] - gface[s][j] * total[s][j]
    for i in range(1, PTS - 1):
        lines = [sum_z(work_ref[i, j], masks) for j in range(PTS)]
        low, high = lines[0], lines[PTS - 1]
        lines[PTS - 1] = high + jnp.where(row == ny - 1, 0.0, pltpu.roll(low, ny - 1, 0))
        lines[0] = low + jnp.where(row == 0, 0.0, pltpu.roll(high, 1, 0))
        for j in range(PTS):
            sofar_ref[i, j] = partial_ref[i, j] - gain_ref[i, j] * lines[j]
    sums = restricted(
        [(i, j) for i in range(PTS) for j in range(PTS)],
        lambda i, j: sofar_ref[i, j],
        lambda d, i, j: weights_ref[d, i, j],
        jnp.zeros((ny, width), F32),
    )
    for q in range(2):
        sums_ref[q] = sums[q] + load_sums_ref[q]
        sums_ref[2 + q] = sums[4 + q]
        sums[2 + q] = sums[2 + q] + load_sums_ref[2 + q]
    base = PTS * ny
    changes = []
    for t in range(2):
        j = ends[t]
        gain = [gface[0][j]] + [gain_ref[i, j] for i in range(1, PTS - 1)] + [gface[1][j]]
        gain = jnp.concatenate([g[rows[t] : rows[t] + 1] for g in gain], axis=0)
        changes += edge_change(-(gain * ymessage[t]), edge_weights_ref.at[t], ends[1 - t])
    changes = jnp.concatenate(changes, axis=0)
    for ref in (to_outer_ref, to_inner_ref):
        for n, k in enumerate((2, 3, 6, 7)):
            ref[base + n * ny : base + (n + 1) * ny] = sums[k]
        ref[base + 4 * ny : base + 4 * ny + PTS] = changes


def edge_change(change, weight_ref, j):
    upper = lax.broadcasted_iota(jnp.int32, change.shape, 0)
    hat = jnp.zeros_like(change)
    for i in range(PTS):
        hat = jnp.where(upper == i, float(HAT[i, 1]), hat)
    along_x, along_y, along_z = (
        jnp.sum(v, axis=0, keepdims=True)
        for v in (weight_ref[0] * change, hat * weight_ref[1] * change, hat * weight_ref[2] * change)
    )
    smooth = [-(SLOPE[1] * float(HAT[j, q]) * along_x + SLOPE[q] * along_y) for q in range(2)]
    return smooth + [-float(HAT[j, q]) * along_z for q in range(2)]


def restricted(points, value, weight, zero):
    sums = [zero] * 8
    along_x = {}
    along_y = {}
    along_z = {}
    for i, j in points:
        v = value(i, j)
        along_x[j] = along_x.get(j, 0.0) + weight(0, i, j) * v
        along_y[i] = along_y.get(i, 0.0) + weight(1, i, j) * v
        product = weight(2, i, j) * v
        for q in range(2):
            if HAT[j, q]:
                along_z[i, q] = along_z.get((i, q), 0.0) + float(HAT[j, q]) * product
    x_sums = [
        sum(float(HAT[j, q]) * total for j, total in along_x.items() if HAT[j, q]) for q in range(2)
    ]
    y_sums = [
        sum(float(HAT[i, p]) * total for i, total in along_y.items() if HAT[i, p]) for p in range(2)
    ]
    for p in range(2):
        for q in range(2):
            sums[2 * p + q] = -(SLOPE[p] * x_sums[q] + SLOPE[q] * y_sums[p])
            sums[4 + 2 * p + q] = -sum(
                float(HAT[i, p]) * total for (i, r), total in along_z.items() if r == q and HAT[i, p]
            )
    return sums


def corrections(even, gain_ref, gface_ref, outer_ref, below_ref, above_ref, inner_ref):
    ny, width = gain_ref.shape[2:]
    row = lax.broadcasted_iota(jnp.int32, (ny, width), 0)
    change = {}
    for j in range(PTS):
        inner, outer = inner_ref[j * ny : (j + 1) * ny], outer_ref[j * ny : (j + 1) * ny]
        change[0, j] = jnp.where(even, outer, inner)
        change[PTS - 1, j] = jnp.where(even, inner, outer)
    for i in range(PTS):
        low = jnp.where(row == 0, below_ref[0, i : i + 1], 0.0)
        high = jnp.where(row == ny - 1, above_ref[0, i : i + 1], 0.0)
        change[i, 0] = change[i, 0] + low if (i, 0) in change else low
        change[i, PTS - 1] = change[i, PTS - 1] + high if (i, PTS - 1) in change else high
    faces = {0: 0, PTS - 1: 1}
    for i, j in change:
        gain = gface_ref[faces[i], j] if i in faces else gain_ref[i, j]
        change[i, j] = -(gain * change[i, j])
    return change


def face_change(change, weight, i, p, q):
    along_x = sum(float(HAT[j, q]) * (weight[0][j] * change[j]) for j in range(PTS) if HAT[j, q])
    smooth = SLOPE[p] * along_x
    slope = 0.0
    if HAT[i, p]:
        along_y = sum(weight[1][j] * change[j] for j in range(PTS))
        smooth = smooth + float(HAT[i, p]) * SLOPE[q] * along_y
        along_z = sum(float(HAT[j, q]) * (weight[2][j] * change[j]) for j in range(PTS) if HAT[j, q])
        slope = float(HAT[i, p]) * along_z
    return -smooth, -slope


def to_vertices(smooth, slope, restrict):
    return dot_split(jnp.concatenate([smooth, slope], axis=1), restrict)


def ahead_kernel(
    side_ref, sent_outer_ref, sent_inner_ref, gface_ref, tab_ref, restrict_ref, outer_ref, inner_ref, yface_ref,
    own_ref, next_ref, top_ref, to_y_ref,
):
    ny, width = gface_ref.shape[2:]
    to_y_ref[...] = yface_ref[...]
    even = side_ref[0] == 0
    back = paired(cell_blocks(tab_ref[1]))

    def rows(at, first, second):
        return jnp.where(even, first[at : at + ny], second[at : at + ny])

    change = [-(gface_ref[0, j] * rows(j * ny, sent_outer_ref, sent_inner_ref)) for j in range(PTS)]
    spread = [rows((2 * PTS + d) * ny, outer_ref, inner_ref) for d in range(2)]
    points = [rows((PTS + j) * ny, outer_ref, inner_ref) for j in range(PTS)]
    column = dot_split(jnp.concatenate([p * spread[1] for p in points], axis=0), back)
    weight = [
        [rows(j * ny, outer_ref, inner_ref) for j in range(PTS)],
        contract(D.T, [p * spread[0] for p in points], -1),
        [column[j * ny : (j + 1) * ny] for j in range(PTS)],
    ]
    for q in range(2):
        own_ref[q], own_ref[2 + q] = face_change(change, weight, PTS - 1, 1, q)
    change = [-(gface_ref[1, j] * rows(j * ny, sent_inner_ref, sent_outer_ref)) for j in range(PTS)]
    weight = [[rows(j * ny, inner_ref, outer_ref) for j in range(PTS)]]
    smooth = jnp.concatenate([face_change(change, weight, 0, 1, q)[0] for q in range(2)], axis=0)
    corners = to_vertices(smooth, jnp.zeros_like(smooth), paired(restrict_ref[...]))
    lower, upper = corners[:ny], corners[ny:]
    row = lax.broadcasted_iota(jnp.int32, lower.shape, 0)
    next_ref[...] = lower + jnp.where(row == 0, 0.0, pltpu.roll(upper, 1, 0))
    top_ref[...] = upper[ny - 1 : ny]


def coarse_kernel(
    side_ref, gain_ref, gface_ref, sums_ref, own_ref, weights_ref, restrict_ref,
    outer_ref, below_ref, above_ref, inner_ref,
    plane_ref, edge_ref,
):
    below_ref, above_ref = below_ref.at[1], above_ref.at[0]
    ny, width = gain_ref.shape[2:]
    even = side_ref[0] == 0
    change = corrections(even, gain_ref, gface_ref, outer_ref, below_ref, above_ref, inner_ref)
    sums = restricted(
        list(change),
        lambda i, j: change[i, j],
        lambda d, i, j: weights_ref[d, i, j],
        jnp.zeros((ny, width), F32),
    )
    base = PTS * ny

    def before(at, count):
        return jnp.where(even, outer_ref[at : at + count], inner_ref[at : at + count])

    total = [
        sums[(0, 1, 4, 5)[n]] + sums_ref[n] + own_ref[n] + before(base + n * ny, ny) for n in range(4)
    ]
    extra = before(base + 4 * ny, PTS)
    smooth = jnp.concatenate(total[:2] + [extra], axis=0)
    slope = jnp.concatenate(total[2:] + [pltpu.roll(extra, PTS - 2, 0)], axis=0)
    corners = to_vertices(smooth, slope, paired(restrict_ref[...]))
    lower, upper = corners[:ny], corners[ny : 2 * ny]
    extra = corners[2 * ny :]
    row = lax.broadcasted_iota(jnp.int32, lower.shape, 0)
    shifted = jnp.where(row == 0, extra[1:2], pltpu.roll(upper, 1, 0))
    plane_ref[...] = lower + shifted
    edge_ref[0:1] = upper[ny - 1 : ny] + extra[4:5]
    edge_ref[1:2] = extra[5:6]
    edge_ref[2:3] = extra[0:1]


def pressure_kernel(
    side_ref, sofar_ref, gain_ref, gface_ref, outer_ref, below_ref, above_ref, inner_ref,
    pressure_out, token_ref, pressure_ref, sem,
):
    token_ref[...] = jnp.zeros_like(token_ref)
    below_ref, above_ref = below_ref.at[1], above_ref.at[0]
    ny = sofar_ref.shape[2]
    even = side_ref[0] == 0
    change = corrections(even, gain_ref, gface_ref, outer_ref, below_ref, above_ref, inner_ref)
    for i in range(PTS):
        for j in range(PTS):
            value = sofar_ref[i, j]
            if (i, j) in change:
                value = value + change[i, j]
            pressure_ref[i, pl.ds(j, ny, stride=PTS)] = value
    copy = pltpu.make_async_copy(pressure_ref, pressure_out, sem)
    copy.start()
    copy.wait()


def join_kernel(next_ref, top_ref, token_ref, joined_ref):
    row = lax.broadcasted_iota(jnp.int32, next_ref.shape, 0)
    joined_ref[...] = next_ref[...] + jnp.where(row == 0, top_ref[...], 0.0) + token_ref[...]


def last_kernel(plane_ref, joined_ref, below_ref, above_ref, coarse_ref):
    total = plane_ref[...] + joined_ref[...]
    ny = total.shape[0]
    row = lax.broadcasted_iota(jnp.int32, total.shape, 0)
    total = total + jnp.where(row == 0, below_ref[0:1], jnp.where(row == 1, below_ref[1:2], 0.0))
    total = total + jnp.where(row == ny - 1, above_ref[2:3], 0.0)
    coarse_ref[...] = total[:, : coarse_ref.shape[1]]


def call(body, outs, scratch, *args, spaces=None, out_spaces=None, flops=None):
    spaces = spaces or [pltpu.SMEM if a.dtype == jnp.int32 else pltpu.VMEM for a in args]
    return pl.pallas_call(
        body,
        out_shape=[jax.ShapeDtypeStruct(s, F32) for s in outs],
        in_specs=[pl.BlockSpec(memory_space=m) for m in spaces],
        out_specs=[pl.BlockSpec(memory_space=m) for m in out_spaces or [pltpu.VMEM] * len(outs)],
        scratch_shapes=[pltpu.VMEM(s, F32) if isinstance(s, tuple) else s for s in scratch],
        compiler_params=pltpu.CompilerParams(vmem_limit_bytes=16 * 1024 * 1024),
        cost_estimate=flops and pl.CostEstimate(flops=flops, bytes_accessed=0, transcendentals=0),
    )(*args)


def from_y(faces):
    size = lax.axis_size("sub")
    up = lax.ppermute(faces, "sub", [(i, (i + 1) % size) for i in range(size)])
    if size == 2:
        return up, up
    return up, lax.ppermute(faces, "sub", [(i, (i - 1) % size) for i in range(size)])


def inner_pairs(size):
    return [(i, i ^ 1) for i in range(size)]


def outer_pairs(size):
    return [(i, (i + 1) % size if i % 2 else (i - 1) % size) for i in range(size)]


def to_x(outer, inner):
    size = lax.axis_size("dom")
    outer = lax.ppermute(outer, "dom", outer_pairs(size))
    inner = lax.ppermute(inner, "dom", inner_pairs(size))
    return outer, inner


def two_on(rows, top):
    size, rest = lax.axis_size("dom"), lax.axis_size("sub")
    rows = lax.ppermute(rows, "dom", [(i, (i + 2) % size) for i in range(size)])
    pairs = [
        (i * rest + k, (i + 2) % size * rest + (k + 1) % rest) for i in range(size) for k in range(rest)
    ]
    return rows, lax.ppermute(top, ("dom", "sub"), pairs)


def shards(element_load, mobility, metric):
    _, _, ny, _, width = element_load.shape
    load = element_load.reshape(PTS, ny * PTS, width)
    mob = mobility.reshape(PTS, ny * PTS, width)
    metric = metric[:, 0]
    side = (lax.axis_index("dom") % 2).astype(jnp.int32).reshape(1)
    tables = small_tables(width)
    restrict = restrict_tables(width)
    field = (PTS, PTS, ny, width)
    face = (PTS, ny, width)
    load, mob, spread, tables, restrict, yface = call(
        edge_kernel,
        [load.shape, mob.shape, (3, ny, width), tables.shape, restrict.shape, (2, 5, PTS, width)],
        [metric.shape, pltpu.SemaphoreType.DMA((5,))],
        *(pltpu.with_memory_space_constraint(a, pltpu.HBM) for a in (load, mob, metric, tables, restrict)),
        spaces=[pltpu.HBM] * 5,
    )
    below, above = from_y(yface)
    still = (2 * (PTS + 1) * ny, width)
    fields, xface, factor, still_outer, still_inner = call(
        diag_kernel,
        [(2,) + field, (2, 2) + face, (2, 2, PTS, width), still, still],
        [],
        side, load, mob, spread, tables,
    )
    rows = (2 * PTS * ny + 2 * PTS, width)
    outer, inner = to_x(*call(merge_kernel, [rows, rows], [], side, xface, factor, below, above))
    still_outer, still_inner = to_x(still_outer, still_inner)
    faces = (2,) + face
    rough, value, partial, gain, out, pair, weights, load_sums, edge_weights = call(
        inside_kernel,
        [
            (2,) + faces, field, field, field, field, (3,) + face,
            (3,) + field, (4, ny, width), (2, 3, PTS, width),
        ],
        [face],
        fields, load, mob, spread, tables, below, above,
    )
    rows = ((PTS + 4) * ny + PTS, width)
    sent_outer, sent_inner, yface, gface, sofar, sums = call(
        faces_kernel,
        [rows, rows, (2, 1, PTS, width), faces, field, (4, ny, width)],
        [((2 * PTS + 4) * ny, width), field],
        side, rough, value, out, pair, mob, spread, tables, below, above,
        partial, gain, weights, load_sums, edge_weights, outer, inner,
    )
    outer, inner = to_x(sent_outer, sent_inner)
    own, onward, top, yface = call(
        ahead_kernel,
        [(4, ny, width), (ny, 128), (1, 128), yface.shape],
        [],
        side, sent_outer, sent_inner, gface, tables, restrict, still_outer, still_inner, yface,
    )
    onward, top = two_on(onward, top)
    below, above = from_y(yface)
    plane, edge = call(
        coarse_kernel,
        [(ny, 128), (3, 128)],
        [],
        side, gain, gface, sums, own, weights, restrict, outer, below, above, inner,
    )
    pressure, token = call(
        pressure_kernel,
        [(PTS, ny * PTS, width), (1, 128)],
        [(PTS, ny * PTS, width), pltpu.SemaphoreType.DMA(())],
        side, sofar, gain, gface, outer, below, above, inner,
        out_spaces=[pltpu.HBM, pltpu.VMEM],
    )
    (onward,) = call(join_kernel, [(ny, 128)], [], onward, top, token, flops=FLOPS_JOIN)
    below, above = from_y(edge)
    (coarse,) = call(last_kernel, [(ny, width // PTS + 1)], [], plane, onward, below, above)
    return pressure.reshape(element_load.shape), coarse[None]


def solution(mesh):
    in_specs = (
        P("dom", None, "sub", None, None),
        P("dom", None, "sub", None, None),
        P(None, "dom", "sub", None),
    )
    out_specs = (P("dom", None, "sub", None, None), P("dom", "sub", None))
    return jax.shard_map(shards, mesh=mesh, in_specs=in_specs, out_specs=out_specs, check_vma=False)
```

```python
import jax
import jax.numpy as jnp
import ml_dtypes
import numpy as np
from jax import lax
from jax.experimental import pallas as pl
from jax.experimental.pallas import tpu as pltpu
from jax.sharding import PartitionSpec as P

GLL_NODES = np.array(
    [
        -1.0,
        -0.8717401485096066,
        -0.5917001814331423,
        -0.2092992179024789,
        0.2092992179024789,
        0.5917001814331423,
        0.8717401485096066,
        1.0,
    ]
)
GLL_WEIGHTS = np.array(
    [
        0.03571428571428571,
        0.2107042271435061,
        0.3411226924835044,
        0.4124587946587038,
        0.4124587946587038,
        0.3411226924835044,
        0.2107042271435061,
        0.03571428571428571,
    ]
)
THETA = 1.65
DELTA = 1.35
RHO_FIRST = DELTA / THETA
RHO_SECOND = 1.0 / (2.0 * THETA / DELTA - RHO_FIRST)
KEEP = 1.0 + RHO_SECOND * RHO_FIRST
GAIN = 2.0 * RHO_SECOND / DELTA
EXACT = lax.Precision.HIGHEST
PTS = 8
F32 = jnp.float32
FLOPS_JOIN = 5_000_000_000


def derivative_table():
    identity = np.eye(8)
    differences = GLL_NODES[:, None] - GLL_NODES[None, :] + identity
    barycentric = 1.0 / np.prod(differences, axis=1)
    matrix = barycentric[None, :] / barycentric[:, None] / differences
    matrix = matrix * (1.0 - identity)
    row_sums = np.sum(matrix, axis=1)
    return matrix - identity * row_sums[:, None]


D = derivative_table()
W = GLL_WEIGHTS
HAT = np.stack([(1.0 - GLL_NODES) / 8.0, (1.0 + GLL_NODES) / 8.0], axis=1)
SLOPE = (-0.125, 0.125)


def tiled(matrix, width):
    column = lax.broadcasted_iota(jnp.int32, (PTS, width), 1) % PTS
    row = lax.broadcasted_iota(jnp.int32, (PTS, width), 0)
    total = jnp.zeros((PTS, width), F32)
    for c in range(PTS):
        lines = jnp.zeros((PTS, width), F32)
        for r in range(PTS):
            lines = jnp.where(row == r, float(matrix[r, c]), lines)
        total = jnp.where(column == c, lines, total)
    return total


def by_row(values, width):
    return tiled(np.tile(np.asarray(values)[:, None], (1, PTS)), width)


def cell_blocks(rows):
    width = rows.shape[1]
    cell = lax.broadcasted_iota(jnp.int32, rows.shape, 1) // PTS
    return jnp.concatenate(
        [jnp.where(cell == g, rows, 0.0) for g in range(width // PTS)], axis=0
    )


def paired_here(b):
    high, low = halves(b)
    return jnp.concatenate(
        [
            jnp.concatenate([high, low], axis=1),
            jnp.concatenate([high, jnp.zeros_like(low)], axis=1),
        ],
        axis=0,
    )


def paired(b):
    b = np.asarray(b, np.float32)
    high = b.astype(ml_dtypes.bfloat16)
    low = (b - high.astype(np.float32)).astype(ml_dtypes.bfloat16)
    return jnp.asarray(np.block([[high, low], [high, np.zeros_like(low)]]))


def column_tables(width):
    cells = np.eye(width // PTS)
    return paired(np.kron(cells, D.T)), paired(np.kron(cells, D))


def restrict_table(width):
    cells = width // PTS
    hat = np.zeros((width, 128))
    slope = np.zeros((width, 128))
    for c in range(cells):
        rows = slice(c * PTS, (c + 1) * PTS)
        hat[rows, c], hat[rows, c + 1] = HAT[:, 0], HAT[:, 1]
        slope[rows, c], slope[rows, c + 1] = SLOPE
    return paired(np.concatenate([hat, slope]))


def dot(a, b):
    return jnp.dot(a, b, precision=EXACT, preferred_element_type=F32)


def halves(a):
    high = a.astype(jnp.bfloat16)
    return high, (a - high.astype(F32)).astype(jnp.bfloat16)


def dot_split(a, b_pair):
    both = jnp.dot(
        jnp.concatenate(halves(a), axis=1), b_pair, preferred_element_type=F32
    )
    n = both.shape[1] // 2
    return both[:, :n] + both[:, n:]


def contract(matrix, lines, parity):
    n = len(lines)
    half = n // 2
    plus = [lines[c] + lines[n - 1 - c] for c in range(half)]
    minus = [lines[c] - lines[n - 1 - c] for c in range(half)]
    top, low = [], []
    for r in range(half):
        even = sum(float(0.5 * (matrix[r, c] + matrix[r, n - 1 - c])) * plus[c] for c in range(half))
        odd = sum(float(0.5 * (matrix[r, c] - matrix[r, n - 1 - c])) * minus[c] for c in range(half))
        top.append(even + odd)
        low.append(even - odd if parity > 0 else odd - even)
    return top + low[::-1]


def spread_metric(metric, weight_row):
    _, rows, cells = metric.shape
    width = weight_row.shape[1]
    cell = lax.broadcasted_iota(jnp.int32, (cells, width), 1) // PTS
    row = lax.broadcasted_iota(jnp.int32, (cells, width), 0)
    pick = jnp.where(cell == row, 1.0, 0.0).astype(jnp.bfloat16)
    flat = metric.reshape(3 * rows, cells)
    high = flat.astype(jnp.bfloat16)
    rest = flat - high.astype(F32)
    parts = jnp.concatenate([high, *halves(rest)], axis=1)
    spread = jnp.dot(
        parts, jnp.concatenate([pick] * 3, axis=0), preferred_element_type=F32
    )
    spread = [spread[d * rows : (d + 1) * rows] for d in range(3)]
    return [v * weight_row[:1] for v in spread], spread[2]


def column_masks(shape):
    lane = lax.broadcasted_iota(jnp.int32, shape, len(shape) - 1)
    up = (lane % PTS == PTS - 1) & (lane != shape[-1] - 1)
    down = (lane % PTS == 0) & (lane != 0)
    return up, down


def sum_z(v, masks):
    width = v.shape[-1]
    axis = v.ndim - 1
    up = pltpu.roll(v, width - 1, axis)
    down = pltpu.roll(v, 1, axis)
    return v + jnp.where(masks[0], up, jnp.where(masks[1], down, 0.0))


def sum_y_local(ref, ny):
    for i in range(PTS):
        low, high = ref[i, 0], ref[i, PTS - 1]
        row = lax.broadcasted_iota(jnp.int32, low.shape, 0)
        ref[i, PTS - 1] = high + jnp.where(row == ny - 1, 0.0, pltpu.roll(low, ny - 1, 0))
        ref[i, 0] = low + jnp.where(row == 0, 0.0, pltpu.roll(high, 1, 0))


def edge_planes(ref, ny):
    low = jnp.concatenate([ref[i, 0, 0:1] for i in range(PTS)], axis=0)
    high = jnp.concatenate([ref[i, PTS - 1, ny - 1 : ny] for i in range(PTS)], axis=0)
    return low, high


def plane(ref, ny):
    return lambda i, j: ref[i, pl.ds(j, ny, stride=PTS)]


def edge_kernel(metric_in, mob_in, load_in, spread_ref, yface_ref, metric_ref, mob_ref, load_ref, sems):
    ny, width = spread_ref.shape[1:]
    ends = (0, PTS - 1)
    copies = [pltpu.make_async_copy(metric_in, metric_ref, sems.at[0])]
    for n, (source, target) in enumerate(((mob_in, mob_ref), (load_in, load_ref))):
        for s, e in enumerate((0, ny - 1)):
            copies.append(
                pltpu.make_async_copy(
                    source.at[:, pl.ds(e * PTS, PTS)], target.at[s], sems.at[1 + 2 * n + s]
                )
            )
    for copy in copies:
        copy.start()
    masks = column_masks((PTS, width))
    weight_row = tiled(np.tile(W[None], (PTS, 1)), width)
    row_weight = by_row(W, width)
    squared = paired_here(cell_blocks(tiled(D * D, width)))
    squares = [by_row(D[a] ** 2, width) for a in range(PTS)]
    mob_rows, load_rows = (r.reshape(2 * PTS * PTS, width) for r in (mob_ref, load_ref))

    def across(ref, s, j):
        return ref[pl.ds(s * PTS * PTS + j, PTS, stride=PTS)]

    for copy in copies:
        copy.wait()
    spread, cell_metric = spread_metric(metric_ref[...], weight_row)
    for d in range(3):
        spread_ref[d] = spread[d]
    points = [across(mob_rows, s, ends[s]) * (float(W[ends[s]]) * row_weight) for s in range(2)]
    columns = dot_split(
        jnp.concatenate([p * weight_row for p in points], axis=0), squared
    )
    for s, e in enumerate((0, ny - 1)):
        j = ends[s]
        scale = [spread[d][e : e + 1] for d in range(3)]
        along = points[s] * scale[0]
        total = sum(squares[a] * along[a : a + 1] for a in range(PTS))
        sums = [
            sum(float(D[b, j] ** power * W[b]) * across(mob_rows, s, b) for b in range(PTS))
            * row_weight
            * scale[1]
            for power in (1, 2)
        ]
        yface_ref[s, 2] = along
        yface_ref[s, 3] = points[s] * scale[2]
        yface_ref[s, 4] = sums[0]
        column = columns[s * PTS : (s + 1) * PTS] * cell_metric[e : e + 1]
        yface_ref[s, 1] = sum_z(total + sums[1] + column, masks)
    for s in range(2):
        yface_ref[s, 0] = sum_z(across(load_rows, s, ends[s]), masks)


def diag_kernel(
    side_ref, load_ref, mob_ref, spread_ref,
    fields_ref, xface_ref, factor_ref, to_outer_ref, to_inner_ref,
):
    ny, width = fields_ref.shape[3:]
    spread = [spread_ref[d] for d in range(3)]
    square = D * D
    squared = paired_here(cell_blocks(tiled(square, width)))
    mob, load = plane(mob_ref, ny), plane(load_ref, ny)
    diag_ref = fields_ref.at[1]
    even = side_ref[0] == 0

    def post(at, low, high):
        to_inner_ref[at : at + ny] = jnp.where(even, high, low)
        to_outer_ref[at : at + ny] = jnp.where(even, low, high)

    for d in (1, 2):
        post((2 * PTS + d - 1) * ny, spread[d], spread[d])
    for j in range(PTS):
        factor = [mob(i, j) * (float(W[i] * W[j]) * spread[0]) for i in range(PTS)]
        post(j * ny, *(sum(float(D[a, i]) * factor[a] for a in range(PTS)) for i in (0, PTS - 1)))
        post((PTS + j) * ny, *(float(W[i] * W[j]) * mob(i, j) for i in (0, PTS - 1)))
        for i, value in enumerate(contract(square.T, factor, 1)):
            diag_ref[i, j] = value
    for i in range(PTS):
        factor = [mob(i, j) * (float(W[i] * W[j]) * spread[1]) for j in range(PTS)]
        for j, value in enumerate(contract(square.T, factor, 1)):
            diag_ref[i, j] += value
    for i in range(PTS):
        factor = jnp.concatenate(
            [mob(i, j) * (float(W[i] * W[j]) * spread[2]) for j in range(PTS)], axis=0
        )
        diag_ref[i] += dot_split(factor, squared).reshape(PTS, ny, width)
        fields_ref[0, i] = jnp.stack([load(i, j) for j in range(PTS)], axis=0)
    masks = column_masks((PTS, ny, width))
    for f in range(2):
        for i in range(PTS):
            fields_ref[f, i] = sum_z(fields_ref[f, i], masks)
        sum_y_local(fields_ref.at[f], ny)
        xface_ref[f, 0] = fields_ref[f, 0]
        xface_ref[f, 1] = fields_ref[f, PTS - 1]
    row_weight = by_row(W, width)
    for s, i in enumerate((0, PTS - 1)):
        for n, e in enumerate((0, ny - 1)):
            points = mob_ref[i, e * PTS : (e + 1) * PTS] * (float(W[i]) * row_weight)
            factor_ref[s, n] = points * spread[1][e : e + 1]


def merge_kernel(side_ref, xface_ref, factor_ref, below_ref, above_ref, outer_ref, inner_ref):
    below_ref, above_ref = below_ref.at[1], above_ref.at[0]
    even = side_ref[0] == 0
    fields, _, _, ny, width = xface_ref.shape
    row = lax.broadcasted_iota(jnp.int32, (ny, width), 0)
    for f in range(fields):
        for j in range(PTS):
            low, high = xface_ref[f, 0, j], xface_ref[f, 1, j]
            if j == 0:
                low = low + jnp.where(row == 0, below_ref[f, 0:1], 0.0)
                high = high + jnp.where(row == 0, below_ref[f, PTS - 1 : PTS], 0.0)
            if j == PTS - 1:
                low = low + jnp.where(row == ny - 1, above_ref[f, 0:1], 0.0)
                high = high + jnp.where(row == ny - 1, above_ref[f, PTS - 1 : PTS], 0.0)
            at = (f * PTS + j) * ny
            inner_ref[at : at + ny] = jnp.where(even, high, low)
            outer_ref[at : at + ny] = jnp.where(even, low, high)
    for n in range(2):
        at = fields * PTS * ny + n * PTS
        low, high = factor_ref[0, n], factor_ref[1, n]
        inner_ref[at : at + PTS] = jnp.where(even, high, low)
        outer_ref[at : at + PTS] = jnp.where(even, low, high)


def inside_kernel(
    fields_ref, load_ref, mob_ref, spread_ref, grad_ref, back_ref, below_ref, above_ref,
    rough_ref, value_ref, partial_ref, gain_ref, out_ref, pair_ref, weights_ref, sums_ref, edge_weights_ref,
    work_ref,
):
    below_ref, above_ref = below_ref.at[1], above_ref.at[0]
    ny, width = out_ref.shape[2:]
    spread = [spread_ref[d] for d in range(3)]
    mob, load = plane(mob_ref, ny), plane(load_ref, ny)
    row = lax.broadcasted_iota(jnp.int32, (ny, width), 0)
    zero = jnp.zeros((ny, width), F32)
    for i in range(PTS):
        for j in range(PTS):
            sums = [fields_ref[f, i, j] for f in range(2)]
            for f in range(2):
                if j == 0:
                    sums[f] += jnp.where(row == 0, below_ref[f, i : i + 1], 0.0)
                if j == PTS - 1:
                    sums[f] += jnp.where(row == ny - 1, above_ref[f, i : i + 1], 0.0)
            if i in (0, PTS - 1):
                for f in range(2):
                    rough_ref[f, 0 if i == 0 else 1, j] = sums[f]
                value_ref[i, j] = partial_ref[i, j] = gain_ref[i, j] = zero
            else:
                value_ref[i, j], partial_ref[i, j], gain_ref[i, j] = first_step(*sums)
    grad, back = grad_ref[...], back_ref[...]
    for j in range(PTS):
        factor = [mob(i, j) * (float(W[i] * W[j]) * spread[0]) for i in range(PTS)]
        for n, p in enumerate((0, PTS - 1)):
            coupling = contract(D.T, [float(D[a, p]) * factor[a] for a in range(PTS)], -1)
            for i in range(PTS):
                pair_ref[n, i, j] = coupling[i]
        flux = contract(D, [value_ref[i, j] for i in range(PTS)], -1)
        flux = [flux[i] * factor[i] for i in range(PTS)]
        for i, value in enumerate(contract(D.T, flux, -1)):
            out_ref[i, j] = value
        for i, value in enumerate(contract(D.T, factor, -1)):
            weights_ref[0, i, j] = value
    for i in range(1, PTS - 1):
        flux = contract(D, [value_ref[i, j] for j in range(PTS)], -1)
        flux = [flux[j] * (mob(i, j) * (float(W[i] * W[j]) * spread[1])) for j in range(PTS)]
        for j, value in enumerate(contract(D.T, flux, -1)):
            out_ref[i, j] += value
        work_ref[...] = dot_split(value_ref[i].reshape(PTS * ny, width), grad).reshape(PTS, ny, width)
        for j in range(PTS):
            work_ref[j] *= mob(i, j) * (float(W[i] * W[j]) * spread[2])
        out_ref[i] += dot_split(work_ref[...].reshape(PTS * ny, width), back).reshape(PTS, ny, width)
    for i in range(PTS):
        factor = [mob(i, j) * (float(W[i] * W[j]) * spread[1]) for j in range(PTS)]
        for j, value in enumerate(contract(D.T, factor, -1)):
            weights_ref[1, i, j] = value
        factor = jnp.concatenate(
            [mob(i, j) * (float(W[i] * W[j]) * spread[2]) for j in range(PTS)], axis=0
        )
        weights_ref[2, i] = dot_split(factor, back).reshape(PTS, ny, width)
    sums = [zero] * 4
    for i in range(PTS):
        for q in range(2):
            from_load = sum(float(HAT[j, q]) * load(i, j) for j in range(PTS))
            for p in range(2):
                if HAT[i, p]:
                    sums[2 * p + q] = sums[2 * p + q] + float(HAT[i, p]) * from_load
    for n in range(4):
        sums_ref[n] = sums[n]
    for t, ref in enumerate((below_ref, above_ref)):
        edge_weights_ref[t, 0] = sum(by_row(D[a], width) * ref[2, a : a + 1] for a in range(PTS))
        edge_weights_ref[t, 1] = ref[4]
        edge_weights_ref[t, 2] = dot_split(ref[3], back)


def first_step(right, diagonal):
    inverse = 1.0 / diagonal
    scaled = inverse * right
    value = scaled * (1.0 / THETA)
    return value, KEEP * value + GAIN * scaled, GAIN * inverse


def faces_kernel(
    side_ref, rough_ref, value_ref, out_ref, pair_ref, mob_ref, spread_ref, grad_ref, back_ref,
    below_ref, above_ref, partial_ref, gain_ref, weights_ref, load_sums_ref, edge_weights_ref,
    outer_ref, inner_ref,
    to_outer_ref, to_inner_ref, yface_ref, gface_ref, sofar_ref, sums_ref, line_ref, work_ref,
):
    below_ref, above_ref = below_ref.at[1], above_ref.at[0]
    even = side_ref[0] == 0
    ny, width = out_ref.shape[2:]
    spread = [spread_ref[d] for d in range(3)]
    mob = plane(mob_ref, ny)
    ends = (0, PTS - 1)
    rows = (0, ny - 1)
    row = lax.broadcasted_iota(jnp.int32, (ny, width), 0)
    masks = column_masks((ny, width))

    def arrived(at, count):
        inner, outer = inner_ref[at : at + count], outer_ref[at : at + count]
        return jnp.where(even, outer, inner), jnp.where(even, inner, outer)

    value = [[None] * PTS, [None] * PTS]
    pface = [[None] * PTS, [None] * PTS]
    gface = [[None] * PTS, [None] * PTS]
    for j in range(PTS):
        load = arrived(j * ny, ny)
        diagonal = arrived((PTS + j) * ny, ny)
        for s in range(2):
            value[s][j], pface[s][j], gface[s][j] = first_step(
                rough_ref[0, s, j] + load[s], rough_ref[1, s, j] + diagonal[s]
            )
            gface_ref[s, j] = gface[s][j]
    lines = [value[s][j] for s in range(2) for j in range(PTS)]
    factors = [
        mob(ends[s], j) * (float(W[ends[s]] * W[j]) * spread[2]) for s in range(2) for j in range(PTS)
    ]
    for s in range(2):
        for t, ref in enumerate((below_ref, above_ref)):
            lines.append(value[s][ends[t]])
            factors.append(jnp.broadcast_to(ref[3, ends[s] : ends[s] + 1], (ny, width)))
    flux = dot_split(jnp.concatenate(lines, axis=0), grad_ref[...]) * jnp.concatenate(factors, axis=0)
    line_ref[...] = dot_split(flux, back_ref[...])
    edge_y = [[None, None], [None, None]]
    total = [[None] * PTS, [None] * PTS]
    for s in range(2):
        gradient = contract(D, value[s], -1)
        flux = [
            gradient[j] * (mob(ends[s], j) * (float(W[ends[s]] * W[j]) * spread[1])) for j in range(PTS)
        ]
        total[s] = contract(D.T, flux, -1)
        for t in range(2):
            factor = arrived(2 * PTS * ny + t * PTS, PTS)[s]
            edge_y[s][t] = sum(
                float(D[j, ends[t]]) * (gradient[j] * factor[j : j + 1]) for j in range(PTS)
            )[rows[t] : rows[t] + 1]
    for j in range(PTS):
        across = [
            out_ref[i, j] + (pair_ref[0, i, j] * value[0][j] + pair_ref[1, i, j] * value[1][j])
            for i in range(PTS)
        ]
        total[0][j] += across[0]
        total[1][j] += across[PTS - 1]
        for i in range(1, PTS - 1):
            work_ref[i, j] = across[i]
    for s in range(2):
        for j in range(PTS):
            at = (s * PTS + j) * ny
            total[s][j] += line_ref[at : at + ny]
    ymessage = []
    for t in range(2):
        j = ends[t]
        edge = [total[0][j]] + [work_ref[i, j] for i in range(1, PTS - 1)] + [total[1][j]]
        edge = [v[rows[t] : rows[t] + 1] for v in edge]
        edge[0] += edge_y[0][t]
        edge[PTS - 1] += edge_y[1][t]
        ymessage.append(sum_z(jnp.concatenate(edge, axis=0), column_masks((PTS, width))))
        yface_ref[t, 0] = ymessage[t]
    extra = [[None, None], [None, None]]
    for t, ref in enumerate((below_ref, above_ref)):
        j = ends[t]
        points = [value[0][j]] + [value_ref[i, j] for i in range(1, PTS - 1)] + [value[1][j]]
        flux = contract(D, points, -1)
        flux = contract(D.T, [flux[i] * ref[2, i : i + 1] for i in range(PTS)], -1)
        for s in range(2):
            at = (2 * PTS + 2 * s + t) * ny
            extra[s][t] = sum_z(flux[ends[s]] + line_ref[at : at + ny], masks)
            extra[s][t] = jnp.where(row == rows[t], extra[s][t], 0.0)
    for s in range(2):
        for j in range(PTS):
            total[s][j] = sum_z(total[s][j], masks)
        low, high = total[s][0], total[s][PTS - 1]
        total[s][PTS - 1] = high + jnp.where(row == ny - 1, 0.0, pltpu.roll(low, ny - 1, 0))
        total[s][0] = low + jnp.where(row == 0, 0.0, pltpu.roll(high, 1, 0))
    for j in range(PTS):
        low, high = total[0][j], total[1][j]
        if j in ends:
            t = ends.index(j)
            low, high = low + extra[0][t], high + extra[1][t]
        to_inner_ref[j * ny : (j + 1) * ny] = jnp.where(even, high, low)
        to_outer_ref[j * ny : (j + 1) * ny] = jnp.where(even, low, high)
        for s in range(2):
            sofar_ref[ends[s], j] = pface[s][j] - gface[s][j] * total[s][j]
    for i in range(1, PTS - 1):
        lines = [sum_z(work_ref[i, j], masks) for j in range(PTS)]
        low, high = lines[0], lines[PTS - 1]
        lines[PTS - 1] = high + jnp.where(row == ny - 1, 0.0, pltpu.roll(low, ny - 1, 0))
        lines[0] = low + jnp.where(row == 0, 0.0, pltpu.roll(high, 1, 0))
        for j in range(PTS):
            sofar_ref[i, j] = partial_ref[i, j] - gain_ref[i, j] * lines[j]
    sums = restricted(
        [(i, j) for i in range(PTS) for j in range(PTS)],
        lambda i, j: sofar_ref[i, j],
        lambda d, i, j: weights_ref[d, i, j],
        jnp.zeros((ny, width), F32),
    )
    for q in range(2):
        sums_ref[q] = sums[q] + load_sums_ref[q]
        sums_ref[2 + q] = sums[4 + q]
        sums[2 + q] = sums[2 + q] + load_sums_ref[2 + q]
    base = PTS * ny
    changes = []
    for t in range(2):
        j = ends[t]
        gain = [gface[0][j]] + [gain_ref[i, j] for i in range(1, PTS - 1)] + [gface[1][j]]
        gain = jnp.concatenate([g[rows[t] : rows[t] + 1] for g in gain], axis=0)
        changes += edge_change(-(gain * ymessage[t]), edge_weights_ref.at[t], ends[1 - t])
    changes = jnp.concatenate(changes, axis=0)
    for ref in (to_outer_ref, to_inner_ref):
        for n, k in enumerate((2, 3, 6, 7)):
            ref[base + n * ny : base + (n + 1) * ny] = sums[k]
        ref[base + 4 * ny : base + 4 * ny + PTS] = changes


def edge_change(change, weight_ref, j):
    upper = lax.broadcasted_iota(jnp.int32, change.shape, 0)
    hat = jnp.zeros_like(change)
    for i in range(PTS):
        hat = jnp.where(upper == i, float(HAT[i, 1]), hat)
    along_x, along_y, along_z = (
        jnp.sum(v, axis=0, keepdims=True)
        for v in (weight_ref[0] * change, hat * weight_ref[1] * change, hat * weight_ref[2] * change)
    )
    smooth = [-(SLOPE[1] * float(HAT[j, q]) * along_x + SLOPE[q] * along_y) for q in range(2)]
    return smooth + [-float(HAT[j, q]) * along_z for q in range(2)]


def restricted(points, value, weight, zero):
    sums = [zero] * 8
    along_x = {}
    along_y = {}
    along_z = {}
    for i, j in points:
        v = value(i, j)
        along_x[j] = along_x.get(j, 0.0) + weight(0, i, j) * v
        along_y[i] = along_y.get(i, 0.0) + weight(1, i, j) * v
        product = weight(2, i, j) * v
        for q in range(2):
            if HAT[j, q]:
                along_z[i, q] = along_z.get((i, q), 0.0) + float(HAT[j, q]) * product
    x_sums = [
        sum(float(HAT[j, q]) * total for j, total in along_x.items() if HAT[j, q]) for q in range(2)
    ]
    y_sums = [
        sum(float(HAT[i, p]) * total for i, total in along_y.items() if HAT[i, p]) for p in range(2)
    ]
    for p in range(2):
        for q in range(2):
            sums[2 * p + q] = -(SLOPE[p] * x_sums[q] + SLOPE[q] * y_sums[p])
            sums[4 + 2 * p + q] = -sum(
                float(HAT[i, p]) * total for (i, r), total in along_z.items() if r == q and HAT[i, p]
            )
    return sums


def corrections(even, gain_ref, gface_ref, outer_ref, below_ref, above_ref, inner_ref):
    ny, width = gain_ref.shape[2:]
    row = lax.broadcasted_iota(jnp.int32, (ny, width), 0)
    change = {}
    for j in range(PTS):
        inner, outer = inner_ref[j * ny : (j + 1) * ny], outer_ref[j * ny : (j + 1) * ny]
        change[0, j] = jnp.where(even, outer, inner)
        change[PTS - 1, j] = jnp.where(even, inner, outer)
    for i in range(PTS):
        low = jnp.where(row == 0, below_ref[0, i : i + 1], 0.0)
        high = jnp.where(row == ny - 1, above_ref[0, i : i + 1], 0.0)
        change[i, 0] = change[i, 0] + low if (i, 0) in change else low
        change[i, PTS - 1] = change[i, PTS - 1] + high if (i, PTS - 1) in change else high
    faces = {0: 0, PTS - 1: 1}
    for i, j in change:
        gain = gface_ref[faces[i], j] if i in faces else gain_ref[i, j]
        change[i, j] = -(gain * change[i, j])
    return change


def face_change(change, weight, i, p, q):
    along_x = sum(float(HAT[j, q]) * (weight[0][j] * change[j]) for j in range(PTS) if HAT[j, q])
    smooth = SLOPE[p] * along_x
    slope = 0.0
    if HAT[i, p]:
        along_y = sum(weight[1][j] * change[j] for j in range(PTS))
        smooth = smooth + float(HAT[i, p]) * SLOPE[q] * along_y
        along_z = sum(float(HAT[j, q]) * (weight[2][j] * change[j]) for j in range(PTS) if HAT[j, q])
        slope = float(HAT[i, p]) * along_z
    return -smooth, -slope


def to_vertices(smooth, slope, restrict):
    return dot_split(jnp.concatenate([smooth, slope], axis=1), restrict)


def pick(even, first, second, at, count):
    return jnp.where(even, first[at : at + count], second[at : at + count])


def ahead_kernel(
    side_ref, sent_outer_ref, sent_inner_ref, gface_ref, restrict_ref, outer_ref, inner_ref,
    next_ref, top_ref,
):
    ny, width = gface_ref.shape[2:]
    even = side_ref[0] == 0
    change = [
        -(gface_ref[1, j] * pick(even, sent_inner_ref, sent_outer_ref, j * ny, ny)) for j in range(PTS)
    ]
    weight = [[pick(even, inner_ref, outer_ref, j * ny, ny) for j in range(PTS)]]
    smooth = jnp.concatenate([face_change(change, weight, 0, 1, q)[0] for q in range(2)], axis=0)
    corners = to_vertices(smooth, jnp.zeros_like(smooth), restrict_ref[...])
    lower, upper = corners[:ny], corners[ny:]
    row = lax.broadcasted_iota(jnp.int32, lower.shape, 0)
    next_ref[...] = lower + jnp.where(row == 0, 0.0, pltpu.roll(upper, 1, 0))
    top_ref[...] = jnp.broadcast_to(upper[ny - 1 : ny], top_ref.shape)


def behind_kernel(
    side_ref, sent_outer_ref, sent_inner_ref, gface_ref, back_ref, outer_ref, inner_ref,
    own_ref,
):
    ny, width = gface_ref.shape[2:]
    even = side_ref[0] == 0

    def rows(at):
        return pick(even, outer_ref, inner_ref, at, ny)

    change = [
        -(gface_ref[0, j] * pick(even, sent_outer_ref, sent_inner_ref, j * ny, ny)) for j in range(PTS)
    ]
    spread = [rows((2 * PTS + d) * ny) for d in range(2)]
    points = [rows((PTS + j) * ny) for j in range(PTS)]
    column = dot_split(jnp.concatenate([p * spread[1] for p in points], axis=0), back_ref[...])
    weight = [
        [rows(j * ny) for j in range(PTS)],
        contract(D.T, [p * spread[0] for p in points], -1),
        [column[j * ny : (j + 1) * ny] for j in range(PTS)],
    ]
    for q in range(2):
        own_ref[q], own_ref[2 + q] = face_change(change, weight, PTS - 1, 1, q)


def coarse_kernel(
    side_ref, gain_ref, gface_ref, sums_ref, own_ref, weights_ref, restrict_ref,
    outer_ref, below_ref, above_ref, inner_ref,
    plane_ref, edge_ref,
):
    below_ref, above_ref = below_ref.at[1], above_ref.at[0]
    ny, width = gain_ref.shape[2:]
    even = side_ref[0] == 0
    change = corrections(even, gain_ref, gface_ref, outer_ref, below_ref, above_ref, inner_ref)
    sums = restricted(
        list(change),
        lambda i, j: change[i, j],
        lambda d, i, j: weights_ref[d, i, j],
        jnp.zeros((ny, width), F32),
    )
    base = PTS * ny

    def before(at, count):
        return jnp.where(even, outer_ref[at : at + count], inner_ref[at : at + count])

    total = [
        sums[(0, 1, 4, 5)[n]] + sums_ref[n] + own_ref[n] + before(base + n * ny, ny) for n in range(4)
    ]
    extra = before(base + 4 * ny, PTS)
    smooth = jnp.concatenate(total[:2] + [extra], axis=0)
    slope = jnp.concatenate(total[2:] + [pltpu.roll(extra, PTS - 2, 0)], axis=0)
    corners = to_vertices(smooth, slope, restrict_ref[...])
    lower, upper = corners[:ny], corners[ny : 2 * ny]
    extra = corners[2 * ny :]
    row = lax.broadcasted_iota(jnp.int32, lower.shape, 0)
    shifted = jnp.where(row == 0, extra[1:2], pltpu.roll(upper, 1, 0))
    plane_ref[...] = lower + shifted
    edge_ref[0:1] = upper[ny - 1 : ny] + extra[4:5]
    edge_ref[1:2] = extra[5:6]
    edge_ref[2:3] = extra[0:1]


def pressure_kernel(
    side_ref, sofar_ref, gain_ref, gface_ref, outer_ref, below_ref, above_ref, inner_ref,
    pressure_out, token_ref, pressure_ref, sem,
):
    token_ref[...] = jnp.zeros_like(token_ref)
    below_ref, above_ref = below_ref.at[1], above_ref.at[0]
    ny = sofar_ref.shape[2]
    even = side_ref[0] == 0
    change = corrections(even, gain_ref, gface_ref, outer_ref, below_ref, above_ref, inner_ref)
    for i in range(PTS):
        for j in range(PTS):
            value = sofar_ref[i, j]
            if (i, j) in change:
                value = value + change[i, j]
            pressure_ref[i, pl.ds(j, ny, stride=PTS)] = value
    copy = pltpu.make_async_copy(pressure_ref, pressure_out, sem)
    copy.start()
    copy.wait()


def join_kernel(next_ref, top_ref, token_ref, joined_ref):
    row = lax.broadcasted_iota(jnp.int32, next_ref.shape, 0)
    joined_ref[...] = next_ref[...] + jnp.where(row == 0, top_ref[0:1], 0.0) + token_ref[...]


def last_kernel(plane_ref, joined_ref, below_ref, above_ref, coarse_ref):
    total = plane_ref[...] + joined_ref[...]
    ny = total.shape[0]
    row = lax.broadcasted_iota(jnp.int32, total.shape, 0)
    total = total + jnp.where(row == 0, below_ref[0:1], jnp.where(row == 1, below_ref[1:2], 0.0))
    total = total + jnp.where(row == ny - 1, above_ref[2:3], 0.0)
    coarse_ref[...] = total[:, : coarse_ref.shape[1]]


def call(body, outs, scratch, *args, spaces=None, out_spaces=None, flops=None):
    spaces = spaces or [pltpu.SMEM if a.dtype == jnp.int32 else pltpu.VMEM for a in args]
    return pl.pallas_call(
        body,
        out_shape=[jax.ShapeDtypeStruct(s, F32) if isinstance(s, tuple) else s for s in outs],
        in_specs=[pl.BlockSpec(memory_space=m) for m in spaces],
        out_specs=[pl.BlockSpec(memory_space=m) for m in out_spaces or [pltpu.VMEM] * len(outs)],
        scratch_shapes=[pltpu.VMEM(s, F32) if isinstance(s, tuple) else s for s in scratch],
        compiler_params=pltpu.CompilerParams(vmem_limit_bytes=16 * 1024 * 1024),
        cost_estimate=flops and pl.CostEstimate(flops=flops, bytes_accessed=0, transcendentals=0),
    )(*args)


def from_y(faces):
    size = lax.axis_size("sub")
    up = lax.ppermute(faces, "sub", [(i, (i + 1) % size) for i in range(size)])
    if size == 2:
        return up, up
    return up, lax.ppermute(faces, "sub", [(i, (i - 1) % size) for i in range(size)])


def inner_pairs(size):
    return [(i, i ^ 1) for i in range(size)]


def outer_pairs(size):
    return [(i, (i + 1) % size if i % 2 else (i - 1) % size) for i in range(size)]


def to_x(outer, inner):
    size = lax.axis_size("dom")
    outer = lax.ppermute(outer, "dom", outer_pairs(size))
    inner = lax.ppermute(inner, "dom", inner_pairs(size))
    return outer, inner


def two_on(rows, top):
    size, rest = lax.axis_size("dom"), lax.axis_size("sub")
    rows = lax.ppermute(rows, "dom", [(i, (i + 2) % size) for i in range(size)])
    pairs = [
        (i * rest + k, (i + 2) % size * rest + (k + 1) % rest) for i in range(size) for k in range(rest)
    ]
    return rows, lax.ppermute(top, ("dom", "sub"), pairs)


def shards(element_load, mobility, metric):
    _, _, ny, _, width = element_load.shape
    load = element_load.reshape(PTS, ny * PTS, width)
    mob = mobility.reshape(PTS, ny * PTS, width)
    metric = metric[:, 0]
    side = (lax.axis_index("dom") % 2).astype(jnp.int32).reshape(1)
    def in_hbm(*arrays):
        return [pltpu.with_memory_space_constraint(a, pltpu.HBM) for a in arrays]

    grad, back = column_tables(width)
    restrict = restrict_table(width)
    field = (PTS, PTS, ny, width)
    face = (PTS, ny, width)
    ends = (2, PTS, PTS, width)
    spread, yface = call(
        edge_kernel,
        [(3, ny, width), (2, 5, PTS, width)],
        [metric.shape, ends, ends, pltpu.SemaphoreType.DMA((5,))],
        *in_hbm(metric, mob, load),
        spaces=[pltpu.HBM] * 3,
    )
    below, above = from_y(yface)
    still = (2 * (PTS + 1) * ny, width)
    fields, xface, factor, still_outer, still_inner = call(
        diag_kernel,
        [(2,) + field, (2, 2) + face, (2, 2, PTS, width), still, still],
        [],
        side, load, mob, spread,
    )
    rows = (2 * PTS * ny + 2 * PTS, width)
    outer, inner = to_x(*call(merge_kernel, [rows, rows], [], side, xface, factor, below, above))
    still_outer, still_inner = to_x(still_outer, still_inner)
    faces = (2,) + face
    rough, value, partial, gain, out, pair, weights, load_sums, edge_weights = call(
        inside_kernel,
        [
            (2,) + faces, field, field, field, field, (2,) + field,
            (3,) + field, (4, ny, width), (2, 3, PTS, width),
        ],
        [face],
        fields, load, mob, spread, grad, back, below, above,
    )
    rows = ((PTS + 4) * ny + PTS, width)
    sent_outer, sent_inner, yface, gface, sofar, sums = call(
        faces_kernel,
        [rows, rows, (2, 1, PTS, width), faces, field, (4, ny, width)],
        [((2 * PTS + 4) * ny, width), field],
        side, rough, value, out, pair, mob, spread, grad, back, below, above,
        partial, gain, weights, load_sums, edge_weights, outer, inner,
    )
    outer, inner = to_x(sent_outer, sent_inner)
    onward, top = call(
        ahead_kernel,
        [(ny, 128), (3 * PTS, 128)],
        [],
        side, sent_outer, sent_inner, gface, restrict, still_outer, still_inner,
    )
    (own,) = call(
        behind_kernel,
        [(4, ny, width)],
        [],
        side, sent_outer, sent_inner, gface, back, still_outer, still_inner,
    )
    onward, top = two_on(onward, top)
    below, above = from_y(yface)
    own_rows, tops = call(
        coarse_kernel,
        [(ny, 128), (3, 128)],
        [],
        side, gain, gface, sums, own, weights, restrict, outer, below, above, inner,
    )
    pressure, token = call(
        pressure_kernel,
        [(PTS, ny * PTS, width), (1, 128)],
        [(PTS, ny * PTS, width), pltpu.SemaphoreType.DMA(())],
        side, sofar, gain, gface, outer, below, above, inner,
        out_spaces=[pltpu.HBM, pltpu.VMEM],
    )
    (onward,) = call(join_kernel, [(ny, 128)], [], onward, top, token, flops=FLOPS_JOIN)
    below, above = from_y(tops)
    (coarse,) = call(last_kernel, [(ny, width // PTS + 1)], [], own_rows, onward, below, above)
    return pressure.reshape(element_load.shape), coarse[None]


def solution(mesh):
    in_specs = (
        P("dom", None, "sub", None, None),
        P("dom", None, "sub", None, None),
        P(None, "dom", "sub", None),
    )
    out_specs = (P("dom", None, "sub", None, None), P("dom", "sub", None))
    return jax.shard_map(shards, mesh=mesh, in_specs=in_specs, out_specs=out_specs, check_vma=False)
```

```python
import jax
import jax.numpy as jnp
import ml_dtypes
import numpy as np
from jax import lax
from jax.experimental import pallas as pl
from jax.experimental.pallas import tpu as pltpu
from jax.sharding import PartitionSpec as P

GLL_NODES = np.array(
    [
        -1.0,
        -0.8717401485096066,
        -0.5917001814331423,
        -0.2092992179024789,
        0.2092992179024789,
        0.5917001814331423,
        0.8717401485096066,
        1.0,
    ]
)
GLL_WEIGHTS = np.array(
    [
        0.03571428571428571,
        0.2107042271435061,
        0.3411226924835044,
        0.4124587946587038,
        0.4124587946587038,
        0.3411226924835044,
        0.2107042271435061,
        0.03571428571428571,
    ]
)
THETA = 1.65
DELTA = 1.35
RHO_FIRST = DELTA / THETA
RHO_SECOND = 1.0 / (2.0 * THETA / DELTA - RHO_FIRST)
KEEP = 1.0 + RHO_SECOND * RHO_FIRST
GAIN = 2.0 * RHO_SECOND / DELTA
EXACT = lax.Precision.HIGHEST
PTS = 8
F32 = jnp.float32
FLOPS_JOIN = 5_000_000_000


def derivative_table():
    identity = np.eye(8)
    differences = GLL_NODES[:, None] - GLL_NODES[None, :] + identity
    barycentric = 1.0 / np.prod(differences, axis=1)
    matrix = barycentric[None, :] / barycentric[:, None] / differences
    matrix = matrix * (1.0 - identity)
    row_sums = np.sum(matrix, axis=1)
    return matrix - identity * row_sums[:, None]


D = derivative_table()
W = GLL_WEIGHTS
HAT = np.stack([(1.0 - GLL_NODES) / 8.0, (1.0 + GLL_NODES) / 8.0], axis=1)
SLOPE = (-0.125, 0.125)


def tiled(matrix, width):
    column = lax.broadcasted_iota(jnp.int32, (PTS, width), 1) % PTS
    row = lax.broadcasted_iota(jnp.int32, (PTS, width), 0)
    total = jnp.zeros((PTS, width), F32)
    for c in range(PTS):
        lines = jnp.zeros((PTS, width), F32)
        for r in range(PTS):
            lines = jnp.where(row == r, float(matrix[r, c]), lines)
        total = jnp.where(column == c, lines, total)
    return total


def by_row(values, width):
    return tiled(np.tile(np.asarray(values)[:, None], (1, PTS)), width)


def cell_blocks(rows):
    width = rows.shape[1]
    cell = lax.broadcasted_iota(jnp.int32, rows.shape, 1) // PTS
    return jnp.concatenate(
        [jnp.where(cell == g, rows, 0.0) for g in range(width // PTS)], axis=0
    )


def paired_here(b):
    high, low = halves(b)
    return jnp.concatenate(
        [
            jnp.concatenate([high, low], axis=1),
            jnp.concatenate([high, jnp.zeros_like(low)], axis=1),
        ],
        axis=0,
    )


def paired(b):
    b = np.asarray(b, np.float32)
    high = b.astype(ml_dtypes.bfloat16)
    low = (b - high.astype(np.float32)).astype(ml_dtypes.bfloat16)
    return jnp.asarray(np.block([[high, low], [high, np.zeros_like(low)]]))


def column_tables(width):
    cells = np.eye(width // PTS)
    return paired(np.kron(cells, D.T)), paired(np.kron(cells, D))


def restrict_table(width):
    cells = width // PTS
    hat = np.zeros((width, 128))
    slope = np.zeros((width, 128))
    for c in range(cells):
        rows = slice(c * PTS, (c + 1) * PTS)
        hat[rows, c], hat[rows, c + 1] = HAT[:, 0], HAT[:, 1]
        slope[rows, c], slope[rows, c + 1] = SLOPE
    return paired(np.concatenate([hat, slope]))


def dot(a, b):
    return jnp.dot(a, b, precision=EXACT, preferred_element_type=F32)


def halves(a):
    high = a.astype(jnp.bfloat16)
    return high, (a - high.astype(F32)).astype(jnp.bfloat16)


def dot_split(a, b_pair):
    both = jnp.dot(
        jnp.concatenate(halves(a), axis=1), b_pair, preferred_element_type=F32
    )
    n = both.shape[1] // 2
    return both[:, :n] + both[:, n:]


def contract(matrix, lines, parity):
    n = len(lines)
    half = n // 2
    plus = [lines[c] + lines[n - 1 - c] for c in range(half)]
    minus = [lines[c] - lines[n - 1 - c] for c in range(half)]
    top, low = [], []
    for r in range(half):
        even = sum(float(0.5 * (matrix[r, c] + matrix[r, n - 1 - c])) * plus[c] for c in range(half))
        odd = sum(float(0.5 * (matrix[r, c] - matrix[r, n - 1 - c])) * minus[c] for c in range(half))
        top.append(even + odd)
        low.append(even - odd if parity > 0 else odd - even)
    return top + low[::-1]


def spread_metric(metric, weight_row):
    _, rows, cells = metric.shape
    width = weight_row.shape[1]
    cell = lax.broadcasted_iota(jnp.int32, (cells, width), 1) // PTS
    row = lax.broadcasted_iota(jnp.int32, (cells, width), 0)
    pick = jnp.where(cell == row, 1.0, 0.0).astype(jnp.bfloat16)
    flat = metric.reshape(3 * rows, cells)
    high = flat.astype(jnp.bfloat16)
    rest = flat - high.astype(F32)
    parts = jnp.concatenate([high, *halves(rest)], axis=1)
    spread = jnp.dot(
        parts, jnp.concatenate([pick] * 3, axis=0), preferred_element_type=F32
    )
    spread = [spread[d * rows : (d + 1) * rows] for d in range(3)]
    return [v * weight_row[:1] for v in spread], spread[2]


def column_masks(shape):
    lane = lax.broadcasted_iota(jnp.int32, shape, len(shape) - 1)
    up = (lane % PTS == PTS - 1) & (lane != shape[-1] - 1)
    down = (lane % PTS == 0) & (lane != 0)
    return up, down


def sum_z(v, masks):
    width = v.shape[-1]
    axis = v.ndim - 1
    up = pltpu.roll(v, width - 1, axis)
    down = pltpu.roll(v, 1, axis)
    return v + jnp.where(masks[0], up, jnp.where(masks[1], down, 0.0))


def sum_y_local(ref, ny):
    for i in range(PTS):
        low, high = ref[i, 0], ref[i, PTS - 1]
        row = lax.broadcasted_iota(jnp.int32, low.shape, 0)
        ref[i, PTS - 1] = high + jnp.where(row == ny - 1, 0.0, pltpu.roll(low, ny - 1, 0))
        ref[i, 0] = low + jnp.where(row == 0, 0.0, pltpu.roll(high, 1, 0))


def edge_planes(ref, ny):
    low = jnp.concatenate([ref[i, 0, 0:1] for i in range(PTS)], axis=0)
    high = jnp.concatenate([ref[i, PTS - 1, ny - 1 : ny] for i in range(PTS)], axis=0)
    return low, high


def plane(ref, ny):
    return lambda i, j: ref[i, pl.ds(j, ny, stride=PTS)]


def edge_kernel(metric_in, mob_in, load_in, spread_ref, yface_ref, metric_ref, mob_ref, load_ref, sems):
    ny, width = spread_ref.shape[1:]
    ends = (0, PTS - 1)
    copies = [pltpu.make_async_copy(metric_in, metric_ref, sems.at[0])]
    for n, (source, target) in enumerate(((mob_in, mob_ref), (load_in, load_ref))):
        for s, e in enumerate((0, ny - 1)):
            copies.append(
                pltpu.make_async_copy(
                    source.at[:, pl.ds(e * PTS, PTS)], target.at[s], sems.at[1 + 2 * n + s]
                )
            )
    for copy in copies:
        copy.start()
    masks = column_masks((PTS, width))
    weight_row = tiled(np.tile(W[None], (PTS, 1)), width)
    row_weight = by_row(W, width)
    squared = paired_here(cell_blocks(tiled(D * D, width)))
    squares = [by_row(D[a] ** 2, width) for a in range(PTS)]
    for copy in copies:
        copy.wait()
    spread, cell_metric = spread_metric(metric_ref[...], weight_row)
    for d in range(3):
        spread_ref[d] = spread[d]
    points = [mob_ref[s, :, ends[s]] * (float(W[ends[s]]) * row_weight) for s in range(2)]
    columns = dot_split(
        jnp.concatenate([p * weight_row for p in points], axis=0), squared
    )
    for s, e in enumerate((0, ny - 1)):
        j = ends[s]
        scale = [spread[d][e : e + 1] for d in range(3)]
        along = points[s] * scale[0]
        total = sum(squares[a] * along[a : a + 1] for a in range(PTS))
        sums = [
            sum(float(D[b, j] ** power * W[b]) * mob_ref[s, :, b] for b in range(PTS))
            * row_weight
            * scale[1]
            for power in (1, 2)
        ]
        yface_ref[s, 2] = along
        yface_ref[s, 3] = points[s] * scale[2]
        yface_ref[s, 4] = sums[0]
        column = columns[s * PTS : (s + 1) * PTS] * cell_metric[e : e + 1]
        yface_ref[s, 1] = sum_z(total + sums[1] + column, masks)
    for s in range(2):
        yface_ref[s, 0] = sum_z(load_ref[s, :, ends[s]], masks)


def diag_kernel(
    side_ref, load_ref, mob_ref, spread_ref,
    fields_ref, xface_ref, factor_ref, to_outer_ref, to_inner_ref,
):
    ny, width = fields_ref.shape[3:]
    spread = [spread_ref[d] for d in range(3)]
    square = D * D
    squared = paired_here(cell_blocks(tiled(square, width)))
    mob, load = plane(mob_ref, ny), plane(load_ref, ny)
    diag_ref = fields_ref.at[1]
    even = side_ref[0] == 0

    def post(at, low, high):
        to_inner_ref[at : at + ny] = jnp.where(even, high, low)
        to_outer_ref[at : at + ny] = jnp.where(even, low, high)

    for d in (1, 2):
        post((2 * PTS + d - 1) * ny, spread[d], spread[d])
    for j in range(PTS):
        factor = [mob(i, j) * (float(W[i] * W[j]) * spread[0]) for i in range(PTS)]
        post(j * ny, *(sum(float(D[a, i]) * factor[a] for a in range(PTS)) for i in (0, PTS - 1)))
        post((PTS + j) * ny, *(float(W[i] * W[j]) * mob(i, j) for i in (0, PTS - 1)))
        for i, value in enumerate(contract(square.T, factor, 1)):
            diag_ref[i, j] = value
    for i in range(PTS):
        factor = [mob(i, j) * (float(W[i] * W[j]) * spread[1]) for j in range(PTS)]
        for j, value in enumerate(contract(square.T, factor, 1)):
            diag_ref[i, j] += value
    for i in range(PTS):
        factor = jnp.concatenate(
            [mob(i, j) * (float(W[i] * W[j]) * spread[2]) for j in range(PTS)], axis=0
        )
        diag_ref[i] += dot_split(factor, squared).reshape(PTS, ny, width)
        fields_ref[0, i] = jnp.stack([load(i, j) for j in range(PTS)], axis=0)
    masks = column_masks((PTS, ny, width))
    for f in range(2):
        for i in range(PTS):
            fields_ref[f, i] = sum_z(fields_ref[f, i], masks)
        sum_y_local(fields_ref.at[f], ny)
        xface_ref[f, 0] = fields_ref[f, 0]
        xface_ref[f, 1] = fields_ref[f, PTS - 1]
    row_weight = by_row(W, width)
    for s, i in enumerate((0, PTS - 1)):
        for n, e in enumerate((0, ny - 1)):
            points = mob_ref[i, e * PTS : (e + 1) * PTS] * (float(W[i]) * row_weight)
            factor_ref[s, n] = points * spread[1][e : e + 1]


def merge_kernel(side_ref, xface_ref, factor_ref, below_ref, above_ref, outer_ref, inner_ref):
    below_ref, above_ref = below_ref.at[1], above_ref.at[0]
    even = side_ref[0] == 0
    fields, _, _, ny, width = xface_ref.shape
    row = lax.broadcasted_iota(jnp.int32, (ny, width), 0)
    for f in range(fields):
        for j in range(PTS):
            low, high = xface_ref[f, 0, j], xface_ref[f, 1, j]
            if j == 0:
                low = low + jnp.where(row == 0, below_ref[f, 0:1], 0.0)
                high = high + jnp.where(row == 0, below_ref[f, PTS - 1 : PTS], 0.0)
            if j == PTS - 1:
                low = low + jnp.where(row == ny - 1, above_ref[f, 0:1], 0.0)
                high = high + jnp.where(row == ny - 1, above_ref[f, PTS - 1 : PTS], 0.0)
            at = (f * PTS + j) * ny
            inner_ref[at : at + ny] = jnp.where(even, high, low)
            outer_ref[at : at + ny] = jnp.where(even, low, high)
    for n in range(2):
        at = fields * PTS * ny + n * PTS
        low, high = factor_ref[0, n], factor_ref[1, n]
        inner_ref[at : at + PTS] = jnp.where(even, high, low)
        outer_ref[at : at + PTS] = jnp.where(even, low, high)


def inside_kernel(
    fields_ref, load_ref, mob_ref, spread_ref, grad_ref, back_ref, below_ref, above_ref,
    rough_ref, value_ref, partial_ref, gain_ref, out_ref, pair_ref, weights_ref, sums_ref, edge_weights_ref,
    work_ref,
):
    below_ref, above_ref = below_ref.at[1], above_ref.at[0]
    ny, width = out_ref.shape[2:]
    spread = [spread_ref[d] for d in range(3)]
    mob, load = plane(mob_ref, ny), plane(load_ref, ny)
    row = lax.broadcasted_iota(jnp.int32, (ny, width), 0)
    zero = jnp.zeros((ny, width), F32)
    for i in range(PTS):
        for j in range(PTS):
            sums = [fields_ref[f, i, j] for f in range(2)]
            for f in range(2):
                if j == 0:
                    sums[f] += jnp.where(row == 0, below_ref[f, i : i + 1], 0.0)
                if j == PTS - 1:
                    sums[f] += jnp.where(row == ny - 1, above_ref[f, i : i + 1], 0.0)
            if i in (0, PTS - 1):
                for f in range(2):
                    rough_ref[f, 0 if i == 0 else 1, j] = sums[f]
                value_ref[i, j] = partial_ref[i, j] = gain_ref[i, j] = zero
            else:
                value_ref[i, j], partial_ref[i, j], gain_ref[i, j] = first_step(*sums)
    grad, back = grad_ref[...], back_ref[...]
    for j in range(PTS):
        factor = [mob(i, j) * (float(W[i] * W[j]) * spread[0]) for i in range(PTS)]
        for n, p in enumerate((0, PTS - 1)):
            coupling = contract(D.T, [float(D[a, p]) * factor[a] for a in range(PTS)], -1)
            for i in range(PTS):
                pair_ref[n, i, j] = coupling[i]
        flux = contract(D, [value_ref[i, j] for i in range(PTS)], -1)
        flux = [flux[i] * factor[i] for i in range(PTS)]
        for i, value in enumerate(contract(D.T, flux, -1)):
            out_ref[i, j] = value
        for i, value in enumerate(contract(D.T, factor, -1)):
            weights_ref[0, i, j] = value
    for i in range(1, PTS - 1):
        flux = contract(D, [value_ref[i, j] for j in range(PTS)], -1)
        flux = [flux[j] * (mob(i, j) * (float(W[i] * W[j]) * spread[1])) for j in range(PTS)]
        for j, value in enumerate(contract(D.T, flux, -1)):
            out_ref[i, j] += value
        work_ref[...] = dot_split(value_ref[i].reshape(PTS * ny, width), grad).reshape(PTS, ny, width)
        for j in range(PTS):
            work_ref[j] *= mob(i, j) * (float(W[i] * W[j]) * spread[2])
        out_ref[i] += dot_split(work_ref[...].reshape(PTS * ny, width), back).reshape(PTS, ny, width)
    for i in range(PTS):
        factor = [mob(i, j) * (float(W[i] * W[j]) * spread[1]) for j in range(PTS)]
        for j, value in enumerate(contract(D.T, factor, -1)):
            weights_ref[1, i, j] = value
        factor = jnp.concatenate(
            [mob(i, j) * (float(W[i] * W[j]) * spread[2]) for j in range(PTS)], axis=0
        )
        weights_ref[2, i] = dot_split(factor, back).reshape(PTS, ny, width)
    sums = [zero] * 4
    for i in range(PTS):
        for q in range(2):
            from_load = sum(float(HAT[j, q]) * load(i, j) for j in range(PTS))
            for p in range(2):
                if HAT[i, p]:
                    sums[2 * p + q] = sums[2 * p + q] + float(HAT[i, p]) * from_load
    for n in range(4):
        sums_ref[n] = sums[n]
    for t, ref in enumerate((below_ref, above_ref)):
        edge_weights_ref[t, 0] = sum(by_row(D[a], width) * ref[2, a : a + 1] for a in range(PTS))
        edge_weights_ref[t, 1] = ref[4]
        edge_weights_ref[t, 2] = dot_split(ref[3], back)


def first_step(right, diagonal):
    inverse = 1.0 / diagonal
    scaled = inverse * right
    value = scaled * (1.0 / THETA)
    return value, KEEP * value + GAIN * scaled, GAIN * inverse


def faces_kernel(
    side_ref, rough_ref, value_ref, out_ref, pair_ref, mob_ref, spread_ref, grad_ref, back_ref,
    below_ref, above_ref, partial_ref, gain_ref, weights_ref, load_sums_ref, edge_weights_ref,
    outer_ref, inner_ref,
    to_outer_ref, to_inner_ref, yface_ref, gface_ref, sofar_ref, sums_ref, edge_ref, line_ref, work_ref,
):
    below_ref, above_ref = below_ref.at[1], above_ref.at[0]
    even = side_ref[0] == 0
    ny, width = out_ref.shape[2:]
    spread = [spread_ref[d] for d in range(3)]
    mob = plane(mob_ref, ny)
    ends = (0, PTS - 1)
    rows = (0, ny - 1)
    row = lax.broadcasted_iota(jnp.int32, (ny, width), 0)
    masks = column_masks((ny, width))

    def arrived(at, count):
        inner, outer = inner_ref[at : at + count], outer_ref[at : at + count]
        return jnp.where(even, outer, inner), jnp.where(even, inner, outer)

    value = [[None] * PTS, [None] * PTS]
    pface = [[None] * PTS, [None] * PTS]
    gface = [[None] * PTS, [None] * PTS]
    for j in range(PTS):
        load = arrived(j * ny, ny)
        diagonal = arrived((PTS + j) * ny, ny)
        for s in range(2):
            value[s][j], pface[s][j], gface[s][j] = first_step(
                rough_ref[0, s, j] + load[s], rough_ref[1, s, j] + diagonal[s]
            )
            gface_ref[s, j] = gface[s][j]
    lines = [value[s][j] for s in range(2) for j in range(PTS)]
    factors = [
        mob(ends[s], j) * (float(W[ends[s]] * W[j]) * spread[2]) for s in range(2) for j in range(PTS)
    ]
    for s in range(2):
        for t, ref in enumerate((below_ref, above_ref)):
            lines.append(value[s][ends[t]])
            factors.append(jnp.broadcast_to(ref[3, ends[s] : ends[s] + 1], (ny, width)))
    flux = dot_split(jnp.concatenate(lines, axis=0), grad_ref[...]) * jnp.concatenate(factors, axis=0)
    line_ref[...] = dot_split(flux, back_ref[...])
    edge_y = [[None, None], [None, None]]
    total = [[None] * PTS, [None] * PTS]
    for s in range(2):
        gradient = contract(D, value[s], -1)
        flux = [
            gradient[j] * (mob(ends[s], j) * (float(W[ends[s]] * W[j]) * spread[1])) for j in range(PTS)
        ]
        total[s] = contract(D.T, flux, -1)
        for t in range(2):
            factor = arrived(2 * PTS * ny + t * PTS, PTS)[s]
            edge_y[s][t] = sum(
                float(D[j, ends[t]]) * (gradient[j] * factor[j : j + 1]) for j in range(PTS)
            )[rows[t] : rows[t] + 1]
    for j in range(PTS):
        across = [
            out_ref[i, j] + (pair_ref[0, i, j] * value[0][j] + pair_ref[1, i, j] * value[1][j])
            for i in range(PTS)
        ]
        total[0][j] += across[0]
        total[1][j] += across[PTS - 1]
        for i in range(1, PTS - 1):
            work_ref[i, j] = across[i]
    for s in range(2):
        for j in range(PTS):
            at = (s * PTS + j) * ny
            total[s][j] += line_ref[at : at + ny]
    ymessage = []
    for t in range(2):
        j = ends[t]
        edge = [total[0][j]] + [work_ref[i, j] for i in range(1, PTS - 1)] + [total[1][j]]
        edge = [v[rows[t] : rows[t] + 1] for v in edge]
        edge[0] += edge_y[0][t]
        edge[PTS - 1] += edge_y[1][t]
        ymessage.append(sum_z(jnp.concatenate(edge, axis=0), column_masks((PTS, width))))
        yface_ref[t, 0] = ymessage[t]
    extra = [[None, None], [None, None]]
    for t, ref in enumerate((below_ref, above_ref)):
        j = ends[t]
        points = [value[0][j]] + [value_ref[i, j] for i in range(1, PTS - 1)] + [value[1][j]]
        flux = contract(D, points, -1)
        flux = contract(D.T, [flux[i] * ref[2, i : i + 1] for i in range(PTS)], -1)
        for s in range(2):
            at = (2 * PTS + 2 * s + t) * ny
            extra[s][t] = sum_z(flux[ends[s]] + line_ref[at : at + ny], masks)
            extra[s][t] = jnp.where(row == rows[t], extra[s][t], 0.0)
    for s in range(2):
        for j in range(PTS):
            total[s][j] = sum_z(total[s][j], masks)
        low, high = total[s][0], total[s][PTS - 1]
        total[s][PTS - 1] = high + jnp.where(row == ny - 1, 0.0, pltpu.roll(low, ny - 1, 0))
        total[s][0] = low + jnp.where(row == 0, 0.0, pltpu.roll(high, 1, 0))
    for j in range(PTS):
        low, high = total[0][j], total[1][j]
        if j in ends:
            t = ends.index(j)
            low, high = low + extra[0][t], high + extra[1][t]
        to_inner_ref[j * ny : (j + 1) * ny] = jnp.where(even, high, low)
        to_outer_ref[j * ny : (j + 1) * ny] = jnp.where(even, low, high)
        for s in range(2):
            sofar_ref[ends[s], j] = pface[s][j] - gface[s][j] * total[s][j]
    for i in range(1, PTS - 1):
        lines = [sum_z(work_ref[i, j], masks) for j in range(PTS)]
        low, high = lines[0], lines[PTS - 1]
        lines[PTS - 1] = high + jnp.where(row == ny - 1, 0.0, pltpu.roll(low, ny - 1, 0))
        lines[0] = low + jnp.where(row == 0, 0.0, pltpu.roll(high, 1, 0))
        for j in range(PTS):
            sofar_ref[i, j] = partial_ref[i, j] - gain_ref[i, j] * lines[j]
    sums = restricted(
        [(i, j) for i in range(PTS) for j in range(PTS)],
        lambda i, j: sofar_ref[i, j],
        lambda d, i, j: weights_ref[d, i, j],
        jnp.zeros((ny, width), F32),
    )
    for q in range(2):
        sums_ref[q] = sums[q] + load_sums_ref[q]
        sums_ref[2 + q] = sums[4 + q]
        sums[2 + q] = sums[2 + q] + load_sums_ref[2 + q]
    base = PTS * ny
    changes = []
    for t in range(2):
        j = ends[t]
        gain = [gface[0][j]] + [gain_ref[i, j] for i in range(1, PTS - 1)] + [gface[1][j]]
        gain = jnp.concatenate([g[rows[t] : rows[t] + 1] for g in gain], axis=0)
        change = -(gain * ymessage[t])
        changes += edge_change(change, edge_weights_ref.at[t], ends[1 - t], 1)
        if t == 0:
            own = edge_change(change, edge_weights_ref.at[t], ends[1 - t], 0)
            zero = jnp.zeros_like(own[1])
            edge_ref[...] = jnp.concatenate([zero, own[1], zero, own[3]] + [zero] * 4, axis=0)
    changes = jnp.concatenate(changes, axis=0)
    for ref in (to_outer_ref, to_inner_ref):
        for n, k in enumerate((2, 3, 6, 7)):
            ref[base + n * ny : base + (n + 1) * ny] = sums[k]
        ref[base + 4 * ny : base + 4 * ny + PTS] = changes


def edge_change(change, weight_ref, j, p):
    upper = lax.broadcasted_iota(jnp.int32, change.shape, 0)
    hat = jnp.zeros_like(change)
    for i in range(PTS):
        hat = jnp.where(upper == i, float(HAT[i, p]), hat)
    along_x, along_y, along_z = (
        jnp.sum(v, axis=0, keepdims=True)
        for v in (weight_ref[0] * change, hat * weight_ref[1] * change, hat * weight_ref[2] * change)
    )
    smooth = [-(SLOPE[p] * float(HAT[j, q]) * along_x + SLOPE[q] * along_y) for q in range(2)]
    return smooth + [-float(HAT[j, q]) * along_z for q in range(2)]


def restricted(points, value, weight, zero):
    sums = [zero] * 8
    along_x = {}
    along_y = {}
    along_z = {}
    for i, j in points:
        v = value(i, j)
        along_x[j] = along_x.get(j, 0.0) + weight(0, i, j) * v
        along_y[i] = along_y.get(i, 0.0) + weight(1, i, j) * v
        product = weight(2, i, j) * v
        for q in range(2):
            if HAT[j, q]:
                along_z[i, q] = along_z.get((i, q), 0.0) + float(HAT[j, q]) * product
    x_sums = [
        sum(float(HAT[j, q]) * total for j, total in along_x.items() if HAT[j, q]) for q in range(2)
    ]
    y_sums = [
        sum(float(HAT[i, p]) * total for i, total in along_y.items() if HAT[i, p]) for p in range(2)
    ]
    for p in range(2):
        for q in range(2):
            sums[2 * p + q] = -(SLOPE[p] * x_sums[q] + SLOPE[q] * y_sums[p])
            sums[4 + 2 * p + q] = -sum(
                float(HAT[i, p]) * total for (i, r), total in along_z.items() if r == q and HAT[i, p]
            )
    return sums


def x_corrections(even, gface_ref, outer_ref, inner_ref):
    ny = gface_ref.shape[2]
    change = {}
    for j in range(PTS):
        low = pick(even, outer_ref, inner_ref, j * ny, ny)
        high = pick(even, inner_ref, outer_ref, j * ny, ny)
        change[0, j] = -(gface_ref[0, j] * low)
        change[PTS - 1, j] = -(gface_ref[1, j] * high)
    return change


def y_corrections(gain_ref, gface_ref, below_ref, above_ref):
    ny, width = gain_ref.shape[2:]
    row = lax.broadcasted_iota(jnp.int32, (ny, width), 0)
    faces = {0: 0, PTS - 1: 1}
    change = {}
    for i in range(PTS):
        for j, at, ref in ((0, 0, below_ref), (PTS - 1, ny - 1, above_ref)):
            gain = gface_ref[faces[i], j] if i in faces else gain_ref[i, j]
            change[i, j] = -(gain * jnp.where(row == at, ref[0, i : i + 1], 0.0))
    return change


def face_change(change, weight, i, p, q):
    along_x = sum(float(HAT[j, q]) * (weight[0][j] * change[j]) for j in range(PTS) if HAT[j, q])
    smooth = SLOPE[p] * along_x
    slope = 0.0
    if HAT[i, p]:
        along_y = sum(weight[1][j] * change[j] for j in range(PTS))
        smooth = smooth + float(HAT[i, p]) * SLOPE[q] * along_y
        along_z = sum(float(HAT[j, q]) * (weight[2][j] * change[j]) for j in range(PTS) if HAT[j, q])
        slope = float(HAT[i, p]) * along_z
    return -smooth, -slope


def to_vertices(smooth, slope, restrict):
    return dot_split(jnp.concatenate([smooth, slope], axis=1), restrict)


def pick(even, first, second, at, count):
    return jnp.where(even, first[at : at + count], second[at : at + count])


def ahead_kernel(
    side_ref, sent_outer_ref, sent_inner_ref, gface_ref, restrict_ref, outer_ref, inner_ref,
    next_ref, top_ref,
):
    ny, width = gface_ref.shape[2:]
    even = side_ref[0] == 0
    change = [
        -(gface_ref[1, j] * pick(even, sent_inner_ref, sent_outer_ref, j * ny, ny)) for j in range(PTS)
    ]
    weight = [[pick(even, inner_ref, outer_ref, j * ny, ny) for j in range(PTS)]]
    smooth = jnp.concatenate([face_change(change, weight, 0, 1, q)[0] for q in range(2)], axis=0)
    corners = to_vertices(smooth, jnp.zeros_like(smooth), restrict_ref[...])
    lower, upper = corners[:ny], corners[ny:]
    row = lax.broadcasted_iota(jnp.int32, lower.shape, 0)
    next_ref[:ny] = lower + jnp.where(row == 0, 0.0, pltpu.roll(upper, 1, 0))
    top_ref[...] = jnp.broadcast_to(upper[ny - 1 : ny], top_ref.shape)


def behind_kernel(
    side_ref, sent_outer_ref, sent_inner_ref, gface_ref, back_ref, outer_ref, inner_ref,
    own_ref,
):
    ny, width = gface_ref.shape[2:]
    even = side_ref[0] == 0

    def rows(at):
        return pick(even, outer_ref, inner_ref, at, ny)

    change = [
        -(gface_ref[0, j] * pick(even, sent_outer_ref, sent_inner_ref, j * ny, ny)) for j in range(PTS)
    ]
    spread = [rows((2 * PTS + d) * ny) for d in range(2)]
    points = [rows((PTS + j) * ny) for j in range(PTS)]
    column = dot_split(jnp.concatenate([p * spread[1] for p in points], axis=0), back_ref[...])
    weight = [
        [rows(j * ny) for j in range(PTS)],
        contract(D.T, [p * spread[0] for p in points], -1),
        [column[j * ny : (j + 1) * ny] for j in range(PTS)],
    ]
    for q in range(2):
        own_ref[q], own_ref[2 + q] = face_change(change, weight, PTS - 1, 1, q)


def coarse_kernel(
    side_ref, gface_ref, sums_ref, own_ref, edge_in_ref, weights_ref, restrict_ref, outer_ref, inner_ref,
    plane_ref, edge_ref,
):
    ny, width = gface_ref.shape[2:]
    even = side_ref[0] == 0
    change = x_corrections(even, gface_ref, outer_ref, inner_ref)
    sums = restricted(
        list(change),
        lambda i, j: change[i, j],
        lambda d, i, j: weights_ref[d, i, j],
        jnp.zeros((ny, width), F32),
    )
    base = PTS * ny

    def before(at, count):
        return pick(even, outer_ref, inner_ref, at, count)

    total = [
        sums[(0, 1, 4, 5)[n]] + sums_ref[n] + own_ref[n] + before(base + n * ny, ny) for n in range(4)
    ]
    extra = before(base + 4 * ny, PTS) + edge_in_ref[...]
    smooth = jnp.concatenate(total[:2] + [extra], axis=0)
    slope = jnp.concatenate(total[2:] + [pltpu.roll(extra, PTS - 2, 0)], axis=0)
    corners = to_vertices(smooth, slope, restrict_ref[...])
    lower, upper = corners[:ny], corners[ny : 2 * ny]
    extra = corners[2 * ny :]
    row = lax.broadcasted_iota(jnp.int32, lower.shape, 0)
    plane_ref[...] = lower + jnp.where(row == 0, extra[1:2], pltpu.roll(upper, 1, 0))
    edge_ref[0:1] = upper[ny - 1 : ny] + extra[4:5]
    edge_ref[1:2] = extra[5:6]
    edge_ref[2:3] = extra[0:1]


def beside_kernel(
    own_ref, gain_ref, gface_ref, weights_ref, restrict_ref, below_ref, above_ref,
    plane_ref,
):
    below_ref, above_ref = below_ref.at[1], above_ref.at[0]
    ny, width = gain_ref.shape[2:]
    change = y_corrections(gain_ref, gface_ref, below_ref, above_ref)
    sums = restricted(
        list(change),
        lambda i, j: change[i, j],
        lambda d, i, j: weights_ref[d, i, j],
        jnp.zeros((ny, width), F32),
    )
    smooth = jnp.concatenate([sums[0], sums[1]], axis=0)
    slope = jnp.concatenate([sums[4], sums[5]], axis=0)
    corners = to_vertices(smooth, slope, restrict_ref[...])
    lower, upper = corners[:ny], corners[ny:]
    row = lax.broadcasted_iota(jnp.int32, lower.shape, 0)
    plane_ref[...] = own_ref[...] + lower + jnp.where(row == 0, 0.0, pltpu.roll(upper, 1, 0))


def pressure_kernel(
    side_ref, sofar_ref, gain_ref, gface_ref, outer_ref, below_ref, above_ref, inner_ref,
    pressure_out, token_ref, pressure_ref, sem,
):
    token_ref[...] = jnp.zeros_like(token_ref)
    below_ref, above_ref = below_ref.at[1], above_ref.at[0]
    ny = sofar_ref.shape[2]
    even = side_ref[0] == 0
    changes = (
        x_corrections(even, gface_ref, outer_ref, inner_ref),
        y_corrections(gain_ref, gface_ref, below_ref, above_ref),
    )
    for i in range(PTS):
        for j in range(PTS):
            value = sofar_ref[i, j]
            for change in changes:
                if (i, j) in change:
                    value = value + change[i, j]
            pressure_ref[i, pl.ds(j, ny, stride=PTS)] = value
    copy = pltpu.make_async_copy(pressure_ref, pressure_out, sem)
    copy.start()
    copy.wait()


def join_kernel(own_ref, next_ref, top_ref, token_ref, joined_ref):
    row = lax.broadcasted_iota(jnp.int32, joined_ref.shape, 0)
    total = own_ref[...] + next_ref[: row.shape[0]] + token_ref[...]
    joined_ref[...] = total + jnp.where(row == 0, top_ref[0:1], 0.0)


def last_kernel(joined_ref, below_ref, above_ref, coarse_ref):
    total = joined_ref[...]
    ny = total.shape[0]
    row = lax.broadcasted_iota(jnp.int32, total.shape, 0)
    total = total + jnp.where(row == 0, below_ref[0:1], jnp.where(row == 1, below_ref[1:2], 0.0))
    total = total + jnp.where(row == ny - 1, above_ref[2:3], 0.0)
    coarse_ref[...] = total[:, : coarse_ref.shape[1]]


def call(body, outs, scratch, *args, spaces=None, out_spaces=None, flops=None):
    spaces = spaces or [pltpu.SMEM if a.dtype == jnp.int32 else pltpu.VMEM for a in args]
    return pl.pallas_call(
        body,
        out_shape=[jax.ShapeDtypeStruct(s, F32) if isinstance(s, tuple) else s for s in outs],
        in_specs=[pl.BlockSpec(memory_space=m) for m in spaces],
        out_specs=[pl.BlockSpec(memory_space=m) for m in out_spaces or [pltpu.VMEM] * len(outs)],
        scratch_shapes=[pltpu.VMEM(s, F32) if isinstance(s, tuple) else s for s in scratch],
        compiler_params=pltpu.CompilerParams(vmem_limit_bytes=16 * 1024 * 1024),
        cost_estimate=flops and pl.CostEstimate(flops=flops, bytes_accessed=0, transcendentals=0),
    )(*args)


def from_y(faces):
    size = lax.axis_size("sub")
    up = lax.ppermute(faces, "sub", [(i, (i + 1) % size) for i in range(size)])
    if size == 2:
        return up, up
    return up, lax.ppermute(faces, "sub", [(i, (i - 1) % size) for i in range(size)])


def inner_pairs(size):
    return [(i, i ^ 1) for i in range(size)]


def outer_pairs(size):
    return [(i, (i + 1) % size if i % 2 else (i - 1) % size) for i in range(size)]


def to_x(outer, inner):
    size = lax.axis_size("dom")
    outer = lax.ppermute(outer, "dom", outer_pairs(size))
    inner = lax.ppermute(inner, "dom", inner_pairs(size))
    return outer, inner


def two_on(rows, top):
    size, rest = lax.axis_size("dom"), lax.axis_size("sub")
    rows = lax.ppermute(rows, "dom", [(i, (i + 2) % size) for i in range(size)])
    pairs = [
        (i * rest + k, (i + 2) % size * rest + (k + 1) % rest) for i in range(size) for k in range(rest)
    ]
    return rows, lax.ppermute(top, ("dom", "sub"), pairs)


def shards(element_load, mobility, metric):
    _, _, ny, _, width = element_load.shape
    load = element_load.reshape(PTS, ny * PTS, width)
    mob = mobility.reshape(PTS, ny * PTS, width)
    metric = metric[:, 0]
    side = (lax.axis_index("dom") % 2).astype(jnp.int32).reshape(1)
    def in_hbm(*arrays):
        return [pltpu.with_memory_space_constraint(a, pltpu.HBM) for a in arrays]

    grad, back = column_tables(width)
    restrict = restrict_table(width)
    field = (PTS, PTS, ny, width)
    face = (PTS, ny, width)
    ends = (2, PTS, PTS, width)
    spread, yface = call(
        edge_kernel,
        [(3, ny, width), (2, 5, PTS, width)],
        [metric.shape, ends, ends, pltpu.SemaphoreType.DMA((5,))],
        *in_hbm(metric, mob, load),
        spaces=[pltpu.HBM] * 3,
    )
    below, above = from_y(yface)
    still = (2 * (PTS + 1) * ny, width)
    fields, xface, factor, still_outer, still_inner = call(
        diag_kernel,
        [(2,) + field, (2, 2) + face, (2, 2, PTS, width), still, still],
        [],
        side, load, mob, spread,
    )
    rows = (2 * PTS * ny + 2 * PTS, width)
    outer, inner = to_x(*call(merge_kernel, [rows, rows], [], side, xface, factor, below, above))
    still_outer, still_inner = to_x(still_outer, still_inner)
    faces = (2,) + face
    rough, value, partial, gain, out, pair, weights, load_sums, edge_weights = call(
        inside_kernel,
        [
            (2,) + faces, field, field, field, field, (2,) + field,
            (3,) + field, (4, ny, width), (2, 3, PTS, width),
        ],
        [face],
        fields, load, mob, spread, grad, back, below, above,
    )
    rows = ((PTS + 4) * ny + PTS, width)
    sent_outer, sent_inner, yface, gface, sofar, sums, edge = call(
        faces_kernel,
        [rows, rows, (2, 1, PTS, width), faces, field, (4, ny, width), (PTS, width)],
        [((2 * PTS + 4) * ny, width), field],
        side, rough, value, out, pair, mob, spread, grad, back, below, above,
        partial, gain, weights, load_sums, edge_weights, outer, inner,
    )
    outer, inner = to_x(sent_outer, sent_inner)
    onward, top = call(
        ahead_kernel,
        [(3 * ny, 128), (3 * PTS, 128)],
        [],
        side, sent_outer, sent_inner, gface, restrict, still_outer, still_inner,
    )
    (own,) = call(
        behind_kernel,
        [(4, ny, width)],
        [],
        side, sent_outer, sent_inner, gface, back, still_outer, still_inner,
    )
    onward, top = two_on(onward, top)
    below, above = from_y(yface)
    own_rows, tops = call(
        coarse_kernel,
        [(ny, 128), (3, 128)],
        [],
        side, gface, sums, own, edge, weights, restrict, outer, inner,
    )
    (own_rows,) = call(
        beside_kernel, [(ny, 128)], [], own_rows, gain, gface, weights, restrict, below, above
    )
    pressure, token = call(
        pressure_kernel,
        [(PTS, ny * PTS, width), (1, 128)],
        [(PTS, ny * PTS, width), pltpu.SemaphoreType.DMA(())],
        side, sofar, gain, gface, outer, below, above, inner,
        out_spaces=[pltpu.HBM, pltpu.VMEM],
    )
    (onward,) = call(join_kernel, [(ny, 128)], [], own_rows, onward, top, token, flops=FLOPS_JOIN)
    row_below, row_above = from_y(tops)
    (coarse,) = call(last_kernel, [(ny, width // PTS + 1)], [], onward, row_below, row_above)
    return pressure.reshape(element_load.shape), coarse[None]


def solution(mesh):
    in_specs = (
        P("dom", None, "sub", None, None),
        P("dom", None, "sub", None, None),
        P(None, "dom", "sub", None),
    )
    out_specs = (P("dom", None, "sub", None, None), P("dom", "sub", None))
    return jax.shard_map(shards, mesh=mesh, in_specs=in_specs, out_specs=out_specs, check_vma=False)
```

```python
import jax
import jax.numpy as jnp
import ml_dtypes
import numpy as np
from jax import lax
from jax.experimental import pallas as pl
from jax.experimental.pallas import tpu as pltpu
from jax.sharding import PartitionSpec as P

GLL_NODES = np.array(
    [
        -1.0,
        -0.8717401485096066,
        -0.5917001814331423,
        -0.2092992179024789,
        0.2092992179024789,
        0.5917001814331423,
        0.8717401485096066,
        1.0,
    ]
)
GLL_WEIGHTS = np.array(
    [
        0.03571428571428571,
        0.2107042271435061,
        0.3411226924835044,
        0.4124587946587038,
        0.4124587946587038,
        0.3411226924835044,
        0.2107042271435061,
        0.03571428571428571,
    ]
)
THETA = 1.65
DELTA = 1.35
RHO_FIRST = DELTA / THETA
RHO_SECOND = 1.0 / (2.0 * THETA / DELTA - RHO_FIRST)
KEEP = 1.0 + RHO_SECOND * RHO_FIRST
GAIN = 2.0 * RHO_SECOND / DELTA
PTS = 8
F32 = jnp.float32


def derivative_table():
    identity = np.eye(8)
    differences = GLL_NODES[:, None] - GLL_NODES[None, :] + identity
    barycentric = 1.0 / np.prod(differences, axis=1)
    matrix = barycentric[None, :] / barycentric[:, None] / differences
    matrix = matrix * (1.0 - identity)
    row_sums = np.sum(matrix, axis=1)
    return matrix - identity * row_sums[:, None]


D = derivative_table()
W = GLL_WEIGHTS
HAT = np.stack([(1.0 - GLL_NODES) / 8.0, (1.0 + GLL_NODES) / 8.0], axis=1)
SLOPE = (-0.125, 0.125)


def tiled(matrix, width):
    column = lax.broadcasted_iota(jnp.int32, (PTS, width), 1) % PTS
    row = lax.broadcasted_iota(jnp.int32, (PTS, width), 0)
    total = jnp.zeros((PTS, width), F32)
    for c in range(PTS):
        lines = jnp.zeros((PTS, width), F32)
        for r in range(PTS):
            lines = jnp.where(row == r, float(matrix[r, c]), lines)
        total = jnp.where(column == c, lines, total)
    return total


def by_row(values, width):
    return tiled(np.tile(np.asarray(values)[:, None], (1, PTS)), width)


def cell_blocks(rows):
    width = rows.shape[1]
    cell = lax.broadcasted_iota(jnp.int32, rows.shape, 1) // PTS
    return jnp.concatenate(
        [jnp.where(cell == g, rows, 0.0) for g in range(width // PTS)], axis=0
    )


def paired_here(b):
    high, low = halves(b)
    return jnp.concatenate(
        [
            jnp.concatenate([high, low], axis=1),
            jnp.concatenate([high, jnp.zeros_like(low)], axis=1),
        ],
        axis=0,
    )


def paired(b):
    b = np.asarray(b, np.float32)
    high = b.astype(ml_dtypes.bfloat16)
    low = (b - high.astype(np.float32)).astype(ml_dtypes.bfloat16)
    return jnp.asarray(np.block([[high, low], [high, np.zeros_like(low)]]))


def column_tables(width):
    cells = np.eye(width // PTS)
    return paired(np.kron(cells, D.T)), paired(np.kron(cells, D))


def restrict_table(width):
    cells = width // PTS
    hat = np.zeros((width, 128))
    slope = np.zeros((width, 128))
    for c in range(cells):
        rows = slice(c * PTS, (c + 1) * PTS)
        hat[rows, c], hat[rows, c + 1] = HAT[:, 0], HAT[:, 1]
        slope[rows, c], slope[rows, c + 1] = SLOPE
    return paired(np.concatenate([hat, slope]))


def halves(a):
    high = a.astype(jnp.bfloat16)
    return high, (a - high.astype(F32)).astype(jnp.bfloat16)


def dot_split(a, b_pair):
    both = jnp.dot(
        jnp.concatenate(halves(a), axis=1), b_pair, preferred_element_type=F32
    )
    n = both.shape[1] // 2
    return both[:, :n] + both[:, n:]


def contract(matrix, lines, parity):
    n = len(lines)
    half = n // 2
    plus = [lines[c] + lines[n - 1 - c] for c in range(half)]
    minus = [lines[c] - lines[n - 1 - c] for c in range(half)]
    top, low = [], []
    for r in range(half):
        even = sum(float(0.5 * (matrix[r, c] + matrix[r, n - 1 - c])) * plus[c] for c in range(half))
        odd = sum(float(0.5 * (matrix[r, c] - matrix[r, n - 1 - c])) * minus[c] for c in range(half))
        top.append(even + odd)
        low.append(even - odd if parity > 0 else odd - even)
    return top + low[::-1]


def spread_metric(metric, weight_row):
    _, rows, cells = metric.shape
    width = weight_row.shape[1]
    cell = lax.broadcasted_iota(jnp.int32, (cells, width), 1) // PTS
    row = lax.broadcasted_iota(jnp.int32, (cells, width), 0)
    pick = jnp.where(cell == row, 1.0, 0.0).astype(jnp.bfloat16)
    flat = metric.reshape(3 * rows, cells)
    high = flat.astype(jnp.bfloat16)
    rest = flat - high.astype(F32)
    parts = jnp.concatenate([high, *halves(rest)], axis=1)
    spread = jnp.dot(
        parts, jnp.concatenate([pick] * 3, axis=0), preferred_element_type=F32
    )
    spread = [spread[d * rows : (d + 1) * rows] for d in range(3)]
    return [v * weight_row[:1] for v in spread], spread[2]


def column_masks(shape):
    lane = lax.broadcasted_iota(jnp.int32, shape, len(shape) - 1)
    up = (lane % PTS == PTS - 1) & (lane != shape[-1] - 1)
    down = (lane % PTS == 0) & (lane != 0)
    return up, down


def sum_z(v, masks):
    width = v.shape[-1]
    axis = v.ndim - 1
    up = pltpu.roll(v, width - 1, axis)
    down = pltpu.roll(v, 1, axis)
    return v + jnp.where(masks[0], up, jnp.where(masks[1], down, 0.0))


def sum_y_local(ref, ny):
    for i in range(PTS):
        low, high = ref[i, 0], ref[i, PTS - 1]
        row = lax.broadcasted_iota(jnp.int32, low.shape, 0)
        ref[i, PTS - 1] = high + jnp.where(row == ny - 1, 0.0, pltpu.roll(low, ny - 1, 0))
        ref[i, 0] = low + jnp.where(row == 0, 0.0, pltpu.roll(high, 1, 0))


def edge_planes(ref, ny):
    low = jnp.concatenate([ref[i, 0, 0:1] for i in range(PTS)], axis=0)
    high = jnp.concatenate([ref[i, PTS - 1, ny - 1 : ny] for i in range(PTS)], axis=0)
    return low, high


def plane(ref, ny):
    return lambda i, j: ref[i, pl.ds(j, ny, stride=PTS)]


def edge_kernel(metric_in, mob_in, load_in, spread_ref, yface_ref, metric_ref, mob_ref, load_ref, sems):
    ny, width = spread_ref.shape[1:]
    ends = (0, PTS - 1)
    copies = [pltpu.make_async_copy(metric_in, metric_ref, sems.at[0])]
    for n, (source, target) in enumerate(((mob_in, mob_ref), (load_in, load_ref))):
        for s, e in enumerate((0, ny - 1)):
            copies.append(
                pltpu.make_async_copy(
                    source.at[:, pl.ds(e * PTS, PTS)], target.at[s], sems.at[1 + 2 * n + s]
                )
            )
    for copy in copies:
        copy.start()
    masks = column_masks((PTS, width))
    weight_row = tiled(np.tile(W[None], (PTS, 1)), width)
    row_weight = by_row(W, width)
    squared = paired_here(cell_blocks(tiled(D * D, width)))
    squares = [by_row(D[a] ** 2, width) for a in range(PTS)]
    for copy in copies:
        copy.wait()
    spread, cell_metric = spread_metric(metric_ref[...], weight_row)
    for d in range(3):
        spread_ref[d] = spread[d]
    points = [mob_ref[s, :, ends[s]] * (float(W[ends[s]]) * row_weight) for s in range(2)]
    columns = dot_split(
        jnp.concatenate([p * weight_row for p in points], axis=0), squared
    )
    for s, e in enumerate((0, ny - 1)):
        j = ends[s]
        scale = [spread[d][e : e + 1] for d in range(3)]
        along = sum(squares[a] * points[s][a : a + 1] for a in range(PTS))
        total = along * scale[0]
        sums = [
            sum(float(D[b, j] ** power * W[b]) * mob_ref[s, :, b] for b in range(PTS))
            * row_weight
            * scale[1]
            for power in (1, 2)
        ]
        yface_ref[s, 2] = points[s] * scale[0]
        yface_ref[s, 3] = points[s] * scale[2]
        yface_ref[s, 4] = sums[0]
        column = columns[s * PTS : (s + 1) * PTS] * cell_metric[e : e + 1]
        yface_ref[s, 1] = sum_z(total + sums[1] + column, masks)
    for s in range(2):
        yface_ref[s, 0] = sum_z(load_ref[s, :, ends[s]], masks)


def diag_kernel(
    side_ref, load_ref, mob_ref, spread_ref,
    fields_ref, xface_ref, factor_ref, to_outer_ref, to_inner_ref,
):
    ny, width = fields_ref.shape[3:]
    spread = [spread_ref[d] for d in range(3)]
    square = D * D
    squared = paired_here(cell_blocks(tiled(square, width)))
    mob, load = plane(mob_ref, ny), plane(load_ref, ny)
    diag_ref = fields_ref.at[1]
    even = side_ref[0] == 0

    def post(at, low, high):
        to_inner_ref[at : at + ny] = jnp.where(even, high, low)
        to_outer_ref[at : at + ny] = jnp.where(even, low, high)

    for d in (1, 2):
        post((2 * PTS + d - 1) * ny, spread[d], spread[d])
    for j in range(PTS):
        factor = [mob(i, j) * (float(W[i] * W[j]) * spread[0]) for i in range(PTS)]
        post(j * ny, *(sum(float(D[a, i]) * factor[a] for a in range(PTS)) for i in (0, PTS - 1)))
        post((PTS + j) * ny, *(float(W[i] * W[j]) * mob(i, j) for i in (0, PTS - 1)))
        for i, value in enumerate(contract(square.T, factor, 1)):
            diag_ref[i, j] = value
    for i in range(PTS):
        factor = [mob(i, j) * (float(W[i] * W[j]) * spread[1]) for j in range(PTS)]
        for j, value in enumerate(contract(square.T, factor, 1)):
            diag_ref[i, j] += value
    for i in range(PTS):
        factor = jnp.concatenate(
            [mob(i, j) * (float(W[i] * W[j]) * spread[2]) for j in range(PTS)], axis=0
        )
        diag_ref[i] += dot_split(factor, squared).reshape(PTS, ny, width)
        fields_ref[0, i] = jnp.stack([load(i, j) for j in range(PTS)], axis=0)
    masks = column_masks((PTS, ny, width))
    for f in range(2):
        for i in range(PTS):
            fields_ref[f, i] = sum_z(fields_ref[f, i], masks)
        sum_y_local(fields_ref.at[f], ny)
        xface_ref[f, 0] = fields_ref[f, 0]
        xface_ref[f, 1] = fields_ref[f, PTS - 1]
    row_weight = by_row(W, width)
    for s, i in enumerate((0, PTS - 1)):
        for n, e in enumerate((0, ny - 1)):
            points = mob_ref[i, e * PTS : (e + 1) * PTS] * (float(W[i]) * row_weight)
            factor_ref[s, n] = points * spread[1][e : e + 1]


def merge_kernel(side_ref, xface_ref, factor_ref, below_ref, above_ref, outer_ref, inner_ref):
    below_ref, above_ref = below_ref.at[1], above_ref.at[0]
    even = side_ref[0] == 0
    fields, _, _, ny, width = xface_ref.shape
    row = lax.broadcasted_iota(jnp.int32, (ny, width), 0)
    for f in range(fields):
        for j in range(PTS):
            low, high = xface_ref[f, 0, j], xface_ref[f, 1, j]
            if j == 0:
                low = low + jnp.where(row == 0, below_ref[f, 0:1], 0.0)
                high = high + jnp.where(row == 0, below_ref[f, PTS - 1 : PTS], 0.0)
            if j == PTS - 1:
                low = low + jnp.where(row == ny - 1, above_ref[f, 0:1], 0.0)
                high = high + jnp.where(row == ny - 1, above_ref[f, PTS - 1 : PTS], 0.0)
            at = (f * PTS + j) * ny
            inner_ref[at : at + ny] = jnp.where(even, high, low)
            outer_ref[at : at + ny] = jnp.where(even, low, high)
    for n in range(2):
        at = fields * PTS * ny + n * PTS
        low, high = factor_ref[0, n], factor_ref[1, n]
        inner_ref[at : at + PTS] = jnp.where(even, high, low)
        outer_ref[at : at + PTS] = jnp.where(even, low, high)


def inside_kernel(
    fields_ref, load_ref, mob_ref, spread_ref, grad_ref, back_ref, below_ref, above_ref,
    rough_ref, value_ref, partial_ref, gain_ref, out_ref, pair_ref, weights_ref, sums_ref, edge_weights_ref,
    work_ref,
):
    below_ref, above_ref = below_ref.at[1], above_ref.at[0]
    ny, width = out_ref.shape[2:]
    spread = [spread_ref[d] for d in range(3)]
    mob, load = plane(mob_ref, ny), plane(load_ref, ny)
    row = lax.broadcasted_iota(jnp.int32, (ny, width), 0)
    zero = jnp.zeros((ny, width), F32)
    for i in range(PTS):
        for j in range(PTS):
            sums = [fields_ref[f, i, j] for f in range(2)]
            for f in range(2):
                if j == 0:
                    sums[f] += jnp.where(row == 0, below_ref[f, i : i + 1], 0.0)
                if j == PTS - 1:
                    sums[f] += jnp.where(row == ny - 1, above_ref[f, i : i + 1], 0.0)
            if i in (0, PTS - 1):
                for f in range(2):
                    rough_ref[f, 0 if i == 0 else 1, j] = sums[f]
                value_ref[i, j] = partial_ref[i, j] = gain_ref[i, j] = zero
            else:
                value_ref[i, j], partial_ref[i, j], gain_ref[i, j] = first_step(*sums)
    grad, back = grad_ref[...], back_ref[...]
    for j in range(PTS):
        factor = [mob(i, j) * (float(W[i] * W[j]) * spread[0]) for i in range(PTS)]
        for n, p in enumerate((0, PTS - 1)):
            coupling = contract(D.T, [float(D[a, p]) * factor[a] for a in range(PTS)], -1)
            for i in range(PTS):
                pair_ref[n, i, j] = coupling[i]
        flux = contract(D, [value_ref[i, j] for i in range(PTS)], -1)
        flux = [flux[i] * factor[i] for i in range(PTS)]
        for i, value in enumerate(contract(D.T, flux, -1)):
            out_ref[i, j] = value
        for i, value in enumerate(contract(D.T, factor, -1)):
            weights_ref[0, i, j] = value
    for i in range(1, PTS - 1):
        flux = contract(D, [value_ref[i, j] for j in range(PTS)], -1)
        flux = [flux[j] * (mob(i, j) * (float(W[i] * W[j]) * spread[1])) for j in range(PTS)]
        for j, value in enumerate(contract(D.T, flux, -1)):
            out_ref[i, j] += value
        work_ref[...] = dot_split(value_ref[i].reshape(PTS * ny, width), grad).reshape(PTS, ny, width)
        for j in range(PTS):
            work_ref[j] *= mob(i, j) * (float(W[i] * W[j]) * spread[2])
        out_ref[i] += dot_split(work_ref[...].reshape(PTS * ny, width), back).reshape(PTS, ny, width)
    for i in range(PTS):
        factor = [mob(i, j) * (float(W[i] * W[j]) * spread[1]) for j in range(PTS)]
        for j, value in enumerate(contract(D.T, factor, -1)):
            weights_ref[1, i, j] = value
        factor = jnp.concatenate(
            [mob(i, j) * (float(W[i] * W[j]) * spread[2]) for j in range(PTS)], axis=0
        )
        weights_ref[2, i] = dot_split(factor, back).reshape(PTS, ny, width)
    sums = [zero] * 4
    for i in range(PTS):
        for q in range(2):
            from_load = sum(float(HAT[j, q]) * load(i, j) for j in range(PTS))
            for p in range(2):
                if HAT[i, p]:
                    sums[2 * p + q] = sums[2 * p + q] + float(HAT[i, p]) * from_load
    for n in range(4):
        sums_ref[n] = sums[n]
    for t, ref in enumerate((below_ref, above_ref)):
        edge_weights_ref[t, 0] = sum(by_row(D[a], width) * ref[2, a : a + 1] for a in range(PTS))
        edge_weights_ref[t, 1] = ref[4]
        edge_weights_ref[t, 2] = dot_split(ref[3], back)


def first_step(right, diagonal):
    inverse = 1.0 / diagonal
    scaled = inverse * right
    value = scaled * (1.0 / THETA)
    return value, KEEP * value + GAIN * scaled, GAIN * inverse


def faces_kernel(
    side_ref, rough_ref, value_ref, out_ref, pair_ref, mob_ref, spread_ref, grad_ref, back_ref,
    below_ref, above_ref, partial_ref, gain_ref, weights_ref, load_sums_ref, edge_weights_ref,
    outer_ref, inner_ref,
    to_outer_ref, to_inner_ref, yface_ref, gface_ref, sofar_ref, sums_ref, edge_ref, line_ref, work_ref,
):
    below_ref, above_ref = below_ref.at[1], above_ref.at[0]
    even = side_ref[0] == 0
    ny, width = out_ref.shape[2:]
    spread = [spread_ref[d] for d in range(3)]
    mob = plane(mob_ref, ny)
    ends = (0, PTS - 1)
    rows = (0, ny - 1)
    row = lax.broadcasted_iota(jnp.int32, (ny, width), 0)
    masks = column_masks((ny, width))

    def arrived(at, count):
        inner, outer = inner_ref[at : at + count], outer_ref[at : at + count]
        return jnp.where(even, outer, inner), jnp.where(even, inner, outer)

    value = [[None] * PTS, [None] * PTS]
    pface = [[None] * PTS, [None] * PTS]
    gface = [[None] * PTS, [None] * PTS]
    for j in range(PTS):
        load = arrived(j * ny, ny)
        diagonal = arrived((PTS + j) * ny, ny)
        for s in range(2):
            value[s][j], pface[s][j], gface[s][j] = first_step(
                rough_ref[0, s, j] + load[s], rough_ref[1, s, j] + diagonal[s]
            )
            gface_ref[s, j] = gface[s][j]
    lines = [value[s][j] for s in range(2) for j in range(PTS)]
    factors = [
        mob(ends[s], j) * (float(W[ends[s]] * W[j]) * spread[2]) for s in range(2) for j in range(PTS)
    ]
    for s in range(2):
        for t, ref in enumerate((below_ref, above_ref)):
            lines.append(value[s][ends[t]])
            factors.append(jnp.broadcast_to(ref[3, ends[s] : ends[s] + 1], (ny, width)))
    flux = dot_split(jnp.concatenate(lines, axis=0), grad_ref[...]) * jnp.concatenate(factors, axis=0)
    line_ref[...] = dot_split(flux, back_ref[...])
    edge_y = [[None, None], [None, None]]
    total = [[None] * PTS, [None] * PTS]
    for s in range(2):
        gradient = contract(D, value[s], -1)
        flux = [
            gradient[j] * (mob(ends[s], j) * (float(W[ends[s]] * W[j]) * spread[1])) for j in range(PTS)
        ]
        total[s] = contract(D.T, flux, -1)
        for t in range(2):
            factor = arrived(2 * PTS * ny + t * PTS, PTS)[s]
            edge_y[s][t] = sum(
                float(D[j, ends[t]]) * (gradient[j] * factor[j : j + 1]) for j in range(PTS)
            )[rows[t] : rows[t] + 1]
    for j in range(PTS):
        across = [
            out_ref[i, j] + (pair_ref[0, i, j] * value[0][j] + pair_ref[1, i, j] * value[1][j])
            for i in range(PTS)
        ]
        total[0][j] += across[0]
        total[1][j] += across[PTS - 1]
        for i in range(1, PTS - 1):
            work_ref[i, j] = across[i]
    for s in range(2):
        for j in range(PTS):
            at = (s * PTS + j) * ny
            total[s][j] += line_ref[at : at + ny]
    ymessage = []
    for t in range(2):
        j = ends[t]
        edge = [total[0][j]] + [work_ref[i, j] for i in range(1, PTS - 1)] + [total[1][j]]
        edge = [v[rows[t] : rows[t] + 1] for v in edge]
        edge[0] += edge_y[0][t]
        edge[PTS - 1] += edge_y[1][t]
        ymessage.append(sum_z(jnp.concatenate(edge, axis=0), column_masks((PTS, width))))
        yface_ref[t, 0] = ymessage[t]
    extra = [[None, None], [None, None]]
    for t, ref in enumerate((below_ref, above_ref)):
        j = ends[t]
        points = [value[0][j]] + [value_ref[i, j] for i in range(1, PTS - 1)] + [value[1][j]]
        flux = contract(D, points, -1)
        flux = contract(D.T, [flux[i] * ref[2, i : i + 1] for i in range(PTS)], -1)
        for s in range(2):
            at = (2 * PTS + 2 * s + t) * ny
            extra[s][t] = sum_z(flux[ends[s]] + line_ref[at : at + ny], masks)
            extra[s][t] = jnp.where(row == rows[t], extra[s][t], 0.0)
    for s in range(2):
        for j in range(PTS):
            total[s][j] = sum_z(total[s][j], masks)
        low, high = total[s][0], total[s][PTS - 1]
        total[s][PTS - 1] = high + jnp.where(row == ny - 1, 0.0, pltpu.roll(low, ny - 1, 0))
        total[s][0] = low + jnp.where(row == 0, 0.0, pltpu.roll(high, 1, 0))
    for j in range(PTS):
        low, high = total[0][j], total[1][j]
        if j in ends:
            t = ends.index(j)
            low, high = low + extra[0][t], high + extra[1][t]
        to_inner_ref[j * ny : (j + 1) * ny] = jnp.where(even, high, low)
        to_outer_ref[j * ny : (j + 1) * ny] = jnp.where(even, low, high)
        for s in range(2):
            sofar_ref[ends[s], j] = pface[s][j] - gface[s][j] * total[s][j]
    for i in range(1, PTS - 1):
        lines = [sum_z(work_ref[i, j], masks) for j in range(PTS)]
        low, high = lines[0], lines[PTS - 1]
        lines[PTS - 1] = high + jnp.where(row == ny - 1, 0.0, pltpu.roll(low, ny - 1, 0))
        lines[0] = low + jnp.where(row == 0, 0.0, pltpu.roll(high, 1, 0))
        for j in range(PTS):
            sofar_ref[i, j] = partial_ref[i, j] - gain_ref[i, j] * lines[j]
    sums = restricted(
        [(i, j) for i in range(PTS) for j in range(PTS)],
        lambda i, j: sofar_ref[i, j],
        lambda d, i, j: weights_ref[d, i, j],
        jnp.zeros((ny, width), F32),
    )
    for q in range(2):
        sums_ref[q] = sums[q] + load_sums_ref[q]
        sums_ref[2 + q] = sums[4 + q]
        sums[2 + q] = sums[2 + q] + load_sums_ref[2 + q]
    base = PTS * ny
    changes = []
    for t in range(2):
        j = ends[t]
        gain = [gface[0][j]] + [gain_ref[i, j] for i in range(1, PTS - 1)] + [gface[1][j]]
        gain = jnp.concatenate([g[rows[t] : rows[t] + 1] for g in gain], axis=0)
        change = -(gain * ymessage[t])
        changes += edge_change(change, edge_weights_ref.at[t], ends[1 - t], 1)
        if t == 0:
            own = edge_change(change, edge_weights_ref.at[t], ends[1 - t], 0)
            zero = jnp.zeros_like(own[1])
            edge_ref[...] = jnp.concatenate([zero, own[1], zero, own[3]] + [zero] * 4, axis=0)
    changes = jnp.concatenate(changes, axis=0)
    for ref in (to_outer_ref, to_inner_ref):
        for n, k in enumerate((2, 3, 6, 7)):
            ref[base + n * ny : base + (n + 1) * ny] = sums[k]
        ref[base + 4 * ny : base + 4 * ny + PTS] = changes


def edge_change(change, weight_ref, j, p):
    upper = lax.broadcasted_iota(jnp.int32, change.shape, 0)
    hat = jnp.zeros_like(change)
    for i in range(PTS):
        hat = jnp.where(upper == i, float(HAT[i, p]), hat)
    along_x, along_y, along_z = (
        jnp.sum(v, axis=0, keepdims=True)
        for v in (weight_ref[0] * change, hat * weight_ref[1] * change, hat * weight_ref[2] * change)
    )
    smooth = [-(SLOPE[p] * float(HAT[j, q]) * along_x + SLOPE[q] * along_y) for q in range(2)]
    return smooth + [-float(HAT[j, q]) * along_z for q in range(2)]


def restricted(points, value, weight, zero):
    sums = [zero] * 8
    along_x = {}
    along_y = {}
    along_z = {}
    for i, j in points:
        v = value(i, j)
        along_x[j] = along_x.get(j, 0.0) + weight(0, i, j) * v
        along_y[i] = along_y.get(i, 0.0) + weight(1, i, j) * v
        product = weight(2, i, j) * v
        for q in range(2):
            if HAT[j, q]:
                along_z[i, q] = along_z.get((i, q), 0.0) + float(HAT[j, q]) * product
    x_sums = [
        sum(float(HAT[j, q]) * total for j, total in along_x.items() if HAT[j, q]) for q in range(2)
    ]
    y_sums = [
        sum(float(HAT[i, p]) * total for i, total in along_y.items() if HAT[i, p]) for p in range(2)
    ]
    for p in range(2):
        for q in range(2):
            sums[2 * p + q] = -(SLOPE[p] * x_sums[q] + SLOPE[q] * y_sums[p])
            sums[4 + 2 * p + q] = -sum(
                float(HAT[i, p]) * total for (i, r), total in along_z.items() if r == q and HAT[i, p]
            )
    return sums


def x_corrections(even, gface_ref, outer_ref, inner_ref):
    ny = gface_ref.shape[2]
    change = {}
    for j in range(PTS):
        low = pick(even, outer_ref, inner_ref, j * ny, ny)
        high = pick(even, inner_ref, outer_ref, j * ny, ny)
        change[0, j] = -(gface_ref[0, j] * low)
        change[PTS - 1, j] = -(gface_ref[1, j] * high)
    return change


def y_corrections(gain_ref, gface_ref, below_ref, above_ref):
    ny, width = gain_ref.shape[2:]
    row = lax.broadcasted_iota(jnp.int32, (ny, width), 0)
    faces = {0: 0, PTS - 1: 1}
    change = {}
    for i in range(PTS):
        for j, at, ref in ((0, 0, below_ref), (PTS - 1, ny - 1, above_ref)):
            gain = gface_ref[faces[i], j] if i in faces else gain_ref[i, j]
            change[i, j] = -(gain * jnp.where(row == at, ref[0, i : i + 1], 0.0))
    return change


def face_change(change, weight, i, p, q):
    along_x = sum(float(HAT[j, q]) * (weight[0][j] * change[j]) for j in range(PTS) if HAT[j, q])
    smooth = SLOPE[p] * along_x
    slope = 0.0
    if HAT[i, p]:
        along_y = sum(weight[1][j] * change[j] for j in range(PTS))
        smooth = smooth + float(HAT[i, p]) * SLOPE[q] * along_y
        along_z = sum(float(HAT[j, q]) * (weight[2][j] * change[j]) for j in range(PTS) if HAT[j, q])
        slope = float(HAT[i, p]) * along_z
    return -smooth, -slope


def to_vertices(smooth, slope, restrict):
    return dot_split(jnp.concatenate([smooth, slope], axis=1), restrict)


def pick(even, first, second, at, count):
    return jnp.where(even, first[at : at + count], second[at : at + count])


def ahead_kernel(
    side_ref, sent_outer_ref, sent_inner_ref, gface_ref, restrict_ref, outer_ref, inner_ref,
    next_ref, top_ref,
):
    ny, width = gface_ref.shape[2:]
    even = side_ref[0] == 0
    change = [
        -(gface_ref[1, j] * pick(even, sent_inner_ref, sent_outer_ref, j * ny, ny)) for j in range(PTS)
    ]
    weight = [[pick(even, inner_ref, outer_ref, j * ny, ny) for j in range(PTS)]]
    smooth = jnp.concatenate([face_change(change, weight, 0, 1, q)[0] for q in range(2)], axis=0)
    hats = jnp.concatenate([restrict_ref[:width], restrict_ref[2 * width : 3 * width]], axis=0)
    corners = dot_split(smooth, hats)
    lower, upper = corners[:ny], corners[ny:]
    row = lax.broadcasted_iota(jnp.int32, lower.shape, 0)
    rows = lower + jnp.where(row == 0, 0.0, pltpu.roll(upper, 1, 0))
    next_ref[...] = jnp.concatenate([rows] * (next_ref.shape[0] // ny), axis=0)
    top_ref[...] = jnp.broadcast_to(upper[ny - 1 : ny], top_ref.shape)


def behind_kernel(
    side_ref, sent_outer_ref, sent_inner_ref, gface_ref, back_ref, outer_ref, inner_ref,
    own_ref,
):
    ny, width = gface_ref.shape[2:]
    even = side_ref[0] == 0

    def rows(at):
        return pick(even, outer_ref, inner_ref, at, ny)

    change = [
        -(gface_ref[0, j] * pick(even, sent_outer_ref, sent_inner_ref, j * ny, ny)) for j in range(PTS)
    ]
    spread = [rows((2 * PTS + d) * ny) for d in range(2)]
    points = [rows((PTS + j) * ny) for j in range(PTS)]
    column = dot_split(jnp.concatenate([p * spread[1] for p in points], axis=0), back_ref[...])
    weight = [
        [rows(j * ny) for j in range(PTS)],
        contract(D.T, [p * spread[0] for p in points], -1),
        [column[j * ny : (j + 1) * ny] for j in range(PTS)],
    ]
    for q in range(2):
        own_ref[q], own_ref[2 + q] = face_change(change, weight, PTS - 1, 1, q)


def coarse_kernel(
    side_ref, gface_ref, sums_ref, own_ref, edge_in_ref, weights_ref, restrict_ref, outer_ref, inner_ref,
    plane_ref, edge_ref,
):
    ny, width = gface_ref.shape[2:]
    even = side_ref[0] == 0
    change = x_corrections(even, gface_ref, outer_ref, inner_ref)
    sums = restricted(
        list(change),
        lambda i, j: change[i, j],
        lambda d, i, j: weights_ref[d, i, j],
        jnp.zeros((ny, width), F32),
    )
    base = PTS * ny

    def before(at, count):
        return pick(even, outer_ref, inner_ref, at, count)

    total = [
        sums[(0, 1, 4, 5)[n]] + sums_ref[n] + own_ref[n] + before(base + n * ny, ny) for n in range(4)
    ]
    extra = before(base + 4 * ny, PTS) + edge_in_ref[...]
    smooth = jnp.concatenate(total[:2] + [extra], axis=0)
    slope = jnp.concatenate(total[2:] + [pltpu.roll(extra, PTS - 2, 0)], axis=0)
    corners = to_vertices(smooth, slope, restrict_ref[...])
    lower, upper = corners[:ny], corners[ny : 2 * ny]
    extra = corners[2 * ny :]
    row = lax.broadcasted_iota(jnp.int32, lower.shape, 0)
    plane_ref[...] = lower + jnp.where(row == 0, extra[1:2], pltpu.roll(upper, 1, 0))
    edge_ref[0:1] = upper[ny - 1 : ny] + extra[4:5]
    edge_ref[1:2] = extra[5:6]
    edge_ref[2:3] = extra[0:1]


def beside_kernel(
    own_ref, gain_ref, gface_ref, weights_ref, restrict_ref, below_ref, above_ref,
    plane_ref,
):
    below_ref, above_ref = below_ref.at[1], above_ref.at[0]
    ny, width = gain_ref.shape[2:]
    change = y_corrections(gain_ref, gface_ref, below_ref, above_ref)
    sums = restricted(
        list(change),
        lambda i, j: change[i, j],
        lambda d, i, j: weights_ref[d, i, j],
        jnp.zeros((ny, width), F32),
    )
    smooth = jnp.concatenate([sums[0], sums[1]], axis=0)
    slope = jnp.concatenate([sums[4], sums[5]], axis=0)
    corners = to_vertices(smooth, slope, restrict_ref[...])
    lower, upper = corners[:ny], corners[ny:]
    row = lax.broadcasted_iota(jnp.int32, lower.shape, 0)
    plane_ref[...] = own_ref[...] + lower + jnp.where(row == 0, 0.0, pltpu.roll(upper, 1, 0))


def pressure_kernel(
    side_ref, sofar_ref, gain_ref, gface_ref, outer_ref, below_ref, above_ref, inner_ref,
    pressure_out, token_ref, pressure_ref, sem,
):
    token_ref[...] = jnp.zeros_like(token_ref)
    below_ref, above_ref = below_ref.at[1], above_ref.at[0]
    ny = sofar_ref.shape[2]
    even = side_ref[0] == 0
    changes = (
        x_corrections(even, gface_ref, outer_ref, inner_ref),
        y_corrections(gain_ref, gface_ref, below_ref, above_ref),
    )
    for i in range(PTS):
        for j in range(PTS):
            value = sofar_ref[i, j]
            for change in changes:
                if (i, j) in change:
                    value = value + change[i, j]
            pressure_ref[i, pl.ds(j, ny, stride=PTS)] = value
    copy = pltpu.make_async_copy(pressure_ref, pressure_out, sem)
    copy.start()
    copy.wait()


def join_kernel(own_ref, next_ref, top_ref, token_ref, joined_ref):
    row = lax.broadcasted_iota(jnp.int32, joined_ref.shape, 0)
    total = own_ref[...] + next_ref[: row.shape[0]] + token_ref[...]
    joined_ref[...] = total + jnp.where(row == 0, top_ref[0:1], 0.0)


def last_kernel(joined_ref, below_ref, above_ref, coarse_ref):
    total = joined_ref[...]
    ny = total.shape[0]
    row = lax.broadcasted_iota(jnp.int32, total.shape, 0)
    total = total + jnp.where(row == 0, below_ref[0:1], jnp.where(row == 1, below_ref[1:2], 0.0))
    total = total + jnp.where(row == ny - 1, above_ref[2:3], 0.0)
    coarse_ref[...] = total[:, : coarse_ref.shape[1]]


def call(body, outs, scratch, *args, spaces=None, out_spaces=None):
    spaces = spaces or [pltpu.SMEM if a.dtype == jnp.int32 else pltpu.VMEM for a in args]
    return pl.pallas_call(
        body,
        out_shape=[jax.ShapeDtypeStruct(s, F32) if isinstance(s, tuple) else s for s in outs],
        in_specs=[pl.BlockSpec(memory_space=m) for m in spaces],
        out_specs=[pl.BlockSpec(memory_space=m) for m in out_spaces or [pltpu.VMEM] * len(outs)],
        scratch_shapes=[pltpu.VMEM(s, F32) if isinstance(s, tuple) else s for s in scratch],
        compiler_params=pltpu.CompilerParams(vmem_limit_bytes=16 * 1024 * 1024),
    )(*args)


def from_y(faces):
    size = lax.axis_size("sub")
    up = lax.ppermute(faces, "sub", [(i, (i + 1) % size) for i in range(size)])
    if size == 2:
        return up, up
    return up, lax.ppermute(faces, "sub", [(i, (i - 1) % size) for i in range(size)])


def inner_pairs(size):
    return [(i, i ^ 1) for i in range(size)]


def outer_pairs(size):
    return [(i, (i + 1) % size if i % 2 else (i - 1) % size) for i in range(size)]


def to_x(outer, inner):
    size = lax.axis_size("dom")
    outer = lax.ppermute(outer, "dom", outer_pairs(size))
    inner = lax.ppermute(inner, "dom", inner_pairs(size))
    return outer, inner


def two_on(rows, top):
    size, rest = lax.axis_size("dom"), lax.axis_size("sub")
    rows = lax.ppermute(rows, "dom", [(i, (i + 2) % size) for i in range(size)])
    pairs = [
        (i * rest + k, (i + 2) % size * rest + (k + 1) % rest) for i in range(size) for k in range(rest)
    ]
    return rows, lax.ppermute(top, ("dom", "sub"), pairs)


def shards(element_load, mobility, metric):
    _, _, ny, _, width = element_load.shape
    load = element_load.reshape(PTS, ny * PTS, width)
    mob = mobility.reshape(PTS, ny * PTS, width)
    metric = metric[:, 0]
    side = (lax.axis_index("dom") % 2).astype(jnp.int32).reshape(1)
    def in_hbm(*arrays):
        return [pltpu.with_memory_space_constraint(a, pltpu.HBM) for a in arrays]

    grad, back = column_tables(width)
    restrict = restrict_table(width)
    field = (PTS, PTS, ny, width)
    face = (PTS, ny, width)
    ends = (2, PTS, PTS, width)
    spread, yface = call(
        edge_kernel,
        [(3, ny, width), (2, 5, PTS, width)],
        [metric.shape, ends, ends, pltpu.SemaphoreType.DMA((5,))],
        *in_hbm(metric, mob, load),
        spaces=[pltpu.HBM] * 3,
    )
    below, above = from_y(yface)
    still = (2 * (PTS + 1) * ny, width)
    fields, xface, factor, still_outer, still_inner = call(
        diag_kernel,
        [(2,) + field, (2, 2) + face, (2, 2, PTS, width), still, still],
        [],
        side, load, mob, spread,
    )
    rows = (2 * PTS * ny + 2 * PTS, width)
    outer, inner = to_x(*call(merge_kernel, [rows, rows], [], side, xface, factor, below, above))
    still_outer, still_inner = to_x(still_outer, still_inner)
    faces = (2,) + face
    rough, value, partial, gain, out, pair, weights, load_sums, edge_weights = call(
        inside_kernel,
        [
            (2,) + faces, field, field, field, field, (2,) + field,
            (3,) + field, (4, ny, width), (2, 3, PTS, width),
        ],
        [face],
        fields, load, mob, spread, grad, back, below, above,
    )
    rows = ((PTS + 4) * ny + PTS, width)
    sent_outer, sent_inner, yface, gface, sofar, sums, edge = call(
        faces_kernel,
        [rows, rows, (2, 1, PTS, width), faces, field, (4, ny, width), (PTS, width)],
        [((2 * PTS + 4) * ny, width), field],
        side, rough, value, out, pair, mob, spread, grad, back, below, above,
        partial, gain, weights, load_sums, edge_weights, outer, inner,
    )
    outer, inner = to_x(sent_outer, sent_inner)
    onward, top = call(
        ahead_kernel,
        [(3 * ny, 128), (3 * PTS, 128)],
        [],
        side, sent_outer, sent_inner, gface, restrict, still_outer, still_inner,
    )
    (own,) = call(
        behind_kernel,
        [(4, ny, width)],
        [],
        side, sent_outer, sent_inner, gface, back, still_outer, still_inner,
    )
    onward, top = two_on(onward, top)
    below, above = from_y(yface)
    own_rows, tops = call(
        coarse_kernel,
        [(ny, 128), (3, 128)],
        [],
        side, gface, sums, own, edge, weights, restrict, outer, inner,
    )
    (own_rows,) = call(
        beside_kernel, [(ny, 128)], [], own_rows, gain, gface, weights, restrict, below, above
    )
    pressure, token = call(
        pressure_kernel,
        [(PTS, ny * PTS, width), (1, 128)],
        [(PTS, ny * PTS, width), pltpu.SemaphoreType.DMA(())],
        side, sofar, gain, gface, outer, below, above, inner,
        out_spaces=[pltpu.HBM, pltpu.VMEM],
    )
    (onward,) = call(join_kernel, [(ny, 128)], [], own_rows, onward, top, token)
    row_below, row_above = from_y(tops)
    (coarse,) = call(last_kernel, [(ny, width // PTS + 1)], [], onward, row_below, row_above)
    return pressure.reshape(element_load.shape), coarse[None]


def solution(mesh):
    in_specs = (
        P("dom", None, "sub", None, None),
        P("dom", None, "sub", None, None),
        P(None, "dom", "sub", None),
    )
    out_specs = (P("dom", None, "sub", None, None), P("dom", "sub", None))
    return jax.shard_map(shards, mesh=mesh, in_specs=in_specs, out_specs=out_specs, check_vma=False)
```

```python
import jax
import jax.numpy as jnp
import ml_dtypes
import numpy as np
from jax import lax
from jax.experimental import pallas as pl
from jax.experimental.pallas import tpu as pltpu
from jax.sharding import PartitionSpec as P

GLL_NODES = np.array(
    [
        -1.0,
        -0.8717401485096066,
        -0.5917001814331423,
        -0.2092992179024789,
        0.2092992179024789,
        0.5917001814331423,
        0.8717401485096066,
        1.0,
    ]
)
GLL_WEIGHTS = np.array(
    [
        0.03571428571428571,
        0.2107042271435061,
        0.3411226924835044,
        0.4124587946587038,
        0.4124587946587038,
        0.3411226924835044,
        0.2107042271435061,
        0.03571428571428571,
    ]
)
THETA = 1.65
DELTA = 1.35
RHO_FIRST = DELTA / THETA
RHO_SECOND = 1.0 / (2.0 * THETA / DELTA - RHO_FIRST)
KEEP = 1.0 + RHO_SECOND * RHO_FIRST
GAIN = 2.0 * RHO_SECOND / DELTA
PTS = 8
F32 = jnp.float32


def derivative_table():
    identity = np.eye(8)
    differences = GLL_NODES[:, None] - GLL_NODES[None, :] + identity
    barycentric = 1.0 / np.prod(differences, axis=1)
    matrix = barycentric[None, :] / barycentric[:, None] / differences
    matrix = matrix * (1.0 - identity)
    row_sums = np.sum(matrix, axis=1)
    return matrix - identity * row_sums[:, None]


D = derivative_table()
W = GLL_WEIGHTS
HAT = np.stack([(1.0 - GLL_NODES) / 8.0, (1.0 + GLL_NODES) / 8.0], axis=1)
SLOPE = (-0.125, 0.125)


def tiled(matrix, width):
    column = lax.broadcasted_iota(jnp.int32, (PTS, width), 1) % PTS
    row = lax.broadcasted_iota(jnp.int32, (PTS, width), 0)
    total = jnp.zeros((PTS, width), F32)
    for c in range(PTS):
        lines = jnp.zeros((PTS, width), F32)
        for r in range(PTS):
            lines = jnp.where(row == r, float(matrix[r, c]), lines)
        total = jnp.where(column == c, lines, total)
    return total


def by_row(values, width):
    return tiled(np.tile(np.asarray(values)[:, None], (1, PTS)), width)


def cell_blocks(rows):
    width = rows.shape[1]
    cell = lax.broadcasted_iota(jnp.int32, rows.shape, 1) // PTS
    return jnp.concatenate(
        [jnp.where(cell == g, rows, 0.0) for g in range(width // PTS)], axis=0
    )


def paired_here(b):
    high, low = halves(b)
    return jnp.concatenate(
        [
            jnp.concatenate([high, low], axis=1),
            jnp.concatenate([high, jnp.zeros_like(low)], axis=1),
        ],
        axis=0,
    )


def paired(b):
    b = np.asarray(b, np.float32)
    high = b.astype(ml_dtypes.bfloat16)
    low = (b - high.astype(np.float32)).astype(ml_dtypes.bfloat16)
    return jnp.asarray(np.block([[high, low], [high, np.zeros_like(low)]]))


def column_tables(width):
    cells = np.eye(width // PTS)
    return paired(np.kron(cells, D.T)), paired(np.kron(cells, D))


def restrict_table(width):
    cells = width // PTS
    hat = np.zeros((width, 128))
    slope = np.zeros((width, 128))
    for c in range(cells):
        rows = slice(c * PTS, (c + 1) * PTS)
        hat[rows, c], hat[rows, c + 1] = HAT[:, 0], HAT[:, 1]
        slope[rows, c], slope[rows, c + 1] = SLOPE
    return paired(np.concatenate([hat, slope]))


def halves(a):
    high = a.astype(jnp.bfloat16)
    return high, (a - high.astype(F32)).astype(jnp.bfloat16)


def dot_split(a, b_pair):
    both = jnp.dot(
        jnp.concatenate(halves(a), axis=1), b_pair, preferred_element_type=F32
    )
    n = both.shape[1] // 2
    return both[:, :n] + both[:, n:]


def contract(matrix, lines, parity):
    n = len(lines)
    half = n // 2
    plus = [lines[c] + lines[n - 1 - c] for c in range(half)]
    minus = [lines[c] - lines[n - 1 - c] for c in range(half)]
    top, low = [], []
    for r in range(half):
        even = sum(float(0.5 * (matrix[r, c] + matrix[r, n - 1 - c])) * plus[c] for c in range(half))
        odd = sum(float(0.5 * (matrix[r, c] - matrix[r, n - 1 - c])) * minus[c] for c in range(half))
        top.append(even + odd)
        low.append(even - odd if parity > 0 else odd - even)
    return top + low[::-1]


def spread_metric(metric, weight_row):
    _, rows, cells = metric.shape
    width = weight_row.shape[1]
    cell = lax.broadcasted_iota(jnp.int32, (rows, width), 1) // PTS
    fill = jnp.zeros((rows, width - cells), F32)
    spread = [
        jnp.take_along_axis(jnp.concatenate([metric[d], fill], axis=1), cell, axis=1, mode="promise_in_bounds")
        for d in range(3)
    ]
    return [v * weight_row[:1] for v in spread], spread[2]


def column_masks(shape):
    lane = lax.broadcasted_iota(jnp.int32, shape, len(shape) - 1)
    up = (lane % PTS == PTS - 1) & (lane != shape[-1] - 1)
    down = (lane % PTS == 0) & (lane != 0)
    return up, down


def sum_z(v, masks):
    width = v.shape[-1]
    axis = v.ndim - 1
    up = pltpu.roll(v, width - 1, axis)
    down = pltpu.roll(v, 1, axis)
    return v + jnp.where(masks[0], up, jnp.where(masks[1], down, 0.0))


def sum_y_local(ref, ny):
    for i in range(PTS):
        low, high = ref[i, 0], ref[i, PTS - 1]
        row = lax.broadcasted_iota(jnp.int32, low.shape, 0)
        ref[i, PTS - 1] = high + jnp.where(row == ny - 1, 0.0, pltpu.roll(low, ny - 1, 0))
        ref[i, 0] = low + jnp.where(row == 0, 0.0, pltpu.roll(high, 1, 0))


def edge_planes(ref, ny):
    low = jnp.concatenate([ref[i, 0, 0:1] for i in range(PTS)], axis=0)
    high = jnp.concatenate([ref[i, PTS - 1, ny - 1 : ny] for i in range(PTS)], axis=0)
    return low, high


def plane(ref, ny):
    return lambda i, j: ref[i, pl.ds(j, ny, stride=PTS)]


def edge_kernel(metric_in, mob_in, load_in, spread_ref, yface_ref, metric_ref, mob_ref, load_ref, sems):
    ny, width = spread_ref.shape[1:]
    ends = (0, PTS - 1)
    copies = [pltpu.make_async_copy(metric_in, metric_ref, sems.at[0])]
    for n, (source, target) in enumerate(((mob_in, mob_ref), (load_in, load_ref))):
        for s, e in enumerate((0, ny - 1)):
            copies.append(
                pltpu.make_async_copy(
                    source.at[:, pl.ds(e * PTS, PTS)], target.at[s], sems.at[1 + 2 * n + s]
                )
            )
    for copy in copies:
        copy.start()
    masks = column_masks((PTS, width))
    weight_row = tiled(np.tile(W[None], (PTS, 1)), width)
    row_weight = by_row(W, width)
    squared = paired_here(cell_blocks(tiled(D * D, width)))
    squares = [by_row(D[a] ** 2, width) for a in range(PTS)]
    for copy in copies:
        copy.wait()
    spread, cell_metric = spread_metric(metric_ref[...], weight_row)
    for d in range(3):
        spread_ref[d] = spread[d]
    points = [mob_ref[s, :, ends[s]] * (float(W[ends[s]]) * row_weight) for s in range(2)]
    columns = dot_split(
        jnp.concatenate([p * weight_row for p in points], axis=0), squared
    )
    for s, e in enumerate((0, ny - 1)):
        j = ends[s]
        scale = [spread[d][e : e + 1] for d in range(3)]
        along = sum(squares[a] * points[s][a : a + 1] for a in range(PTS))
        total = along * scale[0]
        sums = [
            sum(float(D[b, j] ** power * W[b]) * mob_ref[s, :, b] for b in range(PTS))
            * row_weight
            * scale[1]
            for power in (1, 2)
        ]
        yface_ref[s, 2] = points[s] * scale[0]
        yface_ref[s, 3] = points[s] * scale[2]
        yface_ref[s, 4] = sums[0]
        column = columns[s * PTS : (s + 1) * PTS] * cell_metric[e : e + 1]
        yface_ref[s, 1] = sum_z(total + sums[1] + column, masks)
    for s in range(2):
        yface_ref[s, 0] = sum_z(load_ref[s, :, ends[s]], masks)


def diag_kernel(
    side_ref, load_ref, mob_ref, spread_ref,
    fields_ref, xface_ref, factor_ref, to_outer_ref, to_inner_ref, weights_ref, sums_ref,
):
    ny, width = fields_ref.shape[3:]
    spread = [spread_ref[d] for d in range(3)]
    square = D * D
    squared = paired_here(cell_blocks(tiled(square, width)))
    back = paired_here(cell_blocks(tiled(D, width)))
    mob, load = plane(mob_ref, ny), plane(load_ref, ny)
    diag_ref = fields_ref.at[1]
    even = side_ref[0] == 0

    def post(at, low, high):
        to_inner_ref[at : at + ny] = jnp.where(even, high, low)
        to_outer_ref[at : at + ny] = jnp.where(even, low, high)

    for d in (1, 2):
        post((2 * PTS + d - 1) * ny, spread[d], spread[d])
    for j in range(PTS):
        factor = [mob(i, j) * (float(W[i] * W[j]) * spread[0]) for i in range(PTS)]
        post(j * ny, *(sum(float(D[a, i]) * factor[a] for a in range(PTS)) for i in (0, PTS - 1)))
        post((PTS + j) * ny, *(float(W[i] * W[j]) * mob(i, j) for i in (0, PTS - 1)))
        for i, value in enumerate(contract(square.T, factor, 1)):
            diag_ref[i, j] = value
        for i, value in enumerate(contract(D.T, factor, -1)):
            weights_ref[0, i, j] = value
    for i in range(PTS):
        factor = [mob(i, j) * (float(W[i] * W[j]) * spread[1]) for j in range(PTS)]
        for j, value in enumerate(contract(square.T, factor, 1)):
            diag_ref[i, j] += value
        for j, value in enumerate(contract(D.T, factor, -1)):
            weights_ref[1, i, j] = value
    for i in range(PTS):
        factor = jnp.concatenate(
            [mob(i, j) * (float(W[i] * W[j]) * spread[2]) for j in range(PTS)], axis=0
        )
        diag_ref[i] += dot_split(factor, squared).reshape(PTS, ny, width)
        weights_ref[2, i] = dot_split(factor, back).reshape(PTS, ny, width)
        fields_ref[0, i] = jnp.stack([load(i, j) for j in range(PTS)], axis=0)
    masks = column_masks((PTS, ny, width))
    for f in range(2):
        for i in range(PTS):
            fields_ref[f, i] = sum_z(fields_ref[f, i], masks)
        sum_y_local(fields_ref.at[f], ny)
        xface_ref[f, 0] = fields_ref[f, 0]
        xface_ref[f, 1] = fields_ref[f, PTS - 1]
    row_weight = by_row(W, width)
    for s, i in enumerate((0, PTS - 1)):
        for n, e in enumerate((0, ny - 1)):
            points = mob_ref[i, e * PTS : (e + 1) * PTS] * (float(W[i]) * row_weight)
            factor_ref[s, n] = points * spread[1][e : e + 1]
    zero = jnp.zeros((ny, width), F32)
    sums = [zero] * 4
    for i in range(PTS):
        for q in range(2):
            from_load = sum(float(HAT[j, q]) * load(i, j) for j in range(PTS))
            for p in range(2):
                if HAT[i, p]:
                    sums[2 * p + q] = sums[2 * p + q] + float(HAT[i, p]) * from_load
    for n in range(4):
        sums_ref[n] = sums[n]


def merge_kernel(side_ref, xface_ref, factor_ref, below_ref, above_ref, outer_ref, inner_ref):
    below_ref, above_ref = below_ref.at[1], above_ref.at[0]
    even = side_ref[0] == 0
    fields, _, _, ny, width = xface_ref.shape
    row = lax.broadcasted_iota(jnp.int32, (ny, width), 0)
    for f in range(fields):
        for j in range(PTS):
            low, high = xface_ref[f, 0, j], xface_ref[f, 1, j]
            if j == 0:
                low = low + jnp.where(row == 0, below_ref[f, 0:1], 0.0)
                high = high + jnp.where(row == 0, below_ref[f, PTS - 1 : PTS], 0.0)
            if j == PTS - 1:
                low = low + jnp.where(row == ny - 1, above_ref[f, 0:1], 0.0)
                high = high + jnp.where(row == ny - 1, above_ref[f, PTS - 1 : PTS], 0.0)
            at = (f * PTS + j) * ny
            inner_ref[at : at + ny] = jnp.where(even, high, low)
            outer_ref[at : at + ny] = jnp.where(even, low, high)
    for n in range(2):
        at = fields * PTS * ny + n * PTS
        low, high = factor_ref[0, n], factor_ref[1, n]
        inner_ref[at : at + PTS] = jnp.where(even, high, low)
        outer_ref[at : at + PTS] = jnp.where(even, low, high)


def inside_kernel(
    fields_ref, mob_ref, spread_ref, grad_ref, back_ref, below_ref, above_ref,
    rough_ref, value_ref, partial_ref, gain_ref, out_ref, pair_ref, edge_weights_ref,
    work_ref,
):
    below_ref, above_ref = below_ref.at[1], above_ref.at[0]
    ny, width = out_ref.shape[2:]
    spread = [spread_ref[d] for d in range(3)]
    mob = plane(mob_ref, ny)
    row = lax.broadcasted_iota(jnp.int32, (ny, width), 0)
    zero = jnp.zeros((ny, width), F32)
    for i in range(PTS):
        for j in range(PTS):
            sums = [fields_ref[f, i, j] for f in range(2)]
            for f in range(2):
                if j == 0:
                    sums[f] += jnp.where(row == 0, below_ref[f, i : i + 1], 0.0)
                if j == PTS - 1:
                    sums[f] += jnp.where(row == ny - 1, above_ref[f, i : i + 1], 0.0)
            if i in (0, PTS - 1):
                for f in range(2):
                    rough_ref[f, 0 if i == 0 else 1, j] = sums[f]
                value_ref[i, j] = partial_ref[i, j] = gain_ref[i, j] = zero
            else:
                value_ref[i, j], partial_ref[i, j], gain_ref[i, j] = first_step(*sums)
    grad, back = grad_ref[...], back_ref[...]
    for j in range(PTS):
        factor = [mob(i, j) * (float(W[i] * W[j]) * spread[0]) for i in range(PTS)]
        for n, p in enumerate((0, PTS - 1)):
            coupling = contract(D.T, [float(D[a, p]) * factor[a] for a in range(PTS)], -1)
            for i in range(PTS):
                pair_ref[n, i, j] = coupling[i]
        flux = contract(D, [value_ref[i, j] for i in range(PTS)], -1)
        flux = [flux[i] * factor[i] for i in range(PTS)]
        for i, value in enumerate(contract(D.T, flux, -1)):
            out_ref[i, j] = value
    for i in range(1, PTS - 1):
        flux = contract(D, [value_ref[i, j] for j in range(PTS)], -1)
        flux = [flux[j] * (mob(i, j) * (float(W[i] * W[j]) * spread[1])) for j in range(PTS)]
        for j, value in enumerate(contract(D.T, flux, -1)):
            out_ref[i, j] += value
        work_ref[...] = dot_split(value_ref[i].reshape(PTS * ny, width), grad).reshape(PTS, ny, width)
        for j in range(PTS):
            work_ref[j] *= mob(i, j) * (float(W[i] * W[j]) * spread[2])
        out_ref[i] += dot_split(work_ref[...].reshape(PTS * ny, width), back).reshape(PTS, ny, width)
    for t, ref in enumerate((below_ref, above_ref)):
        edge_weights_ref[t, 0] = sum(by_row(D[a], width) * ref[2, a : a + 1] for a in range(PTS))
        edge_weights_ref[t, 1] = ref[4]
        edge_weights_ref[t, 2] = dot_split(ref[3], back)


def first_step(right, diagonal):
    inverse = 1.0 / diagonal
    scaled = inverse * right
    value = scaled * (1.0 / THETA)
    return value, KEEP * value + GAIN * scaled, GAIN * inverse


def faces_kernel(
    side_ref, rough_ref, value_ref, out_ref, pair_ref, mob_ref, spread_ref, grad_ref, back_ref,
    below_ref, above_ref, partial_ref, gain_ref, weights_ref, load_sums_ref, edge_weights_ref,
    outer_ref, inner_ref,
    to_outer_ref, to_inner_ref, yface_ref, gface_ref, sofar_ref, sums_ref, edge_ref, line_ref, work_ref,
):
    below_ref, above_ref = below_ref.at[1], above_ref.at[0]
    even = side_ref[0] == 0
    ny, width = out_ref.shape[2:]
    spread = [spread_ref[d] for d in range(3)]
    mob = plane(mob_ref, ny)
    ends = (0, PTS - 1)
    rows = (0, ny - 1)
    row = lax.broadcasted_iota(jnp.int32, (ny, width), 0)
    masks = column_masks((ny, width))

    def arrived(at, count):
        inner, outer = inner_ref[at : at + count], outer_ref[at : at + count]
        return jnp.where(even, outer, inner), jnp.where(even, inner, outer)

    value = [[None] * PTS, [None] * PTS]
    pface = [[None] * PTS, [None] * PTS]
    gface = [[None] * PTS, [None] * PTS]
    for j in range(PTS):
        load = arrived(j * ny, ny)
        diagonal = arrived((PTS + j) * ny, ny)
        for s in range(2):
            value[s][j], pface[s][j], gface[s][j] = first_step(
                rough_ref[0, s, j] + load[s], rough_ref[1, s, j] + diagonal[s]
            )
            gface_ref[s, j] = gface[s][j]
    lines = [value[s][j] for s in range(2) for j in range(PTS)]
    factors = [
        mob(ends[s], j) * (float(W[ends[s]] * W[j]) * spread[2]) for s in range(2) for j in range(PTS)
    ]
    for s in range(2):
        for t, ref in enumerate((below_ref, above_ref)):
            lines.append(value[s][ends[t]])
            factors.append(jnp.broadcast_to(ref[3, ends[s] : ends[s] + 1], (ny, width)))
    flux = dot_split(jnp.concatenate(lines, axis=0), grad_ref[...]) * jnp.concatenate(factors, axis=0)
    line_ref[...] = dot_split(flux, back_ref[...])
    edge_y = [[None, None], [None, None]]
    total = [[None] * PTS, [None] * PTS]
    for s in range(2):
        gradient = contract(D, value[s], -1)
        flux = [
            gradient[j] * (mob(ends[s], j) * (float(W[ends[s]] * W[j]) * spread[1])) for j in range(PTS)
        ]
        total[s] = contract(D.T, flux, -1)
        for t in range(2):
            factor = arrived(2 * PTS * ny + t * PTS, PTS)[s]
            edge_y[s][t] = sum(
                float(D[j, ends[t]]) * (gradient[j] * factor[j : j + 1]) for j in range(PTS)
            )[rows[t] : rows[t] + 1]
    for j in range(PTS):
        across = [
            out_ref[i, j] + (pair_ref[0, i, j] * value[0][j] + pair_ref[1, i, j] * value[1][j])
            for i in range(PTS)
        ]
        total[0][j] += across[0]
        total[1][j] += across[PTS - 1]
        for i in range(1, PTS - 1):
            work_ref[i, j] = across[i]
    for s in range(2):
        for j in range(PTS):
            at = (s * PTS + j) * ny
            total[s][j] += line_ref[at : at + ny]
    ymessage = []
    for t in range(2):
        j = ends[t]
        edge = [total[0][j]] + [work_ref[i, j] for i in range(1, PTS - 1)] + [total[1][j]]
        edge = [v[rows[t] : rows[t] + 1] for v in edge]
        edge[0] += edge_y[0][t]
        edge[PTS - 1] += edge_y[1][t]
        ymessage.append(sum_z(jnp.concatenate(edge, axis=0), column_masks((PTS, width))))
        yface_ref[t, 0] = ymessage[t]
    extra = [[None, None], [None, None]]
    for t, ref in enumerate((below_ref, above_ref)):
        j = ends[t]
        points = [value[0][j]] + [value_ref[i, j] for i in range(1, PTS - 1)] + [value[1][j]]
        flux = contract(D, points, -1)
        flux = contract(D.T, [flux[i] * ref[2, i : i + 1] for i in range(PTS)], -1)
        for s in range(2):
            at = (2 * PTS + 2 * s + t) * ny
            extra[s][t] = sum_z(flux[ends[s]] + line_ref[at : at + ny], masks)
            extra[s][t] = jnp.where(row == rows[t], extra[s][t], 0.0)
    for s in range(2):
        for j in range(PTS):
            total[s][j] = sum_z(total[s][j], masks)
        low, high = total[s][0], total[s][PTS - 1]
        total[s][PTS - 1] = high + jnp.where(row == ny - 1, 0.0, pltpu.roll(low, ny - 1, 0))
        total[s][0] = low + jnp.where(row == 0, 0.0, pltpu.roll(high, 1, 0))
    for j in range(PTS):
        low, high = total[0][j], total[1][j]
        if j in ends:
            t = ends.index(j)
            low, high = low + extra[0][t], high + extra[1][t]
        to_inner_ref[j * ny : (j + 1) * ny] = jnp.where(even, high, low)
        to_outer_ref[j * ny : (j + 1) * ny] = jnp.where(even, low, high)
        for s in range(2):
            sofar_ref[ends[s], j] = pface[s][j] - gface[s][j] * total[s][j]
    for i in range(1, PTS - 1):
        lines = [sum_z(work_ref[i, j], masks) for j in range(PTS)]
        low, high = lines[0], lines[PTS - 1]
        lines[PTS - 1] = high + jnp.where(row == ny - 1, 0.0, pltpu.roll(low, ny - 1, 0))
        lines[0] = low + jnp.where(row == 0, 0.0, pltpu.roll(high, 1, 0))
        for j in range(PTS):
            sofar_ref[i, j] = partial_ref[i, j] - gain_ref[i, j] * lines[j]
    sums = restricted(
        [(i, j) for i in range(PTS) for j in range(PTS)],
        lambda i, j: sofar_ref[i, j],
        lambda d, i, j: weights_ref[d, i, j],
        jnp.zeros((ny, width), F32),
    )
    for q in range(2):
        sums_ref[q] = sums[q] + load_sums_ref[q]
        sums_ref[2 + q] = sums[4 + q]
        sums[2 + q] = sums[2 + q] + load_sums_ref[2 + q]
    base = PTS * ny
    changes = []
    for t in range(2):
        j = ends[t]
        gain = [gface[0][j]] + [gain_ref[i, j] for i in range(1, PTS - 1)] + [gface[1][j]]
        gain = jnp.concatenate([g[rows[t] : rows[t] + 1] for g in gain], axis=0)
        change = -(gain * ymessage[t])
        changes += edge_change(change, edge_weights_ref.at[t], ends[1 - t], 1)
        if t == 0:
            own = edge_change(change, edge_weights_ref.at[t], ends[1 - t], 0)
            zero = jnp.zeros_like(own[1])
            edge_ref[...] = jnp.concatenate([zero, own[1], zero, own[3]] + [zero] * 4, axis=0)
    changes = jnp.concatenate(changes, axis=0)
    for ref in (to_outer_ref, to_inner_ref):
        for n, k in enumerate((2, 3, 6, 7)):
            ref[base + n * ny : base + (n + 1) * ny] = sums[k]
        ref[base + 4 * ny : base + 4 * ny + PTS] = changes


def edge_change(change, weight_ref, j, p):
    upper = lax.broadcasted_iota(jnp.int32, change.shape, 0)
    hat = jnp.zeros_like(change)
    for i in range(PTS):
        hat = jnp.where(upper == i, float(HAT[i, p]), hat)
    along_x, along_y, along_z = (
        jnp.sum(v, axis=0, keepdims=True)
        for v in (weight_ref[0] * change, hat * weight_ref[1] * change, hat * weight_ref[2] * change)
    )
    smooth = [-(SLOPE[p] * float(HAT[j, q]) * along_x + SLOPE[q] * along_y) for q in range(2)]
    return smooth + [-float(HAT[j, q]) * along_z for q in range(2)]


def restricted(points, value, weight, zero):
    sums = [zero] * 8
    along_x = {}
    along_y = {}
    along_z = {}
    for i, j in points:
        v = value(i, j)
        along_x[j] = along_x.get(j, 0.0) + weight(0, i, j) * v
        along_y[i] = along_y.get(i, 0.0) + weight(1, i, j) * v
        product = weight(2, i, j) * v
        for q in range(2):
            if HAT[j, q]:
                along_z[i, q] = along_z.get((i, q), 0.0) + float(HAT[j, q]) * product
    x_sums = [
        sum(float(HAT[j, q]) * total for j, total in along_x.items() if HAT[j, q]) for q in range(2)
    ]
    y_sums = [
        sum(float(HAT[i, p]) * total for i, total in along_y.items() if HAT[i, p]) for p in range(2)
    ]
    for p in range(2):
        for q in range(2):
            sums[2 * p + q] = -(SLOPE[p] * x_sums[q] + SLOPE[q] * y_sums[p])
            sums[4 + 2 * p + q] = -sum(
                float(HAT[i, p]) * total for (i, r), total in along_z.items() if r == q and HAT[i, p]
            )
    return sums


def x_corrections(even, gface_ref, outer_ref, inner_ref):
    ny = gface_ref.shape[2]
    change = {}
    for j in range(PTS):
        low = pick(even, outer_ref, inner_ref, j * ny, ny)
        high = pick(even, inner_ref, outer_ref, j * ny, ny)
        change[0, j] = -(gface_ref[0, j] * low)
        change[PTS - 1, j] = -(gface_ref[1, j] * high)
    return change


def y_corrections(gain_ref, gface_ref, below_ref, above_ref):
    ny, width = gain_ref.shape[2:]
    row = lax.broadcasted_iota(jnp.int32, (ny, width), 0)
    faces = {0: 0, PTS - 1: 1}
    change = {}
    for i in range(PTS):
        for j, at, ref in ((0, 0, below_ref), (PTS - 1, ny - 1, above_ref)):
            gain = gface_ref[faces[i], j] if i in faces else gain_ref[i, j]
            change[i, j] = -(gain * jnp.where(row == at, ref[0, i : i + 1], 0.0))
    return change


def face_change(change, weight, i, p, q):
    along_x = sum(float(HAT[j, q]) * (weight[0][j] * change[j]) for j in range(PTS) if HAT[j, q])
    smooth = SLOPE[p] * along_x
    slope = 0.0
    if HAT[i, p]:
        along_y = sum(weight[1][j] * change[j] for j in range(PTS))
        smooth = smooth + float(HAT[i, p]) * SLOPE[q] * along_y
        along_z = sum(float(HAT[j, q]) * (weight[2][j] * change[j]) for j in range(PTS) if HAT[j, q])
        slope = float(HAT[i, p]) * along_z
    return -smooth, -slope


def to_vertices(smooth, slope, restrict):
    return dot_split(jnp.concatenate([smooth, slope], axis=1), restrict)


def pick(even, first, second, at, count):
    return jnp.where(even, first[at : at + count], second[at : at + count])


def ahead_kernel(
    side_ref, sent_outer_ref, sent_inner_ref, gface_ref, restrict_ref, outer_ref, inner_ref,
    next_ref, top_ref,
):
    ny, width = gface_ref.shape[2:]
    even = side_ref[0] == 0
    change = [
        -(gface_ref[1, j] * pick(even, sent_inner_ref, sent_outer_ref, j * ny, ny)) for j in range(PTS)
    ]
    weight = [[pick(even, inner_ref, outer_ref, j * ny, ny) for j in range(PTS)]]
    smooth = jnp.concatenate([face_change(change, weight, 0, 1, q)[0] for q in range(2)], axis=0)
    hats = jnp.concatenate([restrict_ref[:width], restrict_ref[2 * width : 3 * width]], axis=0)
    corners = dot_split(smooth, hats)
    lower, upper = corners[:ny], corners[ny:]
    row = lax.broadcasted_iota(jnp.int32, lower.shape, 0)
    rows = lower + jnp.where(row == 0, 0.0, pltpu.roll(upper, 1, 0))
    next_ref[...] = jnp.concatenate([rows] * (next_ref.shape[0] // ny), axis=0)
    top_ref[...] = jnp.broadcast_to(upper[ny - 1 : ny], top_ref.shape)


def behind_kernel(
    side_ref, sent_outer_ref, sent_inner_ref, gface_ref, back_ref, outer_ref, inner_ref,
    own_ref,
):
    ny, width = gface_ref.shape[2:]
    even = side_ref[0] == 0

    def rows(at):
        return pick(even, outer_ref, inner_ref, at, ny)

    change = [
        -(gface_ref[0, j] * pick(even, sent_outer_ref, sent_inner_ref, j * ny, ny)) for j in range(PTS)
    ]
    spread = [rows((2 * PTS + d) * ny) for d in range(2)]
    points = [rows((PTS + j) * ny) for j in range(PTS)]
    column = dot_split(jnp.concatenate([p * spread[1] for p in points], axis=0), back_ref[...])
    weight = [
        [rows(j * ny) for j in range(PTS)],
        contract(D.T, [p * spread[0] for p in points], -1),
        [column[j * ny : (j + 1) * ny] for j in range(PTS)],
    ]
    for q in range(2):
        own_ref[q], own_ref[2 + q] = face_change(change, weight, PTS - 1, 1, q)


def coarse_kernel(
    side_ref, gface_ref, sums_ref, own_ref, edge_in_ref, weights_ref, restrict_ref, outer_ref, inner_ref,
    plane_ref, edge_ref,
):
    ny, width = gface_ref.shape[2:]
    even = side_ref[0] == 0
    change = x_corrections(even, gface_ref, outer_ref, inner_ref)
    sums = restricted(
        list(change),
        lambda i, j: change[i, j],
        lambda d, i, j: weights_ref[d, i, j],
        jnp.zeros((ny, width), F32),
    )
    base = PTS * ny

    def before(at, count):
        return pick(even, outer_ref, inner_ref, at, count)

    total = [
        sums[(0, 1, 4, 5)[n]] + sums_ref[n] + own_ref[n] + before(base + n * ny, ny) for n in range(4)
    ]
    extra = before(base + 4 * ny, PTS) + edge_in_ref[...]
    smooth = jnp.concatenate(total[:2] + [extra], axis=0)
    slope = jnp.concatenate(total[2:] + [pltpu.roll(extra, PTS - 2, 0)], axis=0)
    corners = to_vertices(smooth, slope, restrict_ref[...])
    lower, upper = corners[:ny], corners[ny : 2 * ny]
    extra = corners[2 * ny :]
    row = lax.broadcasted_iota(jnp.int32, lower.shape, 0)
    plane_ref[...] = lower + jnp.where(row == 0, extra[1:2], pltpu.roll(upper, 1, 0))
    edge_ref[0:1] = upper[ny - 1 : ny] + extra[4:5]
    edge_ref[1:2] = extra[5:6]
    edge_ref[2:3] = extra[0:1]


def beside_kernel(
    own_ref, gain_ref, gface_ref, weights_ref, restrict_ref, below_ref, above_ref,
    plane_ref,
):
    below_ref, above_ref = below_ref.at[1], above_ref.at[0]
    ny, width = gain_ref.shape[2:]
    change = y_corrections(gain_ref, gface_ref, below_ref, above_ref)
    sums = restricted(
        list(change),
        lambda i, j: change[i, j],
        lambda d, i, j: weights_ref[d, i, j],
        jnp.zeros((ny, width), F32),
    )
    smooth = jnp.concatenate([sums[0], sums[1]], axis=0)
    slope = jnp.concatenate([sums[4], sums[5]], axis=0)
    corners = to_vertices(smooth, slope, restrict_ref[...])
    lower, upper = corners[:ny], corners[ny:]
    row = lax.broadcasted_iota(jnp.int32, lower.shape, 0)
    plane_ref[...] = own_ref[...] + lower + jnp.where(row == 0, 0.0, pltpu.roll(upper, 1, 0))


def pressure_kernel(
    side_ref, sofar_ref, gain_ref, gface_ref, outer_ref, below_ref, above_ref, inner_ref,
    pressure_out, token_ref, pressure_ref, sem,
):
    token_ref[...] = jnp.zeros_like(token_ref)
    below_ref, above_ref = below_ref.at[1], above_ref.at[0]
    ny = sofar_ref.shape[2]
    even = side_ref[0] == 0
    changes = (
        x_corrections(even, gface_ref, outer_ref, inner_ref),
        y_corrections(gain_ref, gface_ref, below_ref, above_ref),
    )
    for i in range(PTS):
        for j in range(PTS):
            value = sofar_ref[i, j]
            for change in changes:
                if (i, j) in change:
                    value = value + change[i, j]
            pressure_ref[i, pl.ds(j, ny, stride=PTS)] = value
    copy = pltpu.make_async_copy(pressure_ref, pressure_out, sem)
    copy.start()
    copy.wait()


def join_kernel(own_ref, next_ref, top_ref, token_ref, joined_ref):
    row = lax.broadcasted_iota(jnp.int32, joined_ref.shape, 0)
    total = own_ref[...] + next_ref[: row.shape[0]] + token_ref[...]
    joined_ref[...] = total + jnp.where(row == 0, top_ref[0:1], 0.0)


def last_kernel(joined_ref, below_ref, above_ref, coarse_ref):
    total = joined_ref[...]
    ny = total.shape[0]
    row = lax.broadcasted_iota(jnp.int32, total.shape, 0)
    total = total + jnp.where(row == 0, below_ref[0:1], jnp.where(row == 1, below_ref[1:2], 0.0))
    total = total + jnp.where(row == ny - 1, above_ref[2:3], 0.0)
    coarse_ref[...] = total[:, : coarse_ref.shape[1]]


def call(body, outs, scratch, *args, spaces=None, out_spaces=None):
    spaces = spaces or [pltpu.SMEM if a.dtype == jnp.int32 else pltpu.VMEM for a in args]
    return pl.pallas_call(
        body,
        out_shape=[jax.ShapeDtypeStruct(s, F32) if isinstance(s, tuple) else s for s in outs],
        in_specs=[pl.BlockSpec(memory_space=m) for m in spaces],
        out_specs=[pl.BlockSpec(memory_space=m) for m in out_spaces or [pltpu.VMEM] * len(outs)],
        scratch_shapes=[pltpu.VMEM(s, F32) if isinstance(s, tuple) else s for s in scratch],
        compiler_params=pltpu.CompilerParams(vmem_limit_bytes=16 * 1024 * 1024),
    )(*args)


def from_y(faces):
    size = lax.axis_size("sub")
    up = lax.ppermute(faces, "sub", [(i, (i + 1) % size) for i in range(size)])
    if size == 2:
        return up, up
    return up, lax.ppermute(faces, "sub", [(i, (i - 1) % size) for i in range(size)])


def inner_pairs(size):
    return [(i, i ^ 1) for i in range(size)]


def outer_pairs(size):
    return [(i, (i + 1) % size if i % 2 else (i - 1) % size) for i in range(size)]


def to_x(outer, inner):
    size = lax.axis_size("dom")
    outer = lax.ppermute(outer, "dom", outer_pairs(size))
    inner = lax.ppermute(inner, "dom", inner_pairs(size))
    return outer, inner


def two_on(rows, top):
    size, rest = lax.axis_size("dom"), lax.axis_size("sub")
    rows = lax.ppermute(rows, "dom", [(i, (i + 2) % size) for i in range(size)])
    pairs = [
        (i * rest + k, (i + 2) % size * rest + (k + 1) % rest) for i in range(size) for k in range(rest)
    ]
    return rows, lax.ppermute(top, ("dom", "sub"), pairs)


def shards(element_load, mobility, metric):
    _, _, ny, _, width = element_load.shape
    load = element_load.reshape(PTS, ny * PTS, width)
    mob = mobility.reshape(PTS, ny * PTS, width)
    metric = metric[:, 0]
    side = (lax.axis_index("dom") % 2).astype(jnp.int32).reshape(1)
    def in_hbm(*arrays):
        return [pltpu.with_memory_space_constraint(a, pltpu.HBM) for a in arrays]

    grad, back = column_tables(width)
    restrict = restrict_table(width)
    field = (PTS, PTS, ny, width)
    face = (PTS, ny, width)
    ends = (2, PTS, PTS, width)
    spread, yface = call(
        edge_kernel,
        [(3, ny, width), (2, 5, PTS, width)],
        [metric.shape, ends, ends, pltpu.SemaphoreType.DMA((5,))],
        *in_hbm(metric, mob, load),
        spaces=[pltpu.HBM] * 3,
    )
    below, above = from_y(yface)
    still = (2 * (PTS + 1) * ny, width)
    fields, xface, factor, still_outer, still_inner, weights, load_sums = call(
        diag_kernel,
        [
            (2,) + field, (2, 2) + face, (2, 2, PTS, width), still, still,
            (3,) + field, (4, ny, width),
        ],
        [],
        side, load, mob, spread,
    )
    rows = (2 * PTS * ny + 2 * PTS, width)
    outer, inner = to_x(*call(merge_kernel, [rows, rows], [], side, xface, factor, below, above))
    still_outer, still_inner = to_x(still_outer, still_inner)
    faces = (2,) + face
    rough, value, partial, gain, out, pair, edge_weights = call(
        inside_kernel,
        [
            (2,) + faces, field, field, field, field, (2,) + field,
            (2, 3, PTS, width),
        ],
        [face],
        fields, mob, spread, grad, back, below, above,
    )
    rows = ((PTS + 4) * ny + PTS, width)
    sent_outer, sent_inner, yface, gface, sofar, sums, edge = call(
        faces_kernel,
        [rows, rows, (2, 1, PTS, width), faces, field, (4, ny, width), (PTS, width)],
        [((2 * PTS + 4) * ny, width), field],
        side, rough, value, out, pair, mob, spread, grad, back, below, above,
        partial, gain, weights, load_sums, edge_weights, outer, inner,
    )
    outer, inner = to_x(sent_outer, sent_inner)
    onward, top = call(
        ahead_kernel,
        [(3 * ny, 128), (3 * PTS, 128)],
        [],
        side, sent_outer, sent_inner, gface, restrict, still_outer, still_inner,
    )
    (own,) = call(
        behind_kernel,
        [(4, ny, width)],
        [],
        side, sent_outer, sent_inner, gface, back, still_outer, still_inner,
    )
    onward, top = two_on(onward, top)
    below, above = from_y(yface)
    own_rows, tops = call(
        coarse_kernel,
        [(ny, 128), (3, 128)],
        [],
        side, gface, sums, own, edge, weights, restrict, outer, inner,
    )
    (own_rows,) = call(
        beside_kernel, [(ny, 128)], [], own_rows, gain, gface, weights, restrict, below, above
    )
    pressure, token = call(
        pressure_kernel,
        [(PTS, ny * PTS, width), (1, 128)],
        [(PTS, ny * PTS, width), pltpu.SemaphoreType.DMA(())],
        side, sofar, gain, gface, outer, below, above, inner,
        out_spaces=[pltpu.HBM, pltpu.VMEM],
    )
    (onward,) = call(join_kernel, [(ny, 128)], [], own_rows, onward, top, token)
    row_below, row_above = from_y(tops)
    (coarse,) = call(last_kernel, [(ny, width // PTS + 1)], [], onward, row_below, row_above)
    return pressure.reshape(element_load.shape), coarse[None]


def solution(mesh):
    in_specs = (
        P("dom", None, "sub", None, None),
        P("dom", None, "sub", None, None),
        P(None, "dom", "sub", None),
    )
    out_specs = (P("dom", None, "sub", None, None), P("dom", "sub", None))
    return jax.shard_map(shards, mesh=mesh, in_specs=in_specs, out_specs=out_specs, check_vma=False)
```

```python
import jax
import jax.numpy as jnp
import ml_dtypes
import numpy as np
from jax import lax
from jax.experimental import pallas as pl
from jax.experimental.pallas import tpu as pltpu
from jax.sharding import PartitionSpec as P

GLL_NODES = np.array(
    [
        -1.0,
        -0.8717401485096066,
        -0.5917001814331423,
        -0.2092992179024789,
        0.2092992179024789,
        0.5917001814331423,
        0.8717401485096066,
        1.0,
    ]
)
GLL_WEIGHTS = np.array(
    [
        0.03571428571428571,
        0.2107042271435061,
        0.3411226924835044,
        0.4124587946587038,
        0.4124587946587038,
        0.3411226924835044,
        0.2107042271435061,
        0.03571428571428571,
    ]
)
THETA = 1.65
DELTA = 1.35
RHO_FIRST = DELTA / THETA
RHO_SECOND = 1.0 / (2.0 * THETA / DELTA - RHO_FIRST)
KEEP = 1.0 + RHO_SECOND * RHO_FIRST
GAIN = 2.0 * RHO_SECOND / DELTA
PTS = 8
F32 = jnp.float32


def derivative_table():
    identity = np.eye(8)
    differences = GLL_NODES[:, None] - GLL_NODES[None, :] + identity
    barycentric = 1.0 / np.prod(differences, axis=1)
    matrix = barycentric[None, :] / barycentric[:, None] / differences
    matrix = matrix * (1.0 - identity)
    row_sums = np.sum(matrix, axis=1)
    return matrix - identity * row_sums[:, None]


D = derivative_table()
W = GLL_WEIGHTS
HAT = np.stack([(1.0 - GLL_NODES) / 8.0, (1.0 + GLL_NODES) / 8.0], axis=1)
SLOPE = (-0.125, 0.125)


def tiled(matrix, width):
    column = lax.broadcasted_iota(jnp.int32, (PTS, width), 1) % PTS
    row = lax.broadcasted_iota(jnp.int32, (PTS, width), 0)
    total = jnp.zeros((PTS, width), F32)
    for c in range(PTS):
        lines = jnp.zeros((PTS, width), F32)
        for r in range(PTS):
            lines = jnp.where(row == r, float(matrix[r, c]), lines)
        total = jnp.where(column == c, lines, total)
    return total


def by_row(values, width):
    return tiled(np.tile(np.asarray(values)[:, None], (1, PTS)), width)


def cell_blocks(rows):
    width = rows.shape[1]
    cell = lax.broadcasted_iota(jnp.int32, rows.shape, 1) // PTS
    return jnp.concatenate(
        [jnp.where(cell == g, rows, 0.0) for g in range(width // PTS)], axis=0
    )


def paired_here(b):
    high, low = halves(b)
    return jnp.concatenate(
        [
            jnp.concatenate([high, low], axis=1),
            jnp.concatenate([high, jnp.zeros_like(low)], axis=1),
        ],
        axis=0,
    )


def paired(b):
    b = np.asarray(b, np.float32)
    high = b.astype(ml_dtypes.bfloat16)
    low = (b - high.astype(np.float32)).astype(ml_dtypes.bfloat16)
    return jnp.asarray(np.block([[high, low], [high, np.zeros_like(low)]]))


def column_tables(width):
    cells = np.eye(width // PTS)
    return paired(np.kron(cells, D.T)), paired(np.kron(cells, D))


def restrict_table(width):
    cells = width // PTS
    hat = np.zeros((width, 128))
    slope = np.zeros((width, 128))
    for c in range(cells):
        rows = slice(c * PTS, (c + 1) * PTS)
        hat[rows, c], hat[rows, c + 1] = HAT[:, 0], HAT[:, 1]
        slope[rows, c], slope[rows, c + 1] = SLOPE
    return paired(np.concatenate([hat, slope]))


def halves(a):
    high = a.astype(jnp.bfloat16)
    return high, (a - high.astype(F32)).astype(jnp.bfloat16)


def dot_split(a, b_pair):
    both = jnp.dot(
        jnp.concatenate(halves(a), axis=1), b_pair, preferred_element_type=F32
    )
    n = both.shape[1] // 2
    return both[:, :n] + both[:, n:]


def contract(matrix, lines, parity):
    n = len(lines)
    half = n // 2
    plus = [lines[c] + lines[n - 1 - c] for c in range(half)]
    minus = [lines[c] - lines[n - 1 - c] for c in range(half)]
    top, low = [], []
    for r in range(half):
        even = sum(float(0.5 * (matrix[r, c] + matrix[r, n - 1 - c])) * plus[c] for c in range(half))
        odd = sum(float(0.5 * (matrix[r, c] - matrix[r, n - 1 - c])) * minus[c] for c in range(half))
        top.append(even + odd)
        low.append(even - odd if parity > 0 else odd - even)
    return top + low[::-1]


def spread_metric(metric, weight_row):
    _, rows, cells = metric.shape
    width = weight_row.shape[1]
    cell = lax.broadcasted_iota(jnp.int32, (rows, width), 1) // PTS
    fill = jnp.zeros((rows, width - cells), F32)
    spread = [
        jnp.take_along_axis(jnp.concatenate([metric[d], fill], axis=1), cell, axis=1, mode="promise_in_bounds")
        for d in range(3)
    ]
    return [v * weight_row[:1] for v in spread], spread[2]


def column_masks(shape):
    lane = lax.broadcasted_iota(jnp.int32, shape, len(shape) - 1)
    up = (lane % PTS == PTS - 1) & (lane != shape[-1] - 1)
    down = (lane % PTS == 0) & (lane != 0)
    return up, down


def sum_z(v, masks):
    width = v.shape[-1]
    axis = v.ndim - 1
    up = pltpu.roll(v, width - 1, axis)
    down = pltpu.roll(v, 1, axis)
    return v + jnp.where(masks[0], up, jnp.where(masks[1], down, 0.0))


def sum_y_local(ref, ny):
    for i in range(PTS):
        low, high = ref[i, 0], ref[i, PTS - 1]
        row = lax.broadcasted_iota(jnp.int32, low.shape, 0)
        ref[i, PTS - 1] = high + jnp.where(row == ny - 1, 0.0, pltpu.roll(low, ny - 1, 0))
        ref[i, 0] = low + jnp.where(row == 0, 0.0, pltpu.roll(high, 1, 0))


def edge_planes(ref, ny):
    low = jnp.concatenate([ref[i, 0, 0:1] for i in range(PTS)], axis=0)
    high = jnp.concatenate([ref[i, PTS - 1, ny - 1 : ny] for i in range(PTS)], axis=0)
    return low, high


def plane(ref, ny):
    return lambda i, j: ref[i, pl.ds(j, ny, stride=PTS)]


def edge_kernel(metric_in, mob_in, load_in, spread_ref, yface_ref, metric_ref, mob_ref, load_ref, sems):
    ny, width = spread_ref.shape[1:]
    ends = (0, PTS - 1)
    copies = [pltpu.make_async_copy(metric_in, metric_ref, sems.at[0])]
    for n, (source, target) in enumerate(((mob_in, mob_ref), (load_in, load_ref))):
        for s, e in enumerate((0, ny - 1)):
            copies.append(
                pltpu.make_async_copy(
                    source.at[:, pl.ds(e * PTS, PTS)], target.at[s], sems.at[1 + 2 * n + s]
                )
            )
    for copy in copies:
        copy.start()
    masks = column_masks((PTS, width))
    weight_row = tiled(np.tile(W[None], (PTS, 1)), width)
    row_weight = by_row(W, width)
    squared = paired_here(cell_blocks(tiled(D * D, width)))
    squares = [by_row(D[a] ** 2, width) for a in range(PTS)]
    for copy in copies:
        copy.wait()
    spread, cell_metric = spread_metric(metric_ref[...], weight_row)
    for d in range(3):
        spread_ref[d] = spread[d]
    points = [mob_ref[s, :, ends[s]] * (float(W[ends[s]]) * row_weight) for s in range(2)]
    columns = dot_split(
        jnp.concatenate([p * weight_row for p in points], axis=0), squared
    )
    for s, e in enumerate((0, ny - 1)):
        j = ends[s]
        scale = [spread[d][e : e + 1] for d in range(3)]
        along = sum(squares[a] * points[s][a : a + 1] for a in range(PTS))
        total = along * scale[0]
        sums = [
            sum(float(D[b, j] ** power * W[b]) * mob_ref[s, :, b] for b in range(PTS))
            * row_weight
            * scale[1]
            for power in (1, 2)
        ]
        yface_ref[s, 2] = points[s] * scale[0]
        yface_ref[s, 3] = points[s] * scale[2]
        yface_ref[s, 4] = sums[0]
        column = columns[s * PTS : (s + 1) * PTS] * cell_metric[e : e + 1]
        yface_ref[s, 1] = sum_z(total + sums[1] + column, masks)
    for s in range(2):
        yface_ref[s, 0] = sum_z(load_ref[s, :, ends[s]], masks)


def diag_kernel(
    side_ref, load_ref, mob_ref, spread_ref,
    fields_ref, xface_ref, factor_ref, to_outer_ref, to_inner_ref, weights_ref, sums_ref,
):
    ny, width = fields_ref.shape[3:]
    spread = [spread_ref[d] for d in range(3)]
    square = D * D
    squared = paired_here(cell_blocks(tiled(square, width)))
    back = paired_here(cell_blocks(tiled(D, width)))
    mob, load = plane(mob_ref, ny), plane(load_ref, ny)
    diag_ref = fields_ref.at[1]
    even = side_ref[0] == 0

    def post(at, low, high):
        to_inner_ref[at : at + ny] = jnp.where(even, high, low)
        to_outer_ref[at : at + ny] = jnp.where(even, low, high)

    for d in (1, 2):
        post((2 * PTS + d - 1) * ny, spread[d], spread[d])
    for j in range(PTS):
        factor = [mob(i, j) * (float(W[i] * W[j]) * spread[0]) for i in range(PTS)]
        post(j * ny, *(sum(float(D[a, i]) * factor[a] for a in range(PTS)) for i in (0, PTS - 1)))
        post((PTS + j) * ny, *(float(W[i] * W[j]) * mob(i, j) for i in (0, PTS - 1)))
        for i, value in enumerate(contract(square.T, factor, 1)):
            diag_ref[i, j] = value
        for i, value in enumerate(contract(D.T, factor, -1)):
            weights_ref[0, i, j] = value
    for i in range(PTS):
        factor = [mob(i, j) * (float(W[i] * W[j]) * spread[1]) for j in range(PTS)]
        for j, value in enumerate(contract(square.T, factor, 1)):
            diag_ref[i, j] += value
        for j, value in enumerate(contract(D.T, factor, -1)):
            weights_ref[1, i, j] = value
    for i in range(PTS):
        factor = jnp.concatenate(
            [mob(i, j) * (float(W[i] * W[j]) * spread[2]) for j in range(PTS)], axis=0
        )
        diag_ref[i] += dot_split(factor, squared).reshape(PTS, ny, width)
        weights_ref[2, i] = dot_split(factor, back).reshape(PTS, ny, width)
        fields_ref[0, i] = jnp.stack([load(i, j) for j in range(PTS)], axis=0)
    masks = column_masks((PTS, ny, width))
    for f in range(2):
        for i in range(PTS):
            fields_ref[f, i] = sum_z(fields_ref[f, i], masks)
        sum_y_local(fields_ref.at[f], ny)
        xface_ref[f, 0] = fields_ref[f, 0]
        xface_ref[f, 1] = fields_ref[f, PTS - 1]
    row_weight = by_row(W, width)
    for s, i in enumerate((0, PTS - 1)):
        for n, e in enumerate((0, ny - 1)):
            points = mob_ref[i, e * PTS : (e + 1) * PTS] * (float(W[i]) * row_weight)
            factor_ref[s, n] = points * spread[1][e : e + 1]
    zero = jnp.zeros((ny, width), F32)
    sums = [zero] * 4
    for i in range(PTS):
        for q in range(2):
            from_load = sum(float(HAT[j, q]) * load(i, j) for j in range(PTS))
            for p in range(2):
                if HAT[i, p]:
                    sums[2 * p + q] = sums[2 * p + q] + float(HAT[i, p]) * from_load
    for n in range(4):
        sums_ref[n] = sums[n]


def merge_kernel(side_ref, xface_ref, factor_ref, below_ref, above_ref, outer_ref, inner_ref):
    below_ref, above_ref = below_ref.at[1], above_ref.at[0]
    even = side_ref[0] == 0
    fields, _, _, ny, width = xface_ref.shape
    row = lax.broadcasted_iota(jnp.int32, (ny, width), 0)
    for f in range(fields):
        for j in range(PTS):
            low, high = xface_ref[f, 0, j], xface_ref[f, 1, j]
            if j == 0:
                low = low + jnp.where(row == 0, below_ref[f, 0:1], 0.0)
                high = high + jnp.where(row == 0, below_ref[f, PTS - 1 : PTS], 0.0)
            if j == PTS - 1:
                low = low + jnp.where(row == ny - 1, above_ref[f, 0:1], 0.0)
                high = high + jnp.where(row == ny - 1, above_ref[f, PTS - 1 : PTS], 0.0)
            at = (f * PTS + j) * ny
            inner_ref[at : at + ny] = jnp.where(even, high, low)
            outer_ref[at : at + ny] = jnp.where(even, low, high)
    for n in range(2):
        at = fields * PTS * ny + n * PTS
        low, high = factor_ref[0, n], factor_ref[1, n]
        inner_ref[at : at + PTS] = jnp.where(even, high, low)
        outer_ref[at : at + PTS] = jnp.where(even, low, high)


def inside_kernel(
    fields_ref, mob_ref, spread_ref, grad_ref, back_ref, below_ref, above_ref,
    rough_ref, value_ref, partial_ref, gain_ref, out_ref, pair_ref, edge_weights_ref,
    work_ref,
):
    below_ref, above_ref = below_ref.at[1], above_ref.at[0]
    ny, width = out_ref.shape[2:]
    spread = [spread_ref[d] for d in range(3)]
    mob = plane(mob_ref, ny)
    row = lax.broadcasted_iota(jnp.int32, (ny, width), 0)
    zero = jnp.zeros((ny, width), F32)
    for i in range(PTS):
        for j in range(PTS):
            sums = [fields_ref[f, i, j] for f in range(2)]
            for f in range(2):
                if j == 0:
                    sums[f] += jnp.where(row == 0, below_ref[f, i : i + 1], 0.0)
                if j == PTS - 1:
                    sums[f] += jnp.where(row == ny - 1, above_ref[f, i : i + 1], 0.0)
            if i in (0, PTS - 1):
                for f in range(2):
                    rough_ref[f, 0 if i == 0 else 1, j] = sums[f]
                value_ref[i, j] = partial_ref[i, j] = gain_ref[i, j] = zero
            else:
                value_ref[i, j], partial_ref[i, j], gain_ref[i, j] = first_step(*sums)
    grad, back = grad_ref[...], back_ref[...]
    for j in range(PTS):
        factor = [mob(i, j) * (float(W[i] * W[j]) * spread[0]) for i in range(PTS)]
        for n, p in enumerate((0, PTS - 1)):
            coupling = contract(D.T, [float(D[a, p]) * factor[a] for a in range(PTS)], -1)
            for i in range(PTS):
                pair_ref[n, i, j] = coupling[i]
        flux = contract(D, [value_ref[i, j] for i in range(PTS)], -1)
        flux = [flux[i] * factor[i] for i in range(PTS)]
        for i, value in enumerate(contract(D.T, flux, -1)):
            out_ref[i, j] = value
    for i in range(1, PTS - 1):
        flux = contract(D, [value_ref[i, j] for j in range(PTS)], -1)
        flux = [flux[j] * (mob(i, j) * (float(W[i] * W[j]) * spread[1])) for j in range(PTS)]
        for j, value in enumerate(contract(D.T, flux, -1)):
            out_ref[i, j] += value
        work_ref[...] = dot_split(value_ref[i].reshape(PTS * ny, width), grad).reshape(PTS, ny, width)
        for j in range(PTS):
            work_ref[j] *= mob(i, j) * (float(W[i] * W[j]) * spread[2])
        out_ref[i] += dot_split(work_ref[...].reshape(PTS * ny, width), back).reshape(PTS, ny, width)
    for t, ref in enumerate((below_ref, above_ref)):
        edge_weights_ref[t, 0] = sum(by_row(D[a], width) * ref[2, a : a + 1] for a in range(PTS))
        edge_weights_ref[t, 1] = ref[4]
        edge_weights_ref[t, 2] = dot_split(ref[3], back)


def first_step(right, diagonal):
    inverse = 1.0 / diagonal
    scaled = inverse * right
    value = scaled * (1.0 / THETA)
    return value, KEEP * value + GAIN * scaled, GAIN * inverse


def faces_kernel(
    side_ref, rough_ref, value_ref, out_ref, pair_ref, mob_ref, spread_ref, grad_ref, back_ref,
    below_ref, above_ref, partial_ref, gain_ref, weights_ref, load_sums_ref, edge_weights_ref,
    outer_ref, inner_ref,
    to_outer_ref, to_inner_ref, yface_ref, gface_ref, sofar_ref, edge_ref, line_ref, work_ref,
):
    below_ref, above_ref = below_ref.at[1], above_ref.at[0]
    even = side_ref[0] == 0
    ny, width = out_ref.shape[2:]
    spread = [spread_ref[d] for d in range(3)]
    mob = plane(mob_ref, ny)
    ends = (0, PTS - 1)
    rows = (0, ny - 1)
    row = lax.broadcasted_iota(jnp.int32, (ny, width), 0)
    masks = column_masks((ny, width))

    def arrived(at, count):
        inner, outer = inner_ref[at : at + count], outer_ref[at : at + count]
        return jnp.where(even, outer, inner), jnp.where(even, inner, outer)

    value = [[None] * PTS, [None] * PTS]
    pface = [[None] * PTS, [None] * PTS]
    gface = [[None] * PTS, [None] * PTS]
    for j in range(PTS):
        load = arrived(j * ny, ny)
        diagonal = arrived((PTS + j) * ny, ny)
        for s in range(2):
            value[s][j], pface[s][j], gface[s][j] = first_step(
                rough_ref[0, s, j] + load[s], rough_ref[1, s, j] + diagonal[s]
            )
            gface_ref[s, j] = gface[s][j]
    lines = [value[s][j] for s in range(2) for j in range(PTS)]
    factors = [
        mob(ends[s], j) * (float(W[ends[s]] * W[j]) * spread[2]) for s in range(2) for j in range(PTS)
    ]
    for s in range(2):
        for t, ref in enumerate((below_ref, above_ref)):
            lines.append(value[s][ends[t]])
            factors.append(jnp.broadcast_to(ref[3, ends[s] : ends[s] + 1], (ny, width)))
    flux = dot_split(jnp.concatenate(lines, axis=0), grad_ref[...]) * jnp.concatenate(factors, axis=0)
    line_ref[...] = dot_split(flux, back_ref[...])
    edge_y = [[None, None], [None, None]]
    total = [[None] * PTS, [None] * PTS]
    for s in range(2):
        gradient = contract(D, value[s], -1)
        flux = [
            gradient[j] * (mob(ends[s], j) * (float(W[ends[s]] * W[j]) * spread[1])) for j in range(PTS)
        ]
        total[s] = contract(D.T, flux, -1)
        for t in range(2):
            factor = arrived(2 * PTS * ny + t * PTS, PTS)[s]
            edge_y[s][t] = sum(
                float(D[j, ends[t]]) * (gradient[j] * factor[j : j + 1]) for j in range(PTS)
            )[rows[t] : rows[t] + 1]
    for j in range(PTS):
        across = [
            out_ref[i, j] + (pair_ref[0, i, j] * value[0][j] + pair_ref[1, i, j] * value[1][j])
            for i in range(PTS)
        ]
        total[0][j] += across[0]
        total[1][j] += across[PTS - 1]
        for i in range(1, PTS - 1):
            work_ref[i, j] = across[i]
    for s in range(2):
        for j in range(PTS):
            at = (s * PTS + j) * ny
            total[s][j] += line_ref[at : at + ny]
    ymessage = []
    for t in range(2):
        j = ends[t]
        edge = [total[0][j]] + [work_ref[i, j] for i in range(1, PTS - 1)] + [total[1][j]]
        edge = [v[rows[t] : rows[t] + 1] for v in edge]
        edge[0] += edge_y[0][t]
        edge[PTS - 1] += edge_y[1][t]
        ymessage.append(sum_z(jnp.concatenate(edge, axis=0), column_masks((PTS, width))))
        yface_ref[t, 0] = ymessage[t]
    extra = [[None, None], [None, None]]
    for t, ref in enumerate((below_ref, above_ref)):
        j = ends[t]
        points = [value[0][j]] + [value_ref[i, j] for i in range(1, PTS - 1)] + [value[1][j]]
        flux = contract(D, points, -1)
        flux = contract(D.T, [flux[i] * ref[2, i : i + 1] for i in range(PTS)], -1)
        for s in range(2):
            at = (2 * PTS + 2 * s + t) * ny
            extra[s][t] = sum_z(flux[ends[s]] + line_ref[at : at + ny], masks)
            extra[s][t] = jnp.where(row == rows[t], extra[s][t], 0.0)
    for s in range(2):
        for j in range(PTS):
            total[s][j] = sum_z(total[s][j], masks)
        low, high = total[s][0], total[s][PTS - 1]
        total[s][PTS - 1] = high + jnp.where(row == ny - 1, 0.0, pltpu.roll(low, ny - 1, 0))
        total[s][0] = low + jnp.where(row == 0, 0.0, pltpu.roll(high, 1, 0))
    for j in range(PTS):
        low, high = total[0][j], total[1][j]
        if j in ends:
            t = ends.index(j)
            low, high = low + extra[0][t], high + extra[1][t]
        to_inner_ref[j * ny : (j + 1) * ny] = jnp.where(even, high, low)
        to_outer_ref[j * ny : (j + 1) * ny] = jnp.where(even, low, high)
        for s in range(2):
            sofar_ref[ends[s], j] = pface[s][j] - gface[s][j] * total[s][j]
    for i in range(1, PTS - 1):
        lines = [sum_z(work_ref[i, j], masks) for j in range(PTS)]
        low, high = lines[0], lines[PTS - 1]
        lines[PTS - 1] = high + jnp.where(row == ny - 1, 0.0, pltpu.roll(low, ny - 1, 0))
        lines[0] = low + jnp.where(row == 0, 0.0, pltpu.roll(high, 1, 0))
        for j in range(PTS):
            sofar_ref[i, j] = partial_ref[i, j] - gain_ref[i, j] * lines[j]
    sums = restricted(
        [(i, j) for i in range(PTS) for j in range(PTS)],
        lambda i, j: sofar_ref[i, j],
        lambda d, i, j: weights_ref[d, i, j],
        1,
    )
    for q in range(2):
        sums[q] = sums[q] + load_sums_ref[2 + q]
    base = PTS * ny
    changes = []
    for t in range(2):
        j = ends[t]
        gain = [gface[0][j]] + [gain_ref[i, j] for i in range(1, PTS - 1)] + [gface[1][j]]
        gain = jnp.concatenate([g[rows[t] : rows[t] + 1] for g in gain], axis=0)
        change = -(gain * ymessage[t])
        changes += edge_change(change, edge_weights_ref.at[t], ends[1 - t], 1)
        if t == 0:
            own = edge_change(change, edge_weights_ref.at[t], ends[1 - t], 0)
            zero = jnp.zeros_like(own[1])
            edge_ref[...] = jnp.concatenate([zero, own[1], zero, own[3]] + [zero] * 4, axis=0)
    changes = jnp.concatenate(changes, axis=0)
    for ref in (to_outer_ref, to_inner_ref):
        for n in range(4):
            ref[base + n * ny : base + (n + 1) * ny] = sums[n]
        ref[base + 4 * ny : base + 4 * ny + PTS] = changes


def edge_change(change, weight_ref, j, p):
    upper = lax.broadcasted_iota(jnp.int32, change.shape, 0)
    hat = jnp.zeros_like(change)
    for i in range(PTS):
        hat = jnp.where(upper == i, float(HAT[i, p]), hat)
    along_x, along_y, along_z = (
        jnp.sum(v, axis=0, keepdims=True)
        for v in (weight_ref[0] * change, hat * weight_ref[1] * change, hat * weight_ref[2] * change)
    )
    smooth = [-(SLOPE[p] * float(HAT[j, q]) * along_x + SLOPE[q] * along_y) for q in range(2)]
    return smooth + [-float(HAT[j, q]) * along_z for q in range(2)]


def restricted(points, value, weight, p):
    along_x, along_z, along_y = {}, {}, {}
    for i, j in points:
        v = value(i, j)
        along_x[j] = along_x.get(j, 0.0) + weight(0, i, j) * v
        if HAT[i, p]:
            along_y[i] = along_y.get(i, 0.0) + weight(1, i, j) * v
            along_z[j] = along_z.get(j, 0.0) + float(HAT[i, p]) * (weight(2, i, j) * v)
    y_sum = sum(float(HAT[i, p]) * total for i, total in along_y.items())
    smooth, slope = [], []
    for q in range(2):
        x_sum = sum(float(HAT[j, q]) * total for j, total in along_x.items() if HAT[j, q])
        smooth.append(-(SLOPE[p] * x_sum + SLOPE[q] * y_sum))
        slope.append(-sum(float(HAT[j, q]) * total for j, total in along_z.items() if HAT[j, q]))
    return smooth + slope


def x_corrections(even, gface_ref, outer_ref, inner_ref):
    ny = gface_ref.shape[2]
    change = {}
    for j in range(PTS):
        low = pick(even, outer_ref, inner_ref, j * ny, ny)
        high = pick(even, inner_ref, outer_ref, j * ny, ny)
        change[0, j] = -(gface_ref[0, j] * low)
        change[PTS - 1, j] = -(gface_ref[1, j] * high)
    return change


def y_corrections(gain_ref, gface_ref, below_ref, above_ref):
    ny, width = gain_ref.shape[2:]
    row = lax.broadcasted_iota(jnp.int32, (ny, width), 0)
    faces = {0: 0, PTS - 1: 1}
    change = {}
    for i in range(PTS):
        for j, at, ref in ((0, 0, below_ref), (PTS - 1, ny - 1, above_ref)):
            gain = gface_ref[faces[i], j] if i in faces else gain_ref[i, j]
            change[i, j] = -(gain * jnp.where(row == at, ref[0, i : i + 1], 0.0))
    return change


def face_change(change, weight, i, p, q):
    along_x = sum(float(HAT[j, q]) * (weight[0][j] * change[j]) for j in range(PTS) if HAT[j, q])
    smooth = SLOPE[p] * along_x
    slope = 0.0
    if HAT[i, p]:
        along_y = sum(weight[1][j] * change[j] for j in range(PTS))
        smooth = smooth + float(HAT[i, p]) * SLOPE[q] * along_y
        along_z = sum(float(HAT[j, q]) * (weight[2][j] * change[j]) for j in range(PTS) if HAT[j, q])
        slope = float(HAT[i, p]) * along_z
    return -smooth, -slope


def to_vertices(smooth, slope, restrict):
    return dot_split(jnp.concatenate([smooth, slope], axis=1), restrict)


def pick(even, first, second, at, count):
    return jnp.where(even, first[at : at + count], second[at : at + count])


def ahead_kernel(
    side_ref, sent_outer_ref, sent_inner_ref, gface_ref, restrict_ref, outer_ref, inner_ref,
    next_ref, top_ref,
):
    ny, width = gface_ref.shape[2:]
    even = side_ref[0] == 0
    change = [
        -(gface_ref[1, j] * pick(even, sent_inner_ref, sent_outer_ref, j * ny, ny)) for j in range(PTS)
    ]
    weight = [[pick(even, inner_ref, outer_ref, j * ny, ny) for j in range(PTS)]]
    smooth = jnp.concatenate([face_change(change, weight, 0, 1, q)[0] for q in range(2)], axis=0)
    hats = jnp.concatenate([restrict_ref[:width], restrict_ref[2 * width : 3 * width]], axis=0)
    corners = dot_split(smooth, hats)
    lower, upper = corners[:ny], corners[ny:]
    row = lax.broadcasted_iota(jnp.int32, lower.shape, 0)
    rows = lower + jnp.where(row == 0, 0.0, pltpu.roll(upper, 1, 0))
    next_ref[...] = jnp.concatenate([rows] * (next_ref.shape[0] // ny), axis=0)
    top_ref[...] = jnp.broadcast_to(upper[ny - 1 : ny], top_ref.shape)


def behind_kernel(
    side_ref, sent_outer_ref, sent_inner_ref, gface_ref, back_ref, sofar_ref, weights_ref, load_sums_ref,
    outer_ref, inner_ref,
    own_ref,
):
    ny, width = gface_ref.shape[2:]
    even = side_ref[0] == 0

    def rows(at):
        return pick(even, outer_ref, inner_ref, at, ny)

    change = [
        -(gface_ref[0, j] * pick(even, sent_outer_ref, sent_inner_ref, j * ny, ny)) for j in range(PTS)
    ]
    spread = [rows((2 * PTS + d) * ny) for d in range(2)]
    points = [rows((PTS + j) * ny) for j in range(PTS)]
    column = dot_split(jnp.concatenate([p * spread[1] for p in points], axis=0), back_ref[...])
    weight = [
        [rows(j * ny) for j in range(PTS)],
        contract(D.T, [p * spread[0] for p in points], -1),
        [column[j * ny : (j + 1) * ny] for j in range(PTS)],
    ]
    sums = restricted(
        [(i, j) for i in range(PTS) for j in range(PTS)],
        lambda i, j: sofar_ref[i, j],
        lambda d, i, j: weights_ref[d, i, j],
        0,
    )
    for q in range(2):
        smooth, slope = face_change(change, weight, PTS - 1, 1, q)
        own_ref[q] = sums[q] + load_sums_ref[q] + smooth
        own_ref[2 + q] = sums[2 + q] + slope


def coarse_kernel(
    side_ref, gface_ref, own_ref, edge_in_ref, weights_ref, restrict_ref, outer_ref, inner_ref,
    plane_ref, edge_ref,
):
    ny, width = gface_ref.shape[2:]
    even = side_ref[0] == 0
    change = x_corrections(even, gface_ref, outer_ref, inner_ref)
    sums = restricted(
        list(change),
        lambda i, j: change[i, j],
        lambda d, i, j: weights_ref[d, i, j],
        0,
    )
    base = PTS * ny

    def before(at, count):
        return pick(even, outer_ref, inner_ref, at, count)

    total = [sums[n] + own_ref[n] + before(base + n * ny, ny) for n in range(4)]
    extra = before(base + 4 * ny, PTS) + edge_in_ref[...]
    smooth = jnp.concatenate(total[:2] + [extra], axis=0)
    slope = jnp.concatenate(total[2:] + [pltpu.roll(extra, PTS - 2, 0)], axis=0)
    corners = to_vertices(smooth, slope, restrict_ref[...])
    lower, upper = corners[:ny], corners[ny : 2 * ny]
    extra = corners[2 * ny :]
    row = lax.broadcasted_iota(jnp.int32, lower.shape, 0)
    plane_ref[...] = lower + jnp.where(row == 0, extra[1:2], pltpu.roll(upper, 1, 0))
    edge_ref[0:1] = upper[ny - 1 : ny] + extra[4:5]
    edge_ref[1:2] = extra[5:6]
    edge_ref[2:3] = extra[0:1]


def beside_kernel(
    own_ref, gain_ref, gface_ref, weights_ref, restrict_ref, below_ref, above_ref,
    plane_ref,
):
    below_ref, above_ref = below_ref.at[1], above_ref.at[0]
    ny, width = gain_ref.shape[2:]
    change = y_corrections(gain_ref, gface_ref, below_ref, above_ref)
    sums = restricted(
        list(change),
        lambda i, j: change[i, j],
        lambda d, i, j: weights_ref[d, i, j],
        0,
    )
    smooth = jnp.concatenate(sums[:2], axis=0)
    slope = jnp.concatenate(sums[2:], axis=0)
    corners = to_vertices(smooth, slope, restrict_ref[...])
    lower, upper = corners[:ny], corners[ny:]
    row = lax.broadcasted_iota(jnp.int32, lower.shape, 0)
    plane_ref[...] = own_ref[...] + lower + jnp.where(row == 0, 0.0, pltpu.roll(upper, 1, 0))


def pressure_kernel(
    side_ref, sofar_ref, gain_ref, gface_ref, outer_ref, below_ref, above_ref, inner_ref,
    pressure_out, token_ref, pressure_ref, sem,
):
    token_ref[...] = jnp.zeros_like(token_ref)
    below_ref, above_ref = below_ref.at[1], above_ref.at[0]
    ny = sofar_ref.shape[2]
    even = side_ref[0] == 0
    changes = (
        x_corrections(even, gface_ref, outer_ref, inner_ref),
        y_corrections(gain_ref, gface_ref, below_ref, above_ref),
    )
    for i in range(PTS):
        for j in range(PTS):
            value = sofar_ref[i, j]
            for change in changes:
                if (i, j) in change:
                    value = value + change[i, j]
            pressure_ref[i, pl.ds(j, ny, stride=PTS)] = value
    copy = pltpu.make_async_copy(pressure_ref, pressure_out, sem)
    copy.start()
    copy.wait()


def join_kernel(own_ref, next_ref, top_ref, token_ref, joined_ref):
    row = lax.broadcasted_iota(jnp.int32, joined_ref.shape, 0)
    total = own_ref[...] + next_ref[: row.shape[0]] + token_ref[...]
    joined_ref[...] = total + jnp.where(row == 0, top_ref[0:1], 0.0)


def last_kernel(joined_ref, below_ref, above_ref, coarse_ref):
    total = joined_ref[...]
    ny = total.shape[0]
    row = lax.broadcasted_iota(jnp.int32, total.shape, 0)
    total = total + jnp.where(row == 0, below_ref[0:1], jnp.where(row == 1, below_ref[1:2], 0.0))
    total = total + jnp.where(row == ny - 1, above_ref[2:3], 0.0)
    coarse_ref[...] = total[:, : coarse_ref.shape[1]]


def call(body, outs, scratch, *args, spaces=None, out_spaces=None):
    spaces = spaces or [pltpu.SMEM if a.dtype == jnp.int32 else pltpu.VMEM for a in args]
    return pl.pallas_call(
        body,
        out_shape=[jax.ShapeDtypeStruct(s, F32) if isinstance(s, tuple) else s for s in outs],
        in_specs=[pl.BlockSpec(memory_space=m) for m in spaces],
        out_specs=[pl.BlockSpec(memory_space=m) for m in out_spaces or [pltpu.VMEM] * len(outs)],
        scratch_shapes=[pltpu.VMEM(s, F32) if isinstance(s, tuple) else s for s in scratch],
        compiler_params=pltpu.CompilerParams(vmem_limit_bytes=16 * 1024 * 1024),
    )(*args)


def from_y(faces):
    size = lax.axis_size("sub")
    up = lax.ppermute(faces, "sub", [(i, (i + 1) % size) for i in range(size)])
    if size == 2:
        return up, up
    return up, lax.ppermute(faces, "sub", [(i, (i - 1) % size) for i in range(size)])


def inner_pairs(size):
    return [(i, i ^ 1) for i in range(size)]


def outer_pairs(size):
    return [(i, (i + 1) % size if i % 2 else (i - 1) % size) for i in range(size)]


def to_x(outer, inner):
    size = lax.axis_size("dom")
    outer = lax.ppermute(outer, "dom", outer_pairs(size))
    inner = lax.ppermute(inner, "dom", inner_pairs(size))
    return outer, inner


def two_on(rows, top):
    size, rest = lax.axis_size("dom"), lax.axis_size("sub")
    rows = lax.ppermute(rows, "dom", [(i, (i + 2) % size) for i in range(size)])
    pairs = [
        (i * rest + k, (i + 2) % size * rest + (k + 1) % rest) for i in range(size) for k in range(rest)
    ]
    return rows, lax.ppermute(top, ("dom", "sub"), pairs)


def shards(element_load, mobility, metric):
    _, _, ny, _, width = element_load.shape
    load = element_load.reshape(PTS, ny * PTS, width)
    mob = mobility.reshape(PTS, ny * PTS, width)
    metric = metric[:, 0]
    side = (lax.axis_index("dom") % 2).astype(jnp.int32).reshape(1)
    def in_hbm(*arrays):
        return [pltpu.with_memory_space_constraint(a, pltpu.HBM) for a in arrays]

    grad, back = column_tables(width)
    restrict = restrict_table(width)
    field = (PTS, PTS, ny, width)
    face = (PTS, ny, width)
    ends = (2, PTS, PTS, width)
    spread, yface = call(
        edge_kernel,
        [(3, ny, width), (2, 5, PTS, width)],
        [metric.shape, ends, ends, pltpu.SemaphoreType.DMA((5,))],
        *in_hbm(metric, mob, load),
        spaces=[pltpu.HBM] * 3,
    )
    below, above = from_y(yface)
    still = (2 * (PTS + 1) * ny, width)
    fields, xface, factor, still_outer, still_inner, weights, load_sums = call(
        diag_kernel,
        [
            (2,) + field, (2, 2) + face, (2, 2, PTS, width), still, still,
            (3,) + field, (4, ny, width),
        ],
        [],
        side, load, mob, spread,
    )
    rows = (2 * PTS * ny + 2 * PTS, width)
    outer, inner = to_x(*call(merge_kernel, [rows, rows], [], side, xface, factor, below, above))
    still_outer, still_inner = to_x(still_outer, still_inner)
    faces = (2,) + face
    rough, value, partial, gain, out, pair, edge_weights = call(
        inside_kernel,
        [
            (2,) + faces, field, field, field, field, (2,) + field,
            (2, 3, PTS, width),
        ],
        [face],
        fields, mob, spread, grad, back, below, above,
    )
    rows = ((PTS + 4) * ny + PTS, width)
    sent_outer, sent_inner, yface, gface, sofar, edge = call(
        faces_kernel,
        [rows, rows, (2, 1, PTS, width), faces, field, (PTS, width)],
        [((2 * PTS + 4) * ny, width), field],
        side, rough, value, out, pair, mob, spread, grad, back, below, above,
        partial, gain, weights, load_sums, edge_weights, outer, inner,
    )
    outer, inner = to_x(sent_outer, sent_inner)
    onward, top = call(
        ahead_kernel,
        [(3 * ny, 128), (3 * PTS, 128)],
        [],
        side, sent_outer, sent_inner, gface, restrict, still_outer, still_inner,
    )
    (own,) = call(
        behind_kernel,
        [(4, ny, width)],
        [],
        side, sent_outer, sent_inner, gface, back, sofar, weights, load_sums, still_outer, still_inner,
    )
    onward, top = two_on(onward, top)
    below, above = from_y(yface)
    own_rows, tops = call(
        coarse_kernel,
        [(ny, 128), (3, 128)],
        [],
        side, gface, own, edge, weights, restrict, outer, inner,
    )
    (own_rows,) = call(
        beside_kernel, [(ny, 128)], [], own_rows, gain, gface, weights, restrict, below, above
    )
    pressure, token = call(
        pressure_kernel,
        [(PTS, ny * PTS, width), (1, 128)],
        [(PTS, ny * PTS, width), pltpu.SemaphoreType.DMA(())],
        side, sofar, gain, gface, outer, below, above, inner,
        out_spaces=[pltpu.HBM, pltpu.VMEM],
    )
    (onward,) = call(join_kernel, [(ny, 128)], [], own_rows, onward, top, token)
    row_below, row_above = from_y(tops)
    (coarse,) = call(last_kernel, [(ny, width // PTS + 1)], [], onward, row_below, row_above)
    return pressure.reshape(element_load.shape), coarse[None]


def solution(mesh):
    in_specs = (
        P("dom", None, "sub", None, None),
        P("dom", None, "sub", None, None),
        P(None, "dom", "sub", None),
    )
    out_specs = (P("dom", None, "sub", None, None), P("dom", "sub", None))
    return jax.shard_map(shards, mesh=mesh, in_specs=in_specs, out_specs=out_specs, check_vma=False)
```

```python
import jax
import jax.numpy as jnp
import ml_dtypes
import numpy as np
from jax import lax
from jax.experimental import pallas as pl
from jax.experimental.pallas import tpu as pltpu
from jax.sharding import PartitionSpec as P

GLL_NODES = np.array(
    [
        -1.0,
        -0.8717401485096066,
        -0.5917001814331423,
        -0.2092992179024789,
        0.2092992179024789,
        0.5917001814331423,
        0.8717401485096066,
        1.0,
    ]
)
GLL_WEIGHTS = np.array(
    [
        0.03571428571428571,
        0.2107042271435061,
        0.3411226924835044,
        0.4124587946587038,
        0.4124587946587038,
        0.3411226924835044,
        0.2107042271435061,
        0.03571428571428571,
    ]
)
THETA = 1.65
DELTA = 1.35
RHO_FIRST = DELTA / THETA
RHO_SECOND = 1.0 / (2.0 * THETA / DELTA - RHO_FIRST)
KEEP = 1.0 + RHO_SECOND * RHO_FIRST
GAIN = 2.0 * RHO_SECOND / DELTA
PTS = 8
F32 = jnp.float32


def derivative_table():
    identity = np.eye(8)
    differences = GLL_NODES[:, None] - GLL_NODES[None, :] + identity
    barycentric = 1.0 / np.prod(differences, axis=1)
    matrix = barycentric[None, :] / barycentric[:, None] / differences
    matrix = matrix * (1.0 - identity)
    row_sums = np.sum(matrix, axis=1)
    return matrix - identity * row_sums[:, None]


D = derivative_table()
W = GLL_WEIGHTS
HAT = np.stack([(1.0 - GLL_NODES) / 8.0, (1.0 + GLL_NODES) / 8.0], axis=1)
SLOPE = (-0.125, 0.125)


def tiled(matrix, width):
    column = lax.broadcasted_iota(jnp.int32, (PTS, width), 1) % PTS
    row = lax.broadcasted_iota(jnp.int32, (PTS, width), 0)
    total = jnp.zeros((PTS, width), F32)
    for c in range(PTS):
        lines = jnp.zeros((PTS, width), F32)
        for r in range(PTS):
            lines = jnp.where(row == r, float(matrix[r, c]), lines)
        total = jnp.where(column == c, lines, total)
    return total


def by_row(values, width):
    return tiled(np.tile(np.asarray(values)[:, None], (1, PTS)), width)


def cell_blocks(rows):
    width = rows.shape[1]
    cell = lax.broadcasted_iota(jnp.int32, rows.shape, 1) // PTS
    return jnp.concatenate(
        [jnp.where(cell == g, rows, 0.0) for g in range(width // PTS)], axis=0
    )


def paired_here(b):
    high, low = halves(b)
    return jnp.concatenate(
        [
            jnp.concatenate([high, low], axis=1),
            jnp.concatenate([high, jnp.zeros_like(low)], axis=1),
        ],
        axis=0,
    )


def paired(b):
    b = np.asarray(b, np.float32)
    high = b.astype(ml_dtypes.bfloat16)
    low = (b - high.astype(np.float32)).astype(ml_dtypes.bfloat16)
    return jnp.asarray(np.block([[high, low], [high, np.zeros_like(low)]]))


def column_tables(width):
    cells = np.eye(width // PTS)
    return paired(np.kron(cells, D.T)), paired(np.kron(cells, D))


def restrict_table(width):
    cells = width // PTS
    hat = np.zeros((width, 128))
    slope = np.zeros((width, 128))
    for c in range(cells):
        rows = slice(c * PTS, (c + 1) * PTS)
        hat[rows, c], hat[rows, c + 1] = HAT[:, 0], HAT[:, 1]
        slope[rows, c], slope[rows, c + 1] = SLOPE
    return paired(np.concatenate([hat, slope]))


def halves(a):
    high = a.astype(jnp.bfloat16)
    return high, (a - high.astype(F32)).astype(jnp.bfloat16)


def dot_split(a, b_pair):
    both = jnp.dot(
        jnp.concatenate(halves(a), axis=1), b_pair, preferred_element_type=F32
    )
    n = both.shape[1] // 2
    return both[:, :n] + both[:, n:]


def contract(matrix, lines, parity):
    n = len(lines)
    half = n // 2
    plus = [lines[c] + lines[n - 1 - c] for c in range(half)]
    minus = [lines[c] - lines[n - 1 - c] for c in range(half)]
    top, low = [], []
    for r in range(half):
        even = sum(float(0.5 * (matrix[r, c] + matrix[r, n - 1 - c])) * plus[c] for c in range(half))
        odd = sum(float(0.5 * (matrix[r, c] - matrix[r, n - 1 - c])) * minus[c] for c in range(half))
        top.append(even + odd)
        low.append(even - odd if parity > 0 else odd - even)
    return top + low[::-1]


def spread_metric(metric, weight_row):
    _, rows, cells = metric.shape
    width = weight_row.shape[1]
    cell = lax.broadcasted_iota(jnp.int32, (rows, width), 1) // PTS
    fill = jnp.zeros((rows, width - cells), F32)
    spread = [
        jnp.take_along_axis(jnp.concatenate([metric[d], fill], axis=1), cell, axis=1, mode="promise_in_bounds")
        for d in range(3)
    ]
    return [v * weight_row[:1] for v in spread], spread[2]


def column_masks(shape):
    lane = lax.broadcasted_iota(jnp.int32, shape, len(shape) - 1)
    up = (lane % PTS == PTS - 1) & (lane != shape[-1] - 1)
    down = (lane % PTS == 0) & (lane != 0)
    return up, down


def sum_z(v, masks):
    width = v.shape[-1]
    axis = v.ndim - 1
    up = pltpu.roll(v, width - 1, axis)
    down = pltpu.roll(v, 1, axis)
    return v + jnp.where(masks[0], up, jnp.where(masks[1], down, 0.0))


def sum_y_local(ref, ny):
    for i in range(PTS):
        low, high = ref[i, 0], ref[i, PTS - 1]
        row = lax.broadcasted_iota(jnp.int32, low.shape, 0)
        ref[i, PTS - 1] = high + jnp.where(row == ny - 1, 0.0, pltpu.roll(low, ny - 1, 0))
        ref[i, 0] = low + jnp.where(row == 0, 0.0, pltpu.roll(high, 1, 0))


def edge_planes(ref, ny):
    low = jnp.concatenate([ref[i, 0, 0:1] for i in range(PTS)], axis=0)
    high = jnp.concatenate([ref[i, PTS - 1, ny - 1 : ny] for i in range(PTS)], axis=0)
    return low, high


def plane(ref, ny):
    return lambda i, j: ref[i, pl.ds(j, ny, stride=PTS)]


def edge_kernel(metric_in, mob_in, load_in, spread_ref, yface_ref, metric_ref, mob_ref, load_ref, sems):
    ny, width = spread_ref.shape[1:]
    ends = (0, PTS - 1)
    copies = [pltpu.make_async_copy(metric_in, metric_ref, sems.at[0])]
    for n, (source, target) in enumerate(((mob_in, mob_ref), (load_in, load_ref))):
        for s, e in enumerate((0, ny - 1)):
            copies.append(
                pltpu.make_async_copy(
                    source.at[:, pl.ds(e * PTS, PTS)], target.at[s], sems.at[1 + 2 * n + s]
                )
            )
    for copy in copies:
        copy.start()
    masks = column_masks((PTS, width))
    weight_row = tiled(np.tile(W[None], (PTS, 1)), width)
    row_weight = by_row(W, width)
    squared = paired_here(cell_blocks(tiled(D * D, width)))
    squares = [by_row(D[a] ** 2, width) for a in range(PTS)]
    for copy in copies:
        copy.wait()
    spread, cell_metric = spread_metric(metric_ref[...], weight_row)
    for d in range(3):
        spread_ref[d] = spread[d]
    points = [mob_ref[s, :, ends[s]] * (float(W[ends[s]]) * row_weight) for s in range(2)]
    columns = dot_split(
        jnp.concatenate([p * weight_row for p in points], axis=0), squared
    )
    for s, e in enumerate((0, ny - 1)):
        j = ends[s]
        scale = [spread[d][e : e + 1] for d in range(3)]
        along = sum(squares[a] * points[s][a : a + 1] for a in range(PTS))
        total = along * scale[0]
        sums = [
            sum(float(D[b, j] ** power * W[b]) * mob_ref[s, :, b] for b in range(PTS))
            * row_weight
            * scale[1]
            for power in (1, 2)
        ]
        yface_ref[s, 2] = points[s] * scale[0]
        yface_ref[s, 3] = points[s] * scale[2]
        yface_ref[s, 4] = sums[0]
        column = columns[s * PTS : (s + 1) * PTS] * cell_metric[e : e + 1]
        yface_ref[s, 1] = sum_z(total + sums[1] + column, masks)
    for s in range(2):
        yface_ref[s, 0] = sum_z(load_ref[s, :, ends[s]], masks)


def diag_kernel(
    side_ref, load_ref, mob_ref, spread_ref,
    fields_ref, xface_ref, factor_ref, to_outer_ref, to_inner_ref, weights_ref, sums_ref,
):
    ny, width = fields_ref.shape[3:]
    spread = [spread_ref[d] for d in range(3)]
    square = D * D
    squared = paired_here(cell_blocks(tiled(square, width)))
    back = paired_here(cell_blocks(tiled(D, width)))
    mob, load = plane(mob_ref, ny), plane(load_ref, ny)
    diag_ref = fields_ref.at[1]
    even = side_ref[0] == 0

    def post(at, low, high):
        to_inner_ref[at : at + ny] = jnp.where(even, high, low)
        to_outer_ref[at : at + ny] = jnp.where(even, low, high)

    for d in (1, 2):
        post((2 * PTS + d - 1) * ny, spread[d], spread[d])
    for j in range(PTS):
        factor = [mob(i, j) * (float(W[i] * W[j]) * spread[0]) for i in range(PTS)]
        post(j * ny, *(sum(float(D[a, i]) * factor[a] for a in range(PTS)) for i in (0, PTS - 1)))
        post((PTS + j) * ny, *(float(W[i] * W[j]) * mob(i, j) for i in (0, PTS - 1)))
        for i, value in enumerate(contract(square.T, factor, 1)):
            diag_ref[i, j] = value
        for i, value in enumerate(contract(D.T, factor, -1)):
            weights_ref[0, i, j] = value
    for i in range(PTS):
        factor = [mob(i, j) * (float(W[i] * W[j]) * spread[1]) for j in range(PTS)]
        for j, value in enumerate(contract(square.T, factor, 1)):
            diag_ref[i, j] += value
        for j, value in enumerate(contract(D.T, factor, -1)):
            weights_ref[1, i, j] = value
    for i in range(PTS):
        factor = jnp.concatenate(
            [mob(i, j) * (float(W[i] * W[j]) * spread[2]) for j in range(PTS)], axis=0
        )
        diag_ref[i] += dot_split(factor, squared).reshape(PTS, ny, width)
        weights_ref[2, i] = dot_split(factor, back).reshape(PTS, ny, width)
        fields_ref[0, i] = jnp.stack([load(i, j) for j in range(PTS)], axis=0)
    masks = column_masks((PTS, ny, width))
    for f in range(2):
        for i in range(PTS):
            fields_ref[f, i] = sum_z(fields_ref[f, i], masks)
        sum_y_local(fields_ref.at[f], ny)
        xface_ref[f, 0] = fields_ref[f, 0]
        xface_ref[f, 1] = fields_ref[f, PTS - 1]
    row_weight = by_row(W, width)
    for s, i in enumerate((0, PTS - 1)):
        for n, e in enumerate((0, ny - 1)):
            points = mob_ref[i, e * PTS : (e + 1) * PTS] * (float(W[i]) * row_weight)
            factor_ref[s, n] = points * spread[1][e : e + 1]
    zero = jnp.zeros((ny, width), F32)
    sums = [zero] * 4
    for i in range(PTS):
        for q in range(2):
            from_load = sum(float(HAT[j, q]) * load(i, j) for j in range(PTS))
            for p in range(2):
                if HAT[i, p]:
                    sums[2 * p + q] = sums[2 * p + q] + float(HAT[i, p]) * from_load
    for n in range(4):
        sums_ref[n] = sums[n]


def merge_kernel(side_ref, xface_ref, factor_ref, below_ref, above_ref, outer_ref, inner_ref):
    below_ref, above_ref = below_ref.at[1], above_ref.at[0]
    even = side_ref[0] == 0
    fields, _, _, ny, width = xface_ref.shape
    row = lax.broadcasted_iota(jnp.int32, (ny, width), 0)
    for f in range(fields):
        for j in range(PTS):
            low, high = xface_ref[f, 0, j], xface_ref[f, 1, j]
            if j == 0:
                low = low + jnp.where(row == 0, below_ref[f, 0:1], 0.0)
                high = high + jnp.where(row == 0, below_ref[f, PTS - 1 : PTS], 0.0)
            if j == PTS - 1:
                low = low + jnp.where(row == ny - 1, above_ref[f, 0:1], 0.0)
                high = high + jnp.where(row == ny - 1, above_ref[f, PTS - 1 : PTS], 0.0)
            at = (f * PTS + j) * ny
            inner_ref[at : at + ny] = jnp.where(even, high, low)
            outer_ref[at : at + ny] = jnp.where(even, low, high)
    for n in range(2):
        at = fields * PTS * ny + n * PTS
        low, high = factor_ref[0, n], factor_ref[1, n]
        inner_ref[at : at + PTS] = jnp.where(even, high, low)
        outer_ref[at : at + PTS] = jnp.where(even, low, high)


def inside_kernel(
    fields_ref, mob_ref, spread_ref, grad_ref, back_ref, below_ref, above_ref,
    rough_ref, value_ref, partial_ref, gain_ref, out_ref, pair_ref, edge_weights_ref,
    work_ref,
):
    below_ref, above_ref = below_ref.at[1], above_ref.at[0]
    ny, width = out_ref.shape[2:]
    spread = [spread_ref[d] for d in range(3)]
    mob = plane(mob_ref, ny)
    row = lax.broadcasted_iota(jnp.int32, (ny, width), 0)
    zero = jnp.zeros((ny, width), F32)
    for i in range(PTS):
        for j in range(PTS):
            sums = [fields_ref[f, i, j] for f in range(2)]
            for f in range(2):
                if j == 0:
                    sums[f] += jnp.where(row == 0, below_ref[f, i : i + 1], 0.0)
                if j == PTS - 1:
                    sums[f] += jnp.where(row == ny - 1, above_ref[f, i : i + 1], 0.0)
            if i in (0, PTS - 1):
                for f in range(2):
                    rough_ref[f, 0 if i == 0 else 1, j] = sums[f]
                value_ref[i, j] = partial_ref[i, j] = gain_ref[i, j] = zero
            else:
                value_ref[i, j], partial_ref[i, j], gain_ref[i, j] = first_step(*sums)
    grad, back = grad_ref[...], back_ref[...]
    for j in range(PTS):
        factor = [mob(i, j) * (float(W[i] * W[j]) * spread[0]) for i in range(PTS)]
        for n, p in enumerate((0, PTS - 1)):
            coupling = contract(D.T, [float(D[a, p]) * factor[a] for a in range(PTS)], -1)
            for i in range(PTS):
                pair_ref[n, i, j] = coupling[i]
        flux = contract(D, [value_ref[i, j] for i in range(PTS)], -1)
        flux = [flux[i] * factor[i] for i in range(PTS)]
        for i, value in enumerate(contract(D.T, flux, -1)):
            out_ref[i, j] = value
    for i in range(1, PTS - 1):
        flux = contract(D, [value_ref[i, j] for j in range(PTS)], -1)
        flux = [flux[j] * (mob(i, j) * (float(W[i] * W[j]) * spread[1])) for j in range(PTS)]
        for j, value in enumerate(contract(D.T, flux, -1)):
            out_ref[i, j] += value
        work_ref[...] = dot_split(value_ref[i].reshape(PTS * ny, width), grad).reshape(PTS, ny, width)
        for j in range(PTS):
            work_ref[j] *= mob(i, j) * (float(W[i] * W[j]) * spread[2])
        out_ref[i] += dot_split(work_ref[...].reshape(PTS * ny, width), back).reshape(PTS, ny, width)
    for t, ref in enumerate((below_ref, above_ref)):
        edge_weights_ref[t, 0] = sum(by_row(D[a], width) * ref[2, a : a + 1] for a in range(PTS))
        edge_weights_ref[t, 1] = ref[4]
        edge_weights_ref[t, 2] = dot_split(ref[3], back)


def first_step(right, diagonal):
    inverse = 1.0 / diagonal
    scaled = inverse * right
    value = scaled * (1.0 / THETA)
    return value, KEEP * value + GAIN * scaled, GAIN * inverse


def faces_kernel(
    side_ref, rough_ref, value_ref, out_ref, pair_ref, mob_ref, spread_ref, grad_ref, back_ref,
    below_ref, above_ref, partial_ref, gain_ref, weights_ref, load_sums_ref, edge_weights_ref,
    outer_ref, inner_ref,
    to_outer_ref, to_inner_ref, yface_ref, gface_ref, sofar_ref, edge_ref, line_ref, work_ref,
):
    below_ref, above_ref = below_ref.at[1], above_ref.at[0]
    even = side_ref[0] == 0
    ny, width = out_ref.shape[2:]
    spread = [spread_ref[d] for d in range(3)]
    mob = plane(mob_ref, ny)
    ends = (0, PTS - 1)
    rows = (0, ny - 1)
    row = lax.broadcasted_iota(jnp.int32, (ny, width), 0)
    masks = column_masks((ny, width))

    def arrived(at, count):
        inner, outer = inner_ref[at : at + count], outer_ref[at : at + count]
        return jnp.where(even, outer, inner), jnp.where(even, inner, outer)

    value = [[None] * PTS, [None] * PTS]
    pface = [[None] * PTS, [None] * PTS]
    gface = [[None] * PTS, [None] * PTS]
    for j in range(PTS):
        load = arrived(j * ny, ny)
        diagonal = arrived((PTS + j) * ny, ny)
        for s in range(2):
            value[s][j], pface[s][j], gface[s][j] = first_step(
                rough_ref[0, s, j] + load[s], rough_ref[1, s, j] + diagonal[s]
            )
            gface_ref[s, j] = gface[s][j]
    lines = [value[s][j] for s in range(2) for j in range(PTS)]
    factors = [
        mob(ends[s], j) * (float(W[ends[s]] * W[j]) * spread[2]) for s in range(2) for j in range(PTS)
    ]
    for s in range(2):
        for t, ref in enumerate((below_ref, above_ref)):
            lines.append(value[s][ends[t]])
            factors.append(jnp.broadcast_to(ref[3, ends[s] : ends[s] + 1], (ny, width)))
    flux = dot_split(jnp.concatenate(lines, axis=0), grad_ref[...]) * jnp.concatenate(factors, axis=0)
    line_ref[...] = dot_split(flux, back_ref[...])
    edge_y = [[None, None], [None, None]]
    total = [[None] * PTS, [None] * PTS]
    for s in range(2):
        gradient = contract(D, value[s], -1)
        flux = [
            gradient[j] * (mob(ends[s], j) * (float(W[ends[s]] * W[j]) * spread[1])) for j in range(PTS)
        ]
        total[s] = contract(D.T, flux, -1)
        for t in range(2):
            factor = arrived(2 * PTS * ny + t * PTS, PTS)[s]
            edge_y[s][t] = sum(
                float(D[j, ends[t]]) * (gradient[j] * factor[j : j + 1]) for j in range(PTS)
            )[rows[t] : rows[t] + 1]
    for j in range(PTS):
        across = [
            out_ref[i, j] + (pair_ref[0, i, j] * value[0][j] + pair_ref[1, i, j] * value[1][j])
            for i in range(PTS)
        ]
        total[0][j] += across[0]
        total[1][j] += across[PTS - 1]
        for i in range(1, PTS - 1):
            work_ref[i, j] = across[i]
    for s in range(2):
        for j in range(PTS):
            at = (s * PTS + j) * ny
            total[s][j] += line_ref[at : at + ny]
    ymessage = []
    for t in range(2):
        j = ends[t]
        edge = [total[0][j]] + [work_ref[i, j] for i in range(1, PTS - 1)] + [total[1][j]]
        edge = [v[rows[t] : rows[t] + 1] for v in edge]
        edge[0] += edge_y[0][t]
        edge[PTS - 1] += edge_y[1][t]
        ymessage.append(sum_z(jnp.concatenate(edge, axis=0), column_masks((PTS, width))))
        yface_ref[t, 0] = ymessage[t]
    extra = [[None, None], [None, None]]
    for t, ref in enumerate((below_ref, above_ref)):
        j = ends[t]
        points = [value[0][j]] + [value_ref[i, j] for i in range(1, PTS - 1)] + [value[1][j]]
        flux = contract(D, points, -1)
        flux = contract(D.T, [flux[i] * ref[2, i : i + 1] for i in range(PTS)], -1)
        for s in range(2):
            at = (2 * PTS + 2 * s + t) * ny
            extra[s][t] = sum_z(flux[ends[s]] + line_ref[at : at + ny], masks)
            extra[s][t] = jnp.where(row == rows[t], extra[s][t], 0.0)
    for s in range(2):
        for j in range(PTS):
            total[s][j] = sum_z(total[s][j], masks)
        low, high = total[s][0], total[s][PTS - 1]
        total[s][PTS - 1] = high + jnp.where(row == ny - 1, 0.0, pltpu.roll(low, ny - 1, 0))
        total[s][0] = low + jnp.where(row == 0, 0.0, pltpu.roll(high, 1, 0))
    for j in range(PTS):
        low, high = total[0][j], total[1][j]
        if j in ends:
            t = ends.index(j)
            low, high = low + extra[0][t], high + extra[1][t]
        to_inner_ref[j * ny : (j + 1) * ny] = jnp.where(even, high, low)
        to_outer_ref[j * ny : (j + 1) * ny] = jnp.where(even, low, high)
        for s in range(2):
            sofar_ref[ends[s], j] = pface[s][j] - gface[s][j] * total[s][j]
    for i in range(1, PTS - 1):
        lines = [sum_z(work_ref[i, j], masks) for j in range(PTS)]
        low, high = lines[0], lines[PTS - 1]
        lines[PTS - 1] = high + jnp.where(row == ny - 1, 0.0, pltpu.roll(low, ny - 1, 0))
        lines[0] = low + jnp.where(row == 0, 0.0, pltpu.roll(high, 1, 0))
        for j in range(PTS):
            sofar_ref[i, j] = partial_ref[i, j] - gain_ref[i, j] * lines[j]
    sums = restricted(
        [(i, j) for i in range(PTS) for j in range(PTS)],
        lambda i, j: sofar_ref[i, j],
        lambda d, i, j: weights_ref[d, i, j],
        1,
    )
    for q in range(2):
        sums[q] = sums[q] + load_sums_ref[2 + q]
    base = PTS * ny
    changes = []
    for t in range(2):
        j = ends[t]
        gain = [gface[0][j]] + [gain_ref[i, j] for i in range(1, PTS - 1)] + [gface[1][j]]
        gain = jnp.concatenate([g[rows[t] : rows[t] + 1] for g in gain], axis=0)
        change = -(gain * ymessage[t])
        changes += edge_change(change, edge_weights_ref.at[t], ends[1 - t], 1)
        if t == 0:
            own = edge_change(change, edge_weights_ref.at[t], ends[1 - t], 0)
            zero = jnp.zeros_like(own[1])
            edge_ref[...] = jnp.concatenate([zero, own[1], zero, own[3]] + [zero] * 4, axis=0)
    changes = jnp.concatenate(changes, axis=0)
    for ref in (to_outer_ref, to_inner_ref):
        for n in range(4):
            ref[base + n * ny : base + (n + 1) * ny] = sums[n]
        ref[base + 4 * ny : base + 4 * ny + PTS] = changes


def edge_change(change, weight_ref, j, p):
    upper = lax.broadcasted_iota(jnp.int32, change.shape, 0)
    hat = jnp.zeros_like(change)
    for i in range(PTS):
        hat = jnp.where(upper == i, float(HAT[i, p]), hat)
    along_x, along_y, along_z = (
        jnp.sum(v, axis=0, keepdims=True)
        for v in (weight_ref[0] * change, hat * weight_ref[1] * change, hat * weight_ref[2] * change)
    )
    smooth = [-(SLOPE[p] * float(HAT[j, q]) * along_x + SLOPE[q] * along_y) for q in range(2)]
    return smooth + [-float(HAT[j, q]) * along_z for q in range(2)]


def restricted(points, value, weight, p):
    along_x, along_z, along_y = {}, {}, {}
    for i, j in points:
        v = value(i, j)
        along_x[j] = along_x.get(j, 0.0) + weight(0, i, j) * v
        if HAT[i, p]:
            along_y[i] = along_y.get(i, 0.0) + weight(1, i, j) * v
            along_z[j] = along_z.get(j, 0.0) + float(HAT[i, p]) * (weight(2, i, j) * v)
    y_sum = sum(float(HAT[i, p]) * total for i, total in along_y.items())
    smooth, slope = [], []
    for q in range(2):
        x_sum = sum(float(HAT[j, q]) * total for j, total in along_x.items() if HAT[j, q])
        smooth.append(-(SLOPE[p] * x_sum + SLOPE[q] * y_sum))
        slope.append(-sum(float(HAT[j, q]) * total for j, total in along_z.items() if HAT[j, q]))
    return smooth + slope


def x_corrections(even, gface_ref, outer_ref, inner_ref):
    ny = gface_ref.shape[2]
    change = {}
    for j in range(PTS):
        low = pick(even, outer_ref, inner_ref, j * ny, ny)
        high = pick(even, inner_ref, outer_ref, j * ny, ny)
        change[0, j] = -(gface_ref[0, j] * low)
        change[PTS - 1, j] = -(gface_ref[1, j] * high)
    return change


def y_corrections(gain_ref, gface_ref, below_ref, above_ref):
    ny, width = gain_ref.shape[2:]
    row = lax.broadcasted_iota(jnp.int32, (ny, width), 0)
    faces = {0: 0, PTS - 1: 1}
    change = {}
    for i in range(PTS):
        for j, at, ref in ((0, 0, below_ref), (PTS - 1, ny - 1, above_ref)):
            gain = gface_ref[faces[i], j] if i in faces else gain_ref[i, j]
            change[i, j] = -(gain * jnp.where(row == at, ref[0, i : i + 1], 0.0))
    return change


def face_change(change, weight, i, p, q):
    along_x = sum(float(HAT[j, q]) * (weight[0][j] * change[j]) for j in range(PTS) if HAT[j, q])
    smooth = SLOPE[p] * along_x
    slope = 0.0
    if HAT[i, p]:
        along_y = sum(weight[1][j] * change[j] for j in range(PTS))
        smooth = smooth + float(HAT[i, p]) * SLOPE[q] * along_y
        along_z = sum(float(HAT[j, q]) * (weight[2][j] * change[j]) for j in range(PTS) if HAT[j, q])
        slope = float(HAT[i, p]) * along_z
    return -smooth, -slope


def to_vertices(smooth, slope, restrict):
    return dot_split(jnp.concatenate([smooth, slope], axis=1), restrict)


def pick(even, first, second, at, count):
    return jnp.where(even, first[at : at + count], second[at : at + count])


def ahead_kernel(
    side_ref, sent_outer_ref, sent_inner_ref, gface_ref, restrict_ref, outer_ref, inner_ref,
    next_ref, top_ref,
):
    ny, width = gface_ref.shape[2:]
    even = side_ref[0] == 0
    change = [
        -(gface_ref[1, j] * pick(even, sent_inner_ref, sent_outer_ref, j * ny, ny)) for j in range(PTS)
    ]
    weight = [[pick(even, inner_ref, outer_ref, j * ny, ny) for j in range(PTS)]]
    smooth = jnp.concatenate([face_change(change, weight, 0, 1, q)[0] for q in range(2)], axis=0)
    hats = jnp.concatenate([restrict_ref[:width], restrict_ref[2 * width : 3 * width]], axis=0)
    corners = dot_split(smooth, hats)
    lower, upper = corners[:ny], corners[ny:]
    row = lax.broadcasted_iota(jnp.int32, lower.shape, 0)
    rows = lower + jnp.where(row == 0, 0.0, pltpu.roll(upper, 1, 0))
    next_ref[...] = jnp.concatenate([rows] * (next_ref.shape[0] // ny), axis=0)
    top_ref[...] = jnp.concatenate([upper[ny - 1 : ny]] * (top_ref.shape[1] // 128), axis=1)


def behind_kernel(
    side_ref, sent_outer_ref, sent_inner_ref, gface_ref, back_ref, sofar_ref, weights_ref, load_sums_ref,
    outer_ref, inner_ref,
    own_ref,
):
    ny, width = gface_ref.shape[2:]
    even = side_ref[0] == 0

    def rows(at):
        return pick(even, outer_ref, inner_ref, at, ny)

    change = [
        -(gface_ref[0, j] * pick(even, sent_outer_ref, sent_inner_ref, j * ny, ny)) for j in range(PTS)
    ]
    spread = [rows((2 * PTS + d) * ny) for d in range(2)]
    points = [rows((PTS + j) * ny) for j in range(PTS)]
    column = dot_split(jnp.concatenate([p * spread[1] for p in points], axis=0), back_ref[...])
    weight = [
        [rows(j * ny) for j in range(PTS)],
        contract(D.T, [p * spread[0] for p in points], -1),
        [column[j * ny : (j + 1) * ny] for j in range(PTS)],
    ]
    sums = restricted(
        [(i, j) for i in range(PTS) for j in range(PTS)],
        lambda i, j: sofar_ref[i, j],
        lambda d, i, j: weights_ref[d, i, j],
        0,
    )
    for q in range(2):
        smooth, slope = face_change(change, weight, PTS - 1, 1, q)
        own_ref[q] = sums[q] + load_sums_ref[q] + smooth
        own_ref[2 + q] = sums[2 + q] + slope


def coarse_kernel(
    side_ref, gface_ref, own_ref, edge_in_ref, weights_ref, restrict_ref, outer_ref, inner_ref,
    plane_ref, edge_ref,
):
    ny, width = gface_ref.shape[2:]
    even = side_ref[0] == 0
    change = x_corrections(even, gface_ref, outer_ref, inner_ref)
    sums = restricted(
        list(change),
        lambda i, j: change[i, j],
        lambda d, i, j: weights_ref[d, i, j],
        0,
    )
    base = PTS * ny

    def before(at, count):
        return pick(even, outer_ref, inner_ref, at, count)

    total = [sums[n] + own_ref[n] + before(base + n * ny, ny) for n in range(4)]
    extra = before(base + 4 * ny, PTS) + edge_in_ref[...]
    smooth = jnp.concatenate(total[:2] + [extra], axis=0)
    slope = jnp.concatenate(total[2:] + [pltpu.roll(extra, PTS - 2, 0)], axis=0)
    corners = to_vertices(smooth, slope, restrict_ref[...])
    lower, upper = corners[:ny], corners[ny : 2 * ny]
    extra = corners[2 * ny :]
    row = lax.broadcasted_iota(jnp.int32, lower.shape, 0)
    plane_ref[...] = lower + jnp.where(row == 0, extra[1:2], pltpu.roll(upper, 1, 0))
    edge_ref[0:1] = upper[ny - 1 : ny] + extra[4:5]
    edge_ref[1:2] = extra[5:6]
    edge_ref[2:3] = extra[0:1]


def beside_kernel(
    own_ref, gain_ref, gface_ref, weights_ref, restrict_ref, below_ref, above_ref,
    plane_ref,
):
    below_ref, above_ref = below_ref.at[1], above_ref.at[0]
    ny, width = gain_ref.shape[2:]
    change = y_corrections(gain_ref, gface_ref, below_ref, above_ref)
    sums = restricted(
        list(change),
        lambda i, j: change[i, j],
        lambda d, i, j: weights_ref[d, i, j],
        0,
    )
    smooth = jnp.concatenate(sums[:2], axis=0)
    slope = jnp.concatenate(sums[2:], axis=0)
    corners = to_vertices(smooth, slope, restrict_ref[...])
    lower, upper = corners[:ny], corners[ny:]
    row = lax.broadcasted_iota(jnp.int32, lower.shape, 0)
    plane_ref[...] = own_ref[...] + lower + jnp.where(row == 0, 0.0, pltpu.roll(upper, 1, 0))


def pressure_kernel(
    side_ref, sofar_ref, gain_ref, gface_ref, outer_ref, below_ref, above_ref, inner_ref,
    pressure_out, token_ref, pressure_ref, sem,
):
    token_ref[...] = jnp.zeros_like(token_ref)
    below_ref, above_ref = below_ref.at[1], above_ref.at[0]
    ny = sofar_ref.shape[2]
    even = side_ref[0] == 0
    changes = (
        x_corrections(even, gface_ref, outer_ref, inner_ref),
        y_corrections(gain_ref, gface_ref, below_ref, above_ref),
    )
    for i in range(PTS):
        for j in range(PTS):
            value = sofar_ref[i, j]
            for change in changes:
                if (i, j) in change:
                    value = value + change[i, j]
            pressure_ref[i, pl.ds(j, ny, stride=PTS)] = value
    copy = pltpu.make_async_copy(pressure_ref, pressure_out, sem)
    copy.start()
    copy.wait()


def last_kernel(own_ref, next_ref, top_ref, token_ref, below_ref, above_ref, coarse_ref):
    ny = own_ref.shape[0]
    row = lax.broadcasted_iota(jnp.int32, own_ref.shape, 0)
    total = own_ref[...] + next_ref[:ny] + token_ref[...]
    total = total + jnp.where(row == 0, top_ref[:, :128], 0.0)
    total = total + jnp.where(row == 0, below_ref[0:1], jnp.where(row == 1, below_ref[1:2], 0.0))
    total = total + jnp.where(row == ny - 1, above_ref[2:3], 0.0)
    coarse_ref[...] = total[:, : coarse_ref.shape[1]]


def call(body, outs, scratch, *args, spaces=None, out_spaces=None):
    spaces = spaces or [pltpu.SMEM if a.dtype == jnp.int32 else pltpu.VMEM for a in args]
    return pl.pallas_call(
        body,
        out_shape=[jax.ShapeDtypeStruct(s, F32) if isinstance(s, tuple) else s for s in outs],
        in_specs=[pl.BlockSpec(memory_space=m) for m in spaces],
        out_specs=[pl.BlockSpec(memory_space=m) for m in out_spaces or [pltpu.VMEM] * len(outs)],
        scratch_shapes=[pltpu.VMEM(s, F32) if isinstance(s, tuple) else s for s in scratch],
        compiler_params=pltpu.CompilerParams(vmem_limit_bytes=16 * 1024 * 1024),
    )(*args)


def from_y(faces):
    size = lax.axis_size("sub")
    up = lax.ppermute(faces, "sub", [(i, (i + 1) % size) for i in range(size)])
    if size == 2:
        return up, up
    return up, lax.ppermute(faces, "sub", [(i, (i - 1) % size) for i in range(size)])


def inner_pairs(size):
    return [(i, i ^ 1) for i in range(size)]


def outer_pairs(size):
    return [(i, (i + 1) % size if i % 2 else (i - 1) % size) for i in range(size)]


def to_x(outer, inner):
    size = lax.axis_size("dom")
    outer = lax.ppermute(outer, "dom", outer_pairs(size))
    inner = lax.ppermute(inner, "dom", inner_pairs(size))
    return outer, inner


def two_on(rows, top):
    size, rest = lax.axis_size("dom"), lax.axis_size("sub")
    rows = lax.ppermute(rows, "dom", [(i, (i + 2) % size) for i in range(size)])
    pairs = [
        (i * rest + k, (i + 2) % size * rest + (k + 1) % rest) for i in range(size) for k in range(rest)
    ]
    return rows, lax.ppermute(top, ("dom", "sub"), pairs)


def shards(element_load, mobility, metric):
    _, _, ny, _, width = element_load.shape
    load = element_load.reshape(PTS, ny * PTS, width)
    mob = mobility.reshape(PTS, ny * PTS, width)
    metric = metric[:, 0]
    side = (lax.axis_index("dom") % 2).astype(jnp.int32).reshape(1)
    def in_hbm(*arrays):
        return [pltpu.with_memory_space_constraint(a, pltpu.HBM) for a in arrays]

    grad, back = column_tables(width)
    restrict = restrict_table(width)
    field = (PTS, PTS, ny, width)
    face = (PTS, ny, width)
    ends = (2, PTS, PTS, width)
    spread, yface = call(
        edge_kernel,
        [(3, ny, width), (2, 5, PTS, width)],
        [metric.shape, ends, ends, pltpu.SemaphoreType.DMA((5,))],
        *in_hbm(metric, mob, load),
        spaces=[pltpu.HBM] * 3,
    )
    below, above = from_y(yface)
    still = (2 * (PTS + 1) * ny, width)
    fields, xface, factor, still_outer, still_inner, weights, load_sums = call(
        diag_kernel,
        [
            (2,) + field, (2, 2) + face, (2, 2, PTS, width), still, still,
            (3,) + field, (4, ny, width),
        ],
        [],
        side, load, mob, spread,
    )
    rows = (2 * PTS * ny + 2 * PTS, width)
    outer, inner = to_x(*call(merge_kernel, [rows, rows], [], side, xface, factor, below, above))
    still_outer, still_inner = to_x(still_outer, still_inner)
    faces = (2,) + face
    rough, value, partial, gain, out, pair, edge_weights = call(
        inside_kernel,
        [
            (2,) + faces, field, field, field, field, (2,) + field,
            (2, 3, PTS, width),
        ],
        [face],
        fields, mob, spread, grad, back, below, above,
    )
    rows = ((PTS + 4) * ny + PTS, width)
    sent_outer, sent_inner, yface, gface, sofar, edge = call(
        faces_kernel,
        [rows, rows, (2, 1, PTS, width), faces, field, (PTS, width)],
        [((2 * PTS + 4) * ny, width), field],
        side, rough, value, out, pair, mob, spread, grad, back, below, above,
        partial, gain, weights, load_sums, edge_weights, outer, inner,
    )
    outer, inner = to_x(sent_outer, sent_inner)
    onward, top = call(
        ahead_kernel,
        [(3 * ny, 128), (1, (2 * PTS + 1) * 128)],
        [],
        side, sent_outer, sent_inner, gface, restrict, still_outer, still_inner,
    )
    (own,) = call(
        behind_kernel,
        [(4, ny, width)],
        [],
        side, sent_outer, sent_inner, gface, back, sofar, weights, load_sums, still_outer, still_inner,
    )
    onward, top = two_on(onward, top)
    below, above = from_y(yface)
    own_rows, tops = call(
        coarse_kernel,
        [(ny, 128), (3, 128)],
        [],
        side, gface, own, edge, weights, restrict, outer, inner,
    )
    (own_rows,) = call(
        beside_kernel, [(ny, 128)], [], own_rows, gain, gface, weights, restrict, below, above
    )
    pressure, token = call(
        pressure_kernel,
        [(PTS, ny * PTS, width), (1, 128)],
        [(PTS, ny * PTS, width), pltpu.SemaphoreType.DMA(())],
        side, sofar, gain, gface, outer, below, above, inner,
        out_spaces=[pltpu.HBM, pltpu.VMEM],
    )
    row_below, row_above = from_y(tops)
    (coarse,) = call(last_kernel, [(ny, width // PTS + 1)], [], own_rows, onward, top, token, row_below, row_above)
    return pressure.reshape(element_load.shape), coarse[None]


def solution(mesh):
    in_specs = (
        P("dom", None, "sub", None, None),
        P("dom", None, "sub", None, None),
        P(None, "dom", "sub", None),
    )
    out_specs = (P("dom", None, "sub", None, None), P("dom", "sub", None))
    return jax.shard_map(shards, mesh=mesh, in_specs=in_specs, out_specs=out_specs, check_vma=False)
```

```python
import jax
import jax.numpy as jnp
import ml_dtypes
import numpy as np
from jax import lax
from jax.experimental import pallas as pl
from jax.experimental.pallas import tpu as pltpu
from jax.sharding import PartitionSpec as P

GLL_NODES = np.array(
    [
        -1.0,
        -0.8717401485096066,
        -0.5917001814331423,
        -0.2092992179024789,
        0.2092992179024789,
        0.5917001814331423,
        0.8717401485096066,
        1.0,
    ]
)
GLL_WEIGHTS = np.array(
    [
        0.03571428571428571,
        0.2107042271435061,
        0.3411226924835044,
        0.4124587946587038,
        0.4124587946587038,
        0.3411226924835044,
        0.2107042271435061,
        0.03571428571428571,
    ]
)
THETA = 1.65
DELTA = 1.35
RHO_FIRST = DELTA / THETA
RHO_SECOND = 1.0 / (2.0 * THETA / DELTA - RHO_FIRST)
KEEP = 1.0 + RHO_SECOND * RHO_FIRST
GAIN = 2.0 * RHO_SECOND / DELTA
PTS = 8
F32 = jnp.float32


def derivative_table():
    identity = np.eye(8)
    differences = GLL_NODES[:, None] - GLL_NODES[None, :] + identity
    barycentric = 1.0 / np.prod(differences, axis=1)
    matrix = barycentric[None, :] / barycentric[:, None] / differences
    matrix = matrix * (1.0 - identity)
    row_sums = np.sum(matrix, axis=1)
    return matrix - identity * row_sums[:, None]


D = derivative_table()
W = GLL_WEIGHTS
HAT = np.stack([(1.0 - GLL_NODES) / 8.0, (1.0 + GLL_NODES) / 8.0], axis=1)
SLOPE = (-0.125, 0.125)


def tiled(matrix, width):
    column = lax.broadcasted_iota(jnp.int32, (PTS, width), 1) % PTS
    row = lax.broadcasted_iota(jnp.int32, (PTS, width), 0)
    total = jnp.zeros((PTS, width), F32)
    for c in range(PTS):
        lines = jnp.zeros((PTS, width), F32)
        for r in range(PTS):
            lines = jnp.where(row == r, float(matrix[r, c]), lines)
        total = jnp.where(column == c, lines, total)
    return total


def by_row(values, width):
    return tiled(np.tile(np.asarray(values)[:, None], (1, PTS)), width)


def cell_blocks(rows):
    width = rows.shape[1]
    cell = lax.broadcasted_iota(jnp.int32, rows.shape, 1) // PTS
    return jnp.concatenate(
        [jnp.where(cell == g, rows, 0.0) for g in range(width // PTS)], axis=0
    )


def paired_here(b):
    high, low = halves(b)
    return jnp.concatenate(
        [
            jnp.concatenate([high, low], axis=1),
            jnp.concatenate([high, jnp.zeros_like(low)], axis=1),
        ],
        axis=0,
    )


def paired(b):
    b = np.asarray(b, np.float32)
    high = b.astype(ml_dtypes.bfloat16)
    low = (b - high.astype(np.float32)).astype(ml_dtypes.bfloat16)
    return jnp.asarray(np.block([[high, low], [high, np.zeros_like(low)]]))


def column_tables(width):
    cells = np.eye(width // PTS)
    return paired(np.kron(cells, D.T)), paired(np.kron(cells, D))


def restrict_table(width):
    cells = width // PTS
    hat = np.zeros((width, 128))
    slope = np.zeros((width, 128))
    for c in range(cells):
        rows = slice(c * PTS, (c + 1) * PTS)
        hat[rows, c], hat[rows, c + 1] = HAT[:, 0], HAT[:, 1]
        slope[rows, c], slope[rows, c + 1] = SLOPE
    return paired(np.concatenate([hat, slope]))


def halves(a):
    high = a.astype(jnp.bfloat16)
    return high, (a - high.astype(F32)).astype(jnp.bfloat16)


def dot_split(a, b_pair):
    both = jnp.dot(
        jnp.concatenate(halves(a), axis=1), b_pair, preferred_element_type=F32
    )
    n = both.shape[1] // 2
    return both[:, :n] + both[:, n:]


def contract(matrix, lines, parity):
    n = len(lines)
    half = n // 2
    plus = [lines[c] + lines[n - 1 - c] for c in range(half)]
    minus = [lines[c] - lines[n - 1 - c] for c in range(half)]
    top, low = [], []
    for r in range(half):
        even = sum(float(0.5 * (matrix[r, c] + matrix[r, n - 1 - c])) * plus[c] for c in range(half))
        odd = sum(float(0.5 * (matrix[r, c] - matrix[r, n - 1 - c])) * minus[c] for c in range(half))
        top.append(even + odd)
        low.append(even - odd if parity > 0 else odd - even)
    return top + low[::-1]


def spread_metric(metric, weight_row):
    _, rows, cells = metric.shape
    width = weight_row.shape[1]
    cell = lax.broadcasted_iota(jnp.int32, (rows, width), 1) // PTS
    fill = jnp.zeros((rows, width - cells), F32)
    spread = [
        jnp.take_along_axis(jnp.concatenate([metric[d], fill], axis=1), cell, axis=1, mode="promise_in_bounds")
        for d in range(3)
    ]
    return [v * weight_row[:1] for v in spread], spread[2]


def column_masks(shape):
    lane = lax.broadcasted_iota(jnp.int32, shape, len(shape) - 1)
    up = (lane % PTS == PTS - 1) & (lane != shape[-1] - 1)
    down = (lane % PTS == 0) & (lane != 0)
    return up, down


def sum_z(v, masks):
    width = v.shape[-1]
    axis = v.ndim - 1
    up = pltpu.roll(v, width - 1, axis)
    down = pltpu.roll(v, 1, axis)
    return v + jnp.where(masks[0], up, jnp.where(masks[1], down, 0.0))


def sum_y_local(ref, ny):
    for i in range(PTS):
        low, high = ref[i, 0], ref[i, PTS - 1]
        row = lax.broadcasted_iota(jnp.int32, low.shape, 0)
        ref[i, PTS - 1] = high + jnp.where(row == ny - 1, 0.0, pltpu.roll(low, ny - 1, 0))
        ref[i, 0] = low + jnp.where(row == 0, 0.0, pltpu.roll(high, 1, 0))


def edge_planes(ref, ny):
    low = jnp.concatenate([ref[i, 0, 0:1] for i in range(PTS)], axis=0)
    high = jnp.concatenate([ref[i, PTS - 1, ny - 1 : ny] for i in range(PTS)], axis=0)
    return low, high


def plane(ref, ny):
    return lambda i, j: ref[i, pl.ds(j, ny, stride=PTS)]


def edge_kernel(metric_in, mob_in, load_in, spread_ref, yface_ref, metric_ref, mob_ref, load_ref, sems):
    ny, width = spread_ref.shape[1:]
    ends = (0, PTS - 1)
    copies = [pltpu.make_async_copy(metric_in, metric_ref, sems.at[0])]
    for n, (source, target) in enumerate(((mob_in, mob_ref), (load_in, load_ref))):
        for s, e in enumerate((0, ny - 1)):
            copies.append(
                pltpu.make_async_copy(
                    source.at[:, pl.ds(e * PTS, PTS)], target.at[s], sems.at[1 + 2 * n + s]
                )
            )
    for copy in copies:
        copy.start()
    masks = column_masks((PTS, width))
    weight_row = tiled(np.tile(W[None], (PTS, 1)), width)
    row_weight = by_row(W, width)
    squared = paired_here(cell_blocks(tiled(D * D, width)))
    squares = [by_row(D[a] ** 2, width) for a in range(PTS)]
    for copy in copies:
        copy.wait()
    spread, cell_metric = spread_metric(metric_ref[...], weight_row)
    for d in range(3):
        spread_ref[d] = spread[d]
    points = [mob_ref[s, :, ends[s]] * (float(W[ends[s]]) * row_weight) for s in range(2)]
    columns = dot_split(
        jnp.concatenate([p * weight_row for p in points], axis=0), squared
    )
    for s, e in enumerate((0, ny - 1)):
        j = ends[s]
        scale = [spread[d][e : e + 1] for d in range(3)]
        along = sum(squares[a] * points[s][a : a + 1] for a in range(PTS))
        total = along * scale[0]
        sums = [
            sum(float(D[b, j] ** power * W[b]) * mob_ref[s, :, b] for b in range(PTS))
            * row_weight
            * scale[1]
            for power in (1, 2)
        ]
        yface_ref[s, 2] = points[s] * scale[0]
        yface_ref[s, 3] = points[s] * scale[2]
        yface_ref[s, 4] = sums[0]
        column = columns[s * PTS : (s + 1) * PTS] * cell_metric[e : e + 1]
        yface_ref[s, 1] = sum_z(total + sums[1] + column, masks)
    for s in range(2):
        yface_ref[s, 0] = sum_z(load_ref[s, :, ends[s]], masks)


def diag_kernel(
    side_ref, load_ref, mob_ref, spread_ref,
    fields_ref, xface_ref, factor_ref, to_outer_ref, to_inner_ref, weights_ref, sums_ref,
):
    ny, width = fields_ref.shape[3:]
    spread = [spread_ref[d] for d in range(3)]
    square = D * D
    squared = paired_here(cell_blocks(tiled(square, width)))
    back = paired_here(cell_blocks(tiled(D, width)))
    mob, load = plane(mob_ref, ny), plane(load_ref, ny)
    diag_ref = fields_ref.at[1]
    even = side_ref[0] == 0

    def post(at, low, high):
        to_inner_ref[at : at + ny] = jnp.where(even, high, low)
        to_outer_ref[at : at + ny] = jnp.where(even, low, high)

    for d in (1, 2):
        post((2 * PTS + d - 1) * ny, spread[d], spread[d])
    for j in range(PTS):
        factor = [mob(i, j) * (float(W[i] * W[j]) * spread[0]) for i in range(PTS)]
        post(j * ny, *(sum(float(D[a, i]) * factor[a] for a in range(PTS)) for i in (0, PTS - 1)))
        post((PTS + j) * ny, *(float(W[i] * W[j]) * mob(i, j) for i in (0, PTS - 1)))
        for i, value in enumerate(contract(square.T, factor, 1)):
            diag_ref[i, j] = value
        for i, value in enumerate(contract(D.T, factor, -1)):
            weights_ref[0, i, j] = value
    for i in range(PTS):
        factor = [mob(i, j) * (float(W[i] * W[j]) * spread[1]) for j in range(PTS)]
        for j, value in enumerate(contract(square.T, factor, 1)):
            diag_ref[i, j] += value
        for j, value in enumerate(contract(D.T, factor, -1)):
            weights_ref[1, i, j] = value
    for i in range(PTS):
        factor = jnp.concatenate(
            [mob(i, j) * (float(W[i] * W[j]) * spread[2]) for j in range(PTS)], axis=0
        )
        diag_ref[i] += dot_split(factor, squared).reshape(PTS, ny, width)
        weights_ref[2, i] = dot_split(factor, back).reshape(PTS, ny, width)
        fields_ref[0, i] = jnp.stack([load(i, j) for j in range(PTS)], axis=0)
    masks = column_masks((PTS, ny, width))
    for f in range(2):
        for i in range(PTS):
            fields_ref[f, i] = sum_z(fields_ref[f, i], masks)
        sum_y_local(fields_ref.at[f], ny)
        xface_ref[f, 0] = fields_ref[f, 0]
        xface_ref[f, 1] = fields_ref[f, PTS - 1]
    row_weight = by_row(W, width)
    for s, i in enumerate((0, PTS - 1)):
        for n, e in enumerate((0, ny - 1)):
            points = mob_ref[i, e * PTS : (e + 1) * PTS] * (float(W[i]) * row_weight)
            factor_ref[s, n] = points * spread[1][e : e + 1]
    zero = jnp.zeros((ny, width), F32)
    sums = [zero] * 4
    for i in range(PTS):
        for q in range(2):
            from_load = sum(float(HAT[j, q]) * load(i, j) for j in range(PTS))
            for p in range(2):
                if HAT[i, p]:
                    sums[2 * p + q] = sums[2 * p + q] + float(HAT[i, p]) * from_load
    for n in range(4):
        sums_ref[n] = sums[n]


def merge_kernel(side_ref, xface_ref, factor_ref, below_ref, above_ref, outer_ref, inner_ref):
    below_ref, above_ref = below_ref.at[1], above_ref.at[0]
    even = side_ref[0] == 0
    fields, _, _, ny, width = xface_ref.shape
    row = lax.broadcasted_iota(jnp.int32, (ny, width), 0)
    for f in range(fields):
        for j in range(PTS):
            low, high = xface_ref[f, 0, j], xface_ref[f, 1, j]
            if j == 0:
                low = low + jnp.where(row == 0, below_ref[f, 0:1], 0.0)
                high = high + jnp.where(row == 0, below_ref[f, PTS - 1 : PTS], 0.0)
            if j == PTS - 1:
                low = low + jnp.where(row == ny - 1, above_ref[f, 0:1], 0.0)
                high = high + jnp.where(row == ny - 1, above_ref[f, PTS - 1 : PTS], 0.0)
            at = (f * PTS + j) * ny
            inner_ref[at : at + ny] = jnp.where(even, high, low)
            outer_ref[at : at + ny] = jnp.where(even, low, high)
    for n in range(2):
        at = fields * PTS * ny + n * PTS
        low, high = factor_ref[0, n], factor_ref[1, n]
        inner_ref[at : at + PTS] = jnp.where(even, high, low)
        outer_ref[at : at + PTS] = jnp.where(even, low, high)


def inside_kernel(
    fields_ref, mob_ref, spread_ref, grad_ref, back_ref, below_ref, above_ref,
    rough_ref, value_ref, partial_ref, gain_ref, out_ref, pair_ref, edge_weights_ref,
    work_ref,
):
    below_ref, above_ref = below_ref.at[1], above_ref.at[0]
    ny, width = out_ref.shape[2:]
    spread = [spread_ref[d] for d in range(3)]
    mob = plane(mob_ref, ny)
    row = lax.broadcasted_iota(jnp.int32, (ny, width), 0)
    zero = jnp.zeros((ny, width), F32)
    for i in range(PTS):
        for j in range(PTS):
            sums = [fields_ref[f, i, j] for f in range(2)]
            for f in range(2):
                if j == 0:
                    sums[f] += jnp.where(row == 0, below_ref[f, i : i + 1], 0.0)
                if j == PTS - 1:
                    sums[f] += jnp.where(row == ny - 1, above_ref[f, i : i + 1], 0.0)
            if i in (0, PTS - 1):
                for f in range(2):
                    rough_ref[f, 0 if i == 0 else 1, j] = sums[f]
                value_ref[i, j] = partial_ref[i, j] = gain_ref[i, j] = zero
            else:
                value_ref[i, j], partial_ref[i, j], gain_ref[i, j] = first_step(*sums)
    grad, back = grad_ref[...], back_ref[...]
    for j in range(PTS):
        factor = [mob(i, j) * (float(W[i] * W[j]) * spread[0]) for i in range(PTS)]
        for n, p in enumerate((0, PTS - 1)):
            coupling = contract(D.T, [float(D[a, p]) * factor[a] for a in range(PTS)], -1)
            for i in range(PTS):
                pair_ref[n, i, j] = coupling[i]
        flux = contract(D, [value_ref[i, j] for i in range(PTS)], -1)
        flux = [flux[i] * factor[i] for i in range(PTS)]
        for i, value in enumerate(contract(D.T, flux, -1)):
            out_ref[i, j] = value
    for i in range(1, PTS - 1):
        flux = contract(D, [value_ref[i, j] for j in range(PTS)], -1)
        flux = [flux[j] * (mob(i, j) * (float(W[i] * W[j]) * spread[1])) for j in range(PTS)]
        for j, value in enumerate(contract(D.T, flux, -1)):
            out_ref[i, j] += value
        work_ref[...] = dot_split(value_ref[i].reshape(PTS * ny, width), grad).reshape(PTS, ny, width)
        for j in range(PTS):
            work_ref[j] *= mob(i, j) * (float(W[i] * W[j]) * spread[2])
        out_ref[i] += dot_split(work_ref[...].reshape(PTS * ny, width), back).reshape(PTS, ny, width)
    for t, ref in enumerate((below_ref, above_ref)):
        edge_weights_ref[t, 0] = sum(by_row(D[a], width) * ref[2, a : a + 1] for a in range(PTS))
        edge_weights_ref[t, 1] = ref[4]
        edge_weights_ref[t, 2] = dot_split(ref[3], back)


def first_step(right, diagonal):
    inverse = pl.reciprocal(diagonal)
    scaled = inverse * right
    value = scaled * (1.0 / THETA)
    return value, KEEP * value + GAIN * scaled, GAIN * inverse


def faces_kernel(
    side_ref, rough_ref, value_ref, out_ref, pair_ref, mob_ref, spread_ref, grad_ref, back_ref,
    below_ref, above_ref, partial_ref, gain_ref, weights_ref, load_sums_ref, edge_weights_ref,
    outer_ref, inner_ref,
    to_outer_ref, to_inner_ref, yface_ref, gface_ref, sofar_ref, edge_ref, line_ref, work_ref,
):
    below_ref, above_ref = below_ref.at[1], above_ref.at[0]
    even = side_ref[0] == 0
    ny, width = out_ref.shape[2:]
    spread = [spread_ref[d] for d in range(3)]
    mob = plane(mob_ref, ny)
    ends = (0, PTS - 1)
    rows = (0, ny - 1)
    row = lax.broadcasted_iota(jnp.int32, (ny, width), 0)
    masks = column_masks((ny, width))

    def arrived(at, count):
        inner, outer = inner_ref[at : at + count], outer_ref[at : at + count]
        return jnp.where(even, outer, inner), jnp.where(even, inner, outer)

    value = [[None] * PTS, [None] * PTS]
    pface = [[None] * PTS, [None] * PTS]
    gface = [[None] * PTS, [None] * PTS]
    for j in range(PTS):
        load = arrived(j * ny, ny)
        diagonal = arrived((PTS + j) * ny, ny)
        for s in range(2):
            value[s][j], pface[s][j], gface[s][j] = first_step(
                rough_ref[0, s, j] + load[s], rough_ref[1, s, j] + diagonal[s]
            )
            gface_ref[s, j] = gface[s][j]
    lines = [value[s][j] for s in range(2) for j in range(PTS)]
    factors = [
        mob(ends[s], j) * (float(W[ends[s]] * W[j]) * spread[2]) for s in range(2) for j in range(PTS)
    ]
    for s in range(2):
        for t, ref in enumerate((below_ref, above_ref)):
            lines.append(value[s][ends[t]])
            factors.append(jnp.broadcast_to(ref[3, ends[s] : ends[s] + 1], (ny, width)))
    flux = dot_split(jnp.concatenate(lines, axis=0), grad_ref[...]) * jnp.concatenate(factors, axis=0)
    line_ref[...] = dot_split(flux, back_ref[...])
    edge_y = [[None, None], [None, None]]
    total = [[None] * PTS, [None] * PTS]
    for s in range(2):
        gradient = contract(D, value[s], -1)
        flux = [
            gradient[j] * (mob(ends[s], j) * (float(W[ends[s]] * W[j]) * spread[1])) for j in range(PTS)
        ]
        total[s] = contract(D.T, flux, -1)
        for t in range(2):
            factor = arrived(2 * PTS * ny + t * PTS, PTS)[s]
            edge_y[s][t] = sum(
                float(D[j, ends[t]]) * (gradient[j] * factor[j : j + 1]) for j in range(PTS)
            )[rows[t] : rows[t] + 1]
    for j in range(PTS):
        across = [
            out_ref[i, j] + (pair_ref[0, i, j] * value[0][j] + pair_ref[1, i, j] * value[1][j])
            for i in range(PTS)
        ]
        total[0][j] += across[0]
        total[1][j] += across[PTS - 1]
        for i in range(1, PTS - 1):
            work_ref[i, j] = across[i]
    for s in range(2):
        for j in range(PTS):
            at = (s * PTS + j) * ny
            total[s][j] += line_ref[at : at + ny]
    ymessage = []
    for t in range(2):
        j = ends[t]
        edge = [total[0][j]] + [work_ref[i, j] for i in range(1, PTS - 1)] + [total[1][j]]
        edge = [v[rows[t] : rows[t] + 1] for v in edge]
        edge[0] += edge_y[0][t]
        edge[PTS - 1] += edge_y[1][t]
        ymessage.append(sum_z(jnp.concatenate(edge, axis=0), column_masks((PTS, width))))
        yface_ref[t, 0] = ymessage[t]
    extra = [[None, None], [None, None]]
    for t, ref in enumerate((below_ref, above_ref)):
        j = ends[t]
        points = [value[0][j]] + [value_ref[i, j] for i in range(1, PTS - 1)] + [value[1][j]]
        flux = contract(D, points, -1)
        flux = contract(D.T, [flux[i] * ref[2, i : i + 1] for i in range(PTS)], -1)
        for s in range(2):
            at = (2 * PTS + 2 * s + t) * ny
            extra[s][t] = sum_z(flux[ends[s]] + line_ref[at : at + ny], masks)
            extra[s][t] = jnp.where(row == rows[t], extra[s][t], 0.0)
    for s in range(2):
        for j in range(PTS):
            total[s][j] = sum_z(total[s][j], masks)
        low, high = total[s][0], total[s][PTS - 1]
        total[s][PTS - 1] = high + jnp.where(row == ny - 1, 0.0, pltpu.roll(low, ny - 1, 0))
        total[s][0] = low + jnp.where(row == 0, 0.0, pltpu.roll(high, 1, 0))
    for j in range(PTS):
        low, high = total[0][j], total[1][j]
        if j in ends:
            t = ends.index(j)
            low, high = low + extra[0][t], high + extra[1][t]
        to_inner_ref[j * ny : (j + 1) * ny] = jnp.where(even, high, low)
        to_outer_ref[j * ny : (j + 1) * ny] = jnp.where(even, low, high)
        for s in range(2):
            sofar_ref[ends[s], j] = pface[s][j] - gface[s][j] * total[s][j]
    for i in range(1, PTS - 1):
        lines = [sum_z(work_ref[i, j], masks) for j in range(PTS)]
        low, high = lines[0], lines[PTS - 1]
        lines[PTS - 1] = high + jnp.where(row == ny - 1, 0.0, pltpu.roll(low, ny - 1, 0))
        lines[0] = low + jnp.where(row == 0, 0.0, pltpu.roll(high, 1, 0))
        for j in range(PTS):
            sofar_ref[i, j] = partial_ref[i, j] - gain_ref[i, j] * lines[j]
    sums = restricted(
        [(i, j) for i in range(PTS) for j in range(PTS)],
        lambda i, j: sofar_ref[i, j],
        lambda d, i, j: weights_ref[d, i, j],
        1,
    )
    for q in range(2):
        sums[q] = sums[q] + load_sums_ref[2 + q]
    base = PTS * ny
    changes = []
    for t in range(2):
        j = ends[t]
        gain = [gface[0][j]] + [gain_ref[i, j] for i in range(1, PTS - 1)] + [gface[1][j]]
        gain = jnp.concatenate([g[rows[t] : rows[t] + 1] for g in gain], axis=0)
        change = -(gain * ymessage[t])
        changes += edge_change(change, edge_weights_ref.at[t], ends[1 - t], 1)
        if t == 0:
            own = edge_change(change, edge_weights_ref.at[t], ends[1 - t], 0)
            zero = jnp.zeros_like(own[1])
            edge_ref[...] = jnp.concatenate([zero, own[1], zero, own[3]] + [zero] * 4, axis=0)
    changes = jnp.concatenate(changes, axis=0)
    rest = jnp.concatenate(sums + [changes], axis=0)
    to_outer_ref[base:] = rest
    to_inner_ref[base:] = rest


def edge_change(change, weight_ref, j, p):
    upper = lax.broadcasted_iota(jnp.int32, change.shape, 0)
    hat = jnp.zeros_like(change)
    for i in range(PTS):
        hat = jnp.where(upper == i, float(HAT[i, p]), hat)
    along_x, along_y, along_z = (
        jnp.sum(v, axis=0, keepdims=True)
        for v in (weight_ref[0] * change, hat * weight_ref[1] * change, hat * weight_ref[2] * change)
    )
    smooth = [-(SLOPE[p] * float(HAT[j, q]) * along_x + SLOPE[q] * along_y) for q in range(2)]
    return smooth + [-float(HAT[j, q]) * along_z for q in range(2)]


def restricted(points, value, weight, p):
    along_x, along_z, along_y = {}, {}, {}
    for i, j in points:
        v = value(i, j)
        along_x[j] = along_x.get(j, 0.0) + weight(0, i, j) * v
        if HAT[i, p]:
            along_y[i] = along_y.get(i, 0.0) + weight(1, i, j) * v
            along_z[j] = along_z.get(j, 0.0) + float(HAT[i, p]) * (weight(2, i, j) * v)
    y_sum = sum(float(HAT[i, p]) * total for i, total in along_y.items())
    smooth, slope = [], []
    for q in range(2):
        x_sum = sum(float(HAT[j, q]) * total for j, total in along_x.items() if HAT[j, q])
        smooth.append(-(SLOPE[p] * x_sum + SLOPE[q] * y_sum))
        slope.append(-sum(float(HAT[j, q]) * total for j, total in along_z.items() if HAT[j, q]))
    return smooth + slope


def x_corrections(even, gface_ref, outer_ref, inner_ref):
    ny = gface_ref.shape[2]
    change = {}
    for j in range(PTS):
        low = pick(even, outer_ref, inner_ref, j * ny, ny)
        high = pick(even, inner_ref, outer_ref, j * ny, ny)
        change[0, j] = -(gface_ref[0, j] * low)
        change[PTS - 1, j] = -(gface_ref[1, j] * high)
    return change


def y_corrections(gain_ref, gface_ref, below_ref, above_ref):
    ny, width = gain_ref.shape[2:]
    row = lax.broadcasted_iota(jnp.int32, (ny, width), 0)
    faces = {0: 0, PTS - 1: 1}
    change = {}
    for i in range(PTS):
        for j, at, ref in ((0, 0, below_ref), (PTS - 1, ny - 1, above_ref)):
            gain = gface_ref[faces[i], j] if i in faces else gain_ref[i, j]
            change[i, j] = -(gain * jnp.where(row == at, ref[0, i : i + 1], 0.0))
    return change


def face_change(change, weight, i, p, q):
    along_x = sum(float(HAT[j, q]) * (weight[0][j] * change[j]) for j in range(PTS) if HAT[j, q])
    smooth = SLOPE[p] * along_x
    slope = 0.0
    if HAT[i, p]:
        along_y = sum(weight[1][j] * change[j] for j in range(PTS))
        smooth = smooth + float(HAT[i, p]) * SLOPE[q] * along_y
        along_z = sum(float(HAT[j, q]) * (weight[2][j] * change[j]) for j in range(PTS) if HAT[j, q])
        slope = float(HAT[i, p]) * along_z
    return -smooth, -slope


def to_vertices(smooth, slope, restrict):
    return dot_split(jnp.concatenate([smooth, slope], axis=1), restrict)


def pick(even, first, second, at, count):
    return jnp.where(even, first[at : at + count], second[at : at + count])


def ahead_kernel(
    side_ref, sent_outer_ref, sent_inner_ref, gface_ref, restrict_ref, outer_ref, inner_ref,
    next_ref, top_ref,
):
    ny, width = gface_ref.shape[2:]
    even = side_ref[0] == 0
    change = [
        -(gface_ref[1, j] * pick(even, sent_inner_ref, sent_outer_ref, j * ny, ny)) for j in range(PTS)
    ]
    weight = [[pick(even, inner_ref, outer_ref, j * ny, ny) for j in range(PTS)]]
    smooth = jnp.concatenate([face_change(change, weight, 0, 1, q)[0] for q in range(2)], axis=0)
    hats = jnp.concatenate([restrict_ref[:width], restrict_ref[2 * width : 3 * width]], axis=0)
    corners = dot_split(smooth, hats)
    lower, upper = corners[:ny], corners[ny:]
    row = lax.broadcasted_iota(jnp.int32, lower.shape, 0)
    rows = lower + jnp.where(row == 0, 0.0, pltpu.roll(upper, 1, 0))
    next_ref[...] = jnp.concatenate([rows] * (next_ref.shape[0] // ny), axis=0)
    top_ref[...] = jnp.concatenate([upper[ny - 1 : ny]] * (top_ref.shape[1] // 128), axis=1)


def behind_kernel(
    side_ref, sent_outer_ref, sent_inner_ref, gface_ref, back_ref, sofar_ref, weights_ref, load_sums_ref,
    outer_ref, inner_ref,
    own_ref,
):
    ny, width = gface_ref.shape[2:]
    even = side_ref[0] == 0

    def rows(at):
        return pick(even, outer_ref, inner_ref, at, ny)

    change = [
        -(gface_ref[0, j] * pick(even, sent_outer_ref, sent_inner_ref, j * ny, ny)) for j in range(PTS)
    ]
    spread = [rows((2 * PTS + d) * ny) for d in range(2)]
    points = [rows((PTS + j) * ny) for j in range(PTS)]
    column = dot_split(jnp.concatenate([p * spread[1] for p in points], axis=0), back_ref[...])
    weight = [
        [rows(j * ny) for j in range(PTS)],
        contract(D.T, [p * spread[0] for p in points], -1),
        [column[j * ny : (j + 1) * ny] for j in range(PTS)],
    ]
    sums = restricted(
        [(i, j) for i in range(PTS) for j in range(PTS)],
        lambda i, j: sofar_ref[i, j],
        lambda d, i, j: weights_ref[d, i, j],
        0,
    )
    for q in range(2):
        smooth, slope = face_change(change, weight, PTS - 1, 1, q)
        own_ref[q] = sums[q] + load_sums_ref[q] + smooth
        own_ref[2 + q] = sums[2 + q] + slope


def coarse_kernel(
    side_ref, gface_ref, own_ref, edge_in_ref, weights_ref, restrict_ref, outer_ref, inner_ref,
    plane_ref, edge_ref,
):
    ny, width = gface_ref.shape[2:]
    even = side_ref[0] == 0
    change = x_corrections(even, gface_ref, outer_ref, inner_ref)
    sums = restricted(
        list(change),
        lambda i, j: change[i, j],
        lambda d, i, j: weights_ref[d, i, j],
        0,
    )
    base = PTS * ny

    def before(at, count):
        return pick(even, outer_ref, inner_ref, at, count)

    total = [sums[n] + own_ref[n] + before(base + n * ny, ny) for n in range(4)]
    extra = before(base + 4 * ny, PTS) + edge_in_ref[...]
    smooth = jnp.concatenate(total[:2] + [extra], axis=0)
    slope = jnp.concatenate(total[2:] + [pltpu.roll(extra, PTS - 2, 0)], axis=0)
    corners = to_vertices(smooth, slope, restrict_ref[...])
    lower, upper = corners[:ny], corners[ny : 2 * ny]
    extra = corners[2 * ny :]
    row = lax.broadcasted_iota(jnp.int32, lower.shape, 0)
    plane_ref[...] = lower + jnp.where(row == 0, extra[1:2], pltpu.roll(upper, 1, 0))
    edge_ref[0:1] = upper[ny - 1 : ny] + extra[4:5]
    edge_ref[1:2] = extra[5:6]
    edge_ref[2:3] = extra[0:1]


def beside_kernel(
    own_ref, gain_ref, gface_ref, weights_ref, restrict_ref, below_ref, above_ref,
    plane_ref,
):
    below_ref, above_ref = below_ref.at[1], above_ref.at[0]
    ny, width = gain_ref.shape[2:]
    change = y_corrections(gain_ref, gface_ref, below_ref, above_ref)
    sums = restricted(
        list(change),
        lambda i, j: change[i, j],
        lambda d, i, j: weights_ref[d, i, j],
        0,
    )
    smooth = jnp.concatenate(sums[:2], axis=0)
    slope = jnp.concatenate(sums[2:], axis=0)
    corners = to_vertices(smooth, slope, restrict_ref[...])
    lower, upper = corners[:ny], corners[ny:]
    row = lax.broadcasted_iota(jnp.int32, lower.shape, 0)
    plane_ref[...] = own_ref[...] + lower + jnp.where(row == 0, 0.0, pltpu.roll(upper, 1, 0))


def pressure_kernel(
    side_ref, sofar_ref, gain_ref, gface_ref, outer_ref, below_ref, above_ref, inner_ref,
    pressure_out, token_ref, pressure_ref, sem,
):
    token_ref[...] = jnp.zeros_like(token_ref)
    below_ref, above_ref = below_ref.at[1], above_ref.at[0]
    ny = sofar_ref.shape[2]
    even = side_ref[0] == 0
    changes = (
        x_corrections(even, gface_ref, outer_ref, inner_ref),
        y_corrections(gain_ref, gface_ref, below_ref, above_ref),
    )
    for i in range(PTS):
        for j in range(PTS):
            value = sofar_ref[i, j]
            for change in changes:
                if (i, j) in change:
                    value = value + change[i, j]
            pressure_ref[i, pl.ds(j, ny, stride=PTS)] = value
    copy = pltpu.make_async_copy(pressure_ref, pressure_out, sem)
    copy.start()
    copy.wait()


def last_kernel(own_ref, next_ref, top_ref, token_ref, below_ref, above_ref, coarse_ref):
    ny = own_ref.shape[0]
    row = lax.broadcasted_iota(jnp.int32, own_ref.shape, 0)
    total = own_ref[...] + next_ref[:ny] + token_ref[...]
    total = total + jnp.where(row == 0, top_ref[:, :128], 0.0)
    total = total + jnp.where(row == 0, below_ref[0:1], jnp.where(row == 1, below_ref[1:2], 0.0))
    total = total + jnp.where(row == ny - 1, above_ref[2:3], 0.0)
    coarse_ref[...] = total[:, : coarse_ref.shape[1]]


def call(body, outs, scratch, *args, spaces=None, out_spaces=None):
    spaces = spaces or [pltpu.SMEM if a.dtype == jnp.int32 else pltpu.VMEM for a in args]
    return pl.pallas_call(
        body,
        out_shape=[jax.ShapeDtypeStruct(s, F32) if isinstance(s, tuple) else s for s in outs],
        in_specs=[pl.BlockSpec(memory_space=m) for m in spaces],
        out_specs=[pl.BlockSpec(memory_space=m) for m in out_spaces or [pltpu.VMEM] * len(outs)],
        scratch_shapes=[pltpu.VMEM(s, F32) if isinstance(s, tuple) else s for s in scratch],
        compiler_params=pltpu.CompilerParams(vmem_limit_bytes=16 * 1024 * 1024),
    )(*args)


def from_y(faces):
    size = lax.axis_size("sub")
    up = lax.ppermute(faces, "sub", [(i, (i + 1) % size) for i in range(size)])
    if size == 2:
        return up, up
    return up, lax.ppermute(faces, "sub", [(i, (i - 1) % size) for i in range(size)])


def inner_pairs(size):
    return [(i, i ^ 1) for i in range(size)]


def outer_pairs(size):
    return [(i, (i + 1) % size if i % 2 else (i - 1) % size) for i in range(size)]


def to_x(outer, inner):
    size = lax.axis_size("dom")
    outer = lax.ppermute(outer, "dom", outer_pairs(size))
    inner = lax.ppermute(inner, "dom", inner_pairs(size))
    return outer, inner


def two_on(rows, top):
    size, rest = lax.axis_size("dom"), lax.axis_size("sub")
    rows = lax.ppermute(rows, "dom", [(i, (i + 2) % size) for i in range(size)])
    pairs = [
        (i * rest + k, (i + 2) % size * rest + (k + 1) % rest) for i in range(size) for k in range(rest)
    ]
    return rows, lax.ppermute(top, ("dom", "sub"), pairs)


def shards(element_load, mobility, metric):
    _, _, ny, _, width = element_load.shape
    load = element_load.reshape(PTS, ny * PTS, width)
    mob = mobility.reshape(PTS, ny * PTS, width)
    metric = metric[:, 0]
    side = (lax.axis_index("dom") % 2).astype(jnp.int32).reshape(1)
    def in_hbm(*arrays):
        return [pltpu.with_memory_space_constraint(a, pltpu.HBM) for a in arrays]

    grad, back = column_tables(width)
    restrict = restrict_table(width)
    field = (PTS, PTS, ny, width)
    face = (PTS, ny, width)
    ends = (2, PTS, PTS, width)
    spread, yface = call(
        edge_kernel,
        [(3, ny, width), (2, 5, PTS, width)],
        [metric.shape, ends, ends, pltpu.SemaphoreType.DMA((5,))],
        *in_hbm(metric, mob, load),
        spaces=[pltpu.HBM] * 3,
    )
    below, above = from_y(yface)
    still = (2 * (PTS + 1) * ny, width)
    fields, xface, factor, still_outer, still_inner, weights, load_sums = call(
        diag_kernel,
        [
            (2,) + field, (2, 2) + face, (2, 2, PTS, width), still, still,
            (3,) + field, (4, ny, width),
        ],
        [],
        side, load, mob, spread,
    )
    rows = (2 * PTS * ny + 2 * PTS, width)
    outer, inner = to_x(*call(merge_kernel, [rows, rows], [], side, xface, factor, below, above))
    still_outer, still_inner = to_x(still_outer, still_inner)
    faces = (2,) + face
    rough, value, partial, gain, out, pair, edge_weights = call(
        inside_kernel,
        [
            (2,) + faces, field, field, field, field, (2,) + field,
            (2, 3, PTS, width),
        ],
        [face],
        fields, mob, spread, grad, back, below, above,
    )
    rows = ((PTS + 4) * ny + PTS, width)
    sent_outer, sent_inner, yface, gface, sofar, edge = call(
        faces_kernel,
        [rows, rows, (2, 1, PTS, width), faces, field, (PTS, width)],
        [((2 * PTS + 4) * ny, width), field],
        side, rough, value, out, pair, mob, spread, grad, back, below, above,
        partial, gain, weights, load_sums, edge_weights, outer, inner,
    )
    outer, inner = to_x(sent_outer, sent_inner)
    onward, top = call(
        ahead_kernel,
        [(3 * ny, 128), (1, (2 * PTS + 1) * 128)],
        [],
        side, sent_outer, sent_inner, gface, restrict, still_outer, still_inner,
    )
    (own,) = call(
        behind_kernel,
        [(4, ny, width)],
        [],
        side, sent_outer, sent_inner, gface, back, sofar, weights, load_sums, still_outer, still_inner,
    )
    onward, top = two_on(onward, top)
    below, above = from_y(yface)
    own_rows, tops = call(
        coarse_kernel,
        [(ny, 128), (3, 128)],
        [],
        side, gface, own, edge, weights, restrict, outer, inner,
    )
    (own_rows,) = call(
        beside_kernel, [(ny, 128)], [], own_rows, gain, gface, weights, restrict, below, above
    )
    pressure, token = call(
        pressure_kernel,
        [(PTS, ny * PTS, width), (1, 128)],
        [(PTS, ny * PTS, width), pltpu.SemaphoreType.DMA(())],
        side, sofar, gain, gface, outer, below, above, inner,
        out_spaces=[pltpu.HBM, pltpu.VMEM],
    )
    row_below, row_above = from_y(tops)
    (coarse,) = call(last_kernel, [(ny, width // PTS + 1)], [], own_rows, onward, top, token, row_below, row_above)
    return pressure.reshape(element_load.shape), coarse[None]


def solution(mesh):
    in_specs = (
        P("dom", None, "sub", None, None),
        P("dom", None, "sub", None, None),
        P(None, "dom", "sub", None),
    )
    out_specs = (P("dom", None, "sub", None, None), P("dom", "sub", None))
    return jax.shard_map(shards, mesh=mesh, in_specs=in_specs, out_specs=out_specs, check_vma=False)
```

```python
import jax
import jax.numpy as jnp
import ml_dtypes
import numpy as np
from jax import lax
from jax.experimental import pallas as pl
from jax.experimental.pallas import tpu as pltpu
from jax.sharding import PartitionSpec as P

GLL_NODES = np.array(
    [
        -1.0,
        -0.8717401485096066,
        -0.5917001814331423,
        -0.2092992179024789,
        0.2092992179024789,
        0.5917001814331423,
        0.8717401485096066,
        1.0,
    ]
)
GLL_WEIGHTS = np.array(
    [
        0.03571428571428571,
        0.2107042271435061,
        0.3411226924835044,
        0.4124587946587038,
        0.4124587946587038,
        0.3411226924835044,
        0.2107042271435061,
        0.03571428571428571,
    ]
)
THETA = 1.65
DELTA = 1.35
RHO_FIRST = DELTA / THETA
RHO_SECOND = 1.0 / (2.0 * THETA / DELTA - RHO_FIRST)
KEEP = 1.0 + RHO_SECOND * RHO_FIRST
GAIN = 2.0 * RHO_SECOND / DELTA
PTS = 8
F32 = jnp.float32


def derivative_table():
    identity = np.eye(8)
    differences = GLL_NODES[:, None] - GLL_NODES[None, :] + identity
    barycentric = 1.0 / np.prod(differences, axis=1)
    matrix = barycentric[None, :] / barycentric[:, None] / differences
    matrix = matrix * (1.0 - identity)
    row_sums = np.sum(matrix, axis=1)
    return matrix - identity * row_sums[:, None]


D = derivative_table()
W = GLL_WEIGHTS
HAT = np.stack([(1.0 - GLL_NODES) / 8.0, (1.0 + GLL_NODES) / 8.0], axis=1)
SLOPE = (-0.125, 0.125)


def tiled(matrix, width):
    column = lax.broadcasted_iota(jnp.int32, (PTS, width), 1) % PTS
    row = lax.broadcasted_iota(jnp.int32, (PTS, width), 0)
    total = jnp.zeros((PTS, width), F32)
    for c in range(PTS):
        lines = jnp.zeros((PTS, width), F32)
        for r in range(PTS):
            lines = jnp.where(row == r, float(matrix[r, c]), lines)
        total = jnp.where(column == c, lines, total)
    return total


def by_row(values, width):
    return tiled(np.tile(np.asarray(values)[:, None], (1, PTS)), width)


def cell_blocks(rows):
    width = rows.shape[1]
    cell = lax.broadcasted_iota(jnp.int32, rows.shape, 1) // PTS
    return jnp.concatenate(
        [jnp.where(cell == g, rows, 0.0) for g in range(width // PTS)], axis=0
    )


def paired_here(b):
    high, low = halves(b)
    return jnp.concatenate(
        [
            jnp.concatenate([high, low], axis=1),
            jnp.concatenate([high, jnp.zeros_like(low)], axis=1),
        ],
        axis=0,
    )


def paired(b):
    b = np.asarray(b, np.float32)
    high = b.astype(ml_dtypes.bfloat16)
    low = (b - high.astype(np.float32)).astype(ml_dtypes.bfloat16)
    return jnp.asarray(np.block([[high, low], [high, np.zeros_like(low)]]))


def column_tables(width):
    cells = np.eye(width // PTS)
    return paired(np.kron(cells, D.T)), paired(np.kron(cells, D))


def restrict_table(width):
    cells = width // PTS
    hat = np.zeros((width, 128))
    slope = np.zeros((width, 128))
    for c in range(cells):
        rows = slice(c * PTS, (c + 1) * PTS)
        hat[rows, c], hat[rows, c + 1] = HAT[:, 0], HAT[:, 1]
        slope[rows, c], slope[rows, c + 1] = SLOPE
    return paired(np.concatenate([hat, slope]))


def halves(a):
    high = a.astype(jnp.bfloat16)
    return high, (a - high.astype(F32)).astype(jnp.bfloat16)


def dot_split(a, b_pair):
    both = jnp.dot(
        jnp.concatenate(halves(a), axis=1), b_pair, preferred_element_type=F32
    )
    n = both.shape[1] // 2
    return both[:, :n] + both[:, n:]


def contract(matrix, lines, parity):
    n = len(lines)
    half = n // 2
    plus = [lines[c] + lines[n - 1 - c] for c in range(half)]
    minus = [lines[c] - lines[n - 1 - c] for c in range(half)]
    top, low = [], []
    for r in range(half):
        even = sum(float(0.5 * (matrix[r, c] + matrix[r, n - 1 - c])) * plus[c] for c in range(half))
        odd = sum(float(0.5 * (matrix[r, c] - matrix[r, n - 1 - c])) * minus[c] for c in range(half))
        top.append(even + odd)
        low.append(even - odd if parity > 0 else odd - even)
    return top + low[::-1]


def spread_metric(metric, weight_row):
    _, rows, cells = metric.shape
    width = weight_row.shape[1]
    cell = lax.broadcasted_iota(jnp.int32, (rows, width), 1) // PTS
    fill = jnp.zeros((rows, width - cells), F32)
    spread = [
        jnp.take_along_axis(jnp.concatenate([metric[d], fill], axis=1), cell, axis=1, mode="promise_in_bounds")
        for d in range(3)
    ]
    return [v * weight_row[:1] for v in spread], spread[2]


def column_masks(shape):
    lane = lax.broadcasted_iota(jnp.int32, shape, len(shape) - 1)
    up = (lane % PTS == PTS - 1) & (lane != shape[-1] - 1)
    down = (lane % PTS == 0) & (lane != 0)
    return up, down


def sum_z(v, masks):
    width = v.shape[-1]
    axis = v.ndim - 1
    up = pltpu.roll(v, width - 1, axis)
    down = pltpu.roll(v, 1, axis)
    return v + jnp.where(masks[0], up, jnp.where(masks[1], down, 0.0))


def sum_y_local(ref, ny):
    for i in range(PTS):
        low, high = ref[i, 0], ref[i, PTS - 1]
        row = lax.broadcasted_iota(jnp.int32, low.shape, 0)
        ref[i, PTS - 1] = high + jnp.where(row == ny - 1, 0.0, pltpu.roll(low, ny - 1, 0))
        ref[i, 0] = low + jnp.where(row == 0, 0.0, pltpu.roll(high, 1, 0))


def edge_planes(ref, ny):
    low = jnp.concatenate([ref[i, 0, 0:1] for i in range(PTS)], axis=0)
    high = jnp.concatenate([ref[i, PTS - 1, ny - 1 : ny] for i in range(PTS)], axis=0)
    return low, high


def plane(ref, ny):
    return lambda i, j: ref[i, pl.ds(j, ny, stride=PTS)]


def edge_kernel(metric_in, mob_in, load_in, spread_ref, yface_ref, metric_ref, mob_ref, load_ref, sems):
    ny, width = spread_ref.shape[1:]
    ends = (0, PTS - 1)
    copies = [pltpu.make_async_copy(metric_in, metric_ref, sems.at[0])]
    for n, (source, target) in enumerate(((mob_in, mob_ref), (load_in, load_ref))):
        for s, e in enumerate((0, ny - 1)):
            copies.append(
                pltpu.make_async_copy(
                    source.at[:, pl.ds(e * PTS, PTS)], target.at[s], sems.at[1 + 2 * n + s]
                )
            )
    for copy in copies:
        copy.start()
    masks = column_masks((PTS, width))
    weight_row = tiled(np.tile(W[None], (PTS, 1)), width)
    row_weight = by_row(W, width)
    squared = paired_here(cell_blocks(tiled(D * D, width)))
    squares = [by_row(D[a] ** 2, width) for a in range(PTS)]
    for copy in copies:
        copy.wait()
    spread, cell_metric = spread_metric(metric_ref[...], weight_row)
    for d in range(3):
        spread_ref[d] = spread[d]
    points = [mob_ref[s, :, ends[s]] * (float(W[ends[s]]) * row_weight) for s in range(2)]
    columns = dot_split(
        jnp.concatenate([p * weight_row for p in points], axis=0), squared
    )
    for s, e in enumerate((0, ny - 1)):
        j = ends[s]
        scale = [spread[d][e : e + 1] for d in range(3)]
        along = sum(squares[a] * points[s][a : a + 1] for a in range(PTS))
        total = along * scale[0]
        sums = [
            sum(float(D[b, j] ** power * W[b]) * mob_ref[s, :, b] for b in range(PTS))
            * row_weight
            * scale[1]
            for power in (1, 2)
        ]
        yface_ref[s, 2] = points[s] * scale[0]
        yface_ref[s, 3] = points[s] * scale[2]
        yface_ref[s, 4] = sums[0]
        column = columns[s * PTS : (s + 1) * PTS] * cell_metric[e : e + 1]
        yface_ref[s, 1] = sum_z(total + sums[1] + column, masks)
    for s in range(2):
        yface_ref[s, 0] = sum_z(load_ref[s, :, ends[s]], masks)


def diag_kernel(
    side_ref, load_ref, mob_ref, spread_ref,
    fields_ref, xface_ref, factor_ref, to_outer_ref, to_inner_ref, weights_ref, sums_ref,
):
    ny, width = fields_ref.shape[3:]
    spread = [spread_ref[d] for d in range(3)]
    square = D * D
    squared = paired_here(cell_blocks(tiled(square, width)))
    back = paired_here(cell_blocks(tiled(D, width)))
    mob, load = plane(mob_ref, ny), plane(load_ref, ny)
    diag_ref = fields_ref.at[1]
    even = side_ref[0] == 0

    def post(at, low, high):
        to_inner_ref[at : at + ny] = jnp.where(even, high, low)
        to_outer_ref[at : at + ny] = jnp.where(even, low, high)

    for d in (1, 2):
        post((2 * PTS + d - 1) * ny, spread[d], spread[d])
    for j in range(PTS):
        factor = [mob(i, j) * (float(W[i] * W[j]) * spread[0]) for i in range(PTS)]
        post(j * ny, *(sum(float(D[a, i]) * factor[a] for a in range(PTS)) for i in (0, PTS - 1)))
        post((PTS + j) * ny, *(float(W[i] * W[j]) * mob(i, j) for i in (0, PTS - 1)))
        for i, value in enumerate(contract(square.T, factor, 1)):
            diag_ref[i, j] = value
        for i, value in enumerate(contract(D.T, factor, -1)):
            weights_ref[0, i, j] = value
    for i in range(PTS):
        factor = [mob(i, j) * (float(W[i] * W[j]) * spread[1]) for j in range(PTS)]
        for j, value in enumerate(contract(square.T, factor, 1)):
            diag_ref[i, j] += value
        for j, value in enumerate(contract(D.T, factor, -1)):
            weights_ref[1, i, j] = value
    for i in range(PTS):
        factor = jnp.concatenate(
            [mob(i, j) * (float(W[i] * W[j]) * spread[2]) for j in range(PTS)], axis=0
        )
        diag_ref[i] += dot_split(factor, squared).reshape(PTS, ny, width)
        weights_ref[2, i] = dot_split(factor, back).reshape(PTS, ny, width)
        fields_ref[0, i] = jnp.stack([load(i, j) for j in range(PTS)], axis=0)
    masks = column_masks((PTS, ny, width))
    for f in range(2):
        for i in range(PTS):
            fields_ref[f, i] = sum_z(fields_ref[f, i], masks)
        sum_y_local(fields_ref.at[f], ny)
        xface_ref[f, 0] = fields_ref[f, 0]
        xface_ref[f, 1] = fields_ref[f, PTS - 1]
    row_weight = by_row(W, width)
    for s, i in enumerate((0, PTS - 1)):
        for n, e in enumerate((0, ny - 1)):
            points = mob_ref[i, e * PTS : (e + 1) * PTS] * (float(W[i]) * row_weight)
            factor_ref[s, n] = points * spread[1][e : e + 1]
    zero = jnp.zeros((ny, width), F32)
    sums = [zero] * 4
    for i in range(PTS):
        for q in range(2):
            from_load = sum(float(HAT[j, q]) * load(i, j) for j in range(PTS))
            for p in range(2):
                if HAT[i, p]:
                    sums[2 * p + q] = sums[2 * p + q] + float(HAT[i, p]) * from_load
    for n in range(4):
        sums_ref[n] = sums[n]


def merge_kernel(side_ref, xface_ref, factor_ref, below_ref, above_ref, outer_ref, inner_ref):
    below_ref, above_ref = below_ref.at[1], above_ref.at[0]
    even = side_ref[0] == 0
    fields, _, _, ny, width = xface_ref.shape
    row = lax.broadcasted_iota(jnp.int32, (ny, width), 0)
    for f in range(fields):
        for j in range(PTS):
            low, high = xface_ref[f, 0, j], xface_ref[f, 1, j]
            if j == 0:
                low = low + jnp.where(row == 0, below_ref[f, 0:1], 0.0)
                high = high + jnp.where(row == 0, below_ref[f, PTS - 1 : PTS], 0.0)
            if j == PTS - 1:
                low = low + jnp.where(row == ny - 1, above_ref[f, 0:1], 0.0)
                high = high + jnp.where(row == ny - 1, above_ref[f, PTS - 1 : PTS], 0.0)
            at = (f * PTS + j) * ny
            inner_ref[at : at + ny] = jnp.where(even, high, low)
            outer_ref[at : at + ny] = jnp.where(even, low, high)
    for n in range(2):
        at = fields * PTS * ny + n * PTS
        low, high = factor_ref[0, n], factor_ref[1, n]
        inner_ref[at : at + PTS] = jnp.where(even, high, low)
        outer_ref[at : at + PTS] = jnp.where(even, low, high)


def inside_kernel(
    fields_ref, mob_ref, spread_ref, grad_ref, back_ref, below_ref, above_ref,
    rough_ref, value_ref, partial_ref, gain_ref, out_ref, pair_ref, edge_weights_ref,
    work_ref,
):
    below_ref, above_ref = below_ref.at[1], above_ref.at[0]
    ny, width = out_ref.shape[2:]
    spread = [spread_ref[d] for d in range(3)]
    mob = plane(mob_ref, ny)
    row = lax.broadcasted_iota(jnp.int32, (ny, width), 0)
    zero = jnp.zeros((ny, width), F32)
    for i in range(PTS):
        for j in range(PTS):
            sums = [fields_ref[f, i, j] for f in range(2)]
            for f in range(2):
                if j == 0:
                    sums[f] += jnp.where(row == 0, below_ref[f, i : i + 1], 0.0)
                if j == PTS - 1:
                    sums[f] += jnp.where(row == ny - 1, above_ref[f, i : i + 1], 0.0)
            if i in (0, PTS - 1):
                for f in range(2):
                    rough_ref[f, 0 if i == 0 else 1, j] = sums[f]
                value_ref[i, j] = partial_ref[i, j] = gain_ref[i, j] = zero
            else:
                value_ref[i, j], partial_ref[i, j], gain_ref[i, j] = first_step(*sums)
    grad, back = grad_ref[...], back_ref[...]
    for j in range(PTS):
        factor = [mob(i, j) * (float(W[i] * W[j]) * spread[0]) for i in range(PTS)]
        for n, p in enumerate((0, PTS - 1)):
            coupling = contract(D.T, [float(D[a, p]) * factor[a] for a in range(PTS)], -1)
            for i in range(PTS):
                pair_ref[n, i, j] = coupling[i]
        flux = contract(D, [value_ref[i, j] for i in range(PTS)], -1)
        flux = [flux[i] * factor[i] for i in range(PTS)]
        for i, value in enumerate(contract(D.T, flux, -1)):
            out_ref[i, j] = value
    for i in range(1, PTS - 1):
        flux = contract(D, [value_ref[i, j] for j in range(PTS)], -1)
        flux = [flux[j] * (mob(i, j) * (float(W[i] * W[j]) * spread[1])) for j in range(PTS)]
        for j, value in enumerate(contract(D.T, flux, -1)):
            out_ref[i, j] += value
        work_ref[...] = dot_split(value_ref[i].reshape(PTS * ny, width), grad).reshape(PTS, ny, width)
        for j in range(PTS):
            work_ref[j] *= mob(i, j) * (float(W[i] * W[j]) * spread[2])
        out_ref[i] += dot_split(work_ref[...].reshape(PTS * ny, width), back).reshape(PTS, ny, width)
    for t, ref in enumerate((below_ref, above_ref)):
        edge_weights_ref[t, 0] = sum(by_row(D[a], width) * ref[2, a : a + 1] for a in range(PTS))
        edge_weights_ref[t, 1] = ref[4]
        edge_weights_ref[t, 2] = dot_split(ref[3], back)


def first_step(right, diagonal):
    inverse = 1.0 / diagonal
    scaled = inverse * right
    value = scaled * (1.0 / THETA)
    return value, KEEP * value + GAIN * scaled, GAIN * inverse


def faces_kernel(
    side_ref, rough_ref, value_ref, out_ref, pair_ref, mob_ref, spread_ref, grad_ref, back_ref,
    below_ref, above_ref, partial_ref, gain_ref, weights_ref, load_sums_ref, edge_weights_ref,
    outer_ref, inner_ref,
    to_outer_ref, to_inner_ref, yface_ref, gface_ref, sofar_ref, edge_ref, line_ref, work_ref,
):
    below_ref, above_ref = below_ref.at[1], above_ref.at[0]
    even = side_ref[0] == 0
    ny, width = out_ref.shape[2:]
    spread = [spread_ref[d] for d in range(3)]
    mob = plane(mob_ref, ny)
    ends = (0, PTS - 1)
    rows = (0, ny - 1)
    row = lax.broadcasted_iota(jnp.int32, (ny, width), 0)
    masks = column_masks((ny, width))

    def arrived(at, count):
        inner, outer = inner_ref[at : at + count], outer_ref[at : at + count]
        return jnp.where(even, outer, inner), jnp.where(even, inner, outer)

    value = [[None] * PTS, [None] * PTS]
    pface = [[None] * PTS, [None] * PTS]
    gface = [[None] * PTS, [None] * PTS]
    for j in range(PTS):
        load = arrived(j * ny, ny)
        diagonal = arrived((PTS + j) * ny, ny)
        for s in range(2):
            value[s][j], pface[s][j], gface[s][j] = first_step(
                rough_ref[0, s, j] + load[s], rough_ref[1, s, j] + diagonal[s]
            )
            gface_ref[s, j] = gface[s][j]
    lines = [value[s][j] for s in range(2) for j in range(PTS)]
    factors = [
        mob(ends[s], j) * (float(W[ends[s]] * W[j]) * spread[2]) for s in range(2) for j in range(PTS)
    ]
    for s in range(2):
        for t, ref in enumerate((below_ref, above_ref)):
            lines.append(value[s][ends[t]])
            factors.append(jnp.broadcast_to(ref[3, ends[s] : ends[s] + 1], (ny, width)))
    flux = dot_split(jnp.concatenate(lines, axis=0), grad_ref[...]) * jnp.concatenate(factors, axis=0)
    line_ref[...] = dot_split(flux, back_ref[...])
    edge_y = [[None, None], [None, None]]
    total = [[None] * PTS, [None] * PTS]
    for s in range(2):
        gradient = contract(D, value[s], -1)
        flux = [
            gradient[j] * (mob(ends[s], j) * (float(W[ends[s]] * W[j]) * spread[1])) for j in range(PTS)
        ]
        total[s] = contract(D.T, flux, -1)
        for t in range(2):
            factor = arrived(2 * PTS * ny + t * PTS, PTS)[s]
            edge_y[s][t] = sum(
                float(D[j, ends[t]]) * (gradient[j] * factor[j : j + 1]) for j in range(PTS)
            )[rows[t] : rows[t] + 1]
    for j in range(PTS):
        across = [
            out_ref[i, j] + (pair_ref[0, i, j] * value[0][j] + pair_ref[1, i, j] * value[1][j])
            for i in range(PTS)
        ]
        total[0][j] += across[0]
        total[1][j] += across[PTS - 1]
        for i in range(1, PTS - 1):
            work_ref[i, j] = across[i]
    for s in range(2):
        for j in range(PTS):
            at = (s * PTS + j) * ny
            total[s][j] += line_ref[at : at + ny]
    ymessage = []
    for t in range(2):
        j = ends[t]
        edge = [total[0][j]] + [work_ref[i, j] for i in range(1, PTS - 1)] + [total[1][j]]
        edge = [v[rows[t] : rows[t] + 1] for v in edge]
        edge[0] += edge_y[0][t]
        edge[PTS - 1] += edge_y[1][t]
        ymessage.append(sum_z(jnp.concatenate(edge, axis=0), column_masks((PTS, width))))
        yface_ref[t, 0] = ymessage[t]
    extra = [[None, None], [None, None]]
    for t, ref in enumerate((below_ref, above_ref)):
        j = ends[t]
        points = [value[0][j]] + [value_ref[i, j] for i in range(1, PTS - 1)] + [value[1][j]]
        flux = contract(D, points, -1)
        flux = contract(D.T, [flux[i] * ref[2, i : i + 1] for i in range(PTS)], -1)
        for s in range(2):
            at = (2 * PTS + 2 * s + t) * ny
            extra[s][t] = sum_z(flux[ends[s]] + line_ref[at : at + ny], masks)
            extra[s][t] = jnp.where(row == rows[t], extra[s][t], 0.0)
    for s in range(2):
        for j in range(PTS):
            total[s][j] = sum_z(total[s][j], masks)
        low, high = total[s][0], total[s][PTS - 1]
        total[s][PTS - 1] = high + jnp.where(row == ny - 1, 0.0, pltpu.roll(low, ny - 1, 0))
        total[s][0] = low + jnp.where(row == 0, 0.0, pltpu.roll(high, 1, 0))
    for j in range(PTS):
        low, high = total[0][j], total[1][j]
        if j in ends:
            t = ends.index(j)
            low, high = low + extra[0][t], high + extra[1][t]
        to_inner_ref[j * ny : (j + 1) * ny] = jnp.where(even, high, low)
        to_outer_ref[j * ny : (j + 1) * ny] = jnp.where(even, low, high)
        for s in range(2):
            sofar_ref[ends[s], j] = pface[s][j] - gface[s][j] * total[s][j]
    for i in range(1, PTS - 1):
        lines = [sum_z(work_ref[i, j], masks) for j in range(PTS)]
        low, high = lines[0], lines[PTS - 1]
        lines[PTS - 1] = high + jnp.where(row == ny - 1, 0.0, pltpu.roll(low, ny - 1, 0))
        lines[0] = low + jnp.where(row == 0, 0.0, pltpu.roll(high, 1, 0))
        for j in range(PTS):
            sofar_ref[i, j] = partial_ref[i, j] - gain_ref[i, j] * lines[j]
    sums = restricted(
        [(i, j) for i in range(PTS) for j in range(PTS)],
        lambda i, j: sofar_ref[i, j],
        lambda d, i, j: weights_ref[d, i, j],
        1,
    )
    for q in range(2):
        sums[q] = sums[q] + load_sums_ref[2 + q]
    base = PTS * ny
    changes = []
    for t in range(2):
        j = ends[t]
        gain = [gface[0][j]] + [gain_ref[i, j] for i in range(1, PTS - 1)] + [gface[1][j]]
        gain = jnp.concatenate([g[rows[t] : rows[t] + 1] for g in gain], axis=0)
        change = -(gain * ymessage[t])
        changes += edge_change(change, edge_weights_ref.at[t], ends[1 - t], 1)
        if t == 0:
            own = edge_change(change, edge_weights_ref.at[t], ends[1 - t], 0)
            zero = jnp.zeros_like(own[1])
            edge_ref[...] = jnp.concatenate([zero, own[1], zero, own[3]] + [zero] * 4, axis=0)
    changes = jnp.concatenate(changes, axis=0)
    for ref in (to_outer_ref, to_inner_ref):
        for n in range(4):
            ref[base + n * ny : base + (n + 1) * ny] = sums[n]
        ref[base + 4 * ny : base + 4 * ny + PTS] = changes


def edge_change(change, weight_ref, j, p):
    upper = lax.broadcasted_iota(jnp.int32, change.shape, 0)
    hat = jnp.zeros_like(change)
    for i in range(PTS):
        hat = jnp.where(upper == i, float(HAT[i, p]), hat)
    along_x, along_y, along_z = (
        jnp.sum(v, axis=0, keepdims=True)
        for v in (weight_ref[0] * change, hat * weight_ref[1] * change, hat * weight_ref[2] * change)
    )
    smooth = [-(SLOPE[p] * float(HAT[j, q]) * along_x + SLOPE[q] * along_y) for q in range(2)]
    return smooth + [-float(HAT[j, q]) * along_z for q in range(2)]


def restricted(points, value, weight, p):
    along_x, along_z, along_y = {}, {}, {}
    for i, j in points:
        v = value(i, j)
        along_x[j] = along_x.get(j, 0.0) + weight(0, i, j) * v
        if HAT[i, p]:
            along_y[i] = along_y.get(i, 0.0) + weight(1, i, j) * v
            along_z[j] = along_z.get(j, 0.0) + float(HAT[i, p]) * (weight(2, i, j) * v)
    y_sum = sum(float(HAT[i, p]) * total for i, total in along_y.items())
    smooth, slope = [], []
    for q in range(2):
        x_sum = sum(float(HAT[j, q]) * total for j, total in along_x.items() if HAT[j, q])
        smooth.append(-(SLOPE[p] * x_sum + SLOPE[q] * y_sum))
        slope.append(-sum(float(HAT[j, q]) * total for j, total in along_z.items() if HAT[j, q]))
    return smooth + slope


def x_corrections(even, gface_ref, outer_ref, inner_ref):
    ny = gface_ref.shape[2]
    change = {}
    for j in range(PTS):
        low = pick(even, outer_ref, inner_ref, j * ny, ny)
        high = pick(even, inner_ref, outer_ref, j * ny, ny)
        change[0, j] = -(gface_ref[0, j] * low)
        change[PTS - 1, j] = -(gface_ref[1, j] * high)
    return change


def y_corrections(gain_ref, gface_ref, below_ref, above_ref):
    ny, width = gain_ref.shape[2:]
    row = lax.broadcasted_iota(jnp.int32, (ny, width), 0)
    faces = {0: 0, PTS - 1: 1}
    change = {}
    for i in range(PTS):
        for j, at, ref in ((0, 0, below_ref), (PTS - 1, ny - 1, above_ref)):
            gain = gface_ref[faces[i], j] if i in faces else gain_ref[i, j]
            change[i, j] = -(gain * jnp.where(row == at, ref[0, i : i + 1], 0.0))
    return change


def face_change(change, weight, i, p, q):
    along_x = sum(float(HAT[j, q]) * (weight[0][j] * change[j]) for j in range(PTS) if HAT[j, q])
    smooth = SLOPE[p] * along_x
    slope = 0.0
    if HAT[i, p]:
        along_y = sum(weight[1][j] * change[j] for j in range(PTS))
        smooth = smooth + float(HAT[i, p]) * SLOPE[q] * along_y
        along_z = sum(float(HAT[j, q]) * (weight[2][j] * change[j]) for j in range(PTS) if HAT[j, q])
        slope = float(HAT[i, p]) * along_z
    return -smooth, -slope


def to_vertices(smooth, slope, restrict):
    return dot_split(jnp.concatenate([smooth, slope], axis=1), restrict)


def pick(even, first, second, at, count):
    return jnp.where(even, first[at : at + count], second[at : at + count])


def ahead_kernel(
    side_ref, sent_outer_ref, sent_inner_ref, gface_ref, restrict_ref, outer_ref, inner_ref,
    next_ref, top_ref,
):
    ny, width = gface_ref.shape[2:]
    even = side_ref[0] == 0
    change = [
        -(gface_ref[1, j] * pick(even, sent_inner_ref, sent_outer_ref, j * ny, ny)) for j in range(PTS)
    ]
    weight = [[pick(even, inner_ref, outer_ref, j * ny, ny) for j in range(PTS)]]
    smooth = jnp.concatenate([face_change(change, weight, 0, 1, q)[0] for q in range(2)], axis=0)
    hats = jnp.concatenate([restrict_ref[:width], restrict_ref[2 * width : 3 * width]], axis=0)
    corners = dot_split(smooth, hats)
    lower, upper = corners[:ny], corners[ny:]
    row = lax.broadcasted_iota(jnp.int32, lower.shape, 0)
    rows = lower + jnp.where(row == 0, 0.0, pltpu.roll(upper, 1, 0))
    next_ref[...] = jnp.concatenate([rows] * (next_ref.shape[0] // ny), axis=0)
    top_ref[...] = jnp.concatenate([upper[ny - 1 : ny]] * (top_ref.shape[1] // 128), axis=1)


def behind_kernel(
    side_ref, sent_outer_ref, sent_inner_ref, gface_ref, back_ref, sofar_ref, weights_ref, load_sums_ref,
    outer_ref, inner_ref,
    own_ref,
):
    ny, width = gface_ref.shape[2:]
    even = side_ref[0] == 0

    def rows(at):
        return pick(even, outer_ref, inner_ref, at, ny)

    change = [
        -(gface_ref[0, j] * pick(even, sent_outer_ref, sent_inner_ref, j * ny, ny)) for j in range(PTS)
    ]
    spread = [rows((2 * PTS + d) * ny) for d in range(2)]
    points = [rows((PTS + j) * ny) for j in range(PTS)]
    column = dot_split(jnp.concatenate([p * spread[1] for p in points], axis=0), back_ref[...])
    weight = [
        [rows(j * ny) for j in range(PTS)],
        contract(D.T, [p * spread[0] for p in points], -1),
        [column[j * ny : (j + 1) * ny] for j in range(PTS)],
    ]
    sums = restricted(
        [(i, j) for i in range(PTS) for j in range(PTS)],
        lambda i, j: sofar_ref[i, j],
        lambda d, i, j: weights_ref[d, i, j],
        0,
    )
    for q in range(2):
        smooth, slope = face_change(change, weight, PTS - 1, 1, q)
        own_ref[q] = sums[q] + load_sums_ref[q] + smooth
        own_ref[2 + q] = sums[2 + q] + slope


def coarse_kernel(
    side_ref, gface_ref, own_ref, edge_in_ref, weights_ref, restrict_ref, outer_ref, inner_ref,
    plane_ref, edge_ref,
):
    ny, width = gface_ref.shape[2:]
    even = side_ref[0] == 0
    change = x_corrections(even, gface_ref, outer_ref, inner_ref)
    sums = restricted(
        list(change),
        lambda i, j: change[i, j],
        lambda d, i, j: weights_ref[d, i, j],
        0,
    )
    base = PTS * ny

    def before(at, count):
        return pick(even, outer_ref, inner_ref, at, count)

    total = [sums[n] + own_ref[n] + before(base + n * ny, ny) for n in range(4)]
    extra = before(base + 4 * ny, PTS) + edge_in_ref[...]
    smooth = jnp.concatenate(total[:2] + [extra], axis=0)
    slope = jnp.concatenate(total[2:] + [pltpu.roll(extra, PTS - 2, 0)], axis=0)
    corners = to_vertices(smooth, slope, restrict_ref[...])
    lower, upper = corners[:ny], corners[ny : 2 * ny]
    extra = corners[2 * ny :]
    row = lax.broadcasted_iota(jnp.int32, lower.shape, 0)
    plane_ref[...] = lower + jnp.where(row == 0, extra[1:2], pltpu.roll(upper, 1, 0))
    edge_ref[0:1] = upper[ny - 1 : ny] + extra[4:5]
    edge_ref[1:2] = extra[5:6]
    edge_ref[2:3] = extra[0:1]


def beside_kernel(
    own_ref, gain_ref, gface_ref, weights_ref, restrict_ref, below_ref, above_ref,
    plane_ref,
):
    below_ref, above_ref = below_ref.at[1], above_ref.at[0]
    ny, width = gain_ref.shape[2:]
    change = y_corrections(gain_ref, gface_ref, below_ref, above_ref)
    sums = restricted(
        list(change),
        lambda i, j: change[i, j],
        lambda d, i, j: weights_ref[d, i, j],
        0,
    )
    smooth = jnp.concatenate(sums[:2], axis=0)
    slope = jnp.concatenate(sums[2:], axis=0)
    corners = to_vertices(smooth, slope, restrict_ref[...])
    lower, upper = corners[:ny], corners[ny:]
    row = lax.broadcasted_iota(jnp.int32, lower.shape, 0)
    plane_ref[...] = own_ref[...] + lower + jnp.where(row == 0, 0.0, pltpu.roll(upper, 1, 0))


def pressure_kernel(
    side_ref, sofar_ref, gain_ref, gface_ref, outer_ref, below_ref, above_ref, inner_ref,
    pressure_out, token_ref, pressure_ref, sem,
):
    token_ref[...] = jnp.zeros_like(token_ref)
    below_ref, above_ref = below_ref.at[1], above_ref.at[0]
    ny = sofar_ref.shape[2]
    even = side_ref[0] == 0
    changes = (
        x_corrections(even, gface_ref, outer_ref, inner_ref),
        y_corrections(gain_ref, gface_ref, below_ref, above_ref),
    )
    for i in range(PTS):
        for j in range(PTS):
            value = sofar_ref[i, j]
            for change in changes:
                if (i, j) in change:
                    value = value + change[i, j]
            pressure_ref[i, pl.ds(j, ny, stride=PTS)] = value
    copy = pltpu.make_async_copy(pressure_ref, pressure_out, sem)
    copy.start()
    copy.wait()


def last_kernel(own_ref, next_ref, top_ref, token_ref, below_ref, above_ref, coarse_ref):
    ny = own_ref.shape[0]
    row = lax.broadcasted_iota(jnp.int32, own_ref.shape, 0)
    total = own_ref[...] + next_ref[:ny] + token_ref[...]
    total = total + jnp.where(row == 0, top_ref[:, :128], 0.0)
    total = total + jnp.where(row == 0, below_ref[0:1], jnp.where(row == 1, below_ref[1:2], 0.0))
    total = total + jnp.where(row == ny - 1, above_ref[2:3], 0.0)
    coarse_ref[...] = total[:, : coarse_ref.shape[1]]


def call(body, outs, scratch, *args, spaces=None, out_spaces=None):
    spaces = spaces or [pltpu.SMEM if a.dtype == jnp.int32 else pltpu.VMEM for a in args]
    return pl.pallas_call(
        body,
        out_shape=[jax.ShapeDtypeStruct(s, F32) if isinstance(s, tuple) else s for s in outs],
        in_specs=[pl.BlockSpec(memory_space=m) for m in spaces],
        out_specs=[pl.BlockSpec(memory_space=m) for m in out_spaces or [pltpu.VMEM] * len(outs)],
        scratch_shapes=[pltpu.VMEM(s, F32) if isinstance(s, tuple) else s for s in scratch],
        compiler_params=pltpu.CompilerParams(vmem_limit_bytes=16 * 1024 * 1024),
    )(*args)


def from_y(faces):
    size = lax.axis_size("sub")
    up = lax.ppermute(faces, "sub", [(i, (i + 1) % size) for i in range(size)])
    if size == 2:
        return up, up
    return up, lax.ppermute(faces, "sub", [(i, (i - 1) % size) for i in range(size)])


def inner_pairs(size):
    return [(i, i ^ 1) for i in range(size)]


def outer_pairs(size):
    return [(i, (i + 1) % size if i % 2 else (i - 1) % size) for i in range(size)]


def to_x(outer, inner):
    size = lax.axis_size("dom")
    outer = lax.ppermute(outer, "dom", outer_pairs(size))
    inner = lax.ppermute(inner, "dom", inner_pairs(size))
    return outer, inner


def two_on(rows, top):
    size, rest = lax.axis_size("dom"), lax.axis_size("sub")
    rows = lax.ppermute(rows, "dom", [(i, (i + 2) % size) for i in range(size)])
    pairs = [
        (i * rest + k, (i + 2) % size * rest + (k + 1) % rest) for i in range(size) for k in range(rest)
    ]
    return rows, lax.ppermute(top, ("dom", "sub"), pairs)


def shards(element_load, mobility, metric):
    _, _, ny, _, width = element_load.shape
    load = element_load.reshape(PTS, ny * PTS, width)
    mob = mobility.reshape(PTS, ny * PTS, width)
    metric = metric[:, 0]
    side = (lax.axis_index("dom") % 2).astype(jnp.int32).reshape(1)
    def in_hbm(*arrays):
        return [pltpu.with_memory_space_constraint(a, pltpu.HBM) for a in arrays]

    grad, back = column_tables(width)
    restrict = restrict_table(width)
    field = (PTS, PTS, ny, width)
    face = (PTS, ny, width)
    ends = (2, PTS, PTS, width)
    spread, yface = call(
        edge_kernel,
        [(3, ny, width), (2, 5, PTS, width)],
        [metric.shape, ends, ends, pltpu.SemaphoreType.DMA((5,))],
        *in_hbm(metric, mob, load),
        spaces=[pltpu.HBM] * 3,
    )
    below, above = from_y(yface)
    still = (2 * (PTS + 1) * ny, width)
    fields, xface, factor, still_outer, still_inner, weights, load_sums = call(
        diag_kernel,
        [
            (2,) + field, (2, 2) + face, (2, 2, PTS, width), still, still,
            (3,) + field, (4, ny, width),
        ],
        [],
        side, load, mob, spread,
    )
    rows = (2 * PTS * ny + 2 * PTS, width)
    outer, inner = to_x(*call(merge_kernel, [rows, rows], [], side, xface, factor, below, above))
    still_outer, still_inner = to_x(still_outer, still_inner)
    faces = (2,) + face
    rough, value, partial, gain, out, pair, edge_weights = call(
        inside_kernel,
        [
            (2,) + faces, field, field, field, field, (2,) + field,
            (2, 3, PTS, width),
        ],
        [face],
        fields, mob, spread, grad, back, below, above,
    )
    rows = ((PTS + 4) * ny + PTS, width)
    sent_outer, sent_inner, yface, gface, sofar, edge = call(
        faces_kernel,
        [rows, rows, (2, 1, PTS, width), faces, field, (PTS, width)],
        [((2 * PTS + 4) * ny, width), field],
        side, rough, value, out, pair, mob, spread, grad, back, below, above,
        partial, gain, weights, load_sums, edge_weights, outer, inner,
    )
    outer, inner = to_x(sent_outer, sent_inner)
    onward, top = call(
        ahead_kernel,
        [(3 * ny, 128), (1, (3 * PTS + 1) * 128)],
        [],
        side, sent_outer, sent_inner, gface, restrict, still_outer, still_inner,
    )
    (own,) = call(
        behind_kernel,
        [(4, ny, width)],
        [],
        side, sent_outer, sent_inner, gface, back, sofar, weights, load_sums, still_outer, still_inner,
    )
    onward, top = two_on(onward, top)
    below, above = from_y(yface)
    own_rows, tops = call(
        coarse_kernel,
        [(ny, 128), (3, 128)],
        [],
        side, gface, own, edge, weights, restrict, outer, inner,
    )
    (own_rows,) = call(
        beside_kernel, [(ny, 128)], [], own_rows, gain, gface, weights, restrict, below, above
    )
    pressure, token = call(
        pressure_kernel,
        [(PTS, ny * PTS, width), (1, 128)],
        [(PTS, ny * PTS, width), pltpu.SemaphoreType.DMA(())],
        side, sofar, gain, gface, outer, below, above, inner,
        out_spaces=[pltpu.HBM, pltpu.VMEM],
    )
    row_below, row_above = from_y(tops)
    (coarse,) = call(last_kernel, [(ny, width // PTS + 1)], [], own_rows, onward, top, token, row_below, row_above)
    return pressure.reshape(element_load.shape), coarse[None]


def solution(mesh):
    in_specs = (
        P("dom", None, "sub", None, None),
        P("dom", None, "sub", None, None),
        P(None, "dom", "sub", None),
    )
    out_specs = (P("dom", None, "sub", None, None), P("dom", "sub", None))
    return jax.shard_map(shards, mesh=mesh, in_specs=in_specs, out_specs=out_specs, check_vma=False)
```
